32 devices in a mesh: dp: 8 (over z, x), fsdp: 4 (over y, core).
Axes of the slice: x: 2, y: 2, z: 4, core: 2. Of those that a mesh axis runs over, the one named last changes fastest.
Arguments:
- tokens: bfloat16 [32, 1024, 768], P(('dp', 'fsdp')), may hold values from -11 to 11
- lengths: int32 [32], P(('dp', 'fsdp')), may hold values from 256 to 1024, as said below
- buckets: int32 [2047], replicated, may hold values from 0 to 31
- rel_table: float32 [32, 12], replicated, may hold values from -4 to 4
- gain_attn: float32 [768], replicated, may hold values from 0.5 to 1.5
- gain_ff: float32 [768], replicated, may hold values from 0.5 to 1.5
- w_qkv: bfloat16 [768, 2304], replicated, may hold values from -0.21875 to 0.21875
- w_out: bfloat16 [768, 768], replicated, may hold values from -0.875 to 0.875
- w_in: bfloat16 [768, 3072], replicated, may hold values from -0.21875 to 0.21875
- w_down: bfloat16 [3072, 768], replicated, may hold values from -0.109375 to 0.109375
- adapters: bfloat16 [622080], P(('dp', 'fsdp')), may hold values from -5 to 5
- cotangent: bfloat16 [32, 1024, 768], P(('dp', 'fsdp')), may hold values from -6 to 6
Outputs:
- block_out: bfloat16 [32, 1024, 768], P(('dp', 'fsdp'))
- tokens_grad: float32 [32, 1024, 768], P(('dp', 'fsdp'))
- adapters_grad: float32 [622080], P(('dp', 'fsdp'))
- root_squares: float32 [4], replicated
The draws below stay inside these ranges and needn't reach their ends.
Inputs may be any that keep to these rules, and one draw needn't show every extreme that they name: `lengths`: each sequence's count of valid leading positions; in every draw one sequence has all 1024.
All inputs are finite; a program needn't handle non-finite values.
Results may differ from the reference program's by a relative error of at most 0.017.
Values may be sent and summed in bfloat16 or wider, within the bound.
A program may use at most 512 MiB of HBM per device.

```python
import math
import jax
import jax.numpy as jnp
from jax import lax

D = 768
FF = 3072
HEADS = 12
HDIM = 64
BUCKETS = 32
EXPERTS = 10
RANK = 4
LEN = 1024
SEQS = 32
PARAMS = 622080


def draw_tokens(key, part):
    key_noise = jax.random.fold_in(key, 11)
    key_scale = jax.random.fold_in(key, 12)
    noise_values = jnp.clip(jax.random.normal(key_noise, (SEQS, LEN, D), jnp.float32), -4.0, 4.0)
    growth = 8.0
    base_scale = 0.25
    position_ramp = jnp.arange(SEQS).astype(jnp.float32) / max(SEQS - 1, 1)
    jitter = jax.random.uniform(key_scale, (SEQS,), jnp.float32, 0.85, 1.15)
    scales = base_scale * jnp.power(growth, position_ramp) * jitter
    return (noise_values * scales[:, None, None]).astype(jnp.bfloat16)


def draw_lengths(key, part):
    base_lengths = jax.random.randint(jax.random.fold_in(key, 21), (SEQS,), LEN // 4, LEN + 1)
    chosen = jax.random.randint(jax.random.fold_in(key, 22), (), 0, SEQS)
    return jnp.where(jnp.arange(SEQS) == chosen, LEN, base_lengths).astype(jnp.int32)


def draw_adapters(key, part):
    layers = ((D, D, 1.0, 0.5), (D, D, 1.0, 0.5), (D, D, 1.0, 0.5), (D, D, 6.0, 3.0), (D, FF, 1.0, 0.5), (FF, D, 1.3, 0.6))
    members = []
    counter = 0
    for fan_in, fan_out, down_gain, router_gain in layers:
        layout = ((fan_in * EXPERTS * RANK, down_gain / math.sqrt(fan_in)), (EXPERTS * RANK * fan_out, 0.7), (fan_in * EXPERTS, router_gain / math.sqrt(fan_in)))
        for count_of, spread in layout:
            piece_key = jax.random.fold_in(key, 100 + counter)
            counter += 1
            sample = jnp.clip(jax.random.normal(piece_key, (count_of,), jnp.float32), -6.0, 6.0)
            members.append(sample * spread)
    return jnp.concatenate(members).astype(jnp.bfloat16)


def plant(values, rng, low, top_value):
    longest = values.shape.index(max(values.shape))
    spots = []
    for shift in (0, 1):
        where = [jax.random.randint(jax.random.fold_in(rng, axis), (), 0, length) for axis, length in enumerate(values.shape)]
        where[longest] = (where[longest] + shift) % values.shape[longest]
        spots.append(tuple(where))
    return values.at[spots[0]].set(low).at[spots[1]].set(top_value)


def steps_of(key, shape, shards, smallest, largest):
    level = 1.0
    for dim, blocks in shards:
        steps = jax.random.uniform(jax.random.fold_in(jax.random.fold_in(key, 6), dim), (blocks,), jnp.float32, smallest / len(shards), largest / len(shards))
        level = level * jnp.repeat(jnp.exp(steps), shape[dim] // blocks).reshape((-1,) + (1,) * (len(shape) - 1 - dim))
    return level


def normal_values(rng, dims, deviation, limit, shards=(), kind=jnp.bfloat16):
    level = steps_of(rng, dims, shards, -0.22, 0.18) if shards else 1.0
    values = jax.random.normal(rng, dims, jnp.float32) * deviation * level
    return jnp.minimum(jnp.maximum(values, -limit), limit).astype(kind)


def setup_inputs(seed: int = 0) -> dict:
    seeds = jax.random.split(jax.random.key(seed), 13)
    return {
        "tokens": draw_tokens(jax.random.fold_in(seeds[12], 71), 0),
        "lengths": draw_lengths(jax.random.fold_in(seeds[12], 71), 0),
        "buckets": plant(jax.random.randint(seeds[2], (2 * LEN - 1,), 0, BUCKETS), jax.random.fold_in(seeds[2], 1), 0, BUCKETS - 1).astype(jnp.int32),
        "rel_table": normal_values(seeds[3], (BUCKETS, HEADS), 1.0, 4.0, (), jnp.float32),
        "gain_attn": jnp.clip(1.0 + 0.1 * jax.random.normal(seeds[4], (D,), jnp.float32), 0.5, 1.5),
        "gain_ff": jnp.clip(1.0 + 0.1 * jax.random.normal(seeds[5], (D,), jnp.float32), 0.5, 1.5),
        "w_qkv": normal_values(seeds[6], (D, 3 * D), D ** -0.5, 0.21875),
        "w_out": normal_values(seeds[7], (D, D), (D // 16) ** -0.5, 0.875),
        "w_in": normal_values(seeds[8], (D, FF), D ** -0.5, 0.21875),
        "w_down": normal_values(seeds[9], (FF, D), FF ** -0.5, 0.109375),
        "adapters": draw_adapters(jax.random.fold_in(seeds[12], 71), 0),
        "cotangent": normal_values(seeds[11], (SEQS, LEN, D), 1.0, 6.0, ((0, 32),)),
    }


@jax.custom_vjp
def low(v):
    return lax.optimization_barrier(v.astype(jnp.bfloat16)).astype(jnp.float32)

@jax.custom_vjp
def low_back(v):
    return v

def low_keep(v):
    return (low(v), None)

def low_pass(kept, grad):
    return (grad,)

def back_keep(v):
    return (v, None)

def back_low(kept, grad):
    return (low(grad),)
low.defvjp(low_keep, low_pass)
low_back.defvjp(back_keep, back_low)
HIGHEST = lax.Precision.HIGHEST
EPSILON = 1e-06
MASKED = -1000000000.0
GELU_SCALE = 0.7978845608028654
GELU_CUBIC = 0.044715

def gelu_smooth(values):
    return 0.5 * values * (1.0 + jnp.tanh(GELU_SCALE * (values + GELU_CUBIC * values * values * values)))

def unpack_adapters(flat_values):
    result = []
    offset = 0
    for fan_in, fan_out in ((D, D), (D, D), (D, D), (D, D), (D, FF), (FF, D)):
        layout = (((fan_in, EXPERTS * RANK), fan_in * EXPERTS * RANK), ((EXPERTS * RANK, fan_out), EXPERTS * RANK * fan_out), ((fan_in, EXPERTS), fan_in * EXPERTS))
        members = []
        for form_of, count_of in layout:
            members.append(flat_values[offset:offset + count_of].reshape(form_of))
            offset += count_of
        result.append(tuple(members))
    return result

def rms_norm(values, gain):
    return values * lax.rsqrt(lax.optimization_barrier(jnp.mean(values * values, axis=-1, keepdims=True)) + EPSILON) * gain

def mixture(inputs, base, adapter):
    down_proj, up_proj, router = adapter
    dense_out = jnp.dot(inputs, base, precision=HIGHEST)
    logits = low_back(jnp.dot(inputs, router, precision=HIGHEST))
    gate_probs = jax.nn.softmax(logits, axis=-1)
    lowrank = low_back(jnp.dot(inputs, down_proj, precision=HIGHEST))
    mixed_rank = low(lowrank * jnp.repeat(gate_probs, RANK, axis=1))
    return dense_out + jnp.dot(mixed_rank, up_proj, precision=HIGHEST)

def forward(seq_values, flat_values, length, bias, weights, gains):
    w_qkv, w_out, w_in, w_down = weights
    gain_attn, gain_ff = gains
    pieces = unpack_adapters(flat_values)
    normed = low(rms_norm(seq_values, gain_attn))
    heads = []
    for proj_index in range(3):
        columns = w_qkv[:, proj_index * D:(proj_index + 1) * D]
        projected = low(low_back(mixture(normed, columns, pieces[proj_index])))
        heads.append(projected.reshape(LEN, HEADS, HDIM))
    raw_scores = low_back(jnp.einsum('qhd,khd->hqk', heads[0], heads[1], precision=HIGHEST))
    valid_keys = (jnp.arange(LEN) < length)[None, None, :]
    scores = jnp.where(valid_keys, raw_scores * 0.125 + bias, MASKED)
    weights_low = low(jax.nn.softmax(scores, axis=-1))
    attended = jnp.einsum('hqk,khd->qhd', weights_low, heads[2], precision=HIGHEST).reshape(LEN, D)
    attended = low(low_back(attended))
    branch = low_back(mixture(attended, w_out, pieces[3]))
    middle = seq_values + branch
    normed_ff = low(rms_norm(middle, gain_ff))
    hidden = low_back(mixture(normed_ff, w_in, pieces[4]))
    active = low(gelu_smooth(hidden))
    feed_out = low_back(mixture(active, w_down, pieces[5]))
    return (middle + feed_out, (branch, feed_out))

def reference(tokens, lengths, buckets, rel_table, gain_attn, gain_ff, w_qkv, w_out, w_in, w_down, adapters, cotangent):
    inputs_all = tokens.astype(jnp.float32)
    cot_all = cotangent.astype(jnp.float32)
    flat_params = adapters.astype(jnp.float32)
    weights = tuple((member.astype(jnp.float32) for member in (w_qkv, w_out, w_in, w_down)))
    gains = (gain_attn.astype(jnp.float32), gain_ff.astype(jnp.float32))
    offsets = jnp.arange(LEN)[None, :] - jnp.arange(LEN)[:, None] + (LEN - 1)
    bias = jnp.transpose(rel_table.astype(jnp.float32)[buckets[offsets]], (2, 0, 1))

    def step_sequence(carry, packed):
        grad_sum, square_sum = carry
        seq_in, length, seq_cot = packed

        def run(seq_values, flat_values):
            return forward(seq_values, flat_values, length, bias, weights, gains)
        output, pullback, extras = jax.vjp(run, seq_in, flat_params, has_aux=True)
        grad_in, grad_flat = pullback(seq_cot)
        branch, feed_out = extras
        valid_rows = (jnp.arange(LEN) < length).astype(jnp.float32)[:, None]
        squares = jnp.stack([jnp.sum(valid_rows * member * member) for member in (seq_in, branch, feed_out, output)])
        return ((grad_sum + grad_flat, square_sum + squares), (output.astype(jnp.bfloat16), grad_in))
    start_carry = (jnp.zeros((PARAMS,), jnp.float32), jnp.zeros((4,), jnp.float32))
    (grad_sum, square_sum), (block_out, tokens_grad) = lax.scan(step_sequence, start_carry, (inputs_all, lengths, cot_all))
    token_count = jnp.sum(lengths).astype(jnp.float32)
    root_squares = jnp.sqrt(square_sum / (token_count * D))
    return (block_out, tokens_grad, grad_sum, root_squares)
```

```python
import functools

import jax
import jax.numpy as jnp
from jax import lax
from jax.experimental import pallas as pl
from jax.experimental.pallas import tpu as pltpu
from jax.sharding import PartitionSpec as P

D = 768
FF = 3072
HEADS = 12
HDIM = 64
EXPERTS = 10
RANK = 4
COLS = EXPERTS * RANK
LANES = 128

EPSILON = 1e-06
MASKED = -1000000000.0
GELU_SCALE = 0.7978845608028654
GELU_CUBIC = 0.044715
LOG2E = 1.4426950408889634
LN2 = 0.6931471805599453
QUERY_SCALE = 0.125 * LOG2E

ROWS = 256
QBLOCK = 256
VMEM_BYTES = 60 * 1024 * 1024

F32 = jnp.float32
BF16 = jnp.bfloat16


def dot(a, b):
    return lax.dot_general(a, b, (((1,), (0,)), ((), ())), preferred_element_type=F32)


def dot_nt(a, b):
    return lax.dot_general(a, b, (((1,), (1,)), ((), ())), preferred_element_type=F32)


def dot_tn(a, b):
    return lax.dot_general(a, b, (((0,), (0,)), ((), ())), preferred_element_type=F32)


def lane_iota(shape):
    return lax.broadcasted_iota(jnp.int32, shape, 1)


def row_iota(shape):
    return lax.broadcasted_iota(jnp.int32, shape, 0)


def gates_of(logits, groups):
    lane = lane_iota(logits.shape)
    result = jnp.zeros_like(logits)
    for group in range(groups):
        inside = (lane >= group * COLS) & (lane < (group + 1) * COLS)
        peak = jnp.max(jnp.where(inside, logits, -jnp.inf), axis=-1, keepdims=True)
        weights = jnp.where(inside, jnp.exp(logits - peak), 0.0)
        total = jnp.sum(weights, axis=-1, keepdims=True)
        result = result + weights * (4.0 / total)
    return result


def gate_grads(grad_mixed, lowrank, gates, groups):
    lane = lane_iota(gates.shape)
    grad_rank = grad_mixed * gates
    product = grad_mixed * lowrank
    summed = product
    for step in range(1, RANK):
        summed = summed + pltpu.roll(product, LANES - step, 1)
    weighted = gates * product
    centre = jnp.zeros_like(gates)
    for group in range(groups):
        inside = (lane >= group * COLS) & (lane < (group + 1) * COLS)
        part = jnp.sum(jnp.where(inside, weighted, 0.0), axis=-1, keepdims=True)
        centre = centre + jnp.where(inside, part, 0.0)
    grad_logits = jnp.where(lane % RANK == 0, gates * (summed - centre), 0.0)
    return grad_rank, grad_logits


def single_forward(inputs, ar_ref):
    packed = dot(inputs, ar_ref[...])
    lane = lane_iota(packed.shape)
    gates = gates_of(pltpu.roll(packed, 64, 1), 1)
    lowrank = jnp.where(lane < COLS, packed, 0.0)
    return lowrank, gates, (lowrank * gates).astype(BF16)


def single_backward(grad_mixed, lowrank, gates):
    grad_rank, grad_logits = gate_grads(grad_mixed, lowrank, gates, 1)
    return (grad_rank + pltpu.roll(grad_logits, 64, 1)).astype(BF16)


def rms_inverse(values):
    return lax.rsqrt(jnp.mean(values * values, axis=-1, keepdims=True) + EPSILON)


def rms_backward(values, gain, inverse, grad_normed):
    weighted = grad_normed * gain
    return inverse * weighted - values * (
        inverse * inverse * inverse * jnp.mean(values * weighted, axis=-1, keepdims=True)
    )


def params(**more):
    return pltpu.CompilerParams(vmem_limit_bytes=VMEM_BYTES, **more)


def whole(shape):
    zeros = (0,) * len(shape)
    return pl.BlockSpec(shape, lambda *_: zeros)


def project_kernel(
    x_ref, gain_ref, w_ref, ar_ref, b_ref, qt_ref, k_ref, kt_ref, v_ref, vt_ref, zg_ref
):
    values = x_ref[...].astype(F32)
    normed = (values * rms_inverse(values) * gain_ref[...]).astype(BF16)
    packed = dot(normed, ar_ref[...])
    lowrank = packed[:, :LANES]
    gates = gates_of(packed[:, LANES:], 3)
    zg_ref[:, :LANES] = lowrank
    zg_ref[:, LANES:] = gates
    mixed = (lowrank * gates).astype(BF16)
    for index in range(3):
        columns = slice(index * D, (index + 1) * D)
        part = dot(normed, w_ref[:, columns]) + dot(mixed, b_ref[:, columns])
        if index == 0:
            qt_ref[...] = (part * QUERY_SCALE).astype(BF16).T
        else:
            low = part.astype(BF16)
            natural, turned = ((k_ref, kt_ref), (v_ref, vt_ref))[index - 1]
            natural[...] = low
            turned[...] = low.T


def project(x, gain, w_qkv, ar_qkv, b_qkv):
    length = x.shape[0]
    tile = pl.BlockSpec((ROWS, D), lambda i: (i, 0))
    turned = pl.BlockSpec((D, ROWS), lambda i: (0, i))
    natural_shape = jax.ShapeDtypeStruct((length, D), BF16)
    turned_shape = jax.ShapeDtypeStruct((D, length), BF16)
    return pl.pallas_call(
        project_kernel,
        grid=(length // ROWS,),
        in_specs=[
            tile,
            whole((1, D)),
            whole(w_qkv.shape),
            whole(ar_qkv.shape),
            whole(b_qkv.shape),
        ],
        out_specs=[
            turned,
            tile,
            turned,
            tile,
            turned,
            pl.BlockSpec((ROWS, 2 * LANES), lambda i: (i, 0)),
        ],
        out_shape=[
            turned_shape,
            natural_shape,
            turned_shape,
            natural_shape,
            turned_shape,
            jax.ShapeDtypeStruct((length, 2 * LANES), F32),
        ],
        compiler_params=params(),
        name="project",
    )(x, gain, w_qkv, ar_qkv, b_qkv)


def bias_table(offset_row, length):
    spread = jnp.broadcast_to(offset_row, (LANES, 2 * length))
    return pltpu.roll(spread, 2 * length - (LANES - 1), 1, stride=1, stride_axis=0)


def add_bias(scores, table_ref, start, length):
    width = scores.shape[1]
    parts = []
    for block in range(length // LANES):
        offset = start - LANES * block + (length - LANES)
        parts.append(
            scores[block * LANES : (block + 1) * LANES] + table_ref[:, offset : offset + width]
        )
    return jnp.concatenate(parts, axis=0)


def key_extras(length_ref, shape, odd):
    lane = lane_iota(shape) - (0 if odd else HDIM)
    invalid = row_iota(shape) >= length_ref[0]
    extras = jnp.where((lane == 0) & invalid, MASKED, 0.0)
    return jnp.where((lane >= 1) & (lane <= 3), 1.0, extras).astype(BF16)


def head_lanes(odd):
    lane = lane_iota((1, LANES))
    return ((lane >= HDIM) if odd else (lane < HDIM)).astype(F32).astype(BF16)


def extra_rows(rows):
    width = rows[0].shape[1]
    index = row_iota((8, width))
    block = jnp.zeros((8, width), F32)
    for place, row in enumerate(rows):
        block = jnp.where(index == place, row, block)
    return jnp.concatenate([block, jnp.zeros((HDIM - 8, width), F32)], axis=0).astype(BF16)


def split_three(row):
    high = row.astype(BF16).astype(F32)
    middle = (row - high).astype(BF16).astype(F32)
    return high, middle, row - high - middle


def join_rows(rows, extras, odd):
    return jnp.concatenate([extras, rows] if odd else [rows, extras], axis=0)


def attend_kernel(length_ref, off_ref, qt_ref, k_ref, vt_ref, o_ref, lse_ref, table, key_more):
    length = k_ref.shape[0]

    @pl.when(pl.program_id(0) == 0)
    def _():
        for odd in range(2):
            key_more[odd] = key_extras(length_ref, k_ref.shape, odd)

    for odd in range(2):
        half = slice(odd * HDIM, (odd + 1) * HDIM)
        table[odd] = bias_table(off_ref[0, odd : odd + 1, :], length)
        keys = k_ref[...] * head_lanes(odd) + key_more[odd]
        ones = jnp.ones((1, length), F32)
        queries = join_rows(qt_ref[half, :], extra_rows([ones]), odd)
        values = jnp.concatenate([vt_ref[half, :], jnp.ones((16, length), BF16)], axis=0)
        for start in range(0, length, QBLOCK):
            columns = slice(start, start + QBLOCK)
            scores = add_bias(dot(keys, queries[:, columns]), table.at[odd], start, length)
            peak = jnp.max(scores, axis=0, keepdims=True)
            weights = jnp.exp2(scores - peak).astype(BF16)
            summed = dot(values, weights)
            total = summed[HDIM : HDIM + 1]
            o_ref[half, columns] = (summed[:HDIM] / total).astype(BF16)
            lse_ref[0, odd : odd + 1, columns] = peak + jnp.log2(total)


def attend(length_valid, offsets, qt, k, vt):
    length = k.shape[0]
    turned = pl.BlockSpec((LANES, length), lambda p: (p, 0))
    natural = pl.BlockSpec((length, LANES), lambda p: (0, p))
    pair_rows = pl.BlockSpec((1, 2, 2 * length), lambda p: (p, 0, 0))
    return pl.pallas_call(
        attend_kernel,
        grid=(HEADS // 2,),
        in_specs=[
            pl.BlockSpec(memory_space=pltpu.SMEM),
            pair_rows,
            turned,
            natural,
            turned,
        ],
        out_specs=[turned, pl.BlockSpec((1, 2, length), lambda p: (p, 0, 0))],
        out_shape=[
            jax.ShapeDtypeStruct((D, length), BF16),
            jax.ShapeDtypeStruct((HEADS // 2, 2, length), F32),
        ],
        scratch_shapes=[
            pltpu.VMEM((2, LANES, 2 * length), F32),
            pltpu.VMEM((2, length, LANES), BF16),
        ],
        compiler_params=params(),
        name="attend",
    )(length_valid, offsets, qt, k, vt)


def attend_back_kernel(
    length_ref,
    off_ref,
    qt_ref,
    k_ref,
    kt_ref,
    v_ref,
    ot_ref,
    gt_ref,
    lse_ref,
    dq_ref,
    dk_ref,
    dv_ref,
    table,
    key_more,
    weights_all,
    grads_all,
):
    length = k_ref.shape[0]

    @pl.when(pl.program_id(0) == 0)
    def _():
        for odd in range(2):
            key_more[odd] = key_extras(length_ref, k_ref.shape, odd)

    lane = lane_iota((1, LANES))
    first_lanes = lane < HDIM
    grad_query_parts = []
    for odd in range(2):
        half = slice(odd * HDIM, (odd + 1) * HDIM)
        table[odd] = bias_table(off_ref[0, odd : odd + 1, :], length)
        keys = k_ref[...] * head_lanes(odd) + key_more[odd]
        place = lane - (0 if odd else HDIM)
        value_more = ((place >= 0) & (place < 3)).astype(F32).astype(BF16)
        values = v_ref[...] * head_lanes(odd) + value_more
        ones = jnp.ones((1, length), F32)
        lse = lse_ref[0, odd : odd + 1, :]
        queries = join_rows(
            qt_ref[half, :], extra_rows([ones] + [-part for part in split_three(lse)]), odd
        )
        delta = jnp.sum(
            ot_ref[half, :].astype(F32) * gt_ref[half, :].astype(F32), axis=0, keepdims=True
        )
        grads = join_rows(
            gt_ref[half, :], extra_rows([-part for part in split_three(delta)]), odd
        )
        for start in range(0, length, QBLOCK):
            columns = slice(start, start + QBLOCK)
            scores = add_bias(dot(keys, queries[:, columns]), table.at[odd], start, length)
            weights = jnp.exp2(scores)
            weights_all[:, columns] = weights.astype(BF16)
            grad_scores = weights * dot(values, grads[:, columns])
            grads_all[:, columns] = grad_scores.astype(BF16)
        grad_query_parts.append(dot(kt_ref[half, :], grads_all[...]) * 0.125)
        grad_values = dot_nt(weights_all[...], gt_ref[...])
        grad_keys = dot_nt(grads_all[...], qt_ref[...]) * LN2
        if odd:
            dv_ref[...] = jnp.where(first_lanes, even_values, grad_values).astype(BF16)
            dk_ref[...] = jnp.where(first_lanes, even_keys, grad_keys).astype(BF16)
        else:
            even_values, even_keys = grad_values, grad_keys
    dq_ref[...] = jnp.concatenate(grad_query_parts, axis=0).T.astype(BF16)


def attend_back(length_valid, offsets, qt, k, kt, v, ot, gt, lse):
    length = k.shape[0]
    turned = pl.BlockSpec((LANES, length), lambda p: (p, 0))
    natural = pl.BlockSpec((length, LANES), lambda p: (0, p))
    pair_rows = pl.BlockSpec((1, 2, 2 * length), lambda p: (p, 0, 0))
    natural_shape = jax.ShapeDtypeStruct((length, D), BF16)
    return pl.pallas_call(
        attend_back_kernel,
        grid=(HEADS // 2,),
        in_specs=[
            pl.BlockSpec(memory_space=pltpu.SMEM),
            pair_rows,
            turned,
            natural,
            turned,
            natural,
            turned,
            turned,
            pl.BlockSpec((1, 2, length), lambda p: (p, 0, 0)),
        ],
        out_specs=[natural] * 3,
        out_shape=[natural_shape] * 3,
        scratch_shapes=[
            pltpu.VMEM((2, LANES, 2 * length), F32),
            pltpu.VMEM((2, length, LANES), BF16),
            pltpu.VMEM((length, length), BF16),
            pltpu.VMEM((length, length), BF16),
        ],
        compiler_params=params(),
        name="attend_back",
    )(length_valid, offsets, qt, k, kt, v, ot, gt, lse)


def middle_kernel(
    length_ref,
    ot_ref,
    x_ref,
    cot_ref,
    gain_ref,
    w_out_ref,
    w_in_ref,
    w_down_ref,
    ar_out_ref,
    b_out_ref,
    ar_in_ref,
    b_in_ref,
    ar_down_ref,
    b_down_ref,
    out_ref,
    dmid_ref,
    gt_ref,
    sums_ref,
    dar_out_ref,
    db_out_ref,
    dar_in_ref,
    db_in_ref,
    dar_down_ref,
    db_down_ref,
):
    step = pl.program_id(0)

    @pl.when(step == 0)
    def _():
        for ref in (
            sums_ref,
            dar_out_ref,
            db_out_ref,
            dar_in_ref,
            db_in_ref,
            dar_down_ref,
            db_down_ref,
        ):
            ref[...] = jnp.zeros_like(ref)

    attended = ot_ref[...].T
    inputs = x_ref[...].astype(F32)
    gain = gain_ref[...]
    low_out, gates_out, mixed_out = single_forward(attended, ar_out_ref)
    branch = dot(attended, w_out_ref[...]) + dot(mixed_out, b_out_ref[...])
    middle = inputs + branch
    inverse = rms_inverse(middle)
    normed = (middle * inverse * gain).astype(BF16)
    low_in, gates_in, mixed_in = single_forward(normed, ar_in_ref)
    hidden = dot(normed, w_in_ref[...]) + dot(mixed_in, b_in_ref[...])
    square = hidden * hidden
    tangent = jnp.tanh(hidden * (GELU_SCALE + (GELU_SCALE * GELU_CUBIC) * square))
    half = 0.5 + 0.5 * tangent
    smooth = hidden * half
    slope = half + smooth * (1.0 - tangent) * (
        GELU_SCALE + (3.0 * GELU_SCALE * GELU_CUBIC) * square
    )
    active = smooth.astype(BF16)
    low_down, gates_down, mixed_down = single_forward(active, ar_down_ref)
    feed = dot(active, w_down_ref[...]) + dot(mixed_down, b_down_ref[...])
    output = middle + feed
    out_ref[...] = output.astype(BF16)

    rows = row_iota((ROWS, 1)) + step * ROWS
    valid = (rows < length_ref[0]).astype(F32)
    lane = lane_iota((8, LANES))
    totals = jnp.zeros((8, LANES), F32)
    for place, member in enumerate((inputs, branch, feed, output)):
        kept = member * valid
        totals = jnp.where(lane == place, jnp.sum(kept * kept), totals)
    sums_ref[...] += totals

    cot = cot_ref[...]
    delta_down = single_backward(dot_nt(cot, b_down_ref[...]), low_down, gates_down)
    grad_active = dot_nt(cot, w_down_ref[...]) + dot_nt(delta_down, ar_down_ref[...])
    grad_hidden = (grad_active * slope).astype(BF16)
    dar_down_ref[...] += dot_tn(delta_down, active)
    db_down_ref[...] += dot_tn(mixed_down, cot)

    delta_in = single_backward(dot_nt(grad_hidden, b_in_ref[...]), low_in, gates_in)
    grad_normed = dot_nt(grad_hidden, w_in_ref[...]) + dot_nt(delta_in, ar_in_ref[...])
    dar_in_ref[...] += dot_tn(delta_in, normed)
    db_in_ref[...] += dot_tn(mixed_in, grad_hidden)

    grad_middle = cot.astype(F32) + rms_backward(middle, gain, inverse, grad_normed)
    dmid_ref[...] = grad_middle
    grad_branch = grad_middle.astype(BF16)
    delta_out = single_backward(dot_nt(grad_branch, b_out_ref[...]), low_out, gates_out)
    grad_attended = dot_nt(grad_branch, w_out_ref[...]) + dot_nt(delta_out, ar_out_ref[...])
    gt_ref[...] = grad_attended.astype(BF16).T
    dar_out_ref[...] += dot_tn(delta_out, attended)
    db_out_ref[...] += dot_tn(mixed_out, grad_branch)


def middle_part(length_valid, ot, x, cot, gain, w_out, w_in, w_down, adapters):
    length = x.shape[0]
    tile = pl.BlockSpec((ROWS, D), lambda i: (i, 0))
    turned = pl.BlockSpec((D, ROWS), lambda i: (0, i))
    grad_shapes = [
        jax.ShapeDtypeStruct((LANES, width), F32) for width in (D, D, D, FF, FF, D)
    ]
    out_shape = [
        jax.ShapeDtypeStruct((length, D), BF16),
        jax.ShapeDtypeStruct((length, D), F32),
        jax.ShapeDtypeStruct((D, length), BF16),
        jax.ShapeDtypeStruct((8, LANES), F32),
    ] + grad_shapes
    return pl.pallas_call(
        middle_kernel,
        grid=(length // ROWS,),
        in_specs=[pl.BlockSpec(memory_space=pltpu.SMEM), turned, tile, tile]
        + [whole(member.shape) for member in (gain, w_out, w_in, w_down, *adapters)],
        out_specs=[tile, tile, turned] + [whole(member.shape) for member in out_shape[3:]],
        out_shape=out_shape,
        compiler_params=params(),
        name="middle_part",
    )(length_valid, ot, x, cot, gain, w_out, w_in, w_down, *adapters)


def project_back_kernel(
    x_ref,
    gain_ref,
    w_ref,
    ar_ref,
    b_ref,
    zg_ref,
    dq_ref,
    dk_ref,
    dv_ref,
    dmid_ref,
    out_ref,
    dar_ref,
    db_ref,
):
    @pl.when(pl.program_id(0) == 0)
    def _():
        dar_ref[...] = jnp.zeros_like(dar_ref)
        db_ref[...] = jnp.zeros_like(db_ref)

    values = x_ref[...].astype(F32)
    gain = gain_ref[...]
    inverse = rms_inverse(values)
    normed = (values * inverse * gain).astype(BF16)
    lowrank = zg_ref[:, :LANES]
    gates = zg_ref[:, LANES:]
    mixed = (lowrank * gates).astype(BF16)
    grads = (dq_ref[...], dk_ref[...], dv_ref[...])
    grad_normed = jnp.zeros((ROWS, D), F32)
    grad_mixed = jnp.zeros((ROWS, LANES), F32)
    for index, grad in enumerate(grads):
        columns = slice(index * D, (index + 1) * D)
        grad_mixed = grad_mixed + dot_nt(grad, b_ref[:, columns])
        grad_normed = grad_normed + dot_nt(grad, w_ref[:, columns])
        db_ref[:, columns] += dot_tn(mixed, grad)
    grad_rank, grad_logits = gate_grads(grad_mixed, lowrank, gates, 3)
    delta = jnp.concatenate([grad_rank, grad_logits], axis=1).astype(BF16)
    grad_normed = grad_normed + dot_nt(delta, ar_ref[...])
    dar_ref[...] += dot_tn(delta, normed)
    out_ref[...] = dmid_ref[...] + rms_backward(values, gain, inverse, grad_normed)


def project_back(x, gain, w_qkv, ar_qkv, b_qkv, zg, dq, dk, dv, dmid):
    length = x.shape[0]
    tile = pl.BlockSpec((ROWS, D), lambda i: (i, 0))
    out_shape = [
        jax.ShapeDtypeStruct((length, D), F32),
        jax.ShapeDtypeStruct((2 * LANES, D), F32),
        jax.ShapeDtypeStruct((LANES, 3 * D), F32),
    ]
    return pl.pallas_call(
        project_back_kernel,
        grid=(length // ROWS,),
        in_specs=[
            tile,
            whole((1, D)),
            whole(w_qkv.shape),
            whole(ar_qkv.shape),
            whole(b_qkv.shape),
            pl.BlockSpec((ROWS, 2 * LANES), lambda i: (i, 0)),
            tile,
            tile,
            tile,
            tile,
        ],
        out_specs=[tile] + [whole(member.shape) for member in out_shape[1:]],
        out_shape=out_shape,
        compiler_params=params(),
        name="project_back",
    )(x, gain, w_qkv, ar_qkv, b_qkv, zg, dq, dk, dv, dmid)


def unpack_adapters(flat_values):
    result = []
    offset = 0
    for fan_in, fan_out in ((D, D), (D, D), (D, D), (D, D), (D, FF), (FF, D)):
        members = []
        for form in ((fan_in, COLS), (COLS, fan_out), (fan_in, EXPERTS)):
            count = form[0] * form[1]
            members.append(flat_values[offset : offset + count].reshape(form))
            offset += count
        result.append(tuple(members))
    return result


def pack_single(piece):
    down, up, router = piece
    wide = jnp.repeat(router, RANK, axis=1)
    zeros = jnp.zeros((down.shape[0], 64 - COLS), down.dtype)
    packed = jnp.concatenate([down, zeros, wide, zeros], axis=1)
    return packed, jnp.pad(up, ((0, LANES - COLS), (0, 0)))


def pack_three(pieces):
    zeros = jnp.zeros((D, LANES - 3 * COLS), pieces[0][0].dtype)
    packed = jnp.concatenate(
        [piece[0] for piece in pieces]
        + [zeros]
        + [jnp.repeat(piece[2], RANK, axis=1) for piece in pieces]
        + [zeros],
        axis=1,
    )
    ups = [
        jnp.pad(piece[1], ((index * COLS, LANES - (index + 1) * COLS), (0, 0)))
        for index, piece in enumerate(pieces)
    ]
    return packed, jnp.concatenate(ups, axis=1)


def per_device(
    tokens,
    lengths,
    buckets,
    rel_table,
    gain_attn,
    gain_ff,
    w_qkv,
    w_out,
    w_in,
    w_down,
    adapters,
    cotangent,
    axes,
):
    seq_count, length, width = tokens.shape
    x = tokens.reshape(length, width)
    cot = cotangent.reshape(length, width)
    pieces = unpack_adapters(lax.all_gather(adapters, axes, axis=0, tiled=True))
    gain_first = gain_attn.reshape(1, width)
    gain_second = gain_ff.reshape(1, width)

    reversed_buckets = jnp.pad(buckets[::-1], (0, 1))
    hits = (jnp.arange(rel_table.shape[0])[:, None] == reversed_buckets[None, :]).astype(F32)
    offsets = jnp.dot(rel_table.T * LOG2E, hits, precision=lax.Precision.HIGHEST)
    offsets = offsets.reshape(HEADS // 2, 2, 2 * length)

    ar_qkv, b_qkv = pack_three(pieces[:3])
    rest = [member for piece in pieces[3:] for member in pack_single(piece)]

    qt, k, kt, v, vt, zg = project(x, gain_first, w_qkv, ar_qkv, b_qkv)
    ot, lse = attend(lengths, offsets, qt, k, vt)
    block_out, dmid, gt, sums, *grads = middle_part(
        lengths, ot, x, cot, gain_second, w_out, w_in, w_down, rest
    )
    totals, token_count = lax.psum((sums[0, :4], jnp.sum(lengths).astype(F32)), axes)
    root_squares = jnp.sqrt(totals / (token_count * width))
    dq, dk, dv = attend_back(lengths, offsets, qt, k, kt, v, ot, gt, lse)
    tokens_grad, dar_qkv, db_qkv = project_back(
        x, gain_first, w_qkv, ar_qkv, b_qkv, zg, dq, dk, dv, dmid
    )

    flat = []
    for index in range(3):
        first = index * COLS
        flat.append(dar_qkv[first : first + COLS].T)
        flat.append(db_qkv[first : first + COLS, index * D : (index + 1) * D])
        flat.append(dar_qkv[LANES + first : LANES + first + COLS : RANK].T)
    for index in range(3):
        dar, db = grads[2 * index], grads[2 * index + 1]
        flat.append(dar[:COLS].T)
        flat.append(db[:COLS])
        flat.append(dar[64 : 64 + COLS : RANK].T)
    flat_grad = jnp.concatenate([member.reshape(-1) for member in flat])
    grad_shard = lax.psum_scatter(flat_grad, axes, scatter_dimension=0, tiled=True)
    return (
        block_out.reshape(tokens.shape),
        tokens_grad.reshape(tokens.shape),
        grad_shard,
        root_squares,
    )


def solution(mesh):
    axes = tuple(mesh.axis_names)
    sequence = P(axes, None, None)
    placed = (
        sequence,
        P(axes),
        P(),
        P(),
        P(),
        P(),
        P(),
        P(),
        P(),
        P(),
        P(axes),
        sequence,
    )
    return jax.shard_map(
        functools.partial(per_device, axes=axes),
        mesh=mesh,
        in_specs=placed,
        out_specs=(sequence, sequence, P(axes), P()),
        check_vma=False,
    )
```

```python
import functools

import jax
import jax.numpy as jnp
from jax import lax
from jax.experimental import pallas as pl
from jax.experimental.pallas import tpu as pltpu
from jax.sharding import PartitionSpec as P

D = 768
FF = 3072
HEADS = 12
HDIM = 64
EXPERTS = 10
RANK = 4
COLS = EXPERTS * RANK
LANES = 128

EPSILON = 1e-06
MASKED = -1000000000.0
GELU_SCALE = 0.7978845608028654
GELU_CUBIC = 0.044715
LOG2E = 1.4426950408889634
LN2 = 0.6931471805599453
QUERY_SCALE = 0.125 * LOG2E

ROWS = 256
QBLOCK = 256
VMEM_BYTES = 60 * 1024 * 1024

F32 = jnp.float32
BF16 = jnp.bfloat16


def dot(a, b):
    return lax.dot_general(a, b, (((1,), (0,)), ((), ())), preferred_element_type=F32)


def dot_nt(a, b):
    return lax.dot_general(a, b, (((1,), (1,)), ((), ())), preferred_element_type=F32)


def dot_tn(a, b):
    return lax.dot_general(a, b, (((0,), (0,)), ((), ())), preferred_element_type=F32)


def lane_iota(shape):
    return lax.broadcasted_iota(jnp.int32, shape, 1)


def row_iota(shape):
    return lax.broadcasted_iota(jnp.int32, shape, 0)


def gates_of(logits, groups):
    lane = lane_iota(logits.shape)
    result = jnp.zeros_like(logits)
    for group in range(groups):
        inside = (lane >= group * COLS) & (lane < (group + 1) * COLS)
        peak = jnp.max(jnp.where(inside, logits, -jnp.inf), axis=-1, keepdims=True)
        weights = jnp.where(inside, jnp.exp(logits - peak), 0.0)
        total = jnp.sum(weights, axis=-1, keepdims=True)
        result = result + weights * (4.0 / total)
    return result


def gate_grads(grad_mixed, lowrank, gates, groups):
    lane = lane_iota(gates.shape)
    grad_rank = grad_mixed * gates
    product = grad_mixed * lowrank
    summed = product
    for step in range(1, RANK):
        summed = summed + pltpu.roll(product, LANES - step, 1)
    weighted = gates * product
    centre = jnp.zeros_like(gates)
    for group in range(groups):
        inside = (lane >= group * COLS) & (lane < (group + 1) * COLS)
        part = jnp.sum(jnp.where(inside, weighted, 0.0), axis=-1, keepdims=True)
        centre = centre + jnp.where(inside, part, 0.0)
    grad_logits = jnp.where(lane % RANK == 0, gates * (summed - centre), 0.0)
    return grad_rank, grad_logits


def single_forward(inputs, ar_ref):
    packed = dot(inputs, ar_ref[...])
    lane = lane_iota(packed.shape)
    gates = gates_of(pltpu.roll(packed, 64, 1), 1)
    lowrank = jnp.where(lane < COLS, packed, 0.0)
    return lowrank, gates, (lowrank * gates).astype(BF16)


def single_backward(grad_mixed, lowrank, gates):
    grad_rank, grad_logits = gate_grads(grad_mixed, lowrank, gates, 1)
    return (grad_rank + pltpu.roll(grad_logits, 64, 1)).astype(BF16)


def rms_inverse(values):
    return lax.rsqrt(jnp.mean(values * values, axis=-1, keepdims=True) + EPSILON)


def rms_backward(values, gain, inverse, grad_normed):
    weighted = grad_normed * gain
    return inverse * weighted - values * (
        inverse * inverse * inverse * jnp.mean(values * weighted, axis=-1, keepdims=True)
    )


def params(**more):
    return pltpu.CompilerParams(vmem_limit_bytes=VMEM_BYTES, **more)


def whole(shape):
    zeros = (0,) * len(shape)
    return pl.BlockSpec(shape, lambda *_: zeros)


def project_kernel(
    x_ref, gain_ref, w_ref, ar_ref, b_ref, qt_ref, k_ref, kt_ref, v_ref, vt_ref, zg_ref
):
    values = x_ref[...].astype(F32)
    normed = (values * rms_inverse(values) * gain_ref[...]).astype(BF16)
    packed = dot(normed, ar_ref[...])
    lowrank = packed[:, :LANES]
    gates = gates_of(packed[:, LANES:], 3)
    zg_ref[:, :LANES] = lowrank
    zg_ref[:, LANES:] = gates
    mixed = (lowrank * gates).astype(BF16)
    for index in range(3):
        columns = slice(index * D, (index + 1) * D)
        part = dot(normed, w_ref[:, columns]) + dot(mixed, b_ref[:, columns])
        if index == 0:
            qt_ref[...] = (part * QUERY_SCALE).astype(BF16).T
        else:
            low = part.astype(BF16)
            natural, turned = ((k_ref, kt_ref), (v_ref, vt_ref))[index - 1]
            natural[...] = low
            turned[...] = low.T


def project(x, gain, w_qkv, ar_qkv, b_qkv):
    length = x.shape[0]
    tile = pl.BlockSpec((ROWS, D), lambda i: (i, 0))
    turned = pl.BlockSpec((D, ROWS), lambda i: (0, i))
    natural_shape = jax.ShapeDtypeStruct((length, D), BF16)
    turned_shape = jax.ShapeDtypeStruct((D, length), BF16)
    return pl.pallas_call(
        project_kernel,
        grid=(length // ROWS,),
        in_specs=[
            tile,
            whole((1, D)),
            whole(w_qkv.shape),
            whole(ar_qkv.shape),
            whole(b_qkv.shape),
        ],
        out_specs=[
            turned,
            tile,
            turned,
            tile,
            turned,
            pl.BlockSpec((ROWS, 2 * LANES), lambda i: (i, 0)),
        ],
        out_shape=[
            turned_shape,
            natural_shape,
            turned_shape,
            natural_shape,
            turned_shape,
            jax.ShapeDtypeStruct((length, 2 * LANES), F32),
        ],
        compiler_params=params(),
        name="project",
    )(x, gain, w_qkv, ar_qkv, b_qkv)


def bias_table(offset_row, length):
    spread = jnp.broadcast_to(offset_row, (LANES, 2 * length))
    return pltpu.roll(spread, 2 * length - (LANES - 1), 1, stride=1, stride_axis=0)


def add_bias(scores, table_ref, start, length):
    width = scores.shape[1]
    parts = []
    for block in range(length // LANES):
        offset = start - LANES * block + (length - LANES)
        parts.append(
            scores[block * LANES : (block + 1) * LANES] + table_ref[:, offset : offset + width]
        )
    return jnp.concatenate(parts, axis=0)


def key_extras(length_ref, shape, odd):
    lane = lane_iota(shape) - (0 if odd else HDIM)
    invalid = row_iota(shape) >= length_ref[0]
    extras = jnp.where((lane == 0) & invalid, MASKED, 0.0)
    return jnp.where((lane >= 1) & (lane <= 3), 1.0, extras).astype(BF16)


def head_lanes(odd):
    lane = lane_iota((1, LANES))
    return ((lane >= HDIM) if odd else (lane < HDIM)).astype(F32).astype(BF16)


def extra_rows(rows):
    width = rows[0].shape[1]
    index = row_iota((8, width))
    block = jnp.zeros((8, width), F32)
    for place, row in enumerate(rows):
        block = jnp.where(index == place, row, block)
    return jnp.concatenate([block, jnp.zeros((HDIM - 8, width), F32)], axis=0).astype(BF16)


def split_three(row):
    high = row.astype(BF16).astype(F32)
    middle = (row - high).astype(BF16).astype(F32)
    return high, middle, row - high - middle


def join_rows(rows, extras, odd):
    return jnp.concatenate([extras, rows] if odd else [rows, extras], axis=0)


def attend_kernel(length_ref, off_ref, qt_ref, k_ref, vt_ref, o_ref, lse_ref, table, key_more):
    length = k_ref.shape[0]

    @pl.when(pl.program_id(0) == 0)
    def _():
        for odd in range(2):
            key_more[odd] = key_extras(length_ref, k_ref.shape, odd)

    for odd in range(2):
        half = slice(odd * HDIM, (odd + 1) * HDIM)
        table[odd] = bias_table(off_ref[0, odd : odd + 1, :], length)
        keys = k_ref[...] * head_lanes(odd) + key_more[odd]
        ones = jnp.ones((1, length), F32)
        queries = join_rows(qt_ref[half, :], extra_rows([ones]), odd)
        values = jnp.concatenate([vt_ref[half, :], jnp.ones((16, length), BF16)], axis=0)
        for start in range(0, length, QBLOCK):
            columns = slice(start, start + QBLOCK)
            scores = add_bias(dot(keys, queries[:, columns]), table.at[odd], start, length)
            peak = jnp.max(scores, axis=0, keepdims=True)
            weights = jnp.exp2(scores - peak).astype(BF16)
            summed = dot(values, weights)
            total = summed[HDIM : HDIM + 1]
            o_ref[half, columns] = (summed[:HDIM] / total).astype(BF16)
            lse_ref[0, odd : odd + 1, columns] = peak + jnp.log2(total)


def attend(length_valid, offsets, qt, k, vt):
    length = k.shape[0]
    turned = pl.BlockSpec((LANES, length), lambda p: (p, 0))
    natural = pl.BlockSpec((length, LANES), lambda p: (0, p))
    pair_rows = pl.BlockSpec((1, 2, 2 * length), lambda p: (p, 0, 0))
    return pl.pallas_call(
        attend_kernel,
        grid=(HEADS // 2,),
        in_specs=[
            pl.BlockSpec(memory_space=pltpu.SMEM),
            pair_rows,
            turned,
            natural,
            turned,
        ],
        out_specs=[turned, pl.BlockSpec((1, 2, length), lambda p: (p, 0, 0))],
        out_shape=[
            jax.ShapeDtypeStruct((D, length), BF16),
            jax.ShapeDtypeStruct((HEADS // 2, 2, length), F32),
        ],
        scratch_shapes=[
            pltpu.VMEM((2, LANES, 2 * length), F32),
            pltpu.VMEM((2, length, LANES), BF16),
        ],
        compiler_params=params(),
        name="attend",
    )(length_valid, offsets, qt, k, vt)


def attend_back_kernel(
    length_ref,
    off_ref,
    qt_ref,
    k_ref,
    kt_ref,
    v_ref,
    ot_ref,
    gt_ref,
    lse_ref,
    dq_ref,
    dk_ref,
    dv_ref,
    table,
    key_more,
    weights_all,
    grads_all,
):
    length = k_ref.shape[0]

    @pl.when(pl.program_id(0) == 0)
    def _():
        for odd in range(2):
            key_more[odd] = key_extras(length_ref, k_ref.shape, odd)

    lane = lane_iota((1, LANES))
    first_lanes = lane < HDIM
    grad_query_parts = []
    for odd in range(2):
        half = slice(odd * HDIM, (odd + 1) * HDIM)
        table[odd] = bias_table(off_ref[0, odd : odd + 1, :], length)
        keys = k_ref[...] * head_lanes(odd) + key_more[odd]
        place = lane - (0 if odd else HDIM)
        value_more = ((place >= 0) & (place < 3)).astype(F32).astype(BF16)
        values = v_ref[...] * head_lanes(odd) + value_more
        ones = jnp.ones((1, length), F32)
        lse = lse_ref[0, odd : odd + 1, :]
        queries = join_rows(
            qt_ref[half, :], extra_rows([ones] + [-part for part in split_three(lse)]), odd
        )
        delta = jnp.sum(
            ot_ref[half, :].astype(F32) * gt_ref[half, :].astype(F32), axis=0, keepdims=True
        )
        grads = join_rows(
            gt_ref[half, :], extra_rows([-part for part in split_three(delta)]), odd
        )
        for start in range(0, length, QBLOCK):
            columns = slice(start, start + QBLOCK)
            scores = add_bias(dot(keys, queries[:, columns]), table.at[odd], start, length)
            weights = jnp.exp2(scores)
            weights_all[:, columns] = weights.astype(BF16)
            grad_scores = weights * dot(values, grads[:, columns])
            grads_all[:, columns] = grad_scores.astype(BF16)
        grad_query_parts.append(dot(kt_ref[half, :], grads_all[...]) * 0.125)
        grad_values = dot_nt(weights_all[...], gt_ref[...])
        grad_keys = dot_nt(grads_all[...], qt_ref[...]) * LN2
        if odd:
            dv_ref[...] = jnp.where(first_lanes, even_values, grad_values).astype(BF16)
            dk_ref[...] = jnp.where(first_lanes, even_keys, grad_keys).astype(BF16)
        else:
            even_values, even_keys = grad_values, grad_keys
    dq_ref[...] = jnp.concatenate(grad_query_parts, axis=0).T.astype(BF16)


def attend_back(length_valid, offsets, qt, k, kt, v, ot, gt, lse):
    length = k.shape[0]
    turned = pl.BlockSpec((LANES, length), lambda p: (p, 0))
    natural = pl.BlockSpec((length, LANES), lambda p: (0, p))
    pair_rows = pl.BlockSpec((1, 2, 2 * length), lambda p: (p, 0, 0))
    natural_shape = jax.ShapeDtypeStruct((length, D), BF16)
    return pl.pallas_call(
        attend_back_kernel,
        grid=(HEADS // 2,),
        in_specs=[
            pl.BlockSpec(memory_space=pltpu.SMEM),
            pair_rows,
            turned,
            natural,
            turned,
            natural,
            turned,
            turned,
            pl.BlockSpec((1, 2, length), lambda p: (p, 0, 0)),
        ],
        out_specs=[natural] * 3,
        out_shape=[natural_shape] * 3,
        scratch_shapes=[
            pltpu.VMEM((2, LANES, 2 * length), F32),
            pltpu.VMEM((2, length, LANES), BF16),
            pltpu.VMEM((length, length), BF16),
            pltpu.VMEM((length, length), BF16),
        ],
        compiler_params=params(),
        name="attend_back",
    )(length_valid, offsets, qt, k, kt, v, ot, gt, lse)


def middle_kernel(
    length_ref,
    ot_ref,
    x_ref,
    cot_ref,
    gain_ref,
    w_out_ref,
    w_in_ref,
    w_down_ref,
    ar_out_ref,
    b_out_ref,
    ar_in_ref,
    b_in_ref,
    ar_down_ref,
    b_down_ref,
    out_ref,
    dmid_ref,
    gt_ref,
    sums_ref,
    dar_out_ref,
    db_out_ref,
    dar_in_ref,
    db_in_ref,
    dar_down_ref,
    db_down_ref,
):
    step = pl.program_id(0)

    @pl.when(step == 0)
    def _():
        for ref in (
            sums_ref,
            dar_out_ref,
            db_out_ref,
            dar_in_ref,
            db_in_ref,
            dar_down_ref,
            db_down_ref,
        ):
            ref[...] = jnp.zeros_like(ref)

    attended = ot_ref[...].T
    inputs = x_ref[...].astype(F32)
    gain = gain_ref[...]
    low_out, gates_out, mixed_out = single_forward(attended, ar_out_ref)
    branch = dot(attended, w_out_ref[...]) + dot(mixed_out, b_out_ref[...])
    middle = inputs + branch
    inverse = rms_inverse(middle)
    normed = (middle * inverse * gain).astype(BF16)
    low_in, gates_in, mixed_in = single_forward(normed, ar_in_ref)
    hidden = dot(normed, w_in_ref[...]) + dot(mixed_in, b_in_ref[...])
    square = hidden * hidden
    tangent = jnp.tanh(hidden * (GELU_SCALE + (GELU_SCALE * GELU_CUBIC) * square))
    half = 0.5 + 0.5 * tangent
    smooth = hidden * half
    slope = half + smooth * (1.0 - tangent) * (
        GELU_SCALE + (3.0 * GELU_SCALE * GELU_CUBIC) * square
    )
    active = smooth.astype(BF16)
    low_down, gates_down, mixed_down = single_forward(active, ar_down_ref)
    feed = dot(active, w_down_ref[...]) + dot(mixed_down, b_down_ref[...])
    output = middle + feed
    out_ref[...] = output.astype(BF16)

    rows = row_iota((ROWS, 1)) + step * ROWS
    valid = (rows < length_ref[0]).astype(F32)
    lane = lane_iota((8, LANES))
    totals = jnp.zeros((8, LANES), F32)
    for place, member in enumerate((inputs, branch, feed, output)):
        kept = member * valid
        totals = jnp.where(lane == place, jnp.sum(kept * kept), totals)
    sums_ref[...] += totals

    cot = cot_ref[...]
    delta_down = single_backward(dot_nt(cot, b_down_ref[...]), low_down, gates_down)
    grad_active = dot_nt(cot, w_down_ref[...]) + dot_nt(delta_down, ar_down_ref[...])
    grad_hidden = (grad_active * slope).astype(BF16)
    dar_down_ref[...] += dot_tn(delta_down, active)
    db_down_ref[...] += dot_tn(mixed_down, cot)

    delta_in = single_backward(dot_nt(grad_hidden, b_in_ref[...]), low_in, gates_in)
    grad_normed = dot_nt(grad_hidden, w_in_ref[...]) + dot_nt(delta_in, ar_in_ref[...])
    dar_in_ref[...] += dot_tn(delta_in, normed)
    db_in_ref[...] += dot_tn(mixed_in, grad_hidden)

    grad_middle = cot.astype(F32) + rms_backward(middle, gain, inverse, grad_normed)
    dmid_ref[...] = grad_middle
    grad_branch = grad_middle.astype(BF16)
    delta_out = single_backward(dot_nt(grad_branch, b_out_ref[...]), low_out, gates_out)
    grad_attended = dot_nt(grad_branch, w_out_ref[...]) + dot_nt(delta_out, ar_out_ref[...])
    gt_ref[...] = grad_attended.astype(BF16).T
    dar_out_ref[...] += dot_tn(delta_out, attended)
    db_out_ref[...] += dot_tn(mixed_out, grad_branch)


def middle_part(length_valid, ot, x, cot, gain, w_out, w_in, w_down, adapters):
    length = x.shape[0]
    tile = pl.BlockSpec((ROWS, D), lambda i: (i, 0))
    turned = pl.BlockSpec((D, ROWS), lambda i: (0, i))
    grad_shapes = [
        jax.ShapeDtypeStruct((LANES, width), F32) for width in (D, D, D, FF, FF, D)
    ]
    out_shape = [
        jax.ShapeDtypeStruct((length, D), BF16),
        jax.ShapeDtypeStruct((length, D), F32),
        jax.ShapeDtypeStruct((D, length), BF16),
        jax.ShapeDtypeStruct((8, LANES), F32),
    ] + grad_shapes
    return pl.pallas_call(
        middle_kernel,
        grid=(length // ROWS,),
        in_specs=[pl.BlockSpec(memory_space=pltpu.SMEM), turned, tile, tile]
        + [whole(member.shape) for member in (gain, w_out, w_in, w_down, *adapters)],
        out_specs=[tile, tile, turned] + [whole(member.shape) for member in out_shape[3:]],
        out_shape=out_shape,
        compiler_params=params(),
        name="middle_part",
    )(length_valid, ot, x, cot, gain, w_out, w_in, w_down, *adapters)


def project_back_kernel(
    x_ref,
    gain_ref,
    w_ref,
    ar_ref,
    b_ref,
    zg_ref,
    dq_ref,
    dk_ref,
    dv_ref,
    dmid_ref,
    out_ref,
    dar_ref,
    db_ref,
):
    @pl.when(pl.program_id(0) == 0)
    def _():
        dar_ref[...] = jnp.zeros_like(dar_ref)
        db_ref[...] = jnp.zeros_like(db_ref)

    values = x_ref[...].astype(F32)
    gain = gain_ref[...]
    inverse = rms_inverse(values)
    normed = (values * inverse * gain).astype(BF16)
    lowrank = zg_ref[:, :LANES]
    gates = zg_ref[:, LANES:]
    mixed = (lowrank * gates).astype(BF16)
    grads = (dq_ref[...], dk_ref[...], dv_ref[...])
    grad_normed = jnp.zeros((ROWS, D), F32)
    grad_mixed = jnp.zeros((ROWS, LANES), F32)
    for index, grad in enumerate(grads):
        columns = slice(index * D, (index + 1) * D)
        grad_mixed = grad_mixed + dot_nt(grad, b_ref[:, columns])
        grad_normed = grad_normed + dot_nt(grad, w_ref[:, columns])
        db_ref[:, columns] += dot_tn(mixed, grad)
    grad_rank, grad_logits = gate_grads(grad_mixed, lowrank, gates, 3)
    delta = jnp.concatenate([grad_rank, grad_logits], axis=1).astype(BF16)
    grad_normed = grad_normed + dot_nt(delta, ar_ref[...])
    dar_ref[...] += dot_tn(delta, normed)
    out_ref[...] = dmid_ref[...] + rms_backward(values, gain, inverse, grad_normed)


def project_back(x, gain, w_qkv, ar_qkv, b_qkv, zg, dq, dk, dv, dmid):
    length = x.shape[0]
    tile = pl.BlockSpec((ROWS, D), lambda i: (i, 0))
    out_shape = [
        jax.ShapeDtypeStruct((length, D), F32),
        jax.ShapeDtypeStruct((2 * LANES, D), F32),
        jax.ShapeDtypeStruct((LANES, 3 * D), F32),
    ]
    return pl.pallas_call(
        project_back_kernel,
        grid=(length // ROWS,),
        in_specs=[
            tile,
            whole((1, D)),
            whole(w_qkv.shape),
            whole(ar_qkv.shape),
            whole(b_qkv.shape),
            pl.BlockSpec((ROWS, 2 * LANES), lambda i: (i, 0)),
            tile,
            tile,
            tile,
            tile,
        ],
        out_specs=[tile] + [whole(member.shape) for member in out_shape[1:]],
        out_shape=out_shape,
        compiler_params=params(),
        name="project_back",
    )(x, gain, w_qkv, ar_qkv, b_qkv, zg, dq, dk, dv, dmid)


FANS = ((D, D), (D, D), (D, D), (D, D), (D, FF), (FF, D))
PARAM_ROWS = sum((COLS + EXPERTS) * fan_in + COLS * fan_out for fan_in, fan_out in FANS) // LANES


def piece_rows():
    result = []
    row = 0
    for fan_in, fan_out in FANS:
        starts = []
        for count in (fan_in * COLS, COLS * fan_out, fan_in * EXPERTS):
            starts.append(row)
            row += count // LANES
        result.append(tuple(starts))
    return result


def shard_rows(count):
    return -(-count // (LANES * 16)) * 16


def align_in(flat_ref, shard, start):
    first, shift = divmod(start, LANES)
    rows = shard.shape[0]
    if shift == 0:
        flat_ref[first : first + rows] = shard
        return
    turned = pltpu.roll(shard, shift, 1)
    lane = lane_iota((1, LANES))
    zeros = jnp.zeros((8, LANES), F32)
    upper = jnp.concatenate([turned, zeros], axis=0)
    lower = pltpu.roll(upper, 1, 0)
    kept = flat_ref[first : first + 8]
    merged = jnp.where(lane >= shift, upper, lower)
    inside = (row_iota((8, LANES)) == 0) & (lane_iota((8, LANES)) < shift)
    flat_ref[first : first + 8] = jnp.where(inside, kept, merged[:8])
    flat_ref[first + 8 : first + 8 + rows] = merged[8:]


def align_out(flat_ref, rows, start):
    first, shift = divmod(start, LANES)
    if shift == 0:
        return flat_ref[first : first + rows]
    block = flat_ref[first : first + rows + 8]
    turned = pltpu.roll(block, LANES - shift, 1)
    below = pltpu.roll(turned, rows + 7, 0)
    lane = lane_iota((1, LANES))
    return jnp.where(lane < LANES - shift, turned, below)[:rows]


def narrow_to_rows(flat_ref, base, fan_in, width, place, out_ref):
    period = 640 // width
    groups = fan_in // period
    lines = [flat_ref[pl.ds(base + k, groups, stride=5), :] for k in range(5)]
    lane = lane_iota((1, LANES))
    for b in range(period):
        first, shift = divmod(width * b, LANES)
        amount = (place - shift) % LANES
        value = lines[first] if amount == 0 else pltpu.roll(lines[first], amount, 1)
        if shift + width > LANES:
            value = jnp.where(
                lane < place + LANES - shift, value, pltpu.roll(lines[first + 1], amount, 1)
            )
        inside = (lane >= place) & (lane < place + width)
        out_ref[pl.ds(b, groups, stride=period), :] = jnp.where(inside, value, 0.0)


def rows_to_narrow(in_ref, fan_in, width, place, flat_ref, base):
    period = 640 // width
    groups = fan_in // period
    lane = lane_iota((1, LANES))
    lines = [jnp.zeros((groups, LANES), F32) for _ in range(5)]
    for b in range(period):
        first, shift = divmod(width * b, LANES)
        amount = (shift - place) % LANES
        value = in_ref[pl.ds(b, groups, stride=period), :]
        value = value if amount == 0 else pltpu.roll(value, amount, 1)
        inside = (lane >= shift) & (lane < shift + width)
        lines[first] = jnp.where(inside, value, lines[first])
        if shift + width > LANES:
            lines[first + 1] = jnp.where(lane < shift + width - LANES, value, lines[first + 1])
    for k in range(5):
        flat_ref[pl.ds(base + k, groups, stride=5), :] = lines[k]


def spread_matrix(place):
    row = row_iota((LANES, LANES))
    lane = lane_iota((LANES, LANES)) - place
    hit = (lane >= RANK * row) & (lane < RANK * row + RANK) & (row < EXPERTS)
    return jnp.where(hit, 1.0, 0.0).astype(BF16)


def unpack_kernel(
    count,
    shards_ref,
    ar_qkv_ref,
    b_qkv_ref,
    ar_out_ref,
    b_out_ref,
    ar_in_ref,
    b_in_ref,
    ar_down_ref,
    b_down_ref,
    flat,
    down,
    router,
):
    shards = shards_ref.shape[0]
    for index in range(shards):
        align_in(flat, shards_ref[index].astype(F32), index * count)
    starts = piece_rows()

    def ups(base, fan_out, first, out_ref, column):
        width = fan_out // LANES
        above = jnp.zeros((first, LANES), F32)
        below = jnp.zeros((LANES - COLS - first, LANES), F32)
        for k in range(width):
            part = flat[pl.ds(base + k, COLS, stride=width), :]
            parts = [part, below] if first == 0 else [above, part, below]
            lanes = slice(column + k * LANES, column + (k + 1) * LANES)
            out_ref[:, lanes] = jnp.concatenate(parts, axis=0).astype(BF16)

    packed_down = jnp.zeros((D, LANES), F32)
    packed_router = jnp.zeros((D, LANES), F32)
    for index in range(3):
        base_a, base_b, base_r = starts[index]
        narrow_to_rows(flat, base_a, D, COLS, index * COLS, down)
        narrow_to_rows(flat, base_r, D, EXPERTS, 0, router)
        packed_down = packed_down + down[:D]
        packed_router = packed_router + dot(router[:D].astype(BF16), spread_matrix(index * COLS))
        ups(base_b, D, index * COLS, b_qkv_ref, index * D)
    ar_qkv_ref[:, :LANES] = packed_down.astype(BF16)
    ar_qkv_ref[:, LANES:] = packed_router.astype(BF16)
    members = ((ar_out_ref, b_out_ref), (ar_in_ref, b_in_ref), (ar_down_ref, b_down_ref))
    for index, (ar_ref, b_ref) in zip(range(3, 6), members):
        base_a, base_b, base_r = starts[index]
        fan_in, fan_out = FANS[index]
        narrow_to_rows(flat, base_a, fan_in, COLS, 0, down)
        narrow_to_rows(flat, base_r, fan_in, EXPERTS, 0, router)
        wide = dot(router[:fan_in].astype(BF16), spread_matrix(64))
        ar_ref[...] = (down[:fan_in] + wide).astype(BF16)
        ups(base_b, fan_out, 0, b_ref, 0)


def unpack(shards, count):
    rows = shards.shape[1]
    shapes = ((D, 2 * LANES), (LANES, 3 * D), (D, LANES), (LANES, D), (D, LANES), (LANES, FF), (FF, LANES), (LANES, D))
    return pl.pallas_call(
        functools.partial(unpack_kernel, count),
        in_specs=[pl.BlockSpec(memory_space=pltpu.VMEM)],
        out_specs=[pl.BlockSpec(memory_space=pltpu.VMEM)] * len(shapes),
        out_shape=[jax.ShapeDtypeStruct(shape, BF16) for shape in shapes],
        scratch_shapes=[
            pltpu.VMEM((PARAM_ROWS + rows + 20, LANES), F32),
            pltpu.VMEM((FF, LANES), F32),
            pltpu.VMEM((FF, LANES), F32),
        ],
        compiler_params=params(),
        name="unpack",
    )(shards)


def gather_matrix(place):
    row = row_iota((LANES, LANES)) - place
    lane = lane_iota((LANES, LANES))
    return jnp.where((row == RANK * lane) & (lane < EXPERTS), 1.0, 0.0).astype(BF16)


def assemble_kernel(
    count,
    dar_qkv_ref,
    db_qkv_ref,
    dar_out_ref,
    db_out_ref,
    dar_in_ref,
    db_in_ref,
    dar_down_ref,
    db_down_ref,
    shards_ref,
    flat,
    down,
    router,
):
    starts = piece_rows()

    def ups(base, fan_out, first, grad_ref, column):
        width = fan_out // LANES
        for k in range(width):
            lanes = slice(column + k * LANES, column + (k + 1) * LANES)
            flat[pl.ds(base + k, COLS, stride=width), :] = grad_ref[first : first + COLS, lanes]

    def routers(packed, place):
        matrix = gather_matrix(place)
        high = packed.astype(BF16)
        return dot(high, matrix) + dot((packed - high.astype(F32)).astype(BF16), matrix)

    members = (
        (3, dar_out_ref, db_out_ref),
        (4, dar_in_ref, db_in_ref),
        (5, dar_down_ref, db_down_ref),
    )
    for index, dar_ref, db_ref in members:
        base_a, base_b, base_r = starts[index]
        fan_in, fan_out = FANS[index]
        packed = dar_ref[...].T
        down[:fan_in] = packed
        rows_to_narrow(down, fan_in, COLS, 0, flat, base_a)
        router[:fan_in] = routers(packed, 64)
        rows_to_narrow(router, fan_in, EXPERTS, 0, flat, base_r)
        ups(base_b, fan_out, 0, db_ref, 0)
    packed = dar_qkv_ref[:LANES].T
    packed_router = dar_qkv_ref[LANES:].T
    down[:D] = packed
    for index in range(3):
        base_a, base_b, base_r = starts[index]
        rows_to_narrow(down, D, COLS, index * COLS, flat, base_a)
        router[:D] = routers(packed_router, index * COLS)
        rows_to_narrow(router, D, EXPERTS, 0, flat, base_r)
        ups(base_b, D, index * COLS, db_qkv_ref, index * D)
    shards, rows = shards_ref.shape[0], shards_ref.shape[1]
    for index in range(shards):
        shards_ref[index] = align_out(flat, rows, index * count)


def assemble(grads, shards, count):
    rows = shard_rows(count)
    return pl.pallas_call(
        functools.partial(assemble_kernel, count),
        in_specs=[pl.BlockSpec(memory_space=pltpu.VMEM)] * len(grads),
        out_specs=pl.BlockSpec(memory_space=pltpu.VMEM),
        out_shape=jax.ShapeDtypeStruct((shards, rows, LANES), F32),
        scratch_shapes=[
            pltpu.VMEM((PARAM_ROWS + rows + 20, LANES), F32),
            pltpu.VMEM((FF, LANES), F32),
            pltpu.VMEM((FF, LANES), F32),
        ],
        compiler_params=params(),
        name="assemble",
    )(*grads)


MESH = pl.DeviceIdType.MESH


def place_of(axes, sizes):
    me = lax.axis_index(axes[0]) * sizes[1] + lax.axis_index(axes[1])

    def coordinates(number):
        return (number // sizes[1], number % sizes[1])

    return me, coordinates


def partners_of(me):
    low = me % 8
    core = low % 2
    y = (low // 2) % 2
    x = low // 4
    over_x = low + 4 * (1 - 2 * x)
    over_y = low + 2 * (1 - 2 * y)
    first = over_x * (1 - core) + over_y * core
    second = over_y * (1 - core) + over_x * core
    both = first + second - low
    other = 1 - 2 * core
    return low, first, second, both, other, over_x, over_y


def greet(peers):
    barrier = pltpu.get_barrier_semaphore()
    for peer in peers:
        pl.semaphore_signal(barrier, inc=1, device_id=peer, device_id_type=MESH)
    pl.semaphore_wait(barrier, len(peers))


def gather_kernel(axes, sizes, shard_ref, out_ref, send, receive, local):
    me, coordinates = place_of(axes, sizes)
    groups = out_ref.shape[0]
    group = me // 8
    low, first, second, both, other, over_x, over_y = partners_of(me)

    def device(group_index, low_index):
        return coordinates(group_index * 8 + low_index)

    others = [(group + step) % groups for step in range(1, groups)]
    peers = [device(index, low) for index in others]
    peers += [device(group, partner) for partner in (first, second, low + other)]
    greet(peers)
    counter = [0]

    def start(source, target, peer):
        index = counter[0]
        counter[0] += 1
        copy = pltpu.make_async_remote_copy(
            src_ref=source,
            dst_ref=target,
            send_sem=send.at[index],
            recv_sem=receive.at[index],
            device_id=peer,
            device_id_type=MESH,
        )
        copy.start()
        return copy

    own = pltpu.make_async_copy(shard_ref, out_ref.at[group, low], local)
    own.start()
    around = [start(shard_ref, out_ref.at[group, low], device(index, low)) for index in others]
    own.wait()
    for copy in around:
        copy.wait()

    def push(part, partner):
        return start(out_ref.at[:, part], out_ref.at[:, part], device(group, partner))

    one = push(low, first)
    two = push(low, second)
    core_own = push(low, low + other)
    one.wait()
    three = push(first, second)
    core_first = push(first, low + other)
    two.wait()
    core_second = push(second, low + other)
    three.wait()
    core_both = push(both, low + other)
    for copy in (core_own, core_first, core_second, core_both):
        copy.wait()


def gather(shard, axes, sizes):
    groups = sizes[0] * sizes[1] // 8
    copies = groups - 1 + 7
    return pl.pallas_call(
        functools.partial(gather_kernel, axes, sizes),
        in_specs=[pl.BlockSpec(memory_space=pltpu.VMEM)],
        out_specs=pl.BlockSpec(memory_space=pltpu.VMEM),
        out_shape=jax.ShapeDtypeStruct((groups, 8, *shard.shape), shard.dtype),
        scratch_shapes=[
            pltpu.SemaphoreType.DMA((copies,)),
            pltpu.SemaphoreType.DMA((copies,)),
            pltpu.SemaphoreType.DMA,
        ],
        compiler_params=params(collective_id=0, has_side_effects=True),
        name="gather",
    )(shard)


def reduce_kernel(
    axes, sizes, parts_ref, sums_ref, out_ref, total_ref, outbox, inbox, near_out, near_in, far_in, own, send, receive
):
    me, coordinates = place_of(axes, sizes)
    groups = parts_ref.shape[0]
    group = me // 8
    low, first, second, both, other, over_x, over_y = partners_of(me)

    def device(group_index, low_index):
        return coordinates(group_index * 8 + low_index)

    others = [(group + step) % groups for step in range(1, groups)]
    peers = [device(index, low) for index in others]
    peers += [device(group, partner) for partner in (first, second, low + other)]
    greet(peers)
    counter = [0]

    def start(source, target, peer):
        index = counter[0]
        counter[0] += 1
        copy = pltpu.make_async_remote_copy(
            src_ref=source,
            dst_ref=target,
            send_sem=send.at[index],
            recv_sem=receive.at[index],
            device_id=peer,
            device_id_type=MESH,
        )
        copy.start()
        return copy

    def push(slot, value, partner):
        outbox[slot] = value.astype(BF16)
        return start(outbox.at[slot], inbox.at[slot], device(group, partner))

    def push_sums(slot, value, partner):
        near_out[slot] = value
        return start(near_out.at[slot], near_in.at[slot], device(group, partner))

    mate = low + other
    sums = sums_ref[...]
    sums_core = push_sums(0, sums, mate)
    core = [
        push(slot, parts_ref[:, part + other], mate)
        for slot, part in enumerate((first, both, second, low))
    ]
    core[0].wait()
    half_second = parts_ref[:, second] + inbox[0].astype(F32)
    to_second = push(4, half_second, second)
    core[1].wait()
    half_both = parts_ref[:, both] + inbox[1].astype(F32)
    to_both = push(5, half_both, second)
    sums_core.wait()
    sums = sums + near_in[0]
    sums_x = push_sums(1, sums, over_x)
    core[2].wait()
    half_first = parts_ref[:, first] + inbox[2].astype(F32)
    core[3].wait()
    half_low = parts_ref[:, low] + inbox[3].astype(F32)
    to_both.wait()
    quarter_first = half_first + inbox[5].astype(F32)
    to_first = push(6, quarter_first, first)
    sums_x.wait()
    sums = sums + near_in[1]
    sums_y = push_sums(2, sums, over_y)
    to_second.wait()
    half_low = half_low + inbox[4].astype(F32)
    to_first.wait()
    own[...] = half_low + inbox[6].astype(F32)
    outbox[7] = own[...].astype(BF16)
    around = [
        start(outbox.at[7, index], far_in.at[step], device(index, low))
        for step, index in enumerate(others)
    ]
    sums_y.wait()
    near_out[3] = sums + near_in[2]
    around_sums = [
        start(near_out.at[3], near_in.at[4 + group], device(index, low))
        for index in others
    ]
    near_in[4 + group] = near_out[3]
    total = own[group]
    for step, copy in enumerate(around):
        copy.wait()
        total = total + far_in[step].astype(F32)
    out_ref[...] = total
    for copy in around_sums:
        copy.wait()
    whole_sum = near_in[4]
    for index in range(1, groups):
        whole_sum = whole_sum + near_in[4 + index]
    total_ref[...] = whole_sum


def reduce_scatter(parts, sums, axes, sizes):
    groups, _, rows, lanes = parts.shape
    copies = 7 + 3 + 2 * (groups - 1)
    return pl.pallas_call(
        functools.partial(reduce_kernel, axes, sizes),
        in_specs=[pl.BlockSpec(memory_space=pltpu.VMEM)] * 2,
        out_specs=[pl.BlockSpec(memory_space=pltpu.VMEM)] * 2,
        out_shape=[
            jax.ShapeDtypeStruct((rows, lanes), F32),
            jax.ShapeDtypeStruct(sums.shape, F32),
        ],
        scratch_shapes=[
            pltpu.VMEM((8, groups, rows, lanes), BF16),
            pltpu.VMEM((7, groups, rows, lanes), BF16),
            pltpu.VMEM((4, *sums.shape), F32),
            pltpu.VMEM((4 + groups, *sums.shape), F32),
            pltpu.VMEM((groups - 1, rows, lanes), BF16),
            pltpu.VMEM((groups, rows, lanes), F32),
            pltpu.SemaphoreType.DMA((copies,)),
            pltpu.SemaphoreType.DMA((copies,)),
        ],
        compiler_params=params(collective_id=1, has_side_effects=True),
        name="reduce_scatter",
    )(parts, sums)


def per_device(
    tokens,
    lengths,
    buckets,
    rel_table,
    gain_attn,
    gain_ff,
    w_qkv,
    w_out,
    w_in,
    w_down,
    adapters,
    cotangent,
    axes,
    sizes,
):
    seq_count, length, width = tokens.shape
    x = tokens.reshape(length, width)
    cot = cotangent.reshape(length, width)
    devices = sizes[0] * sizes[1]
    count = adapters.shape[0]
    rows = shard_rows(count)
    shard = jnp.pad(adapters, (0, rows * LANES - count)).reshape(rows, LANES)
    if devices == 1:
        shards = shard[None]
    else:
        shards = gather(shard, axes, sizes).reshape(devices, rows, LANES)
    ar_qkv, b_qkv, *rest = unpack(shards, count)
    gain_first = gain_attn.reshape(1, width)
    gain_second = gain_ff.reshape(1, width)

    reversed_buckets = jnp.pad(buckets[::-1], (0, 1))
    hits = (jnp.arange(rel_table.shape[0])[:, None] == reversed_buckets[None, :]).astype(F32)
    offsets = jnp.dot(rel_table.T * LOG2E, hits, precision=lax.Precision.HIGHEST)
    offsets = offsets.reshape(HEADS // 2, 2, 2 * length)

    qt, k, kt, v, vt, zg = project(x, gain_first, w_qkv, ar_qkv, b_qkv)
    ot, lse = attend(lengths, offsets, qt, k, vt)
    block_out, dmid, gt, sums, *grads = middle_part(
        lengths, ot, x, cot, gain_second, w_out, w_in, w_down, rest
    )
    dq, dk, dv = attend_back(lengths, offsets, qt, k, kt, v, ot, gt, lse)
    tokens_grad, dar_qkv, db_qkv = project_back(
        x, gain_first, w_qkv, ar_qkv, b_qkv, zg, dq, dk, dv, dmid
    )

    parts = assemble((dar_qkv, db_qkv, *grads), devices, count)
    sums = jnp.where(jnp.arange(LANES)[None, :] == 4, jnp.sum(lengths).astype(F32), sums)
    if devices == 1:
        mine, sums = parts[0], sums
    else:
        parts = parts.reshape(devices // 8, 8, rows, LANES)
        mine, sums = reduce_scatter(parts, sums, axes, sizes)
    grad_shard = mine.reshape(-1)[:count]
    root_squares = jnp.sqrt(sums[0, :4] / (sums[0, 4] * width))
    return (
        block_out.reshape(tokens.shape),
        tokens_grad.reshape(tokens.shape),
        grad_shard,
        root_squares,
    )


def solution(mesh):
    axes = tuple(mesh.axis_names)
    sizes = tuple(mesh.shape[axis] for axis in axes)
    sequence = P(axes, None, None)
    placed = (
        sequence,
        P(axes),
        P(),
        P(),
        P(),
        P(),
        P(),
        P(),
        P(),
        P(),
        P(axes),
        sequence,
    )
    return jax.shard_map(
        functools.partial(per_device, axes=axes, sizes=sizes),
        mesh=mesh,
        in_specs=placed,
        out_specs=(sequence, sequence, P(axes), P()),
        check_vma=False,
    )
```

```python
import functools

import jax
import jax.numpy as jnp
from jax import lax
from jax.experimental import pallas as pl
from jax.experimental.pallas import tpu as pltpu
from jax.sharding import PartitionSpec as P

D = 768
FF = 3072
HEADS = 12
HDIM = 64
EXPERTS = 10
RANK = 4
FANS = ((D, D), (D, D), (D, D), (D, D), (D, FF), (FF, D))
COLS = EXPERTS * RANK
LANES = 128

EPSILON = 1e-06
MASKED = -1000000000.0
GELU_SCALE = 0.7978845608028654
GELU_CUBIC = 0.044715
LOG2E = 1.4426950408889634
LN2 = 0.6931471805599453
QUERY_SCALE = 0.125 * LOG2E

ROWS = 256
MIDDLE_ROWS = 512
CHUNK = 512
QBLOCK = 256
UP_ROWS = 48
DOWN_ROWS = 2 * COLS
VMEM_BYTES = 60 * 1024 * 1024

F32 = jnp.float32
BF16 = jnp.bfloat16


def dot(a, b):
    return lax.dot_general(a, b, (((1,), (0,)), ((), ())), preferred_element_type=F32)


def dot_nt(a, b):
    return lax.dot_general(a, b, (((1,), (1,)), ((), ())), preferred_element_type=F32)


def dot_tn(a, b):
    return lax.dot_general(a, b, (((0,), (0,)), ((), ())), preferred_element_type=F32)


def lane_iota(shape):
    return lax.broadcasted_iota(jnp.int32, shape, 1)


def row_iota(shape):
    return lax.broadcasted_iota(jnp.int32, shape, 0)


def gates_of(logits):
    weights = jnp.exp(logits - jnp.max(logits, axis=0, keepdims=True))
    return weights * (4.0 / jnp.sum(weights, axis=0, keepdims=True))


def gate_grads(grad_mixed, lowrank, gates):
    product = grad_mixed * lowrank
    summed = product
    for step in range(1, RANK):
        summed = summed + pltpu.roll(product, COLS - step, 0)
    centre = jnp.sum(gates * product, axis=0, keepdims=True)
    first = row_iota(gates.shape) % RANK == 0
    return grad_mixed * gates, jnp.where(first, gates * (summed - centre), 0.0)


def pad_rows(value, rows):
    return jnp.concatenate([value, jnp.zeros((rows - value.shape[0], value.shape[1]), F32)], axis=0)


def single_gates(packed):
    turned = packed.T
    lowrank = turned[:COLS]
    gates = gates_of(turned[COLS : 2 * COLS])
    mixed = pad_rows(lowrank * gates, LANES).astype(BF16)
    return lowrank, gates, mixed, mixed.T


def single_deltas(grad_mixed, lowrank, gates):
    parts = gate_grads(grad_mixed.T[:COLS], lowrank, gates)
    delta = pad_rows(jnp.concatenate(parts, axis=0), LANES).astype(BF16)
    return delta, delta.T


def rms_inverse(values):
    return lax.rsqrt(jnp.mean(values * values, axis=-1, keepdims=True) + EPSILON)


def rms_backward(values, gain, inverse, grad_normed):
    weighted = grad_normed * gain
    return inverse * weighted - values * (
        inverse * inverse * inverse * jnp.mean(values * weighted, axis=-1, keepdims=True)
    )


def params(**more):
    return pltpu.CompilerParams(vmem_limit_bytes=VMEM_BYTES, **more)


def whole(shape):
    zeros = (0,) * len(shape)
    return pl.BlockSpec(shape, lambda *_: zeros, pipeline_mode=pl.Buffered(1))


def project_kernel(
    x_ref, gain_ref, w_ref, ar_ref, b_ref, qt_ref, k_ref, kt_ref, v_ref, vt_ref, zg_ref
):
    values = x_ref[...].astype(F32)
    normed = (values * rms_inverse(values) * gain_ref[...]).astype(BF16)
    packed = dot(normed, ar_ref[...]).T
    lowrank = packed[: 3 * COLS]
    gates = jnp.concatenate(
        [gates_of(packed[first : first + COLS]) for first in range(3 * COLS, 6 * COLS, COLS)], axis=0
    )
    zg_ref[: 3 * COLS] = lowrank
    zg_ref[3 * COLS :] = gates
    mixed = pad_rows(lowrank * gates, LANES).astype(BF16).T
    for index in range(3):
        columns = slice(index * D, (index + 1) * D)
        part = dot(normed, w_ref[:, columns]) + dot(mixed, b_ref[:, columns])
        if index == 0:
            qt_ref[...] = (part * QUERY_SCALE).astype(BF16).T
        else:
            low = part.astype(BF16)
            natural, turned = ((k_ref, kt_ref), (v_ref, vt_ref))[index - 1]
            natural[...] = low
            turned[...] = low.T


def project(x, gain, w_qkv, ar_qkv, b_qkv):
    length = x.shape[0]
    tile = pl.BlockSpec((ROWS, D), lambda i: (i, 0))
    turned = pl.BlockSpec((D, ROWS), lambda i: (0, i))
    natural_shape = jax.ShapeDtypeStruct((length, D), BF16)
    turned_shape = jax.ShapeDtypeStruct((D, length), BF16)
    return pl.pallas_call(
        project_kernel,
        grid=(length // ROWS,),
        in_specs=[
            tile,
            whole((1, D)),
            whole(w_qkv.shape),
            whole(ar_qkv.shape),
            whole(b_qkv.shape),
        ],
        out_specs=[
            turned,
            tile,
            turned,
            tile,
            turned,
            pl.BlockSpec((6 * COLS, ROWS), lambda i: (0, i)),
        ],
        out_shape=[
            turned_shape,
            natural_shape,
            turned_shape,
            natural_shape,
            turned_shape,
            jax.ShapeDtypeStruct((6 * COLS, length), F32),
        ],
        compiler_params=params(),
        name="project",
    )(x, gain, w_qkv, ar_qkv, b_qkv)


def bias_table(offset_row, length):
    spread = jnp.broadcast_to(offset_row, (LANES, 2 * length))
    return pltpu.roll(spread, 2 * length - (LANES - 1), 1, stride=1, stride_axis=0)


def add_bias(scores, table_ref, start, length):
    width = scores.shape[1]
    parts = []
    for block in range(length // LANES):
        offset = start - LANES * block + (length - LANES)
        parts.append(
            scores[block * LANES : (block + 1) * LANES] + table_ref[:, offset : offset + width]
        )
    return jnp.concatenate(parts, axis=0)


def key_extras(length_ref, shape, odd):
    lane = lane_iota(shape) - (0 if odd else HDIM)
    invalid = row_iota(shape) >= length_ref[0]
    extras = jnp.where((lane == 0) & invalid, MASKED, 0.0)
    return jnp.where((lane >= 1) & (lane <= 3), 1.0, extras).astype(BF16)


def head_lanes(odd):
    lane = lane_iota((1, LANES))
    return ((lane >= HDIM) if odd else (lane < HDIM)).astype(F32).astype(BF16)


def extra_rows(rows):
    width = rows[0].shape[1]
    index = row_iota((8, width))
    block = jnp.zeros((8, width), F32)
    for place, row in enumerate(rows):
        block = jnp.where(index == place, row, block)
    return jnp.concatenate([block, jnp.zeros((HDIM - 8, width), F32)], axis=0).astype(BF16)


def split_three(row):
    high = row.astype(BF16).astype(F32)
    middle = (row - high).astype(BF16).astype(F32)
    return high, middle, row - high - middle


def join_rows(rows, extras, odd):
    return jnp.concatenate([extras, rows] if odd else [rows, extras], axis=0)


def attend_kernel(length_ref, off_ref, qt_ref, k_ref, vt_ref, o_ref, lse_ref, table, key_more):
    length = k_ref.shape[0]

    @pl.when(pl.program_id(0) == 0)
    def _():
        for odd in range(2):
            key_more[odd] = key_extras(length_ref, k_ref.shape, odd)

    for odd in range(2):
        half = slice(odd * HDIM, (odd + 1) * HDIM)
        table[odd] = bias_table(off_ref[0, odd : odd + 1, :], length)
        keys = k_ref[...] * head_lanes(odd) + key_more[odd]
        ones = jnp.ones((1, length), F32)
        queries = join_rows(qt_ref[half, :], extra_rows([ones]), odd)
        values = jnp.concatenate([vt_ref[half, :], jnp.ones((16, length), BF16)], axis=0)
        starts = range(0, length, QBLOCK)
        scores = [
            add_bias(dot(keys, queries[:, start : start + QBLOCK]), table.at[odd], start, length)
            for start in starts
        ]
        peaks = [jnp.max(part, axis=0, keepdims=True) for part in scores]
        weights = [jnp.exp2(part - peak).astype(BF16) for part, peak in zip(scores, peaks)]
        for start, peak, part in zip(starts, peaks, weights):
            columns = slice(start, start + QBLOCK)
            summed = dot(values, part)
            total = summed[HDIM : HDIM + 1]
            o_ref[half, columns] = (summed[:HDIM] / total).astype(BF16)
            lse_ref[0, odd : odd + 1, columns] = peak + jnp.log2(total)


def attend(length_valid, offsets, qt, k, vt):
    length = k.shape[0]
    turned = pl.BlockSpec((LANES, length), lambda p: (p, 0))
    natural = pl.BlockSpec((length, LANES), lambda p: (0, p))
    pair_rows = pl.BlockSpec((1, 2, 2 * length), lambda p: (p, 0, 0))
    return pl.pallas_call(
        attend_kernel,
        grid=(HEADS // 2,),
        in_specs=[
            pl.BlockSpec(memory_space=pltpu.SMEM),
            pair_rows,
            turned,
            natural,
            turned,
        ],
        out_specs=[turned, pl.BlockSpec((1, 2, length), lambda p: (p, 0, 0))],
        out_shape=[
            jax.ShapeDtypeStruct((D, length), BF16),
            jax.ShapeDtypeStruct((HEADS // 2, 2, length), F32),
        ],
        scratch_shapes=[
            pltpu.VMEM((2, LANES, 2 * length), F32),
            pltpu.VMEM((2, length, LANES), BF16),
        ],
        compiler_params=params(),
        name="attend",
    )(length_valid, offsets, qt, k, vt)


def attend_back_kernel(
    length_ref,
    off_ref,
    qt_ref,
    k_ref,
    kt_ref,
    v_ref,
    ot_ref,
    gt_ref,
    lse_ref,
    dq_ref,
    dk_ref,
    dv_ref,
    table,
    key_more,
    weights_all,
    grads_all,
):
    length = k_ref.shape[0]

    @pl.when(pl.program_id(0) == 0)
    def _():
        for odd in range(2):
            key_more[odd] = key_extras(length_ref, k_ref.shape, odd)

    lane = lane_iota((1, LANES))
    first_lanes = lane < HDIM
    grad_query_parts = []
    for odd in range(2):
        half = slice(odd * HDIM, (odd + 1) * HDIM)
        table[odd] = bias_table(off_ref[0, odd : odd + 1, :], length)
        keys = k_ref[...] * head_lanes(odd) + key_more[odd]
        place = lane - (0 if odd else HDIM)
        value_more = ((place >= 0) & (place < 3)).astype(F32).astype(BF16)
        values = v_ref[...] * head_lanes(odd) + value_more
        ones = jnp.ones((1, length), F32)
        lse = lse_ref[0, odd : odd + 1, :]
        queries = join_rows(
            qt_ref[half, :], extra_rows([ones] + [-part for part in split_three(lse)]), odd
        )
        delta = jnp.sum(
            ot_ref[half, :].astype(F32) * gt_ref[half, :].astype(F32), axis=0, keepdims=True
        )
        grads = join_rows(
            gt_ref[half, :], extra_rows([-part for part in split_three(delta)]), odd
        )
        for start in range(0, length, QBLOCK):
            columns = slice(start, start + QBLOCK)
            scores = add_bias(dot(keys, queries[:, columns]), table.at[odd], start, length)
            weights = jnp.exp2(scores)
            weights_all[:, columns] = weights.astype(BF16)
            grad_scores = weights * dot(values, grads[:, columns])
            grads_all[:, columns] = grad_scores.astype(BF16)
        grad_query_parts.append(dot(kt_ref[half, :], grads_all[...]) * 0.125)
        grad_values = dot_nt(weights_all[...], gt_ref[...])
        grad_keys = dot_nt(grads_all[...], qt_ref[...]) * LN2
        if odd:
            dv_ref[...] = jnp.where(first_lanes, even_values, grad_values).astype(BF16)
            dk_ref[...] = jnp.where(first_lanes, even_keys, grad_keys).astype(BF16)
        else:
            even_values, even_keys = grad_values, grad_keys
    dq_ref[...] = jnp.concatenate(grad_query_parts, axis=0).T.astype(BF16)


def attend_back(length_valid, offsets, qt, k, kt, v, ot, gt, lse):
    length = k.shape[0]
    turned = pl.BlockSpec((LANES, length), lambda p: (p, 0))
    natural = pl.BlockSpec((length, LANES), lambda p: (0, p))
    pair_rows = pl.BlockSpec((1, 2, 2 * length), lambda p: (p, 0, 0))
    natural_shape = jax.ShapeDtypeStruct((length, D), BF16)
    return pl.pallas_call(
        attend_back_kernel,
        grid=(HEADS // 2,),
        in_specs=[
            pl.BlockSpec(memory_space=pltpu.SMEM),
            pair_rows,
            turned,
            natural,
            turned,
            natural,
            turned,
            turned,
            pl.BlockSpec((1, 2, length), lambda p: (p, 0, 0)),
        ],
        out_specs=[natural] * 3,
        out_shape=[natural_shape] * 3,
        scratch_shapes=[
            pltpu.VMEM((2, LANES, 2 * length), F32),
            pltpu.VMEM((2, length, LANES), BF16),
            pltpu.VMEM((length, length), BF16),
            pltpu.VMEM((length, length), BF16),
        ],
        compiler_params=params(),
        name="attend_back",
    )(length_valid, offsets, qt, k, kt, v, ot, gt, lse)


def middle_kernel(
    length_ref,
    ot_ref,
    x_ref,
    cot_ref,
    gain_ref,
    w_out_ref,
    w_in_ref,
    w_down_ref,
    ar_out_ref,
    b_out_ref,
    ar_in_ref,
    b_in_ref,
    ar_down_ref,
    b_down_ref,
    out_ref,
    dmid_ref,
    gt_ref,
    sums_ref,
    dar_out_ref,
    db_out_ref,
    dar_in_ref,
    db_in_ref,
    dar_down_ref,
    db_down_ref,
    active,
    slope,
    sloped,
    grad_hidden,
    feeds,
):
    step = pl.program_id(0)

    @pl.when(step == 0)
    def _():
        for ref in (
            sums_ref,
            dar_out_ref,
            db_out_ref,
            dar_in_ref,
            db_in_ref,
            dar_down_ref,
            db_down_ref,
        ):
            ref[...] = jnp.zeros_like(ref)

    attended = ot_ref[...].T
    inputs = x_ref[...].astype(F32)
    gain = gain_ref[...]
    cot = cot_ref[...]

    packed_out = dot(attended, ar_out_ref[...])
    branch = dot(attended, w_out_ref[...])
    low_out, gates_out, mixed_out, natural = single_gates(packed_out)
    grad_mixed_down = dot_nt(cot, b_down_ref[...])
    branch = branch + dot(natural, b_out_ref[...])
    middle = inputs + branch
    inverse = rms_inverse(middle)
    normed = (middle * inverse * gain).astype(BF16)

    packed_in = dot(normed, ar_in_ref[...])
    low_in, gates_in, mixed_in, natural = single_gates(packed_in)

    def columns_of(index):
        return pl.ds(pl.multiple_of(index * CHUNK, CHUNK), CHUNK)

    def hidden_of(chunk):
        return dot(normed, w_in_ref[:, chunk]) + dot(natural, b_in_ref[:, chunk])

    def activate(chunk, values):
        grad_dense = dot_nt(cot, w_down_ref[chunk])
        square = values * values
        tangent = jnp.tanh(values * (GELU_SCALE + (GELU_SCALE * GELU_CUBIC) * square))
        half = 0.5 + 0.5 * tangent
        smooth = values * half
        active[:, chunk] = smooth.astype(BF16)
        steep = half + smooth * (1.0 - tangent) * (
            GELU_SCALE + (3.0 * GELU_SCALE * GELU_CUBIC) * square
        )
        slope[:, chunk] = steep.astype(BF16)
        sloped[:, chunk] = grad_dense * steep

    def forward_pair(pair, _):
        chunk_a = columns_of(2 * pair)
        chunk_b = columns_of(2 * pair + 1)
        hidden_a = hidden_of(chunk_a)
        hidden_b = hidden_of(chunk_b)
        activate(chunk_a, hidden_a)
        activate(chunk_b, hidden_b)
        return 0

    lax.fori_loop(0, FF // (2 * CHUNK), forward_pair, 0)

    packed_down = dot(active[...], ar_down_ref[...])
    def feed_part(index, _):
        part = pl.ds(pl.multiple_of(index * 256, 256), 256)
        feeds[:, part] = dot(active[...], w_down_ref[:, part])
        return 0

    lax.fori_loop(0, 3, feed_part, 0)
    feed = feeds[...]
    low_down, gates_down, mixed_down, natural = single_gates(packed_down)
    delta_down, natural_delta = single_deltas(grad_mixed_down, low_down, gates_down)
    db_down_ref[...] += dot(mixed_down[:UP_ROWS], cot)
    feed = feed + dot(natural, b_down_ref[...])
    output = middle + feed
    out_ref[...] = output.astype(BF16)

    def backward_chunk(index, _):
        chunk = columns_of(index)
        grad_low = dot_nt(natural_delta, ar_down_ref[chunk])
        grad_hidden[:, chunk] = (
            sloped[:, chunk] + grad_low * slope[:, chunk].astype(F32)
        ).astype(BF16)
        return 0

    lax.fori_loop(0, FF // CHUNK, backward_chunk, 0)
    dar_down_ref[...] += dot(delta_down[:DOWN_ROWS], active[...])

    rows = row_iota((MIDDLE_ROWS, 1)) + step * MIDDLE_ROWS
    valid = (rows < length_ref[0]).astype(F32)
    lane = lane_iota((8, LANES))
    totals = jnp.zeros((8, LANES), F32)
    for place, member in enumerate((inputs, branch, feed, output)):
        kept = member * valid
        totals = jnp.where(lane == place, jnp.sum(kept * kept), totals)
    sums_ref[...] += totals

    grad_mixed = dot_nt(grad_hidden[...], b_in_ref[...])
    def back_part(index, _):
        part = pl.ds(pl.multiple_of(index * 256, 256), 256)
        feeds[:, part] = dot_nt(grad_hidden[...], w_in_ref[part])
        return 0

    lax.fori_loop(0, 3, back_part, 0)
    grad_normed = feeds[...]
    delta_in, natural_delta = single_deltas(grad_mixed, low_in, gates_in)
    db_in_ref[...] += dot(mixed_in[:UP_ROWS], grad_hidden[...])
    grad_normed = grad_normed + dot_nt(natural_delta, ar_in_ref[...])
    dar_in_ref[...] += dot(delta_in[:DOWN_ROWS], normed)

    grad_middle = cot.astype(F32) + rms_backward(middle, gain, inverse, grad_normed)
    dmid_ref[...] = grad_middle
    grad_branch = grad_middle.astype(BF16)
    grad_mixed = dot_nt(grad_branch, b_out_ref[...])
    grad_attended = dot_nt(grad_branch, w_out_ref[...])
    delta_out, natural_delta = single_deltas(grad_mixed, low_out, gates_out)
    grad_attended = grad_attended + dot_nt(natural_delta, ar_out_ref[...])
    gt_ref[...] = grad_attended.astype(BF16).T
    dar_out_ref[...] += dot(delta_out[:DOWN_ROWS], attended)
    db_out_ref[...] += dot(mixed_out[:UP_ROWS], grad_branch)


def middle_part(length_valid, ot, x, cot, gain, w_out, w_in, w_down, adapters):
    length = x.shape[0]
    tile = pl.BlockSpec((MIDDLE_ROWS, D), lambda i: (i, 0))
    turned = pl.BlockSpec((D, MIDDLE_ROWS), lambda i: (0, i))
    grad_shapes = [
        jax.ShapeDtypeStruct(shape, F32)
        for fan_in, fan_out in FANS[3:]
        for shape in ((DOWN_ROWS, fan_in), (UP_ROWS, fan_out))
    ]
    out_shape = [
        jax.ShapeDtypeStruct((length, D), BF16),
        jax.ShapeDtypeStruct((length, D), F32),
        jax.ShapeDtypeStruct((D, length), BF16),
        jax.ShapeDtypeStruct((8, LANES), F32),
    ] + grad_shapes
    return pl.pallas_call(
        middle_kernel,
        grid=(length // MIDDLE_ROWS,),
        in_specs=[pl.BlockSpec(memory_space=pltpu.SMEM), turned, tile, tile]
        + [whole(member.shape) for member in (gain, w_out, w_in, w_down, *adapters)],
        out_specs=[tile, tile, turned] + [whole(member.shape) for member in out_shape[3:]],
        out_shape=out_shape,
        scratch_shapes=[
            pltpu.VMEM((MIDDLE_ROWS, FF), BF16),
            pltpu.VMEM((MIDDLE_ROWS, FF), BF16),
            pltpu.VMEM((MIDDLE_ROWS, FF), F32),
            pltpu.VMEM((MIDDLE_ROWS, FF), BF16),
            pltpu.VMEM((MIDDLE_ROWS, D), F32),
        ],
        compiler_params=params(),
        name="middle_part",
    )(length_valid, ot, x, cot, gain, w_out, w_in, w_down, *adapters)


def project_back_kernel(
    x_ref,
    gain_ref,
    w_ref,
    ar_ref,
    b_ref,
    zg_ref,
    dq_ref,
    dk_ref,
    dv_ref,
    dmid_ref,
    out_ref,
    dar_ref,
    db_ref,
):
    @pl.when(pl.program_id(0) == 0)
    def _():
        dar_ref[...] = jnp.zeros_like(dar_ref)
        db_ref[...] = jnp.zeros_like(db_ref)

    values = x_ref[...].astype(F32)
    gain = gain_ref[...]
    inverse = rms_inverse(values)
    normed = (values * inverse * gain).astype(BF16)
    lowrank = zg_ref[: 3 * COLS]
    gates = zg_ref[3 * COLS :]
    mixed = pad_rows(lowrank * gates, LANES).astype(BF16)
    grads = (dq_ref[...], dk_ref[...], dv_ref[...])
    columns = [slice(index * D, (index + 1) * D) for index in range(3)]
    grad_mixed = jnp.zeros((ROWS, LANES), F32)
    for grad, lanes in zip(grads, columns):
        grad_mixed = grad_mixed + dot_nt(grad, b_ref[:, lanes])
    grad_normed = jnp.zeros((ROWS, D), F32)
    for grad, lanes in zip(grads, columns):
        grad_normed = grad_normed + dot_nt(grad, w_ref[:, lanes])
        db_ref[:, lanes] += dot(mixed, grad)
    turned = grad_mixed.T
    parts = []
    for first in range(0, 3 * COLS, COLS):
        rows = slice(first, first + COLS)
        parts.append(gate_grads(turned[rows], lowrank[rows], gates[rows]))
    delta = jnp.concatenate([part[0] for part in parts] + [part[1] for part in parts], axis=0)
    delta = pad_rows(delta, 2 * LANES).astype(BF16)
    grad_normed = grad_normed + dot_nt(delta.T, ar_ref[...])
    dar_ref[...] += dot(delta, normed)
    out_ref[...] = dmid_ref[...] + rms_backward(values, gain, inverse, grad_normed)


def project_back(x, gain, w_qkv, ar_qkv, b_qkv, zg, dq, dk, dv, dmid):
    length = x.shape[0]
    tile = pl.BlockSpec((ROWS, D), lambda i: (i, 0))
    out_shape = [
        jax.ShapeDtypeStruct((length, D), F32),
        jax.ShapeDtypeStruct((2 * LANES, D), F32),
        jax.ShapeDtypeStruct((LANES, 3 * D), F32),
    ]
    return pl.pallas_call(
        project_back_kernel,
        grid=(length // ROWS,),
        in_specs=[
            tile,
            whole((1, D)),
            whole(w_qkv.shape),
            whole(ar_qkv.shape),
            whole(b_qkv.shape),
            pl.BlockSpec((6 * COLS, ROWS), lambda i: (0, i)),
            tile,
            tile,
            tile,
            tile,
        ],
        out_specs=[tile] + [whole(member.shape) for member in out_shape[1:]],
        out_shape=out_shape,
        compiler_params=params(),
        name="project_back",
    )(x, gain, w_qkv, ar_qkv, b_qkv, zg, dq, dk, dv, dmid)


PARAM_ROWS = sum((COLS + EXPERTS) * fan_in + COLS * fan_out for fan_in, fan_out in FANS) // LANES


def piece_rows():
    result = []
    row = 0
    for fan_in, fan_out in FANS:
        starts = []
        for count in (fan_in * COLS, COLS * fan_out, fan_in * EXPERTS):
            starts.append(row)
            row += count // LANES
        result.append(tuple(starts))
    return result


def shard_rows(count):
    return -(-count // (LANES * 16)) * 16


def align_in(flat_ref, shard, start):
    first, shift = divmod(start, LANES)
    rows = shard.shape[0]
    if shift == 0:
        flat_ref[first : first + rows] = shard
        return
    turned = pltpu.roll(shard, shift, 1)
    lane = lane_iota((1, LANES))
    zeros = jnp.zeros((8, LANES), F32)
    upper = jnp.concatenate([turned, zeros], axis=0)
    lower = pltpu.roll(upper, 1, 0)
    kept = flat_ref[first : first + 8]
    merged = jnp.where(lane >= shift, upper, lower)
    inside = (row_iota((8, LANES)) == 0) & (lane_iota((8, LANES)) < shift)
    flat_ref[first : first + 8] = jnp.where(inside, kept, merged[:8])
    flat_ref[first + 8 : first + 8 + rows] = merged[8:]


def align_out(flat_ref, rows, start):
    first, shift = divmod(start, LANES)
    if shift == 0:
        return flat_ref[first : first + rows]
    block = flat_ref[first : first + rows + 8]
    turned = pltpu.roll(block, LANES - shift, 1)
    below = pltpu.roll(turned, rows + 7, 0)
    lane = lane_iota((1, LANES))
    return jnp.where(lane < LANES - shift, turned, below)[:rows]


def narrow_to_rows(flat_ref, base, fan_in, width, place, out_ref):
    period = 640 // width
    groups = fan_in // period
    lines = [flat_ref[pl.ds(base + k, groups, stride=5), :] for k in range(5)]
    lane = lane_iota((1, LANES))
    for b in range(period):
        first, shift = divmod(width * b, LANES)
        amount = (place - shift) % LANES
        value = lines[first] if amount == 0 else pltpu.roll(lines[first], amount, 1)
        if shift + width > LANES:
            value = jnp.where(
                lane < place + LANES - shift, value, pltpu.roll(lines[first + 1], amount, 1)
            )
        inside = (lane >= place) & (lane < place + width)
        out_ref[pl.ds(b, groups, stride=period), :] = jnp.where(inside, value, 0.0)


def rows_to_narrow(in_ref, fan_in, width, place, flat_ref, base):
    period = 640 // width
    groups = fan_in // period
    lane = lane_iota((1, LANES))
    lines = [jnp.zeros((groups, LANES), F32) for _ in range(5)]
    for b in range(period):
        first, shift = divmod(width * b, LANES)
        amount = (shift - place) % LANES
        value = in_ref[pl.ds(b, groups, stride=period), :]
        value = value if amount == 0 else pltpu.roll(value, amount, 1)
        inside = (lane >= shift) & (lane < shift + width)
        lines[first] = jnp.where(inside, value, lines[first])
        if shift + width > LANES:
            lines[first + 1] = jnp.where(lane < shift + width - LANES, value, lines[first + 1])
    for k in range(5):
        flat_ref[pl.ds(base + k, groups, stride=5), :] = lines[k]


def spread_matrix(place):
    row = row_iota((LANES, LANES))
    lane = lane_iota((LANES, LANES)) - place
    hit = (lane >= RANK * row) & (lane < RANK * row + RANK) & (row < EXPERTS)
    return jnp.where(hit, 1.0, 0.0).astype(BF16)


def unpack_kernel(
    count,
    shards_ref,
    ar_qkv_ref,
    b_qkv_ref,
    ar_out_ref,
    b_out_ref,
    ar_in_ref,
    b_in_ref,
    ar_down_ref,
    b_down_ref,
    flat,
    down,
    router,
):
    shards = shards_ref.shape[0]
    for index in range(shards):
        align_in(flat, shards_ref[index].astype(F32), index * count)
    starts = piece_rows()

    def ups(base, fan_out, first, out_ref, column):
        width = fan_out // LANES
        above = jnp.zeros((first, LANES), F32)
        below = jnp.zeros((LANES - COLS - first, LANES), F32)
        for k in range(width):
            part = flat[pl.ds(base + k, COLS, stride=width), :]
            parts = [part, below] if first == 0 else [above, part, below]
            lanes = slice(column + k * LANES, column + (k + 1) * LANES)
            out_ref[:, lanes] = jnp.concatenate(parts, axis=0).astype(BF16)

    packed = [jnp.zeros((D, LANES), F32) for _ in range(2)]
    for index in range(3):
        base_a, base_b, base_r = starts[index]
        narrow_to_rows(flat, base_a, D, COLS, index * COLS, down)
        narrow_to_rows(flat, base_r, D, EXPERTS, 0, router)
        packed[0] = packed[0] + down[:D]
        for half in range(2):
            matrix = spread_matrix((3 + index) * COLS - half * LANES)
            packed[half] = packed[half] + dot(router[:D].astype(BF16), matrix)
        ups(base_b, D, index * COLS, b_qkv_ref, index * D)
    ar_qkv_ref[:, :LANES] = packed[0].astype(BF16)
    ar_qkv_ref[:, LANES:] = packed[1].astype(BF16)
    members = ((ar_out_ref, b_out_ref), (ar_in_ref, b_in_ref), (ar_down_ref, b_down_ref))
    for index, (ar_ref, b_ref) in zip(range(3, 6), members):
        base_a, base_b, base_r = starts[index]
        fan_in, fan_out = FANS[index]
        narrow_to_rows(flat, base_a, fan_in, COLS, 0, down)
        narrow_to_rows(flat, base_r, fan_in, EXPERTS, 0, router)
        wide = dot(router[:fan_in].astype(BF16), spread_matrix(COLS))
        ar_ref[...] = (down[:fan_in] + wide).astype(BF16)
        ups(base_b, fan_out, 0, b_ref, 0)


def unpack(shards, count):
    rows = shards.shape[1]
    shapes = ((D, 2 * LANES), (LANES, 3 * D), (D, LANES), (LANES, D), (D, LANES), (LANES, FF), (FF, LANES), (LANES, D))
    return pl.pallas_call(
        functools.partial(unpack_kernel, count),
        in_specs=[pl.BlockSpec(memory_space=pltpu.VMEM)],
        out_specs=[pl.BlockSpec(memory_space=pltpu.VMEM)] * len(shapes),
        out_shape=[jax.ShapeDtypeStruct(shape, BF16) for shape in shapes],
        scratch_shapes=[
            pltpu.VMEM((PARAM_ROWS + rows + 20, LANES), F32),
            pltpu.VMEM((FF, LANES), F32),
            pltpu.VMEM((FF, LANES), F32),
        ],
        compiler_params=params(),
        name="unpack",
    )(shards)


def gather_matrix(place):
    row = row_iota((LANES, LANES)) - place
    lane = lane_iota((LANES, LANES))
    return jnp.where((row == RANK * lane) & (lane < EXPERTS), 1.0, 0.0).astype(BF16)


def assemble_kernel(
    count,
    dar_qkv_ref,
    db_qkv_ref,
    dar_out_ref,
    db_out_ref,
    dar_in_ref,
    db_in_ref,
    dar_down_ref,
    db_down_ref,
    shards_ref,
    flat,
    down,
    router,
):
    starts = piece_rows()

    def ups(base, fan_out, first, grad_ref, column):
        width = fan_out // LANES
        for k in range(width):
            lanes = slice(column + k * LANES, column + (k + 1) * LANES)
            flat[pl.ds(base + k, COLS, stride=width), :] = grad_ref[first : first + COLS, lanes]

    def routers(packed, place):
        matrix = gather_matrix(place)
        high = packed.astype(BF16)
        return dot(high, matrix) + dot((packed - high.astype(F32)).astype(BF16), matrix)

    members = (
        (3, dar_out_ref, db_out_ref),
        (4, dar_in_ref, db_in_ref),
        (5, dar_down_ref, db_down_ref),
    )
    for index, dar_ref, db_ref in members:
        base_a, base_b, base_r = starts[index]
        fan_in, fan_out = FANS[index]
        packed = pad_rows(dar_ref[...], LANES).T
        down[:fan_in] = packed
        rows_to_narrow(down, fan_in, COLS, 0, flat, base_a)
        router[:fan_in] = routers(packed, COLS)
        rows_to_narrow(router, fan_in, EXPERTS, 0, flat, base_r)
        ups(base_b, fan_out, 0, db_ref, 0)
    down[:D] = dar_qkv_ref[:LANES].T
    first_router = 3 * COLS
    packed_router = dar_qkv_ref[first_router : first_router + LANES].T
    for index in range(3):
        base_a, base_b, base_r = starts[index]
        rows_to_narrow(down, D, COLS, index * COLS, flat, base_a)
        router[:D] = routers(packed_router, index * COLS)
        rows_to_narrow(router, D, EXPERTS, 0, flat, base_r)
        ups(base_b, D, index * COLS, db_qkv_ref, index * D)
    shards, rows = shards_ref.shape[0], shards_ref.shape[1]
    for index in range(shards):
        shards_ref[index] = align_out(flat, rows, index * count)


def assemble(grads, shards, count):
    rows = shard_rows(count)
    return pl.pallas_call(
        functools.partial(assemble_kernel, count),
        in_specs=[pl.BlockSpec(memory_space=pltpu.VMEM)] * len(grads),
        out_specs=pl.BlockSpec(memory_space=pltpu.VMEM),
        out_shape=jax.ShapeDtypeStruct((shards, rows, LANES), F32),
        scratch_shapes=[
            pltpu.VMEM((PARAM_ROWS + rows + 20, LANES), F32),
            pltpu.VMEM((FF, LANES), F32),
            pltpu.VMEM((FF, LANES), F32),
        ],
        compiler_params=params(),
        name="assemble",
    )(*grads)


MESH = pl.DeviceIdType.MESH


def place_of(axes, sizes):
    me = lax.axis_index(axes[0]) * sizes[1] + lax.axis_index(axes[1])

    def coordinates(number):
        return (number // sizes[1], number % sizes[1])

    return me, coordinates


def partners_of(me):
    low = me % 8
    core = low % 2
    y = (low // 2) % 2
    x = low // 4
    over_x = low + 4 * (1 - 2 * x)
    over_y = low + 2 * (1 - 2 * y)
    first = over_x * (1 - core) + over_y * core
    second = over_y * (1 - core) + over_x * core
    both = first + second - low
    other = 1 - 2 * core
    return low, first, second, both, other, over_x, over_y


def greet(peers):
    barrier = pltpu.get_barrier_semaphore()
    for peer in peers:
        pl.semaphore_signal(barrier, inc=1, device_id=peer, device_id_type=MESH)
    pl.semaphore_wait(barrier, len(peers))


def gather_kernel(axes, sizes, shard_ref, out_ref, send, receive, local):
    me, coordinates = place_of(axes, sizes)
    groups = out_ref.shape[0]
    group = me // 8
    low, first, second, both, other, over_x, over_y = partners_of(me)

    def device(group_index, low_index):
        return coordinates(group_index * 8 + low_index)

    others = [(group + step) % groups for step in range(1, groups)]
    peers = [device(index, low) for index in others]
    peers += [device(group, partner) for partner in (first, second, low + other)]
    greet(peers)
    counter = [0]

    def start(source, target, peer):
        index = counter[0]
        counter[0] += 1
        copy = pltpu.make_async_remote_copy(
            src_ref=source,
            dst_ref=target,
            send_sem=send.at[index],
            recv_sem=receive.at[index],
            device_id=peer,
            device_id_type=MESH,
        )
        copy.start()
        return copy

    own = pltpu.make_async_copy(shard_ref, out_ref.at[group, low], local)
    own.start()
    around = [start(shard_ref, out_ref.at[group, low], device(index, low)) for index in others]
    own.wait()
    for copy in around:
        copy.wait()

    def push(part, partner):
        return start(out_ref.at[:, part], out_ref.at[:, part], device(group, partner))

    one = push(low, first)
    two = push(low, second)
    core_own = push(low, low + other)
    one.wait()
    three = push(first, second)
    core_first = push(first, low + other)
    two.wait()
    core_second = push(second, low + other)
    three.wait()
    core_both = push(both, low + other)
    for copy in (core_own, core_first, core_second, core_both):
        copy.wait()


def gather(shard, axes, sizes):
    groups = sizes[0] * sizes[1] // 8
    copies = groups - 1 + 7
    return pl.pallas_call(
        functools.partial(gather_kernel, axes, sizes),
        in_specs=[pl.BlockSpec(memory_space=pltpu.VMEM)],
        out_specs=pl.BlockSpec(memory_space=pltpu.VMEM),
        out_shape=jax.ShapeDtypeStruct((groups, 8, *shard.shape), shard.dtype),
        scratch_shapes=[
            pltpu.SemaphoreType.DMA((copies,)),
            pltpu.SemaphoreType.DMA((copies,)),
            pltpu.SemaphoreType.DMA,
        ],
        compiler_params=params(collective_id=0, has_side_effects=True),
        name="gather",
    )(shard)


def reduce_kernel(
    axes, sizes, parts_ref, sums_ref, out_ref, total_ref, outbox, inbox, near_out, near_in, far_in, own, send, receive
):
    me, coordinates = place_of(axes, sizes)
    groups = parts_ref.shape[0]
    group = me // 8
    low, first, second, both, other, over_x, over_y = partners_of(me)

    def device(group_index, low_index):
        return coordinates(group_index * 8 + low_index)

    others = [(group + step) % groups for step in range(1, groups)]
    peers = [device(index, low) for index in others]
    peers += [device(group, partner) for partner in (first, second, low + other)]
    greet(peers)
    counter = [0]

    def start(source, target, peer):
        index = counter[0]
        counter[0] += 1
        copy = pltpu.make_async_remote_copy(
            src_ref=source,
            dst_ref=target,
            send_sem=send.at[index],
            recv_sem=receive.at[index],
            device_id=peer,
            device_id_type=MESH,
        )
        copy.start()
        return copy

    def push(slot, value, partner):
        outbox[slot] = value.astype(BF16)
        return start(outbox.at[slot], inbox.at[slot], device(group, partner))

    def push_sums(slot, value, partner):
        near_out[slot] = value
        return start(near_out.at[slot], near_in.at[slot], device(group, partner))

    mate = low + other
    sums = sums_ref[...]
    sums_core = push_sums(0, sums, mate)
    core = [
        push(slot, parts_ref[:, part + other], mate)
        for slot, part in enumerate((first, both, second, low))
    ]
    core[0].wait()
    half_second = parts_ref[:, second] + inbox[0].astype(F32)
    to_second = push(4, half_second, second)
    core[1].wait()
    half_both = parts_ref[:, both] + inbox[1].astype(F32)
    to_both = push(5, half_both, second)
    sums_core.wait()
    sums = sums + near_in[0]
    sums_x = push_sums(1, sums, over_x)
    core[2].wait()
    half_first = parts_ref[:, first] + inbox[2].astype(F32)
    core[3].wait()
    half_low = parts_ref[:, low] + inbox[3].astype(F32)
    to_both.wait()
    quarter_first = half_first + inbox[5].astype(F32)
    to_first = push(6, quarter_first, first)
    sums_x.wait()
    sums = sums + near_in[1]
    sums_y = push_sums(2, sums, over_y)
    to_second.wait()
    half_low = half_low + inbox[4].astype(F32)
    to_first.wait()
    own[...] = half_low + inbox[6].astype(F32)
    outbox[7] = own[...].astype(BF16)
    around = [
        start(outbox.at[7, index], far_in.at[step], device(index, low))
        for step, index in enumerate(others)
    ]
    sums_y.wait()
    near_out[3] = sums + near_in[2]
    around_sums = [
        start(near_out.at[3], near_in.at[4 + group], device(index, low))
        for index in others
    ]
    near_in[4 + group] = near_out[3]
    total = own[group]
    for step, copy in enumerate(around):
        copy.wait()
        total = total + far_in[step].astype(F32)
    out_ref[...] = total
    for copy in around_sums:
        copy.wait()
    whole_sum = near_in[4]
    for index in range(1, groups):
        whole_sum = whole_sum + near_in[4 + index]
    total_ref[...] = whole_sum


def reduce_scatter(parts, sums, axes, sizes):
    groups, _, rows, lanes = parts.shape
    copies = 7 + 3 + 2 * (groups - 1)
    return pl.pallas_call(
        functools.partial(reduce_kernel, axes, sizes),
        in_specs=[pl.BlockSpec(memory_space=pltpu.VMEM)] * 2,
        out_specs=[pl.BlockSpec(memory_space=pltpu.VMEM)] * 2,
        out_shape=[
            jax.ShapeDtypeStruct((rows, lanes), F32),
            jax.ShapeDtypeStruct(sums.shape, F32),
        ],
        scratch_shapes=[
            pltpu.VMEM((8, groups, rows, lanes), BF16),
            pltpu.VMEM((7, groups, rows, lanes), BF16),
            pltpu.VMEM((4, *sums.shape), F32),
            pltpu.VMEM((4 + groups, *sums.shape), F32),
            pltpu.VMEM((groups - 1, rows, lanes), BF16),
            pltpu.VMEM((groups, rows, lanes), F32),
            pltpu.SemaphoreType.DMA((copies,)),
            pltpu.SemaphoreType.DMA((copies,)),
        ],
        compiler_params=params(collective_id=1, has_side_effects=True),
        name="reduce_scatter",
    )(parts, sums)


def per_device(
    tokens,
    lengths,
    buckets,
    rel_table,
    gain_attn,
    gain_ff,
    w_qkv,
    w_out,
    w_in,
    w_down,
    adapters,
    cotangent,
    axes,
    sizes,
):
    seq_count, length, width = tokens.shape
    x = tokens.reshape(length, width)
    cot = cotangent.reshape(length, width)
    devices = sizes[0] * sizes[1]
    count = adapters.shape[0]
    rows = shard_rows(count)
    shard = jnp.pad(adapters, (0, rows * LANES - count)).reshape(rows, LANES)
    if devices == 1:
        shards = shard[None]
    else:
        shards = gather(shard, axes, sizes).reshape(devices, rows, LANES)
    ar_qkv, b_qkv, *rest = unpack(shards, count)
    gain_first = gain_attn.reshape(1, width)
    gain_second = gain_ff.reshape(1, width)

    reversed_buckets = jnp.pad(buckets[::-1], (0, 1))
    hits = (jnp.arange(rel_table.shape[0])[:, None] == reversed_buckets[None, :]).astype(F32)
    offsets = jnp.dot(rel_table.T * LOG2E, hits, precision=lax.Precision.HIGHEST)
    offsets = offsets.reshape(HEADS // 2, 2, 2 * length)

    qt, k, kt, v, vt, zg = project(x, gain_first, w_qkv, ar_qkv, b_qkv)
    ot, lse = attend(lengths, offsets, qt, k, vt)
    block_out, dmid, gt, sums, *grads = middle_part(
        lengths, ot, x, cot, gain_second, w_out, w_in, w_down, rest
    )
    dq, dk, dv = attend_back(lengths, offsets, qt, k, kt, v, ot, gt, lse)
    tokens_grad, dar_qkv, db_qkv = project_back(
        x, gain_first, w_qkv, ar_qkv, b_qkv, zg, dq, dk, dv, dmid
    )

    parts = assemble((dar_qkv, db_qkv, *grads), devices, count)
    sums = jnp.where(jnp.arange(LANES)[None, :] == 4, jnp.sum(lengths).astype(F32), sums)
    if devices == 1:
        mine, sums = parts[0], sums
    else:
        parts = parts.reshape(devices // 8, 8, rows, LANES)
        mine, sums = reduce_scatter(parts, sums, axes, sizes)
    grad_shard = mine.reshape(-1)[:count]
    root_squares = jnp.sqrt(sums[0, :4] / (sums[0, 4] * width))
    return (
        block_out.reshape(tokens.shape),
        tokens_grad.reshape(tokens.shape),
        grad_shard,
        root_squares,
    )


def solution(mesh):
    axes = tuple(mesh.axis_names)
    sizes = tuple(mesh.shape[axis] for axis in axes)
    sequence = P(axes, None, None)
    placed = (
        sequence,
        P(axes),
        P(),
        P(),
        P(),
        P(),
        P(),
        P(),
        P(),
        P(),
        P(axes),
        sequence,
    )
    return jax.shard_map(
        functools.partial(per_device, axes=axes, sizes=sizes),
        mesh=mesh,
        in_specs=placed,
        out_specs=(sequence, sequence, P(axes), P()),
        check_vma=False,
    )
```

```python
import functools

import jax
import jax.numpy as jnp
from jax import lax
from jax.experimental import pallas as pl
from jax.experimental.pallas import tpu as pltpu
from jax.sharding import PartitionSpec as P

D = 768
FF = 3072
HEADS = 12
HDIM = 64
EXPERTS = 10
RANK = 4
FANS = ((D, D), (D, D), (D, D), (D, D), (D, FF), (FF, D))
COLS = EXPERTS * RANK
LANES = 128

EPSILON = 1e-06
MASKED = -1000000000.0
GELU_SCALE = 0.7978845608028654
GELU_CUBIC = 0.044715
LOG2E = 1.4426950408889634
LN2 = 0.6931471805599453
QUERY_SCALE = 0.125 * LOG2E

ROWS = 256
MIDDLE_ROWS = 512
CHUNK = 512
QBLOCK = 256
UP_ROWS = 48
DOWN_ROWS = 2 * COLS
VMEM_BYTES = 60 * 1024 * 1024

F32 = jnp.float32
BF16 = jnp.bfloat16


def dot(a, b):
    return lax.dot_general(a, b, (((1,), (0,)), ((), ())), preferred_element_type=F32)


def dot_nt(a, b):
    return lax.dot_general(a, b, (((1,), (1,)), ((), ())), preferred_element_type=F32)


def dot_tn(a, b):
    return lax.dot_general(a, b, (((0,), (0,)), ((), ())), preferred_element_type=F32)


def lane_iota(shape):
    return lax.broadcasted_iota(jnp.int32, shape, 1)


def row_iota(shape):
    return lax.broadcasted_iota(jnp.int32, shape, 0)


def gates_of(logits):
    weights = jnp.exp(logits - jnp.max(logits, axis=0, keepdims=True))
    return weights * (4.0 / jnp.sum(weights, axis=0, keepdims=True))


def gate_grads(grad_mixed, lowrank, gates):
    product = grad_mixed * lowrank
    summed = product
    for step in range(1, RANK):
        summed = summed + pltpu.roll(product, COLS - step, 0)
    centre = jnp.sum(gates * product, axis=0, keepdims=True)
    first = row_iota(gates.shape) % RANK == 0
    return grad_mixed * gates, jnp.where(first, gates * (summed - centre), 0.0)


def pad_rows(value, rows):
    return jnp.concatenate([value, jnp.zeros((rows - value.shape[0], value.shape[1]), F32)], axis=0)


def single_gates(packed):
    turned = packed.T
    lowrank = turned[:COLS]
    gates = gates_of(turned[COLS : 2 * COLS])
    mixed = pad_rows(lowrank * gates, LANES).astype(BF16)
    return lowrank, gates, mixed, mixed.T


def single_deltas(grad_mixed, lowrank, gates):
    parts = gate_grads(grad_mixed.T[:COLS], lowrank, gates)
    delta = pad_rows(jnp.concatenate(parts, axis=0), LANES).astype(BF16)
    return delta, delta.T


def rms_inverse(values):
    return lax.rsqrt(jnp.mean(values * values, axis=-1, keepdims=True) + EPSILON)


def rms_backward(values, gain, inverse, grad_normed):
    weighted = grad_normed * gain
    return inverse * weighted - values * (
        inverse * inverse * inverse * jnp.mean(values * weighted, axis=-1, keepdims=True)
    )


def params(**more):
    return pltpu.CompilerParams(vmem_limit_bytes=VMEM_BYTES, **more)


def whole(shape):
    zeros = (0,) * len(shape)
    return pl.BlockSpec(shape, lambda *_: zeros, pipeline_mode=pl.Buffered(1))


def project_kernel(
    link,
    shard_ref,
    x_ref,
    gain_ref,
    w_ref,
    ar_ref,
    b_ref,
    qt_ref,
    k_ref,
    kt_ref,
    v_ref,
    vt_ref,
    zg_ref,
    shards_ref,
    landing,
    send,
    receive,
    local,
):
    step = pl.program_id(0)
    if link is not None:
        axes, sizes, span = link
        ring = Ring(axes, sizes, send, receive)
        phases = gather_phases(ring, span, shard_ref, landing, local)
        for turn, phase in enumerate(phases[:4]):
            pl.when(step == turn)(phase)
    values = x_ref[...].astype(F32)
    normed = (values * rms_inverse(values) * gain_ref[...]).astype(BF16)
    packed = dot(normed, ar_ref[...]).T
    lowrank = packed[: 3 * COLS]
    gates = jnp.concatenate(
        [gates_of(packed[first : first + COLS]) for first in range(3 * COLS, 6 * COLS, COLS)], axis=0
    )
    zg_ref[: 3 * COLS] = lowrank
    zg_ref[3 * COLS :] = gates
    mixed = pad_rows(lowrank * gates, LANES).astype(BF16).T
    for index in range(3):
        columns = slice(index * D, (index + 1) * D)
        part = dot(normed, w_ref[:, columns]) + dot(mixed, b_ref[:, columns])
        if index == 0:
            qt_ref[...] = (part * QUERY_SCALE).astype(BF16).T
        else:
            low = part.astype(BF16)
            natural, turned = ((k_ref, kt_ref), (v_ref, vt_ref))[index - 1]
            natural[...] = low
            turned[...] = low.T

    if link is not None:

        @pl.when(step == pl.num_programs(0) - 1)
        def _():
            phases[4]()
            shards_ref[...] = landing[...]


def project(x, gain, w_qkv, ar_qkv, b_qkv, shard, axes, sizes, span):
    length = x.shape[0]
    devices = sizes[0] * sizes[1]
    link = None if devices == 1 else (axes, sizes, span)
    groups = max(devices // 8, 1)
    landing = (max(span[1] - span[0], 1), 8, *shard.shape)
    if link is None:
        landing = (1, 8, 16, LANES)
    tile = pl.BlockSpec((ROWS, D), lambda i: (i, 0))
    turned = pl.BlockSpec((D, ROWS), lambda i: (0, i))
    natural_shape = jax.ShapeDtypeStruct((length, D), BF16)
    turned_shape = jax.ShapeDtypeStruct((D, length), BF16)
    return pl.pallas_call(
        functools.partial(project_kernel, link),
        grid=(length // ROWS,),
        in_specs=[
            whole(shard.shape),
            tile,
            whole((1, D)),
            whole(w_qkv.shape),
            whole(ar_qkv.shape),
            whole(b_qkv.shape),
        ],
        out_specs=[
            turned,
            tile,
            turned,
            tile,
            turned,
            pl.BlockSpec((6 * COLS, ROWS), lambda i: (0, i)),
            whole(landing),
        ],
        out_shape=[
            turned_shape,
            natural_shape,
            turned_shape,
            natural_shape,
            turned_shape,
            jax.ShapeDtypeStruct((6 * COLS, length), F32),
            jax.ShapeDtypeStruct(landing, BF16),
        ],
        scratch_shapes=[pltpu.VMEM(landing, BF16), *gather_semaphores(groups)],
        compiler_params=params()
        if link is None
        else params(collective_id=1, has_side_effects=True),
        name="project",
    )(shard, x, gain, w_qkv, ar_qkv, b_qkv)


def bias_table(offset_row, length):
    spread = jnp.broadcast_to(offset_row, (LANES, 2 * length))
    return pltpu.roll(spread, 2 * length - (LANES - 1), 1, stride=1, stride_axis=0)


def add_bias(scores, table_ref, start, length):
    width = scores.shape[1]
    parts = []
    for block in range(length // LANES):
        offset = start - LANES * block + (length - LANES)
        parts.append(
            scores[block * LANES : (block + 1) * LANES] + table_ref[:, offset : offset + width]
        )
    return jnp.concatenate(parts, axis=0)


def key_extras(length_ref, shape, odd):
    lane = lane_iota(shape) - (0 if odd else HDIM)
    invalid = row_iota(shape) >= length_ref[0]
    extras = jnp.where((lane == 0) & invalid, MASKED, 0.0)
    return jnp.where((lane >= 1) & (lane <= 3), 1.0, extras).astype(BF16)


def head_lanes(odd):
    lane = lane_iota((1, LANES))
    return ((lane >= HDIM) if odd else (lane < HDIM)).astype(F32).astype(BF16)


def extra_rows(rows):
    width = rows[0].shape[1]
    index = row_iota((8, width))
    block = jnp.zeros((8, width), F32)
    for place, row in enumerate(rows):
        block = jnp.where(index == place, row, block)
    return jnp.concatenate([block, jnp.zeros((HDIM - 8, width), F32)], axis=0).astype(BF16)


def split_three(row):
    high = row.astype(BF16).astype(F32)
    middle = (row - high).astype(BF16).astype(F32)
    return high, middle, row - high - middle


def join_rows(rows, extras, odd):
    return jnp.concatenate([extras, rows] if odd else [rows, extras], axis=0)


def attend_kernel(length_ref, off_ref, qt_ref, k_ref, vt_ref, o_ref, lse_ref, table, key_more):
    length = k_ref.shape[0]

    @pl.when(pl.program_id(0) == 0)
    def _():
        for odd in range(2):
            key_more[odd] = key_extras(length_ref, k_ref.shape, odd)

    for odd in range(2):
        half = slice(odd * HDIM, (odd + 1) * HDIM)
        row = 2 * pl.program_id(0) + odd
        table[odd] = bias_table(off_ref[pl.ds(row, 1), :], length)
        keys = k_ref[...] * head_lanes(odd) + key_more[odd]
        ones = jnp.ones((1, length), F32)
        queries = join_rows(qt_ref[half, :], extra_rows([ones]), odd)
        values = jnp.concatenate([vt_ref[half, :], jnp.ones((16, length), BF16)], axis=0)
        starts = range(0, length, QBLOCK)
        scores = [
            add_bias(dot(keys, queries[:, start : start + QBLOCK]), table.at[odd], start, length)
            for start in starts
        ]
        peaks = [jnp.max(part, axis=0, keepdims=True) for part in scores]
        weights = [jnp.exp2(part - peak).astype(BF16) for part, peak in zip(scores, peaks)]
        for start, peak, part in zip(starts, peaks, weights):
            columns = slice(start, start + QBLOCK)
            summed = dot(values, part)
            total = summed[HDIM : HDIM + 1]
            o_ref[half, columns] = (summed[:HDIM] / total).astype(BF16)
            lse_ref[0, odd : odd + 1, columns] = peak + jnp.log2(total)


def attend(length_valid, offsets, qt, k, vt):
    length = k.shape[0]
    turned = pl.BlockSpec((LANES, length), lambda p: (p, 0))
    natural = pl.BlockSpec((length, LANES), lambda p: (0, p))
    return pl.pallas_call(
        attend_kernel,
        grid=(HEADS // 2,),
        in_specs=[
            pl.BlockSpec(memory_space=pltpu.SMEM),
            whole(offsets.shape),
            turned,
            natural,
            turned,
        ],
        out_specs=[turned, pl.BlockSpec((1, 2, length), lambda p: (p, 0, 0))],
        out_shape=[
            jax.ShapeDtypeStruct((D, length), BF16),
            jax.ShapeDtypeStruct((HEADS // 2, 2, length), F32),
        ],
        scratch_shapes=[
            pltpu.VMEM((2, LANES, 2 * length), F32),
            pltpu.VMEM((2, length, LANES), BF16),
        ],
        compiler_params=params(),
        name="attend",
    )(length_valid, offsets, qt, k, vt)


def attend_back_kernel(
    link,
    length_ref,
    off_ref,
    qt_ref,
    k_ref,
    kt_ref,
    v_ref,
    ot_ref,
    gt_ref,
    lse_ref,
    parts_ref,
    sums_ref,
    dq_ref,
    dk_ref,
    dv_ref,
    rest_ref,
    roots_ref,
    table,
    key_more,
    weights_all,
    grads_all,
    *scratch,
):
    length = k_ref.shape[0]
    step = pl.program_id(0)

    def finish_sums(total):
        roots_ref[...] = jnp.sqrt(total / (total[:, 4:5] * D))

    if link is None:
        finish_sums(sums_ref[...])
    else:
        axes, sizes, span = link
        *boxes, total, near_out, near_in, send, receive = scratch
        ring = Ring(axes, sizes, send, receive)
        phases = reduce_phases(
            ring, span, parts_ref, (*boxes, total), sums_ref, (near_out, near_in)
        )
        for turn, phase in enumerate(phases[:4]):
            pl.when(step == turn)(phase)

        @pl.when(step == pl.num_programs(0) - 1)
        def _():
            phases[4](finish_sums)
            rest_ref[...] = total[...]

    @pl.when(pl.program_id(0) == 0)
    def _():
        for odd in range(2):
            key_more[odd] = key_extras(length_ref, k_ref.shape, odd)

    lane = lane_iota((1, LANES))
    first_lanes = lane < HDIM
    grad_query_parts = []
    for odd in range(2):
        half = slice(odd * HDIM, (odd + 1) * HDIM)
        row = 2 * pl.program_id(0) + odd
        table[odd] = bias_table(off_ref[pl.ds(row, 1), :], length)
        keys = k_ref[...] * head_lanes(odd) + key_more[odd]
        place = lane - (0 if odd else HDIM)
        value_more = ((place >= 0) & (place < 3)).astype(F32).astype(BF16)
        values = v_ref[...] * head_lanes(odd) + value_more
        ones = jnp.ones((1, length), F32)
        lse = lse_ref[0, odd : odd + 1, :]
        queries = join_rows(
            qt_ref[half, :], extra_rows([ones] + [-part for part in split_three(lse)]), odd
        )
        delta = jnp.sum(
            ot_ref[half, :].astype(F32) * gt_ref[half, :].astype(F32), axis=0, keepdims=True
        )
        grads = join_rows(
            gt_ref[half, :], extra_rows([-part for part in split_three(delta)]), odd
        )
        for start in range(0, length, QBLOCK):
            columns = slice(start, start + QBLOCK)
            scores = add_bias(dot(keys, queries[:, columns]), table.at[odd], start, length)
            weights = jnp.exp2(scores)
            weights_all[:, columns] = weights.astype(BF16)
            grad_scores = weights * dot(values, grads[:, columns])
            grads_all[:, columns] = grad_scores.astype(BF16)
        grad_query_parts.append(dot(kt_ref[half, :], grads_all[...]) * 0.125)
        grad_values = dot_nt(weights_all[...], gt_ref[...])
        grad_keys = dot_nt(grads_all[...], qt_ref[...]) * LN2
        if odd:
            dv_ref[...] = jnp.where(first_lanes, even_values, grad_values).astype(BF16)
            dk_ref[...] = jnp.where(first_lanes, even_keys, grad_keys).astype(BF16)
        else:
            even_values, even_keys = grad_values, grad_keys
    dq_ref[...] = jnp.concatenate(grad_query_parts, axis=0).T.astype(BF16)


def attend_back(
    length_valid, offsets, qt, k, kt, v, ot, gt, lse, parts, sums, axes, sizes, span
):
    length = k.shape[0]
    devices = sizes[0] * sizes[1]
    link = None if devices == 1 else (axes, sizes, span)
    rows = parts.shape[-2]
    rest_rows = rows if link else 8
    more = []
    if link:
        groups = devices // 8
        copies = 10 + 2 * groups
        more = reduce_scratch(groups, span[1] - span[0], rows) + [
            pltpu.VMEM((rows, LANES), F32),
            pltpu.VMEM((4, *sums.shape), F32),
            pltpu.VMEM((3 + groups, *sums.shape), F32),
            pltpu.SemaphoreType.DMA((copies,)),
            pltpu.SemaphoreType.DMA((copies,)),
        ]
    turned = pl.BlockSpec((LANES, length), lambda p: (p, 0))
    natural = pl.BlockSpec((length, LANES), lambda p: (0, p))
    natural_shape = jax.ShapeDtypeStruct((length, D), BF16)
    return pl.pallas_call(
        functools.partial(attend_back_kernel, link),
        grid=(HEADS // 2,),
        in_specs=[
            pl.BlockSpec(memory_space=pltpu.SMEM),
            whole(offsets.shape),
            turned,
            natural,
            turned,
            natural,
            turned,
            turned,
            pl.BlockSpec((1, 2, length), lambda p: (p, 0, 0)),
            whole(parts.shape) if link else pl.BlockSpec(memory_space=pl.ANY),
            whole(sums.shape),
        ],
        out_specs=[natural] * 3 + [whole((rest_rows, LANES)), whole(sums.shape)],
        out_shape=[natural_shape] * 3
        + [
            jax.ShapeDtypeStruct((rest_rows, LANES), F32),
            jax.ShapeDtypeStruct(sums.shape, F32),
        ],
        scratch_shapes=[
            pltpu.VMEM((2, LANES, 2 * length), F32),
            pltpu.VMEM((2, length, LANES), BF16),
            pltpu.VMEM((length, length), BF16),
            pltpu.VMEM((length, length), BF16),
        ]
        + more,
        compiler_params=params(collective_id=2, has_side_effects=True) if link else params(),
        name="attend_back",
    )(length_valid, offsets, qt, k, kt, v, ot, gt, lse, parts, sums)


def middle_kernel(
    length_ref,
    ot_ref,
    x_ref,
    cot_ref,
    gain_ref,
    w_out_ref,
    w_in_hbm,
    w_down_hbm,
    ar_out_ref,
    b_out_ref,
    ar_in_ref,
    b_in_ref,
    ar_down_ref,
    b_down_ref,
    out_ref,
    dmid_ref,
    gt_ref,
    sums_ref,
    dar_out_ref,
    db_out_ref,
    dar_in_ref,
    db_in_ref,
    dar_down_ref,
    db_down_ref,
    active,
    slope,
    sloped,
    grad_hidden,
    feeds,
    w_in_ref,
    w_down_ref,
    loaded,
):
    step = pl.program_id(0)
    loads = [
        pltpu.make_async_copy(w_in_hbm, w_in_ref, loaded.at[0]),
        pltpu.make_async_copy(w_down_hbm, w_down_ref, loaded.at[1]),
    ]

    @pl.when(step == 0)
    def _():
        for load in loads:
            load.start()
        for ref in (
            sums_ref,
            dar_out_ref,
            db_out_ref,
            dar_in_ref,
            db_in_ref,
            dar_down_ref,
            db_down_ref,
        ):
            ref[...] = jnp.zeros_like(ref)

    attended = ot_ref[...].T
    inputs = x_ref[...].astype(F32)
    gain = gain_ref[...]
    cot = cot_ref[...]

    packed_out = dot(attended, ar_out_ref[...])
    branch = dot(attended, w_out_ref[...])
    low_out, gates_out, mixed_out, natural = single_gates(packed_out)
    grad_mixed_down = dot_nt(cot, b_down_ref[...])
    branch = branch + dot(natural, b_out_ref[...])
    middle = inputs + branch
    inverse = rms_inverse(middle)
    normed = (middle * inverse * gain).astype(BF16)

    packed_in = dot(normed, ar_in_ref[...])
    low_in, gates_in, mixed_in, natural = single_gates(packed_in)

    def columns_of(index):
        return pl.ds(pl.multiple_of(index * CHUNK, CHUNK), CHUNK)

    def hidden_of(chunk):
        return dot(normed, w_in_ref[:, chunk]) + dot(natural, b_in_ref[:, chunk])

    def activate(chunk, values):
        grad_dense = dot_nt(cot, w_down_ref[chunk])
        square = values * values
        tangent = jnp.tanh(values * (GELU_SCALE + (GELU_SCALE * GELU_CUBIC) * square))
        half = 0.5 + 0.5 * tangent
        smooth = values * half
        active[:, chunk] = smooth.astype(BF16)
        steep = half + smooth * (1.0 - tangent) * (
            GELU_SCALE + (3.0 * GELU_SCALE * GELU_CUBIC) * square
        )
        slope[:, chunk] = steep.astype(BF16)
        sloped[:, chunk] = grad_dense * steep

    def forward_pair(pair, _):
        chunk_a = columns_of(2 * pair)
        chunk_b = columns_of(2 * pair + 1)
        hidden_a = hidden_of(chunk_a)
        hidden_b = hidden_of(chunk_b)
        activate(chunk_a, hidden_a)
        activate(chunk_b, hidden_b)
        return 0

    @pl.when(step == 0)
    def _():
        for load in loads:
            load.wait()

    lax.fori_loop(0, FF // (2 * CHUNK), forward_pair, 0)

    packed_down = dot(active[...], ar_down_ref[...])
    def feed_part(index, _):
        part = pl.ds(pl.multiple_of(index * 256, 256), 256)
        feeds[:, part] = dot(active[...], w_down_ref[:, part])
        return 0

    lax.fori_loop(0, 3, feed_part, 0)
    feed = feeds[...]
    low_down, gates_down, mixed_down, natural = single_gates(packed_down)
    delta_down, natural_delta = single_deltas(grad_mixed_down, low_down, gates_down)
    db_down_ref[...] += dot(mixed_down[:UP_ROWS], cot)
    feed = feed + dot(natural, b_down_ref[...])
    output = middle + feed
    out_ref[...] = output.astype(BF16)

    def backward_chunk(index, _):
        chunk = columns_of(index)
        grad_low = dot_nt(natural_delta, ar_down_ref[chunk])
        grad_hidden[:, chunk] = (
            sloped[:, chunk] + grad_low * slope[:, chunk].astype(F32)
        ).astype(BF16)
        return 0

    lax.fori_loop(0, FF // CHUNK, backward_chunk, 0)
    dar_down_ref[...] += dot(delta_down[:DOWN_ROWS], active[...])

    rows = row_iota((MIDDLE_ROWS, 1)) + step * MIDDLE_ROWS
    valid = (rows < length_ref[0]).astype(F32)
    lane = lane_iota((8, LANES))
    totals = jnp.where((lane == 4) & (step == 0), length_ref[0].astype(F32), 0.0)
    for place, member in enumerate((inputs, branch, feed, output)):
        kept = member * valid
        totals = jnp.where(lane == place, jnp.sum(kept * kept), totals)
    sums_ref[...] += totals

    grad_mixed = dot_nt(grad_hidden[...], b_in_ref[...])
    def back_part(index, _):
        part = pl.ds(pl.multiple_of(index * 256, 256), 256)
        feeds[:, part] = dot_nt(grad_hidden[...], w_in_ref[part])
        return 0

    lax.fori_loop(0, 3, back_part, 0)
    grad_normed = feeds[...]
    delta_in, natural_delta = single_deltas(grad_mixed, low_in, gates_in)
    db_in_ref[...] += dot(mixed_in[:UP_ROWS], grad_hidden[...])
    grad_normed = grad_normed + dot_nt(natural_delta, ar_in_ref[...])
    dar_in_ref[...] += dot(delta_in[:DOWN_ROWS], normed)

    grad_middle = cot.astype(F32) + rms_backward(middle, gain, inverse, grad_normed)
    dmid_ref[...] = grad_middle
    grad_branch = grad_middle.astype(BF16)
    grad_mixed = dot_nt(grad_branch, b_out_ref[...])
    grad_attended = dot_nt(grad_branch, w_out_ref[...])
    delta_out, natural_delta = single_deltas(grad_mixed, low_out, gates_out)
    grad_attended = grad_attended + dot_nt(natural_delta, ar_out_ref[...])
    gt_ref[...] = grad_attended.astype(BF16).T
    dar_out_ref[...] += dot(delta_out[:DOWN_ROWS], attended)
    db_out_ref[...] += dot(mixed_out[:UP_ROWS], grad_branch)


def middle_part(length_valid, ot, x, cot, gain, w_out, w_in, w_down, adapters):
    length = x.shape[0]
    tile = pl.BlockSpec((MIDDLE_ROWS, D), lambda i: (i, 0))
    turned = pl.BlockSpec((D, MIDDLE_ROWS), lambda i: (0, i))
    grad_shapes = [
        jax.ShapeDtypeStruct(shape, F32)
        for fan_in, fan_out in FANS[3:]
        for shape in ((DOWN_ROWS, fan_in), (UP_ROWS, fan_out))
    ]
    out_shape = [
        jax.ShapeDtypeStruct((length, D), BF16),
        jax.ShapeDtypeStruct((length, D), F32),
        jax.ShapeDtypeStruct((D, length), BF16),
        jax.ShapeDtypeStruct((8, LANES), F32),
    ] + grad_shapes
    return pl.pallas_call(
        middle_kernel,
        grid=(length // MIDDLE_ROWS,),
        in_specs=[pl.BlockSpec(memory_space=pltpu.SMEM), turned, tile, tile]
        + [whole(gain.shape), whole(w_out.shape)]
        + [pl.BlockSpec(memory_space=pl.ANY)] * 2
        + [whole(member.shape) for member in adapters],
        out_specs=[tile, tile, turned] + [whole(member.shape) for member in out_shape[3:]],
        out_shape=out_shape,
        scratch_shapes=[
            pltpu.VMEM((MIDDLE_ROWS, FF), BF16),
            pltpu.VMEM((MIDDLE_ROWS, FF), BF16),
            pltpu.VMEM((MIDDLE_ROWS, FF), F32),
            pltpu.VMEM((MIDDLE_ROWS, FF), BF16),
            pltpu.VMEM((MIDDLE_ROWS, D), F32),
            pltpu.VMEM(w_in.shape, BF16),
            pltpu.VMEM(w_down.shape, BF16),
            pltpu.SemaphoreType.DMA((2,)),
        ],
        compiler_params=params(),
        name="middle_part",
    )(length_valid, ot, x, cot, gain, w_out, w_in, w_down, *adapters)


def project_back_kernel(
    x_ref,
    gain_ref,
    w_ref,
    ar_ref,
    b_ref,
    zg_ref,
    dq_ref,
    dk_ref,
    dv_ref,
    dmid_ref,
    out_ref,
    dar_ref,
    db_ref,
):
    @pl.when(pl.program_id(0) == 0)
    def _():
        dar_ref[...] = jnp.zeros_like(dar_ref)
        db_ref[...] = jnp.zeros_like(db_ref)

    values = x_ref[...].astype(F32)
    gain = gain_ref[...]
    inverse = rms_inverse(values)
    normed = (values * inverse * gain).astype(BF16)
    lowrank = zg_ref[: 3 * COLS]
    gates = zg_ref[3 * COLS :]
    mixed = pad_rows(lowrank * gates, LANES).astype(BF16)
    grads = (dq_ref[...], dk_ref[...], dv_ref[...])
    columns = [slice(index * D, (index + 1) * D) for index in range(3)]
    grad_mixed = jnp.zeros((ROWS, LANES), F32)
    for grad, lanes in zip(grads, columns):
        grad_mixed = grad_mixed + dot_nt(grad, b_ref[:, lanes])
    grad_normed = jnp.zeros((ROWS, D), F32)
    for grad, lanes in zip(grads, columns):
        grad_normed = grad_normed + dot_nt(grad, w_ref[:, lanes])
        db_ref[:, lanes] += dot(mixed, grad)
    turned = grad_mixed.T
    parts = []
    for first in range(0, 3 * COLS, COLS):
        rows = slice(first, first + COLS)
        parts.append(gate_grads(turned[rows], lowrank[rows], gates[rows]))
    delta = jnp.concatenate([part[0] for part in parts] + [part[1] for part in parts], axis=0)
    delta = pad_rows(delta, 2 * LANES).astype(BF16)
    grad_normed = grad_normed + dot_nt(delta.T, ar_ref[...])
    dar_ref[...] += dot(delta, normed)
    out_ref[...] = dmid_ref[...] + rms_backward(values, gain, inverse, grad_normed)


def project_back(x, gain, w_qkv, ar_qkv, b_qkv, zg, dq, dk, dv, dmid):
    length = x.shape[0]
    tile = pl.BlockSpec((ROWS, D), lambda i: (i, 0))
    out_shape = [
        jax.ShapeDtypeStruct((length, D), F32),
        jax.ShapeDtypeStruct((2 * LANES, D), F32),
        jax.ShapeDtypeStruct((LANES, 3 * D), F32),
    ]
    return pl.pallas_call(
        project_back_kernel,
        grid=(length // ROWS,),
        in_specs=[
            tile,
            whole((1, D)),
            whole(w_qkv.shape),
            whole(ar_qkv.shape),
            whole(b_qkv.shape),
            pl.BlockSpec((6 * COLS, ROWS), lambda i: (0, i)),
            tile,
            tile,
            tile,
            tile,
        ],
        out_specs=[tile] + [whole(member.shape) for member in out_shape[1:]],
        out_shape=out_shape,
        compiler_params=params(),
        name="project_back",
    )(x, gain, w_qkv, ar_qkv, b_qkv, zg, dq, dk, dv, dmid)


PARAM_ROWS = sum((COLS + EXPERTS) * fan_in + COLS * fan_out for fan_in, fan_out in FANS) // LANES


def piece_rows():
    result = []
    row = 0
    for fan_in, fan_out in FANS:
        starts = []
        for count in (fan_in * COLS, COLS * fan_out, fan_in * EXPERTS):
            starts.append(row)
            row += count // LANES
        result.append(tuple(starts))
    return result


def shard_rows(count):
    return -(-count // (LANES * 16)) * 16


def align_in(flat_ref, shard, start):
    first, shift = divmod(start, LANES)
    rows = shard.shape[0]
    if shift == 0:
        flat_ref[first : first + rows] = shard
        return
    turned = pltpu.roll(shard, shift, 1)
    lane = lane_iota((1, LANES))
    zeros = jnp.zeros((8, LANES), F32)
    upper = jnp.concatenate([turned, zeros], axis=0)
    lower = pltpu.roll(upper, 1, 0)
    kept = flat_ref[first : first + 8]
    merged = jnp.where(lane >= shift, upper, lower)
    inside = (row_iota((8, LANES)) == 0) & (lane_iota((8, LANES)) < shift)
    flat_ref[first : first + 8] = jnp.where(inside, kept, merged[:8])
    flat_ref[first + 8 : first + 8 + rows] = merged[8:]


def align_out(flat_ref, rows, start):
    first, shift = divmod(start, LANES)
    if shift == 0:
        return flat_ref[first : first + rows]
    block = flat_ref[first : first + rows + 8]
    turned = pltpu.roll(block, LANES - shift, 1)
    below = pltpu.roll(turned, rows + 7, 0)
    lane = lane_iota((1, LANES))
    return jnp.where(lane < LANES - shift, turned, below)[:rows]


GROUP = 64


def narrow_to_rows(flat_ref, fan_in, items, out_ref):
    groups = fan_in // GROUP
    lane = lane_iota((1, LANES))
    lines = [
        [
            flat_ref[pl.ds(base + k, groups, stride=width * GROUP // LANES), :]
            for k in range(width * GROUP // LANES)
        ]
        for base, width, _ in items
    ]
    for b in range(GROUP):
        result = jnp.zeros((groups, LANES), F32)
        for line, (_, width, place) in zip(lines, items):
            first, shift = divmod(width * b, LANES)
            amount = (place - shift) % LANES
            value = line[first] if amount == 0 else pltpu.roll(line[first], amount, 1)
            if shift + width > LANES:
                value = jnp.where(
                    lane < place + LANES - shift, value, pltpu.roll(line[first + 1], amount, 1)
                )
            inside = (lane >= place) & (lane < place + width)
            result = jnp.where(inside, value, result)
        out_ref[pl.ds(b, groups, stride=GROUP), :] = result


def rows_to_narrow(in_ref, fan_in, items, flat_ref):
    groups = fan_in // GROUP
    lane = lane_iota((1, LANES))
    lines = [
        [jnp.zeros((groups, LANES), F32) for _ in range(width * GROUP // LANES)]
        for _, width, _ in items
    ]
    for b in range(GROUP):
        source = in_ref[pl.ds(b, groups, stride=GROUP), :]
        for line, (_, width, place) in zip(lines, items):
            first, shift = divmod(width * b, LANES)
            amount = (shift - place) % LANES
            value = source if amount == 0 else pltpu.roll(source, amount, 1)
            inside = (lane >= shift) & (lane < shift + width)
            line[first] = jnp.where(inside, value, line[first])
            if shift + width > LANES:
                line[first + 1] = jnp.where(lane < shift + width - LANES, value, line[first + 1])
    for line, (base, width, _) in zip(lines, items):
        for k, value in enumerate(line):
            flat_ref[pl.ds(base + k, groups, stride=width * GROUP // LANES), :] = value


def spread_matrix(experts, source, place):
    row = row_iota((LANES, LANES)) - source
    lane = lane_iota((LANES, LANES)) - place
    hit = (lane >= RANK * row) & (lane < RANK * row + RANK) & (row >= 0) & (row < experts)
    return jnp.where(hit, 1.0, 0.0)


def keep_matrix():
    row = row_iota((LANES, LANES))
    return jnp.where((row == lane_iota((LANES, LANES))) & (row < COLS), 1.0, 0.0)


FIRST_COUNT = sum((COLS + EXPERTS) * fan_in + COLS * fan_out for fan_in, fan_out in FANS[:3])


def unpack_ups(flat, base, fan_out, first, out_ref, column):
    width = fan_out // LANES
    above = jnp.zeros((first, LANES), F32)
    below = jnp.zeros((LANES - COLS - first, LANES), F32)
    for k in range(width):
        part = flat[pl.ds(base + k, COLS, stride=width), :]
        parts = [part, below] if first == 0 else [above, part, below]
        lanes = slice(column + k * LANES, column + (k + 1) * LANES)
        out_ref[:, lanes] = jnp.concatenate(parts, axis=0).astype(BF16)


def unpack_first_kernel(
    count, shards_ref, buckets_ref, table_ref, ar_ref, b_ref, off_ref, flat, down, router
):
    for index in range(-(-FIRST_COUNT // count)):
        align_in(flat, shards_ref[index].astype(F32), index * count)
    starts = piece_rows()
    narrow_to_rows(flat, D, [(starts[k][0], COLS, k * COLS) for k in range(3)], down)
    narrow_to_rows(flat, D, [(starts[k][2], EXPERTS, k * EXPERTS) for k in range(3)], router)
    routers = router[...].astype(BF16)
    for half in range(2):
        matrix = spread_matrix(3 * EXPERTS, 0, 3 * COLS - half * LANES).astype(BF16)
        packed = dot(routers, matrix)
        packed = packed if half else packed + down[...]
        ar_ref[:, half * LANES : (half + 1) * LANES] = packed.astype(BF16)
    for index in range(3):
        unpack_ups(flat, starts[index][1], D, index * COLS, b_ref, index * D)
    buckets = buckets_ref[...]
    hits = jnp.where(row_iota((table_ref.shape[0], buckets.shape[1])) == buckets, LOG2E, 0.0)
    off_ref[...] = lax.dot_general(
        table_ref[...],
        hits,
        (((0,), (0,)), ((), ())),
        preferred_element_type=F32,
        precision=lax.Precision.HIGHEST,
    )


def flat_rows(count):
    return PARAM_ROWS + shard_rows(count) + 20


def unpack_first(shards, buckets, rel_table, count):
    return pl.pallas_call(
        functools.partial(unpack_first_kernel, count),
        in_specs=[pl.BlockSpec(memory_space=pltpu.VMEM)] * 3,
        out_specs=[pl.BlockSpec(memory_space=pltpu.VMEM)] * 3,
        out_shape=[
            jax.ShapeDtypeStruct((D, 2 * LANES), BF16),
            jax.ShapeDtypeStruct((LANES, 3 * D), BF16),
            jax.ShapeDtypeStruct((HEADS, buckets.shape[1]), F32),
        ],
        scratch_shapes=[
            pltpu.VMEM((flat_rows(count), LANES), F32),
            pltpu.VMEM((D, LANES), F32),
            pltpu.VMEM((D, LANES), F32),
        ],
        compiler_params=params(),
        name="unpack_first",
    )(shards, buckets, rel_table)


def unpack_rest_kernel(count, first_ref, rest_ref, *refs):
    *outs, flat, work = refs
    split = first_ref.shape[0]
    for index in range(FIRST_COUNT // count, PARAM_ROWS * LANES // count):
        shard = first_ref[index] if index < split else rest_ref[index - split]
        align_in(flat, shard.astype(F32), index * count)
    starts = piece_rows()
    matrix = (keep_matrix() + spread_matrix(EXPERTS, COLS, COLS)).astype(BF16)
    for index in range(3, 6):
        base_a, base_b, base_r = starts[index]
        fan_in, fan_out = FANS[index]
        ar_ref, b_ref = outs[2 * index - 6], outs[2 * index - 5]
        narrow_to_rows(flat, fan_in, [(base_a, COLS, 0), (base_r, EXPERTS, COLS)], work)
        ar_ref[...] = dot(work[:fan_in].astype(BF16), matrix).astype(BF16)
        unpack_ups(flat, base_b, fan_out, 0, b_ref, 0)


def unpack_rest(first, rest, count):
    shapes = [shape for fan_in, fan_out in FANS[3:] for shape in ((fan_in, LANES), (LANES, fan_out))]
    return pl.pallas_call(
        functools.partial(unpack_rest_kernel, count),
        in_specs=[pl.BlockSpec(memory_space=pltpu.VMEM)] * 2,
        out_specs=[pl.BlockSpec(memory_space=pltpu.VMEM)] * len(shapes),
        out_shape=[jax.ShapeDtypeStruct(shape, BF16) for shape in shapes],
        scratch_shapes=[
            pltpu.VMEM((flat_rows(count), LANES), F32),
            pltpu.VMEM((FF, LANES), F32),
        ],
        compiler_params=params(),
        name="unpack_rest",
    )(first, rest)


def split_dot(value, matrix):
    high = value.astype(BF16)
    return dot(high, matrix) + dot((value - high.astype(F32)).astype(BF16), matrix)


def first_of_four(experts, source, place):
    row = row_iota((LANES, LANES)) - source
    lane = lane_iota((LANES, LANES)) - place
    hit = (row == RANK * lane) & (lane >= 0) & (lane < experts)
    return jnp.where(hit, 1.0, 0.0)


def assemble_ups(flat, base, fan_out, first, grad_ref, column):
    width = fan_out // LANES
    for k in range(width):
        lanes = slice(column + k * LANES, column + (k + 1) * LANES)
        flat[pl.ds(base + k, COLS, stride=width), :] = grad_ref[first : first + COLS, lanes]


def assemble_rest_kernel(count, split, *refs):
    *ins, shards_ref, more_ref, flat, work = refs
    starts = piece_rows()
    matrix = (keep_matrix() + first_of_four(EXPERTS, COLS, COLS)).astype(BF16)
    for index in range(3, 6):
        base_a, base_b, base_r = starts[index]
        fan_in, fan_out = FANS[index]
        dar_ref, db_ref = ins[2 * index - 6], ins[2 * index - 5]
        work[:fan_in] = split_dot(pad_rows(dar_ref[...], LANES).T, matrix)
        rows_to_narrow(work, fan_in, [(base_a, COLS, 0), (base_r, EXPERTS, COLS)], flat)
        assemble_ups(flat, base_b, fan_out, 0, db_ref, 0)
    for index in range(shards_ref.shape[0]):
        shards_ref[index] = align_out(flat, shards_ref.shape[1], (split + index) * count)
    begin = FIRST_COUNT // LANES
    more_ref[...] = flat[begin : begin + more_ref.shape[0]]


def assemble_rest(grads, devices, split, count):
    rows = shard_rows(count)
    more = (split * count - FIRST_COUNT) // (8 * LANES) * 8 + 16
    return pl.pallas_call(
        functools.partial(assemble_rest_kernel, count, split),
        in_specs=[pl.BlockSpec(memory_space=pltpu.VMEM)] * len(grads),
        out_specs=[pl.BlockSpec(memory_space=pltpu.VMEM)] * 2,
        out_shape=[
            jax.ShapeDtypeStruct((max(devices - split, 1), rows, LANES), F32),
            jax.ShapeDtypeStruct((more, LANES), F32),
        ],
        scratch_shapes=[
            pltpu.VMEM((flat_rows(count), LANES), F32),
            pltpu.VMEM((FF, LANES), F32),
        ],
        compiler_params=params(),
        name="assemble_rest",
    )(*grads)


def assemble_first_kernel(count, dar_ref, db_ref, more_ref, shards_ref, flat, down, router):
    starts = piece_rows()
    down[...] = dar_ref[:LANES].T
    rows_to_narrow(down, D, [(starts[k][0], COLS, k * COLS) for k in range(3)], flat)
    first_router = 3 * COLS
    turned = dar_ref[first_router : first_router + LANES].T
    router[...] = split_dot(turned, first_of_four(3 * EXPERTS, 0, 0).astype(BF16))
    rows_to_narrow(router, D, [(starts[k][2], EXPERTS, k * EXPERTS) for k in range(3)], flat)
    for index in range(3):
        assemble_ups(flat, starts[index][1], D, index * COLS, db_ref, index * D)
    begin = FIRST_COUNT // LANES
    flat[begin : begin + more_ref.shape[0]] = more_ref[...]
    for index in range(shards_ref.shape[0]):
        shards_ref[index] = align_out(flat, shards_ref.shape[1], index * count)


def assemble_first(dar, db, more, split, count):
    rows = shard_rows(count)
    return pl.pallas_call(
        functools.partial(assemble_first_kernel, count),
        in_specs=[pl.BlockSpec(memory_space=pltpu.VMEM)] * 3,
        out_specs=pl.BlockSpec(memory_space=pltpu.VMEM),
        out_shape=jax.ShapeDtypeStruct((split, rows, LANES), F32),
        scratch_shapes=[
            pltpu.VMEM((flat_rows(count), LANES), F32),
            pltpu.VMEM((D, LANES), F32),
            pltpu.VMEM((D, LANES), F32),
        ],
        compiler_params=params(),
        name="assemble_first",
    )(dar, db, more)


MESH = pl.DeviceIdType.MESH


def place_of(axes, sizes):
    me = lax.axis_index(axes[0]) * sizes[1] + lax.axis_index(axes[1])

    def coordinates(number):
        return (number // sizes[1], number % sizes[1])

    return me, coordinates


def partners_of(me):
    low = me % 8
    core = low % 2
    y = (low // 2) % 2
    x = low // 4
    over_x = low + 4 * (1 - 2 * x)
    over_y = low + 2 * (1 - 2 * y)
    first = over_x * (1 - core) + over_y * core
    second = over_y * (1 - core) + over_x * core
    both = first + second - low
    other = 1 - 2 * core
    return low, first, second, both, other, over_x, over_y


def greet(peers):
    barrier = pltpu.get_barrier_semaphore()
    for peer in peers:
        pl.semaphore_signal(barrier, inc=1, device_id=peer, device_id_type=MESH)
    pl.semaphore_wait(barrier, len(peers))


class Ring:
    def __init__(self, axes, sizes, send, receive):
        self.me, self.coordinates = place_of(axes, sizes)
        self.groups = sizes[0] * sizes[1] // 8
        self.group = self.me // 8
        places = partners_of(self.me)
        self.low, self.first, self.second, self.both, self.other, self.over_x, self.over_y = places
        self.mate = self.low + self.other
        self.send, self.receive = send, receive
        self.copies = {}

    def device(self, group, low):
        return self.coordinates(group * 8 + low)

    def greet(self):
        peers = [
            self.device((self.group + step) % self.groups, self.low)
            for step in range(1, self.groups)
        ]
        peers += [self.device(self.group, low) for low in (self.first, self.second, self.mate)]
        greet(peers)

    def copy(self, slot, source, target, peer, arrival=None):
        return pltpu.make_async_remote_copy(
            src_ref=source,
            dst_ref=target,
            send_sem=self.send.at[slot],
            recv_sem=self.receive.at[slot if arrival is None else arrival],
            device_id=peer,
            device_id_type=MESH,
        )


def gather_phases(ring, span, shard_ref, out_ref, local):
    begin, end = span
    base = ring.groups
    inside = (ring.group >= begin) & (ring.group < end)

    def around(step):
        target = (ring.group + step) % ring.groups
        return ring.copy(
            step,
            shard_ref,
            out_ref.at[ring.group - begin, ring.low],
            ring.device(target, ring.low),
            base + 7 + ring.group,
        )

    def arrived(group):
        return ring.copy(
            0,
            shard_ref,
            out_ref.at[group - begin, ring.low],
            ring.device(group, ring.low),
            base + 7 + group,
        )

    def push(slot, part, partner):
        return ring.copy(
            base + slot, out_ref.at[:, part], out_ref.at[:, part], ring.device(ring.group, partner)
        )

    one = push(0, ring.low, ring.first)
    two = push(1, ring.low, ring.second)
    three = push(2, ring.first, ring.second)
    cores = [
        push(3 + index, part, ring.mate)
        for index, part in enumerate((ring.low, ring.first, ring.second, ring.both))
    ]

    def own():
        return pltpu.make_async_copy(
            shard_ref, out_ref.at[ring.group - begin, ring.low], local
        )

    def phase0():
        ring.greet()

        @pl.when(inside)
        def _():
            own().start()
            for step in range(1, ring.groups):
                around(step).start()

    def phase1():
        @pl.when(inside)
        def _():
            own().wait()
            for step in range(1, ring.groups):
                around(step).wait_send()

        for group in range(begin, end):

            @pl.when(ring.group != group)
            def _():
                arrived(group).wait_recv()

        for copy in (one, two, cores[0]):
            copy.start()

    def phase2():
        one.wait()
        three.start()
        cores[1].start()

    def phase3():
        two.wait()
        cores[2].start()
        three.wait()
        cores[3].start()

    def phase4():
        for copy in cores:
            copy.wait()

    return phase0, phase1, phase2, phase3, phase4


def gather_semaphores(groups):
    return [
        pltpu.SemaphoreType.DMA((groups + 7,)),
        pltpu.SemaphoreType.DMA((2 * groups + 7,)),
        pltpu.SemaphoreType.DMA,
    ]


def gather_kernel(axes, sizes, span, shard_ref, out_ref, send, receive, local):
    for phase in gather_phases(Ring(axes, sizes, send, receive), span, shard_ref, out_ref, local):
        phase()


def gather(shard, axes, sizes, span):
    groups = sizes[0] * sizes[1] // 8
    return pl.pallas_call(
        functools.partial(gather_kernel, axes, sizes, span),
        in_specs=[pl.BlockSpec(memory_space=pltpu.VMEM)],
        out_specs=pl.BlockSpec(memory_space=pltpu.VMEM),
        out_shape=jax.ShapeDtypeStruct((span[1] - span[0], 8, *shard.shape), shard.dtype),
        scratch_shapes=gather_semaphores(groups),
        compiler_params=params(collective_id=0, has_side_effects=True),
        name="gather",
    )(shard)


def reduce_phases(ring, span, parts_ref, boxes, sums_ref=None, sum_boxes=None):
    begin, end = span
    outbox, inbox, half, own, far_out, far_in, out_ref = boxes
    groups = ring.groups
    inside = (ring.group >= begin) & (ring.group < end)
    core_parts = (ring.first, ring.both, ring.second, ring.low)
    near = [ring.mate] * 4 + [ring.second, ring.second, ring.first]

    def push(slot):
        return ring.copy(slot, outbox.at[slot], inbox.at[slot], ring.device(ring.group, near[slot]))

    def fill(slot, value):
        outbox[slot] = value.astype(BF16)
        push(slot).start()

    def around(group):
        return ring.copy(
            7 + group - begin,
            far_out.at[group - begin],
            far_in.at[ring.group],
            ring.device(group, ring.low),
            7 + ring.group,
        )

    def arrived(group):
        return ring.copy(
            7,
            far_out.at[0],
            far_in.at[group],
            ring.device(group, ring.low),
            7 + group,
        )

    base = 7 + groups
    sum_peers = (ring.mate, ring.over_x, ring.over_y)

    def push_sums(slot):
        near_out, near_in = sum_boxes
        return ring.copy(
            base + slot,
            near_out.at[slot],
            near_in.at[slot],
            ring.device(ring.group, sum_peers[slot]),
        )

    def around_sums(step):
        near_out, near_in = sum_boxes
        target = (ring.group + step) % groups
        return ring.copy(
            base + 2 + step,
            near_out.at[3],
            near_in.at[3 + ring.group],
            ring.device(target, ring.low),
        )

    def start_sums(slot, value):
        if sum_boxes is not None:
            sum_boxes[0][slot] = value
            push_sums(slot).start()

    def phase0():
        ring.greet()
        if sum_boxes is not None:
            start_sums(0, sums_ref[...])
        for slot, part in enumerate(core_parts):
            fill(slot, parts_ref[:, part + ring.other])

    def phase1():
        push(0).wait()
        fill(4, parts_ref[:, ring.second] + inbox[0].astype(F32))
        push(1).wait()
        fill(5, parts_ref[:, ring.both] + inbox[1].astype(F32))
        if sum_boxes is not None:
            push_sums(0).wait()
            start_sums(1, sum_boxes[0][0] + sum_boxes[1][0])
        push(2).wait()
        half[...] = parts_ref[:, ring.first] + inbox[2].astype(F32)
        push(3).wait()
        own[...] = parts_ref[:, ring.low] + inbox[3].astype(F32)

    def phase2():
        push(5).wait()
        fill(6, half[...] + inbox[5].astype(F32))
        if sum_boxes is not None:
            push_sums(1).wait()
            start_sums(2, sum_boxes[0][1] + sum_boxes[1][1])
        push(4).wait()
        own[...] = own[...] + inbox[4].astype(F32)

    def phase3():
        push(6).wait()
        own[...] = own[...] + inbox[6].astype(F32)
        far_out[...] = own[...].astype(BF16)
        for group in range(begin, end):

            @pl.when(ring.group != group)
            def _():
                around(group).start()

        if sum_boxes is not None:
            near_out, near_in = sum_boxes
            push_sums(2).wait()
            near_out[3] = near_out[2] + near_in[2]
            for step in range(1, groups):
                around_sums(step).start()
            near_in[3 + ring.group] = near_out[3]

    def phase4(finish_sums=None):
        for group in range(begin, end):

            @pl.when(ring.group != group)
            def _():
                around(group).wait_send()

        @pl.when(inside)
        def _():
            for group in range(groups):

                @pl.when(ring.group != group)
                def _():
                    arrived(group).wait_recv()

            total = own[ring.group - begin]
            for step in range(1, groups):
                total = total + far_in[(ring.group + step) % groups].astype(F32)
            out_ref[...] = total

        if sum_boxes is not None:
            near_out, near_in = sum_boxes
            for step in range(1, groups):
                around_sums(step).wait()
            whole_sum = near_in[3]
            for index in range(1, groups):
                whole_sum = whole_sum + near_in[3 + index]
            finish_sums(whole_sum)

    return phase0, phase1, phase2, phase3, phase4


def reduce_scratch(groups, count, rows):
    return [
        pltpu.VMEM((7, count, rows, LANES), BF16),
        pltpu.VMEM((7, count, rows, LANES), BF16),
        pltpu.VMEM((count, rows, LANES), F32),
        pltpu.VMEM((count, rows, LANES), F32),
        pltpu.VMEM((count, rows, LANES), BF16),
        pltpu.VMEM((groups, rows, LANES), BF16),
    ]


def reduce_kernel(axes, sizes, span, parts_ref, rest_ref, out_ref, *scratch):
    *boxes, total, send, receive = scratch
    ring = Ring(axes, sizes, send, receive)
    for phase in reduce_phases(ring, span, parts_ref, (*boxes, total)):
        phase()
    first = (ring.group >= span[0]) & (ring.group < span[1])

    @pl.when(first)
    def _():
        out_ref[...] = total[...]

    @pl.when(jnp.logical_not(first))
    def _():
        out_ref[...] = rest_ref[...]


def reduce_scatter(parts, rest, axes, sizes, span):
    count, _, rows, lanes = parts.shape
    groups = sizes[0] * sizes[1] // 8
    copies = 7 + groups
    return pl.pallas_call(
        functools.partial(reduce_kernel, axes, sizes, span),
        in_specs=[pl.BlockSpec(memory_space=pltpu.VMEM)] * 2,
        out_specs=pl.BlockSpec(memory_space=pltpu.VMEM),
        out_shape=jax.ShapeDtypeStruct((rows, lanes), F32),
        scratch_shapes=reduce_scratch(groups, count, rows)
        + [
            pltpu.VMEM((rows, lanes), F32),
            pltpu.SemaphoreType.DMA((copies,)),
            pltpu.SemaphoreType.DMA((copies,)),
        ],
        compiler_params=params(collective_id=3, has_side_effects=True),
        name="reduce_scatter",
    )(parts, rest)


def per_device(
    tokens,
    lengths,
    buckets,
    rel_table,
    gain_attn,
    gain_ff,
    w_qkv,
    w_out,
    w_in,
    w_down,
    adapters,
    cotangent,
    axes,
    sizes,
):
    seq_count, length, width = tokens.shape
    x = tokens.reshape(length, width)
    cot = cotangent.reshape(length, width)
    gain_first = gain_attn.reshape(1, width)
    gain_second = gain_ff.reshape(1, width)
    devices = sizes[0] * sizes[1]
    count = adapters.shape[0]
    rows = shard_rows(count)
    shard = jnp.pad(adapters, (0, rows * LANES - count)).reshape(rows, LANES)
    groups = devices // 8
    split_groups = min(-(-FIRST_COUNT // (8 * count)), max(groups - 1, 1))
    split = min(8 * split_groups, devices)
    first_span, rest_span = (0, split_groups), (split_groups, groups)
    if devices == 1:
        first = shard[None]
    else:
        first = gather(shard, axes, sizes, first_span).reshape(split, rows, LANES)
    reversed_buckets = jnp.pad(buckets[::-1], (0, 1)).reshape(1, 2 * length)
    ar_qkv, b_qkv, offsets = unpack_first(first, reversed_buckets, rel_table, count)
    qt, k, kt, v, vt, zg, rest = project(
        x, gain_first, w_qkv, ar_qkv, b_qkv, shard, axes, sizes, rest_span
    )
    rest = rest.reshape(-1, *rest.shape[2:])
    ot, lse = attend(lengths, offsets, qt, k, vt)
    packed = unpack_rest(first, rest, count)
    block_out, dmid, gt, sums, *grads = middle_part(
        lengths, ot, x, cot, gain_second, w_out, w_in, w_down, packed
    )
    parts, more = assemble_rest(grads, devices, split, count)
    if devices > 1:
        parts = parts.reshape(groups - split_groups, 8, rows, LANES)
    dq, dk, dv, rest_sum, roots = attend_back(
        lengths, offsets, qt, k, kt, v, ot, gt, lse, parts, sums, axes, sizes, rest_span
    )
    tokens_grad, dar_qkv, db_qkv = project_back(
        x, gain_first, w_qkv, ar_qkv, b_qkv, zg, dq, dk, dv, dmid
    )

    parts = assemble_first(dar_qkv, db_qkv, more, split, count)
    if devices == 1:
        mine = parts[0]
    else:
        parts = parts.reshape(split_groups, 8, rows, LANES)
        mine = reduce_scatter(parts, rest_sum, axes, sizes, first_span)
    grad_shard = mine.reshape(-1)[:count]
    root_squares = roots[0, :4]
    return (
        block_out.reshape(tokens.shape),
        tokens_grad.reshape(tokens.shape),
        grad_shard,
        root_squares,
    )


def solution(mesh):
    axes = tuple(mesh.axis_names)
    sizes = tuple(mesh.shape[axis] for axis in axes)
    sequence = P(axes, None, None)
    placed = (
        sequence,
        P(axes),
        P(),
        P(),
        P(),
        P(),
        P(),
        P(),
        P(),
        P(),
        P(axes),
        sequence,
    )
    return jax.shard_map(
        functools.partial(per_device, axes=axes, sizes=sizes),
        mesh=mesh,
        in_specs=placed,
        out_specs=(sequence, sequence, P(axes), P()),
        check_vma=False,
    )
```

```python
import functools

import jax
import jax.numpy as jnp
from jax import lax
from jax.experimental import pallas as pl
from jax.experimental.pallas import tpu as pltpu
from jax.sharding import PartitionSpec as P

D = 768
FF = 3072
HEADS = 12
HDIM = 64
EXPERTS = 10
RANK = 4
FANS = ((D, D), (D, D), (D, D), (D, D), (D, FF), (FF, D))
COLS = EXPERTS * RANK
LANES = 128

EPSILON = 1e-06
MASKED = -1000000000.0
GELU_SCALE = 0.7978845608028654
GELU_CUBIC = 0.044715
LOG2E = 1.4426950408889634
LN2 = 0.6931471805599453
QUERY_SCALE = 0.125 * LOG2E

ROWS = 256
MIDDLE_ROWS = 512
CHUNK = 512
QBLOCK = 256
UP_ROWS = 48
DOWN_ROWS = 2 * COLS
VMEM_BYTES = 60 * 1024 * 1024

F32 = jnp.float32
BF16 = jnp.bfloat16


def dot(a, b):
    return lax.dot_general(a, b, (((1,), (0,)), ((), ())), preferred_element_type=F32)


def dot_nt(a, b):
    return lax.dot_general(a, b, (((1,), (1,)), ((), ())), preferred_element_type=F32)


def dot_tn(a, b):
    return lax.dot_general(a, b, (((0,), (0,)), ((), ())), preferred_element_type=F32)


def lane_iota(shape):
    return lax.broadcasted_iota(jnp.int32, shape, 1)


def row_iota(shape):
    return lax.broadcasted_iota(jnp.int32, shape, 0)


def gates_of(logits):
    weights = jnp.exp(logits - jnp.max(logits, axis=0, keepdims=True))
    return weights * (4.0 / jnp.sum(weights, axis=0, keepdims=True))


def gate_grads(grad_mixed, lowrank, gates):
    product = grad_mixed * lowrank
    summed = product
    for step in range(1, RANK):
        summed = summed + pltpu.roll(product, COLS - step, 0)
    centre = jnp.sum(gates * product, axis=0, keepdims=True)
    first = row_iota(gates.shape) % RANK == 0
    return grad_mixed * gates, jnp.where(first, gates * (summed - centre), 0.0)


def pad_rows(value, rows):
    return jnp.concatenate([value, jnp.zeros((rows - value.shape[0], value.shape[1]), F32)], axis=0)


def single_gates(packed):
    turned = packed.T
    lowrank = turned[:COLS]
    gates = gates_of(turned[COLS : 2 * COLS])
    mixed = pad_rows(lowrank * gates, LANES).astype(BF16)
    return lowrank, gates, mixed, mixed.T


def single_deltas(grad_mixed, lowrank, gates):
    parts = gate_grads(grad_mixed.T[:COLS], lowrank, gates)
    delta = pad_rows(jnp.concatenate(parts, axis=0), LANES).astype(BF16)
    return delta, delta.T


def rms_inverse(values):
    return lax.rsqrt(jnp.mean(values * values, axis=-1, keepdims=True) + EPSILON)


def rms_backward(values, gain, inverse, grad_normed):
    weighted = grad_normed * gain
    return inverse * weighted - values * (
        inverse * inverse * inverse * jnp.mean(values * weighted, axis=-1, keepdims=True)
    )


def params(**more):
    return pltpu.CompilerParams(vmem_limit_bytes=VMEM_BYTES, **more)


def whole(shape):
    zeros = (0,) * len(shape)
    return pl.BlockSpec(shape, lambda *_: zeros, pipeline_mode=pl.Buffered(1))


def bias_table(offset_row, length):
    spread = jnp.broadcast_to(offset_row, (LANES, 2 * length))
    return pltpu.roll(spread, 2 * length - (LANES - 1), 1, stride=1, stride_axis=0)


def add_bias(scores, table_ref, start, length):
    width = scores.shape[1]
    parts = []
    for block in range(length // LANES):
        offset = start - LANES * block + (length - LANES)
        parts.append(
            scores[block * LANES : (block + 1) * LANES] + table_ref[:, offset : offset + width]
        )
    return jnp.concatenate(parts, axis=0)


def key_extras(length_ref, shape, odd):
    lane = lane_iota(shape) - (0 if odd else HDIM)
    invalid = row_iota(shape) >= length_ref[0]
    extras = jnp.where((lane == 0) & invalid, MASKED, 0.0)
    return jnp.where((lane >= 1) & (lane <= 3), 1.0, extras).astype(BF16)


def head_lanes(odd):
    lane = lane_iota((1, LANES))
    return ((lane >= HDIM) if odd else (lane < HDIM)).astype(F32).astype(BF16)


def extra_rows(rows):
    width = rows[0].shape[1]
    index = row_iota((8, width))
    block = jnp.zeros((8, width), F32)
    for place, row in enumerate(rows):
        block = jnp.where(index == place, row, block)
    return jnp.concatenate([block, jnp.zeros((HDIM - 8, width), F32)], axis=0).astype(BF16)


def split_three(row):
    high = row.astype(BF16).astype(F32)
    middle = (row - high).astype(BF16).astype(F32)
    return high, middle, row - high - middle


def join_rows(rows, extras, odd):
    return jnp.concatenate([extras, rows] if odd else [rows, extras], axis=0)


def attend_kernel(length_ref, off_ref, qt_ref, k_ref, vt_ref, o_ref, lse_ref, table, key_more):
    length = k_ref.shape[0]

    @pl.when(pl.program_id(0) == 0)
    def _():
        for odd in range(2):
            key_more[odd] = key_extras(length_ref, k_ref.shape, odd)

    for odd in range(2):
        half = slice(odd * HDIM, (odd + 1) * HDIM)
        row = 2 * pl.program_id(0) + odd
        table[odd] = bias_table(off_ref[pl.ds(row, 1), :], length)
        keys = k_ref[...] * head_lanes(odd) + key_more[odd]
        ones = jnp.ones((1, length), F32)
        queries = join_rows(qt_ref[half, :], extra_rows([ones]), odd)
        values = jnp.concatenate([vt_ref[half, :], jnp.ones((16, length), BF16)], axis=0)
        starts = range(0, length, QBLOCK)
        scores = [
            add_bias(dot(keys, queries[:, start : start + QBLOCK]), table.at[odd], start, length)
            for start in starts
        ]
        peaks = [jnp.max(part, axis=0, keepdims=True) for part in scores]
        weights = [jnp.exp2(part - peak).astype(BF16) for part, peak in zip(scores, peaks)]
        for start, peak, part in zip(starts, peaks, weights):
            columns = slice(start, start + QBLOCK)
            summed = dot(values, part)
            total = summed[HDIM : HDIM + 1]
            o_ref[half, columns] = (summed[:HDIM] / total).astype(BF16)
            lse_ref[0, odd : odd + 1, columns] = peak + jnp.log2(total)


def attend(length_valid, offsets, qt, k, vt):
    length = k.shape[0]
    turned = pl.BlockSpec((LANES, length), lambda p: (p, 0))
    natural = pl.BlockSpec((length, LANES), lambda p: (0, p))
    return pl.pallas_call(
        attend_kernel,
        grid=(HEADS // 2,),
        in_specs=[
            pl.BlockSpec(memory_space=pltpu.SMEM),
            whole(offsets.shape),
            turned,
            natural,
            turned,
        ],
        out_specs=[turned, pl.BlockSpec((1, 2, length), lambda p: (p, 0, 0))],
        out_shape=[
            jax.ShapeDtypeStruct((D, length), BF16),
            jax.ShapeDtypeStruct((HEADS // 2, 2, length), F32),
        ],
        scratch_shapes=[
            pltpu.VMEM((2, LANES, 2 * length), F32),
            pltpu.VMEM((2, length, LANES), BF16),
        ],
        compiler_params=params(),
        name="attend",
    )(length_valid, offsets, qt, k, vt)


def attend_back_kernel(
    length_ref,
    off_ref,
    qt_ref,
    k_ref,
    kt_ref,
    v_ref,
    ot_ref,
    gt_ref,
    lse_ref,
    dq_ref,
    dk_ref,
    dv_ref,
    table,
    key_more,
    weights_all,
    grads_all,
):
    length = k_ref.shape[0]

    @pl.when(pl.program_id(0) == 0)
    def _():
        for odd in range(2):
            key_more[odd] = key_extras(length_ref, k_ref.shape, odd)

    lane = lane_iota((1, LANES))
    first_lanes = lane < HDIM
    grad_query_parts = []
    for odd in range(2):
        half = slice(odd * HDIM, (odd + 1) * HDIM)
        row = 2 * pl.program_id(0) + odd
        table[odd] = bias_table(off_ref[pl.ds(row, 1), :], length)
        keys = k_ref[...] * head_lanes(odd) + key_more[odd]
        place = lane - (0 if odd else HDIM)
        value_more = ((place >= 0) & (place < 3)).astype(F32).astype(BF16)
        values = v_ref[...] * head_lanes(odd) + value_more
        ones = jnp.ones((1, length), F32)
        lse = lse_ref[0, odd : odd + 1, :]
        queries = join_rows(
            qt_ref[half, :], extra_rows([ones] + [-part for part in split_three(lse)]), odd
        )
        delta = jnp.sum(
            ot_ref[half, :].astype(F32) * gt_ref[half, :].astype(F32), axis=0, keepdims=True
        )
        grads = join_rows(
            gt_ref[half, :], extra_rows([-part for part in split_three(delta)]), odd
        )
        for start in range(0, length, QBLOCK):
            columns = slice(start, start + QBLOCK)
            scores = add_bias(dot(keys, queries[:, columns]), table.at[odd], start, length)
            weights = jnp.exp2(scores)
            weights_all[:, columns] = weights.astype(BF16)
            grad_scores = weights * dot(values, grads[:, columns])
            grads_all[:, columns] = grad_scores.astype(BF16)
        grad_query_parts.append(dot(kt_ref[half, :], grads_all[...]) * 0.125)
        grad_values = dot_nt(weights_all[...], gt_ref[...])
        grad_keys = dot_nt(grads_all[...], qt_ref[...]) * LN2
        if odd:
            dv_ref[...] = jnp.where(first_lanes, even_values, grad_values).astype(BF16)
            dk_ref[...] = jnp.where(first_lanes, even_keys, grad_keys).astype(BF16)
        else:
            even_values, even_keys = grad_values, grad_keys
    dq_ref[...] = jnp.concatenate(grad_query_parts, axis=0).T.astype(BF16)


def attend_back(length_valid, offsets, qt, k, kt, v, ot, gt, lse):
    length = k.shape[0]
    turned = pl.BlockSpec((LANES, length), lambda p: (p, 0))
    natural = pl.BlockSpec((length, LANES), lambda p: (0, p))
    natural_shape = jax.ShapeDtypeStruct((length, D), BF16)
    return pl.pallas_call(
        attend_back_kernel,
        grid=(HEADS // 2,),
        in_specs=[
            pl.BlockSpec(memory_space=pltpu.SMEM),
            whole(offsets.shape),
            turned,
            natural,
            turned,
            natural,
            turned,
            turned,
            pl.BlockSpec((1, 2, length), lambda p: (p, 0, 0)),
        ],
        out_specs=[natural] * 3,
        out_shape=[natural_shape] * 3,
        scratch_shapes=[
            pltpu.VMEM((2, LANES, 2 * length), F32),
            pltpu.VMEM((2, length, LANES), BF16),
            pltpu.VMEM((length, length), BF16),
            pltpu.VMEM((length, length), BF16),
        ],
        compiler_params=params(),
        name="attend_back",
    )(length_valid, offsets, qt, k, kt, v, ot, gt, lse)


def middle_kernel(
    length_ref,
    ot_ref,
    x_ref,
    cot_ref,
    gain_ref,
    w_out_ref,
    w_in_hbm,
    w_down_hbm,
    ar_out_ref,
    b_out_ref,
    ar_in_ref,
    b_in_ref,
    ar_down_ref,
    b_down_ref,
    out_ref,
    dmid_ref,
    gt_ref,
    sums_ref,
    dar_out_ref,
    db_out_ref,
    dar_in_ref,
    db_in_ref,
    dar_down_ref,
    db_down_ref,
    active,
    slope,
    sloped,
    grad_hidden,
    feeds,
    w_in_ref,
    w_down_ref,
    loaded,
):
    step = pl.program_id(0)
    loads = [
        pltpu.make_async_copy(w_in_hbm, w_in_ref, loaded.at[0]),
        pltpu.make_async_copy(w_down_hbm, w_down_ref, loaded.at[1]),
    ]

    @pl.when(step == 0)
    def _():
        for load in loads:
            load.start()
        for ref in (
            sums_ref,
            dar_out_ref,
            db_out_ref,
            dar_in_ref,
            db_in_ref,
            dar_down_ref,
            db_down_ref,
        ):
            ref[...] = jnp.zeros_like(ref)

    attended = ot_ref[...].T
    inputs = x_ref[...].astype(F32)
    gain = gain_ref[...]
    cot = cot_ref[...]

    packed_out = dot(attended, ar_out_ref[...])
    branch = dot(attended, w_out_ref[...])
    low_out, gates_out, mixed_out, natural = single_gates(packed_out)
    grad_mixed_down = dot_nt(cot, b_down_ref[...])
    branch = branch + dot(natural, b_out_ref[...])
    middle = inputs + branch
    inverse = rms_inverse(middle)
    normed = (middle * inverse * gain).astype(BF16)

    packed_in = dot(normed, ar_in_ref[...])
    low_in, gates_in, mixed_in, natural = single_gates(packed_in)

    def columns_of(index):
        return pl.ds(pl.multiple_of(index * CHUNK, CHUNK), CHUNK)

    def hidden_of(chunk):
        return dot(normed, w_in_ref[:, chunk]) + dot(natural, b_in_ref[:, chunk])

    def activate(chunk, values):
        grad_dense = dot_nt(cot, w_down_ref[chunk])
        square = values * values
        tangent = jnp.tanh(values * (GELU_SCALE + (GELU_SCALE * GELU_CUBIC) * square))
        half = 0.5 + 0.5 * tangent
        smooth = values * half
        active[:, chunk] = smooth.astype(BF16)
        steep = half + smooth * (1.0 - tangent) * (
            GELU_SCALE + (3.0 * GELU_SCALE * GELU_CUBIC) * square
        )
        slope[:, chunk] = steep.astype(BF16)
        sloped[:, chunk] = grad_dense * steep

    def forward_pair(pair, _):
        chunk_a = columns_of(2 * pair)
        chunk_b = columns_of(2 * pair + 1)
        hidden_a = hidden_of(chunk_a)
        hidden_b = hidden_of(chunk_b)
        activate(chunk_a, hidden_a)
        activate(chunk_b, hidden_b)
        return 0

    @pl.when(step == 0)
    def _():
        for load in loads:
            load.wait()

    lax.fori_loop(0, FF // (2 * CHUNK), forward_pair, 0)

    packed_down = dot(active[...], ar_down_ref[...])
    def feed_part(index, _):
        part = pl.ds(pl.multiple_of(index * 256, 256), 256)
        feeds[:, part] = dot(active[...], w_down_ref[:, part])
        return 0

    lax.fori_loop(0, 3, feed_part, 0)
    feed = feeds[...]
    low_down, gates_down, mixed_down, natural = single_gates(packed_down)
    delta_down, natural_delta = single_deltas(grad_mixed_down, low_down, gates_down)
    db_down_ref[...] += dot(mixed_down[:UP_ROWS], cot)
    feed = feed + dot(natural, b_down_ref[...])
    output = middle + feed
    out_ref[...] = output.astype(BF16)

    def backward_chunk(index, _):
        chunk = columns_of(index)
        grad_low = dot_nt(natural_delta, ar_down_ref[chunk])
        grad_hidden[:, chunk] = (
            sloped[:, chunk] + grad_low * slope[:, chunk].astype(F32)
        ).astype(BF16)
        return 0

    lax.fori_loop(0, FF // CHUNK, backward_chunk, 0)
    dar_down_ref[...] += dot(delta_down[:DOWN_ROWS], active[...])

    rows = row_iota((MIDDLE_ROWS, 1)) + step * MIDDLE_ROWS
    valid = (rows < length_ref[0]).astype(F32)
    lane = lane_iota((8, LANES))
    totals = jnp.where((lane == 4) & (step == 0), length_ref[0].astype(F32), 0.0)
    for place, member in enumerate((inputs, branch, feed, output)):
        kept = member * valid
        totals = jnp.where(lane == place, jnp.sum(kept * kept), totals)
    sums_ref[...] += totals

    grad_mixed = dot_nt(grad_hidden[...], b_in_ref[...])
    def back_part(index, _):
        part = pl.ds(pl.multiple_of(index * 256, 256), 256)
        feeds[:, part] = dot_nt(grad_hidden[...], w_in_ref[part])
        return 0

    lax.fori_loop(0, 3, back_part, 0)
    grad_normed = feeds[...]
    delta_in, natural_delta = single_deltas(grad_mixed, low_in, gates_in)
    db_in_ref[...] += dot(mixed_in[:UP_ROWS], grad_hidden[...])
    grad_normed = grad_normed + dot_nt(natural_delta, ar_in_ref[...])
    dar_in_ref[...] += dot(delta_in[:DOWN_ROWS], normed)

    grad_middle = cot.astype(F32) + rms_backward(middle, gain, inverse, grad_normed)
    dmid_ref[...] = grad_middle
    grad_branch = grad_middle.astype(BF16)
    grad_mixed = dot_nt(grad_branch, b_out_ref[...])
    grad_attended = dot_nt(grad_branch, w_out_ref[...])
    delta_out, natural_delta = single_deltas(grad_mixed, low_out, gates_out)
    grad_attended = grad_attended + dot_nt(natural_delta, ar_out_ref[...])
    gt_ref[...] = grad_attended.astype(BF16).T
    dar_out_ref[...] += dot(delta_out[:DOWN_ROWS], attended)
    db_out_ref[...] += dot(mixed_out[:UP_ROWS], grad_branch)


def middle_part(length_valid, ot, x, cot, gain, w_out, w_in, w_down, adapters):
    length = x.shape[0]
    tile = pl.BlockSpec((MIDDLE_ROWS, D), lambda i: (i, 0))
    turned = pl.BlockSpec((D, MIDDLE_ROWS), lambda i: (0, i))
    grad_shapes = [
        jax.ShapeDtypeStruct(shape, F32)
        for fan_in, fan_out in FANS[3:]
        for shape in ((DOWN_ROWS, fan_in), (UP_ROWS, fan_out))
    ]
    out_shape = [
        jax.ShapeDtypeStruct((length, D), BF16),
        jax.ShapeDtypeStruct((length, D), F32),
        jax.ShapeDtypeStruct((D, length), BF16),
        jax.ShapeDtypeStruct((8, LANES), F32),
    ] + grad_shapes
    return pl.pallas_call(
        middle_kernel,
        grid=(length // MIDDLE_ROWS,),
        in_specs=[pl.BlockSpec(memory_space=pltpu.SMEM), turned, tile, tile]
        + [whole(gain.shape), whole(w_out.shape)]
        + [pl.BlockSpec(memory_space=pl.ANY)] * 2
        + [whole(member.shape) for member in adapters],
        out_specs=[tile, tile, turned] + [whole(member.shape) for member in out_shape[3:]],
        out_shape=out_shape,
        scratch_shapes=[
            pltpu.VMEM((MIDDLE_ROWS, FF), BF16),
            pltpu.VMEM((MIDDLE_ROWS, FF), BF16),
            pltpu.VMEM((MIDDLE_ROWS, FF), F32),
            pltpu.VMEM((MIDDLE_ROWS, FF), BF16),
            pltpu.VMEM((MIDDLE_ROWS, D), F32),
            pltpu.VMEM(w_in.shape, BF16),
            pltpu.VMEM(w_down.shape, BF16),
            pltpu.SemaphoreType.DMA((2,)),
        ],
        compiler_params=params(),
        name="middle_part",
    )(length_valid, ot, x, cot, gain, w_out, w_in, w_down, *adapters)


def project_back_kernel(
    x_ref,
    gain_ref,
    w_ref,
    ar_ref,
    b_ref,
    zg_ref,
    dq_ref,
    dk_ref,
    dv_ref,
    dmid_ref,
    out_ref,
    dar_ref,
    db_ref,
):
    @pl.when(pl.program_id(0) == 0)
    def _():
        dar_ref[...] = jnp.zeros_like(dar_ref)
        db_ref[...] = jnp.zeros_like(db_ref)

    values = x_ref[...].astype(F32)
    gain = gain_ref[...]
    inverse = rms_inverse(values)
    normed = (values * inverse * gain).astype(BF16)
    lowrank = zg_ref[: 3 * COLS]
    gates = zg_ref[3 * COLS :]
    mixed = pad_rows(lowrank * gates, LANES).astype(BF16)
    grads = (dq_ref[...], dk_ref[...], dv_ref[...])
    columns = [slice(index * D, (index + 1) * D) for index in range(3)]
    grad_mixed = jnp.zeros((ROWS, LANES), F32)
    for grad, lanes in zip(grads, columns):
        grad_mixed = grad_mixed + dot_nt(grad, b_ref[:, lanes])
    grad_normed = jnp.zeros((ROWS, D), F32)
    for grad, lanes in zip(grads, columns):
        grad_normed = grad_normed + dot_nt(grad, w_ref[:, lanes])
        db_ref[:, lanes] += dot(mixed, grad)
    turned = grad_mixed.T
    parts = []
    for first in range(0, 3 * COLS, COLS):
        rows = slice(first, first + COLS)
        parts.append(gate_grads(turned[rows], lowrank[rows], gates[rows]))
    delta = jnp.concatenate([part[0] for part in parts] + [part[1] for part in parts], axis=0)
    delta = pad_rows(delta, 2 * LANES).astype(BF16)
    grad_normed = grad_normed + dot_nt(delta.T, ar_ref[...])
    dar_ref[...] += dot(delta, normed)
    out_ref[...] = dmid_ref[...] + rms_backward(values, gain, inverse, grad_normed)


def project_back(x, gain, w_qkv, ar_qkv, b_qkv, zg, dq, dk, dv, dmid):
    length = x.shape[0]
    tile = pl.BlockSpec((ROWS, D), lambda i: (i, 0))
    out_shape = [
        jax.ShapeDtypeStruct((length, D), F32),
        jax.ShapeDtypeStruct((2 * LANES, D), F32),
        jax.ShapeDtypeStruct((LANES, 3 * D), F32),
    ]
    return pl.pallas_call(
        project_back_kernel,
        grid=(length // ROWS,),
        in_specs=[
            tile,
            whole((1, D)),
            whole(w_qkv.shape),
            whole(ar_qkv.shape),
            whole(b_qkv.shape),
            pl.BlockSpec((6 * COLS, ROWS), lambda i: (0, i)),
            tile,
            tile,
            tile,
            tile,
        ],
        out_specs=[tile] + [whole(member.shape) for member in out_shape[1:]],
        out_shape=out_shape,
        compiler_params=params(),
        name="project_back",
    )(x, gain, w_qkv, ar_qkv, b_qkv, zg, dq, dk, dv, dmid)


PARAM_ROWS = sum((COLS + EXPERTS) * fan_in + COLS * fan_out for fan_in, fan_out in FANS) // LANES


def piece_rows():
    result = []
    row = 0
    for fan_in, fan_out in FANS:
        starts = []
        for count in (fan_in * COLS, COLS * fan_out, fan_in * EXPERTS):
            starts.append(row)
            row += count // LANES
        result.append(tuple(starts))
    return result


def shard_rows(count):
    return -(-count // (LANES * 16)) * 16


def align_in(flat_ref, shard, start):
    first, shift = divmod(start, LANES)
    rows = shard.shape[0]
    if shift == 0:
        flat_ref[first : first + rows] = shard
        return
    turned = pltpu.roll(shard, shift, 1)
    lane = lane_iota((1, LANES))
    zeros = jnp.zeros((8, LANES), F32)
    upper = jnp.concatenate([turned, zeros], axis=0)
    lower = pltpu.roll(upper, 1, 0)
    kept = flat_ref[first : first + 8]
    merged = jnp.where(lane >= shift, upper, lower)
    inside = (row_iota((8, LANES)) == 0) & (lane_iota((8, LANES)) < shift)
    flat_ref[first : first + 8] = jnp.where(inside, kept, merged[:8])
    flat_ref[first + 8 : first + 8 + rows] = merged[8:]


def align_out(flat_ref, rows, start):
    first, shift = divmod(start, LANES)
    if shift == 0:
        return flat_ref[first : first + rows]
    block = flat_ref[first : first + rows + 8]
    turned = pltpu.roll(block, LANES - shift, 1)
    below = pltpu.roll(turned, rows + 7, 0)
    lane = lane_iota((1, LANES))
    return jnp.where(lane < LANES - shift, turned, below)[:rows]


GROUP = 64


def narrow_to_rows(flat_ref, fan_in, items, out_ref):
    groups = fan_in // GROUP
    lane = lane_iota((1, LANES))
    lines = [
        [
            flat_ref[pl.ds(base + k, groups, stride=width * GROUP // LANES), :]
            for k in range(width * GROUP // LANES)
        ]
        for base, width, _ in items
    ]
    for b in range(GROUP):
        result = jnp.zeros((groups, LANES), F32)
        for line, (_, width, place) in zip(lines, items):
            first, shift = divmod(width * b, LANES)
            amount = (place - shift) % LANES
            value = line[first] if amount == 0 else pltpu.roll(line[first], amount, 1)
            if shift + width > LANES:
                value = jnp.where(
                    lane < place + LANES - shift, value, pltpu.roll(line[first + 1], amount, 1)
                )
            inside = (lane >= place) & (lane < place + width)
            result = jnp.where(inside, value, result)
        out_ref[pl.ds(b, groups, stride=GROUP), :] = result


def rows_to_narrow(in_ref, fan_in, items, flat_ref):
    groups = fan_in // GROUP
    lane = lane_iota((1, LANES))
    lines = [
        [jnp.zeros((groups, LANES), F32) for _ in range(width * GROUP // LANES)]
        for _, width, _ in items
    ]
    for b in range(GROUP):
        source = in_ref[pl.ds(b, groups, stride=GROUP), :]
        for line, (_, width, place) in zip(lines, items):
            first, shift = divmod(width * b, LANES)
            amount = (shift - place) % LANES
            value = source if amount == 0 else pltpu.roll(source, amount, 1)
            inside = (lane >= shift) & (lane < shift + width)
            line[first] = jnp.where(inside, value, line[first])
            if shift + width > LANES:
                line[first + 1] = jnp.where(lane < shift + width - LANES, value, line[first + 1])
    for line, (base, width, _) in zip(lines, items):
        for k, value in enumerate(line):
            flat_ref[pl.ds(base + k, groups, stride=width * GROUP // LANES), :] = value


def spread_matrix(experts, source, place):
    row = row_iota((LANES, LANES)) - source
    lane = lane_iota((LANES, LANES)) - place
    hit = (lane >= RANK * row) & (lane < RANK * row + RANK) & (row >= 0) & (row < experts)
    return jnp.where(hit, 1.0, 0.0)


def keep_matrix():
    row = row_iota((LANES, LANES))
    return jnp.where((row == lane_iota((LANES, LANES))) & (row < COLS), 1.0, 0.0)


FIRST_COUNT = sum((COLS + EXPERTS) * fan_in + COLS * fan_out for fan_in, fan_out in FANS[:3])


def unpack_ups(flat, base, fan_out, first, out_ref, column):
    width = fan_out // LANES
    above = jnp.zeros((first, LANES), F32)
    below = jnp.zeros((LANES - COLS - first, LANES), F32)
    for k in range(width):
        part = flat[pl.ds(base + k, COLS, stride=width), :]
        parts = [part, below] if first == 0 else [above, part, below]
        lanes = slice(column + k * LANES, column + (k + 1) * LANES)
        out_ref[:, lanes] = jnp.concatenate(parts, axis=0).astype(BF16)


def unpack_first(flat, ar_ref, b_ref, down, router):
    starts = piece_rows()
    narrow_to_rows(flat, D, [(starts[k][0], COLS, k * COLS) for k in range(3)], down)
    narrow_to_rows(flat, D, [(starts[k][2], EXPERTS, k * EXPERTS) for k in range(3)], router)
    routers = router[...].astype(BF16)
    for half in range(2):
        matrix = spread_matrix(3 * EXPERTS, 0, 3 * COLS - half * LANES).astype(BF16)
        packed = dot(routers, matrix)
        packed = packed if half else packed + down[...]
        ar_ref[:, half * LANES : (half + 1) * LANES] = packed.astype(BF16)
    for index in range(3):
        unpack_ups(flat, starts[index][1], D, index * COLS, b_ref, index * D)


def flat_rows(count):
    return PARAM_ROWS + shard_rows(count) + 20


def unpack_rest(flat, outs, work):
    starts = piece_rows()
    matrix = (keep_matrix() + spread_matrix(EXPERTS, COLS, COLS)).astype(BF16)
    for index in range(3, 6):
        base_a, base_b, base_r = starts[index]
        fan_in, fan_out = FANS[index]
        ar_ref, b_ref = outs[2 * index - 6], outs[2 * index - 5]
        narrow_to_rows(flat, fan_in, [(base_a, COLS, 0), (base_r, EXPERTS, COLS)], work)
        ar_ref[...] = dot(work[:fan_in].astype(BF16), matrix).astype(BF16)
        unpack_ups(flat, base_b, fan_out, 0, b_ref, 0)


def split_dot(value, matrix):
    high = value.astype(BF16)
    return dot(high, matrix) + dot((value - high.astype(F32)).astype(BF16), matrix)


def first_of_four(experts, source, place):
    row = row_iota((LANES, LANES)) - source
    lane = lane_iota((LANES, LANES)) - place
    hit = (row == RANK * lane) & (lane >= 0) & (lane < experts)
    return jnp.where(hit, 1.0, 0.0)


def assemble_ups(flat, base, fan_out, first, grad_ref, column):
    width = fan_out // LANES
    for k in range(width):
        lanes = slice(column + k * LANES, column + (k + 1) * LANES)
        flat[pl.ds(base + k, COLS, stride=width), :] = grad_ref[first : first + COLS, lanes]


def assemble_rest(flat, grads, work):
    starts = piece_rows()
    matrix = (keep_matrix() + first_of_four(EXPERTS, COLS, COLS)).astype(BF16)
    for index in range(3, 6):
        base_a, base_b, base_r = starts[index]
        fan_in, fan_out = FANS[index]
        dar_ref, db_ref = grads[2 * index - 6], grads[2 * index - 5]
        work[:fan_in] = split_dot(pad_rows(dar_ref[...], LANES).T, matrix)
        rows_to_narrow(work, fan_in, [(base_a, COLS, 0), (base_r, EXPERTS, COLS)], flat)
        assemble_ups(flat, base_b, fan_out, 0, db_ref, 0)


def assemble_first(flat, dar_ref, db_ref, down, router):
    starts = piece_rows()
    down[...] = dar_ref[:LANES].T
    rows_to_narrow(down, D, [(starts[k][0], COLS, k * COLS) for k in range(3)], flat)
    first_router = 3 * COLS
    turned = dar_ref[first_router : first_router + LANES].T
    router[...] = split_dot(turned, first_of_four(3 * EXPERTS, 0, 0).astype(BF16))
    rows_to_narrow(router, D, [(starts[k][2], EXPERTS, k * EXPERTS) for k in range(3)], flat)
    for index in range(3):
        assemble_ups(flat, starts[index][1], D, index * COLS, db_ref, index * D)


MESH = pl.DeviceIdType.MESH


def place_of(axes, sizes):
    me = lax.axis_index(axes[0]) * sizes[1] + lax.axis_index(axes[1])

    def coordinates(number):
        return (number // sizes[1], number % sizes[1])

    return me, coordinates


def partners_of(me):
    low = me % 8
    core = low % 2
    y = (low // 2) % 2
    x = low // 4
    over_x = low + 4 * (1 - 2 * x)
    over_y = low + 2 * (1 - 2 * y)
    first = over_x * (1 - core) + over_y * core
    second = over_y * (1 - core) + over_x * core
    both = first + second - low
    other = 1 - 2 * core
    return low, first, second, both, other, over_x, over_y


def greet(peers):
    barrier = pltpu.get_barrier_semaphore()
    for peer in peers:
        pl.semaphore_signal(barrier, inc=1, device_id=peer, device_id_type=MESH)
    pl.semaphore_wait(barrier, len(peers))


class Ring:
    def __init__(self, axes, sizes, send, receive):
        self.me, self.coordinates = place_of(axes, sizes)
        self.groups = sizes[0] * sizes[1] // 8
        self.group = self.me // 8
        places = partners_of(self.me)
        self.low, self.first, self.second, self.both, self.other, self.over_x, self.over_y = places
        self.mate = self.low + self.other
        self.send, self.receive = send, receive
        self.copies = {}

    def device(self, group, low):
        return self.coordinates(group * 8 + low)

    def greet(self):
        peers = [
            self.device((self.group + step) % self.groups, self.low)
            for step in range(1, self.groups)
        ]
        peers += [self.device(self.group, low) for low in (self.first, self.second, self.mate)]
        greet(peers)

    def copy(self, slot, source, target, peer, arrival=None):
        return pltpu.make_async_remote_copy(
            src_ref=source,
            dst_ref=target,
            send_sem=self.send.at[slot],
            recv_sem=self.receive.at[slot if arrival is None else arrival],
            device_id=peer,
            device_id_type=MESH,
        )


def gather_phases(ring, span, shard_ref, out_ref, local, greets):
    begin, end = span
    base = ring.groups
    inside = (ring.group >= begin) & (ring.group < end)

    def around(step):
        target = (ring.group + step) % ring.groups
        return ring.copy(
            step,
            shard_ref,
            out_ref.at[ring.group - begin, ring.low],
            ring.device(target, ring.low),
            base + 7 + ring.group,
        )

    def arrived(group):
        return ring.copy(
            0,
            shard_ref,
            out_ref.at[group - begin, ring.low],
            ring.device(group, ring.low),
            base + 7 + group,
        )

    def push(slot, part, partner):
        return ring.copy(
            base + slot, out_ref.at[:, part], out_ref.at[:, part], ring.device(ring.group, partner)
        )

    one = push(0, ring.low, ring.first)
    two = push(1, ring.low, ring.second)
    three = push(2, ring.first, ring.second)
    cores = [
        push(3 + index, part, ring.mate)
        for index, part in enumerate((ring.low, ring.first, ring.second, ring.both))
    ]

    def own():
        return pltpu.make_async_copy(
            shard_ref, out_ref.at[ring.group - begin, ring.low], local
        )

    def phase0():
        if greets:
            ring.greet()

        @pl.when(inside)
        def _():
            own().start()
            for step in range(1, ring.groups):
                around(step).start()

    def phase1():
        @pl.when(inside)
        def _():
            own().wait()
            for step in range(1, ring.groups):
                around(step).wait_send()

        for group in range(begin, end):

            @pl.when(ring.group != group)
            def _():
                arrived(group).wait_recv()

        for copy in (one, two, cores[0]):
            copy.start()

    def phase2():
        one.wait()
        three.start()
        cores[1].start()

    def phase3():
        two.wait()
        cores[2].start()
        three.wait()
        cores[3].start()

    def phase4():
        for copy in cores:
            copy.wait()

    return phase0, phase1, phase2, phase3, phase4


def gather_semaphores(groups):
    return [
        pltpu.SemaphoreType.DMA((groups + 7,)),
        pltpu.SemaphoreType.DMA((2 * groups + 7,)),
        pltpu.SemaphoreType.DMA,
    ]


def start_kernel(
    link,
    count,
    shard_ref,
    buckets_ref,
    table_ref,
    gain_ref,
    x_hbm,
    w_hbm,
    *refs,
):
    hbm_outs, off_ref, ar_ref, b_ref = refs[:6], refs[6], refs[7], refs[8]
    rest_refs = refs[9:15]
    x_ref, w_ref, normed, dense = refs[15:19]
    outs = refs[19:25]
    qt_ref, k_ref, kt_ref, v_ref, vt_ref, zg_ref = outs
    flat, down, router, work, loaded, stored, *more = refs[25:]
    loads = [
        pltpu.make_async_copy(x_hbm, x_ref, loaded.at[0]),
        pltpu.make_async_copy(w_hbm, w_ref, loaded.at[1]),
    ]
    stores = [
        pltpu.make_async_copy(source, target, stored.at[index])
        for index, (source, target) in enumerate(zip(outs, hbm_outs))
    ]
    for load in loads:
        load.start()
    if link is None:
        first = [lambda: None] * 5
        rest = first

        def shard_of(index):
            return shard_ref[...]
    else:
        axes, sizes, spans = link
        land_a, land_b, *sems = more
        first = gather_phases(
            Ring(axes, sizes, *sems[:2]), spans[0], shard_ref, land_a, sems[2], True
        )
        rest = gather_phases(
            Ring(axes, sizes, *sems[3:5]), spans[1], shard_ref, land_b, sems[5], False
        )

        def shard_of(index):
            group, low = divmod(index, 8)
            begin = spans[1][0]
            return land_a[group, low] if group < begin else land_b[group - begin, low]

    def rows_of(index):
        return pl.ds(pl.multiple_of(index * ROWS, ROWS), ROWS)

    def dense_tile(index, _):
        rows = rows_of(index)
        values = x_ref[rows].astype(F32)
        low = (values * rms_inverse(values) * gain_ref[...]).astype(BF16)
        normed[rows] = low
        dense[rows] = dot(low, w_ref[...])
        return 0

    def project_tile(index, _):
        rows = rows_of(index)
        packed = dot(normed[rows], ar_ref[...]).T
        lowrank = packed[: 3 * COLS]
        gates = jnp.concatenate(
            [gates_of(packed[place : place + COLS]) for place in range(3 * COLS, 6 * COLS, COLS)],
            axis=0,
        )
        zg_ref[: 3 * COLS, rows] = lowrank
        zg_ref[3 * COLS :, rows] = gates
        mixed = pad_rows(lowrank * gates, LANES).astype(BF16).T
        for part in range(3):
            columns = slice(part * D, (part + 1) * D)
            value = dense[rows, columns] + dot(mixed, b_ref[:, columns])
            if part == 0:
                qt_ref[:, rows] = (value * QUERY_SCALE).astype(BF16).T
            else:
                low = value.astype(BF16)
                natural, turned = ((k_ref, kt_ref), (v_ref, vt_ref))[part - 1]
                natural[rows] = low
                turned[:, rows] = low.T
        return 0

    tiles = x_ref.shape[0] // ROWS
    first[0]()
    rest[0]()
    for load in loads:
        load.wait()
    lax.fori_loop(0, tiles // 2, dense_tile, 0)
    first[1]()
    rest[1]()
    lax.fori_loop(tiles // 2, tiles, dense_tile, 0)
    buckets = buckets_ref[...]
    hits = jnp.where(row_iota((table_ref.shape[0], buckets.shape[1])) == buckets, LOG2E, 0.0)
    off_ref[...] = lax.dot_general(
        table_ref[...],
        hits,
        (((0,), (0,)), ((), ())),
        preferred_element_type=F32,
        precision=lax.Precision.HIGHEST,
    )
    for step in range(2, 5):
        first[step]()
        if step < 4:
            rest[step]()

    for index in range(-(-FIRST_COUNT // count)):
        align_in(flat, shard_of(index).astype(F32), index * count)
    unpack_first(flat, ar_ref, b_ref, down, router)
    lax.fori_loop(0, tiles, project_tile, 0)
    for store in stores:
        store.start()
    rest[4]()
    for index in range(FIRST_COUNT // count, PARAM_ROWS * LANES // count):
        align_in(flat, shard_of(index).astype(F32), index * count)
    unpack_rest(flat, rest_refs, work)
    for store in stores:
        store.wait()


def start(x, gain, w_qkv, shard, buckets, rel_table, count, axes, sizes, spans):
    length = x.shape[0]
    groups = sizes[0] * sizes[1] // 8
    link = (axes, sizes, spans) if groups else None
    rest_shapes = [
        shape for fan_in, fan_out in FANS[3:] for shape in ((fan_in, LANES), (LANES, fan_out))
    ]
    wide = [
        ((D, length), BF16),
        ((length, D), BF16),
        ((D, length), BF16),
        ((length, D), BF16),
        ((D, length), BF16),
        ((6 * COLS, length), F32),
    ]
    small = [
        ((HEADS, buckets.shape[1]), F32),
        ((D, 2 * LANES), BF16),
        ((LANES, 3 * D), BF16),
    ] + [(shape, BF16) for shape in rest_shapes]
    scratch = [
        pltpu.VMEM(x.shape, BF16),
        pltpu.VMEM(w_qkv.shape, BF16),
        pltpu.VMEM(x.shape, BF16),
        pltpu.VMEM((length, 3 * D), F32),
    ]
    scratch += [pltpu.VMEM(*member) for member in wide]
    scratch += [
        pltpu.VMEM((flat_rows(count), LANES), F32),
        pltpu.VMEM((D, LANES), F32),
        pltpu.VMEM((D, LANES), F32),
        pltpu.VMEM((FF, LANES), F32),
        pltpu.SemaphoreType.DMA((2,)),
        pltpu.SemaphoreType.DMA((len(wide),)),
    ]
    if link:
        scratch += [pltpu.VMEM((end - begin, 8, *shard.shape), BF16) for begin, end in spans]
        scratch += gather_semaphores(groups) * 2
    vmem = pl.BlockSpec(memory_space=pltpu.VMEM)
    anywhere = pl.BlockSpec(memory_space=pl.ANY)
    return pl.pallas_call(
        functools.partial(start_kernel, link, count),
        in_specs=[vmem] * 4 + [anywhere] * 2,
        out_specs=[anywhere] * len(wide) + [vmem] * len(small),
        out_shape=[jax.ShapeDtypeStruct(*member) for member in wide + small],
        scratch_shapes=scratch,
        compiler_params=params(collective_id=0, has_side_effects=True) if link else params(),
        name="start",
    )(shard, buckets, rel_table, gain, x, w_qkv)


def reduce_phases(ring, span, parts_ref, boxes, greets, sums_ref=None, sum_boxes=None):
    begin, end = span
    outbox, inbox, half, own, far_out, far_in, out_ref = boxes
    groups = ring.groups
    inside = (ring.group >= begin) & (ring.group < end)
    core_parts = (ring.first, ring.both, ring.second, ring.low)
    near = [ring.mate] * 4 + [ring.second, ring.second, ring.first]

    def push(slot):
        return ring.copy(slot, outbox.at[slot], inbox.at[slot], ring.device(ring.group, near[slot]))

    def fill(slot, value):
        outbox[slot] = value.astype(BF16)
        push(slot).start()

    def around(group):
        return ring.copy(
            7 + group - begin,
            far_out.at[group - begin],
            far_in.at[ring.group],
            ring.device(group, ring.low),
            7 + ring.group,
        )

    def arrived(group):
        return ring.copy(
            7,
            far_out.at[0],
            far_in.at[group],
            ring.device(group, ring.low),
            7 + group,
        )

    base = 7 + groups
    sum_peers = (ring.mate, ring.over_x, ring.over_y)

    def push_sums(slot):
        near_out, near_in = sum_boxes
        return ring.copy(
            base + slot,
            near_out.at[slot],
            near_in.at[slot],
            ring.device(ring.group, sum_peers[slot]),
        )

    def around_sums(step):
        near_out, near_in = sum_boxes
        target = (ring.group + step) % groups
        return ring.copy(
            base + 2 + step,
            near_out.at[3],
            near_in.at[3 + ring.group],
            ring.device(target, ring.low),
        )

    def start_sums(slot, value):
        if sum_boxes is not None:
            sum_boxes[0][slot] = value
            push_sums(slot).start()

    def phase0():
        if greets:
            ring.greet()
        if sum_boxes is not None:
            start_sums(0, sums_ref[...])
        for slot, part in enumerate(core_parts):
            fill(slot, parts_ref[:, part + ring.other])

    def phase1():
        push(0).wait()
        fill(4, parts_ref[:, ring.second] + inbox[0].astype(F32))
        push(1).wait()
        fill(5, parts_ref[:, ring.both] + inbox[1].astype(F32))
        if sum_boxes is not None:
            push_sums(0).wait()
            start_sums(1, sum_boxes[0][0] + sum_boxes[1][0])
        push(2).wait()
        half[...] = parts_ref[:, ring.first] + inbox[2].astype(F32)
        push(3).wait()
        own[...] = parts_ref[:, ring.low] + inbox[3].astype(F32)

    def phase2():
        push(5).wait()
        fill(6, half[...] + inbox[5].astype(F32))
        if sum_boxes is not None:
            push_sums(1).wait()
            start_sums(2, sum_boxes[0][1] + sum_boxes[1][1])
        push(4).wait()
        own[...] = own[...] + inbox[4].astype(F32)

    def phase3():
        push(6).wait()
        own[...] = own[...] + inbox[6].astype(F32)
        far_out[...] = own[...].astype(BF16)
        for group in range(begin, end):

            @pl.when(ring.group != group)
            def _():
                around(group).start()

        if sum_boxes is not None:
            near_out, near_in = sum_boxes
            push_sums(2).wait()
            near_out[3] = near_out[2] + near_in[2]
            for step in range(1, groups):
                around_sums(step).start()
            near_in[3 + ring.group] = near_out[3]

    def phase4(finish_sums=None):
        for group in range(begin, end):

            @pl.when(ring.group != group)
            def _():
                around(group).wait_send()

        @pl.when(inside)
        def _():
            for group in range(groups):

                @pl.when(ring.group != group)
                def _():
                    arrived(group).wait_recv()

            total = own[ring.group - begin]
            for step in range(1, groups):
                total = total + far_in[(ring.group + step) % groups].astype(F32)
            out_ref[...] = total

        if sum_boxes is not None:
            near_out, near_in = sum_boxes
            for step in range(1, groups):
                around_sums(step).wait()
            whole_sum = near_in[3]
            for index in range(1, groups):
                whole_sum = whole_sum + near_in[3 + index]
            finish_sums(whole_sum)

    return phase0, phase1, phase2, phase3, phase4


def reduce_scratch(groups, count, rows):
    return [
        pltpu.VMEM((7, count, rows, LANES), BF16),
        pltpu.VMEM((7, count, rows, LANES), BF16),
        pltpu.VMEM((count, rows, LANES), F32),
        pltpu.VMEM((count, rows, LANES), F32),
        pltpu.VMEM((count, rows, LANES), BF16),
        pltpu.VMEM((groups, rows, LANES), BF16),
    ]


def finish_kernel(link, count, dar_ref, db_ref, *refs):
    grads, sums_ref = refs[:6], refs[6]
    out_ref, roots_ref, flat, down, router, work, *more = refs[7:]

    def finish_sums(total):
        roots_ref[...] = jnp.sqrt(total / (total[:, 4:5] * D))

    assemble_rest(flat, grads, work)
    if link is None:
        assemble_first(flat, dar_ref, db_ref, down, router)
        out_ref[...] = align_out(flat, out_ref.shape[0], 0)
        finish_sums(sums_ref[...])
        return
    axes, sizes, spans = link
    parts_a, parts_b, near_out, near_in, *more = more
    boxes_a, boxes_b, sems = more[:7], more[7:14], more[14:]
    rows = out_ref.shape[0]
    split = spans[1][0]

    def align(parts, span):
        for group in range(*span):
            for low in range(8):
                parts[group - span[0], low] = align_out(flat, rows, (8 * group + low) * count)

    ring = Ring(axes, sizes, sems[0], sems[1])
    rest = reduce_phases(ring, spans[1], parts_b, boxes_b, True, sums_ref, (near_out, near_in))
    first = reduce_phases(
        Ring(axes, sizes, sems[2], sems[3]), spans[0], parts_a, boxes_a, False
    )
    align(parts_b, spans[1])
    rest[0]()
    assemble_first(flat, dar_ref, db_ref, down, router)
    align(parts_a, spans[0])
    first[0]()
    for step in range(1, 4):
        rest[step]()
        first[step]()
    rest[4](finish_sums)
    first[4]()

    @pl.when(ring.group < split)
    def _():
        out_ref[...] = boxes_a[6][...]

    @pl.when(ring.group >= split)
    def _():
        out_ref[...] = boxes_b[6][...]


def finish(dar, db, grads, sums, count, axes, sizes, spans):
    rows = shard_rows(count)
    groups = sizes[0] * sizes[1] // 8
    link = (axes, sizes, spans) if groups else None
    scratch = [
        pltpu.VMEM((flat_rows(count), LANES), F32),
        pltpu.VMEM((D, LANES), F32),
        pltpu.VMEM((D, LANES), F32),
        pltpu.VMEM((FF, LANES), F32),
    ]
    if link:
        widths = [end - begin for begin, end in spans]
        scratch += [pltpu.VMEM((width, 8, rows, LANES), F32) for width in widths]
        scratch += [
            pltpu.VMEM((4, *sums.shape), F32),
            pltpu.VMEM((3 + groups, *sums.shape), F32),
        ]
        for width in widths:
            scratch += reduce_scratch(groups, width, rows) + [pltpu.VMEM((rows, LANES), F32)]
        scratch += [pltpu.SemaphoreType.DMA((10 + 2 * groups,))] * 4
    vmem = pl.BlockSpec(memory_space=pltpu.VMEM)
    return pl.pallas_call(
        functools.partial(finish_kernel, link, count),
        in_specs=[vmem] * (3 + len(grads)),
        out_specs=[vmem] * 2,
        out_shape=[
            jax.ShapeDtypeStruct((rows, LANES), F32),
            jax.ShapeDtypeStruct(sums.shape, F32),
        ],
        scratch_shapes=scratch,
        compiler_params=params(collective_id=1, has_side_effects=True) if link else params(),
        name="finish",
    )(dar, db, *grads, sums)


def per_device(
    tokens,
    lengths,
    buckets,
    rel_table,
    gain_attn,
    gain_ff,
    w_qkv,
    w_out,
    w_in,
    w_down,
    adapters,
    cotangent,
    axes,
    sizes,
):
    seq_count, length, width = tokens.shape
    x = tokens.reshape(length, width)
    cot = cotangent.reshape(length, width)
    gain_first = gain_attn.reshape(1, width)
    gain_second = gain_ff.reshape(1, width)
    devices = sizes[0] * sizes[1]
    count = adapters.shape[0]
    rows = shard_rows(count)
    shard = jnp.pad(adapters, (0, rows * LANES - count)).reshape(rows, LANES)
    groups = devices // 8
    split_groups = min(-(-FIRST_COUNT // (8 * count)), max(groups - 1, 1))
    spans = ((0, split_groups), (split_groups, groups))
    reversed_buckets = jnp.pad(buckets[::-1], (0, 1)).reshape(1, 2 * length)
    qt, k, kt, v, vt, zg, offsets, ar_qkv, b_qkv, *packed = start(
        x, gain_first, w_qkv, shard, reversed_buckets, rel_table, count, axes, sizes, spans
    )
    ot, lse = attend(lengths, offsets, qt, k, vt)
    block_out, dmid, gt, sums, *grads = middle_part(
        lengths, ot, x, cot, gain_second, w_out, w_in, w_down, packed
    )
    dq, dk, dv = attend_back(lengths, offsets, qt, k, kt, v, ot, gt, lse)
    tokens_grad, dar_qkv, db_qkv = project_back(
        x, gain_first, w_qkv, ar_qkv, b_qkv, zg, dq, dk, dv, dmid
    )

    mine, roots = finish(dar_qkv, db_qkv, grads, sums, count, axes, sizes, spans)
    grad_shard = mine.reshape(-1)[:count]
    root_squares = roots[0, :4]
    return (
        block_out.reshape(tokens.shape),
        tokens_grad.reshape(tokens.shape),
        grad_shard,
        root_squares,
    )


def solution(mesh):
    axes = tuple(mesh.axis_names)
    sizes = tuple(mesh.shape[axis] for axis in axes)
    sequence = P(axes, None, None)
    placed = (
        sequence,
        P(axes),
        P(),
        P(),
        P(),
        P(),
        P(),
        P(),
        P(),
        P(),
        P(axes),
        sequence,
    )
    return jax.shard_map(
        functools.partial(per_device, axes=axes, sizes=sizes),
        mesh=mesh,
        in_specs=placed,
        out_specs=(sequence, sequence, P(axes), P()),
        check_vma=False,
    )
```

```python
import functools

import jax
import jax.numpy as jnp
from jax import lax
from jax.experimental import pallas as pl
from jax.experimental.pallas import tpu as pltpu
from jax.sharding import PartitionSpec as P

D = 768
FF = 3072
HEADS = 12
HDIM = 64
EXPERTS = 10
RANK = 4
FANS = ((D, D), (D, D), (D, D), (D, D), (D, FF), (FF, D))
COLS = EXPERTS * RANK
LANES = 128

EPSILON = 1e-06
MASKED = -1000000000.0
GELU_SCALE = 0.7978845608028654
GELU_CUBIC = 0.044715
LOG2E = 1.4426950408889634
LN2 = 0.6931471805599453
QUERY_SCALE = 0.125 * LOG2E

ROWS = 256
MIDDLE_ROWS = 512
CHUNK = 512
QBLOCK = 256
UP_ROWS = 48
DOWN_ROWS = 2 * COLS
VMEM_BYTES = 60 * 1024 * 1024

F32 = jnp.float32
BF16 = jnp.bfloat16


def dot(a, b):
    return lax.dot_general(a, b, (((1,), (0,)), ((), ())), preferred_element_type=F32)


def dot_nt(a, b):
    return lax.dot_general(a, b, (((1,), (1,)), ((), ())), preferred_element_type=F32)


def dot_tn(a, b):
    return lax.dot_general(a, b, (((0,), (0,)), ((), ())), preferred_element_type=F32)


def lane_iota(shape):
    return lax.broadcasted_iota(jnp.int32, shape, 1)


def row_iota(shape):
    return lax.broadcasted_iota(jnp.int32, shape, 0)


def gates_of(logits):
    weights = jnp.exp(logits - jnp.max(logits, axis=0, keepdims=True))
    return weights * (4.0 / jnp.sum(weights, axis=0, keepdims=True))


def gate_grads(grad_mixed, lowrank, gates):
    product = grad_mixed * lowrank
    summed = product
    for step in range(1, RANK):
        summed = summed + pltpu.roll(product, COLS - step, 0)
    centre = jnp.sum(gates * product, axis=0, keepdims=True)
    first = row_iota(gates.shape) % RANK == 0
    return grad_mixed * gates, jnp.where(first, gates * (summed - centre), 0.0)


def pad_rows(value, rows):
    return jnp.concatenate([value, jnp.zeros((rows - value.shape[0], value.shape[1]), F32)], axis=0)


def single_gates(packed):
    turned = packed.T
    lowrank = turned[:COLS]
    gates = gates_of(turned[COLS : 2 * COLS])
    mixed = pad_rows(lowrank * gates, LANES).astype(BF16)
    return lowrank, gates, mixed, mixed.T


def single_deltas(grad_mixed, lowrank, gates):
    parts = gate_grads(grad_mixed.T[:COLS], lowrank, gates)
    delta = pad_rows(jnp.concatenate(parts, axis=0), LANES).astype(BF16)
    return delta, delta.T


def rms_inverse(values):
    return lax.rsqrt(jnp.mean(values * values, axis=-1, keepdims=True) + EPSILON)


def rms_backward(values, gain, inverse, grad_normed):
    weighted = grad_normed * gain
    return inverse * weighted - values * (
        inverse * inverse * inverse * jnp.mean(values * weighted, axis=-1, keepdims=True)
    )


def params(**more):
    return pltpu.CompilerParams(vmem_limit_bytes=VMEM_BYTES, **more)


def whole(shape):
    zeros = (0,) * len(shape)
    return pl.BlockSpec(shape, lambda *_: zeros, pipeline_mode=pl.Buffered(1))


def bias_table(offset_row, length):
    spread = jnp.broadcast_to(offset_row, (LANES, 2 * length))
    return pltpu.roll(spread, 2 * length - (LANES - 1), 1, stride=1, stride_axis=0)


def add_bias(scores, table_ref, start, length):
    width = scores.shape[1]
    parts = []
    for block in range(length // LANES):
        offset = start - LANES * block + (length - LANES)
        parts.append(
            scores[block * LANES : (block + 1) * LANES] + table_ref[:, offset : offset + width]
        )
    return jnp.concatenate(parts, axis=0)


def key_extras(length_ref, shape, odd):
    lane = lane_iota(shape) - (0 if odd else HDIM)
    invalid = row_iota(shape) >= length_ref[0]
    extras = jnp.where((lane == 0) & invalid, MASKED, 0.0)
    return jnp.where((lane >= 1) & (lane <= 3), 1.0, extras).astype(BF16)


def head_lanes(odd):
    lane = lane_iota((1, LANES))
    return ((lane >= HDIM) if odd else (lane < HDIM)).astype(F32).astype(BF16)


def extra_rows(rows):
    width = rows[0].shape[1]
    index = row_iota((8, width))
    block = jnp.zeros((8, width), F32)
    for place, row in enumerate(rows):
        block = jnp.where(index == place, row, block)
    return jnp.concatenate([block, jnp.zeros((HDIM - 8, width), F32)], axis=0).astype(BF16)


def split_three(row):
    high = row.astype(BF16).astype(F32)
    middle = (row - high).astype(BF16).astype(F32)
    return high, middle, row - high - middle


def join_rows(rows, extras, odd):
    return jnp.concatenate([extras, rows] if odd else [rows, extras], axis=0)


def attend_kernel(
    length_ref, off_ref, qt_ref, k_ref, kt_ref, vt_ref, o_ref, lse_ref, table, key_more
):
    length = k_ref.shape[0]
    step = pl.program_id(0)

    @pl.when(step == 0)
    def _():
        for odd in range(2):
            key_more[odd] = key_extras(length_ref, k_ref.shape, odd)

    starts = range(0, length, QBLOCK)
    ones = jnp.ones((1, length), F32)

    def half_of(odd):
        return slice(odd * HDIM, (odd + 1) * HDIM)

    def keys_of(odd):
        return k_ref[...] * head_lanes(odd) + key_more[odd]

    def values_of(odd):
        return jnp.concatenate([vt_ref[half_of(odd), :], jnp.ones((16, length), BF16)], axis=0)

    def finish(odd, start, shift, weights):
        columns = slice(start, start + QBLOCK)
        summed = dot(values_of(odd), weights)
        total = summed[HDIM : HDIM + 1]
        o_ref[half_of(odd), columns] = (summed[:HDIM] / total).astype(BF16)
        lse_ref[0, odd : odd + 1, columns] = shift + jnp.log2(total)
        return total

    def bounded(odd):
        offsets = off_ref[pl.ds(2 * step + odd, 1), :]
        table[odd] = bias_table(offsets, length)
        squares = jnp.square(kt_ref[half_of(odd), :].astype(F32))
        sizes = jnp.sum(squares, axis=0, keepdims=True)
        sizes = jnp.where(lane_iota(sizes.shape) < length_ref[0], sizes, 0.0)
        largest = jnp.max(sizes, axis=1, keepdims=True)
        rows = qt_ref[half_of(odd), :].astype(F32)
        norms = jnp.sqrt(jnp.sum(rows * rows, axis=0, keepdims=True) * largest)
        bound = 1.001 * norms + jnp.max(offsets, axis=1, keepdims=True)
        queries = join_rows(
            qt_ref[half_of(odd), :],
            extra_rows([ones] + [-part for part in split_three(bound)]),
            odd,
        )
        keys = keys_of(odd)
        scores = [dot(keys, queries[:, start : start + QBLOCK]) for start in starts]
        weights = [
            jnp.exp2(add_bias(part, table.at[odd], start, length)).astype(BF16)
            for part, start in zip(scores, starts)
        ]
        least = None
        for start, part in zip(starts, weights):
            total = finish(odd, start, bound[:, start : start + QBLOCK], part)
            least = total if least is None else jnp.minimum(least, total)
        return least

    def exact(odd):
        queries = join_rows(qt_ref[half_of(odd), :], extra_rows([ones]), odd)
        keys = keys_of(odd)
        for start in starts:
            columns = slice(start, start + QBLOCK)
            scores = add_bias(dot(keys, queries[:, columns]), table.at[odd], start, length)
            peak = jnp.max(scores, axis=0, keepdims=True)
            finish(odd, start, peak, jnp.exp2(scores - peak).astype(BF16))

    least = jnp.minimum(bounded(0), bounded(1))

    @pl.when(jnp.logical_not(jnp.min(least) > 2.0**-100))
    def _():
        for odd in range(2):
            exact(odd)


def attend(length_valid, offsets, qt, k, kt, vt):
    length = k.shape[0]
    turned = pl.BlockSpec((LANES, length), lambda p: (p, 0))
    natural = pl.BlockSpec((length, LANES), lambda p: (0, p))
    return pl.pallas_call(
        attend_kernel,
        grid=(HEADS // 2,),
        in_specs=[
            pl.BlockSpec(memory_space=pltpu.SMEM),
            whole(offsets.shape),
            turned,
            natural,
            turned,
            turned,
        ],
        out_specs=[turned, pl.BlockSpec((1, 2, length), lambda p: (p, 0, 0))],
        out_shape=[
            jax.ShapeDtypeStruct((D, length), BF16),
            jax.ShapeDtypeStruct((HEADS // 2, 2, length), F32),
        ],
        scratch_shapes=[
            pltpu.VMEM((2, LANES, 2 * length), F32),
            pltpu.VMEM((2, length, LANES), BF16),
        ],
        compiler_params=params(),
        name="attend",
    )(length_valid, offsets, qt, k, kt, vt)


def middle_kernel(
    length_ref,
    ot_ref,
    x_ref,
    cot_ref,
    gain_ref,
    w_out_ref,
    w_in_hbm,
    w_down_hbm,
    ar_out_ref,
    b_out_ref,
    ar_in_ref,
    b_in_ref,
    ar_down_ref,
    b_down_ref,
    out_ref,
    dmid_ref,
    gt_ref,
    sums_ref,
    dar_out_ref,
    db_out_ref,
    dar_in_ref,
    db_in_ref,
    dar_down_ref,
    db_down_ref,
    active,
    slope,
    sloped,
    grad_hidden,
    feeds,
    w_in_ref,
    w_down_ref,
    loaded,
):
    step = pl.program_id(0)
    loads = [
        pltpu.make_async_copy(w_in_hbm, w_in_ref, loaded.at[0]),
        pltpu.make_async_copy(w_down_hbm, w_down_ref, loaded.at[1]),
    ]

    @pl.when(step == 0)
    def _():
        for load in loads:
            load.start()
        for ref in (
            sums_ref,
            dar_out_ref,
            db_out_ref,
            dar_in_ref,
            db_in_ref,
            dar_down_ref,
            db_down_ref,
        ):
            ref[...] = jnp.zeros_like(ref)

    attended = ot_ref[...].T
    inputs = x_ref[...].astype(F32)
    gain = gain_ref[...].reshape(1, D)
    cot = cot_ref[...]

    packed_out = dot(attended, ar_out_ref[...])
    branch = dot(attended, w_out_ref[...])
    low_out, gates_out, mixed_out, natural = single_gates(packed_out)
    grad_mixed_down = dot_nt(cot, b_down_ref[...])
    branch = branch + dot(natural, b_out_ref[...])
    middle = inputs + branch
    inverse = rms_inverse(middle)
    normed = (middle * inverse * gain).astype(BF16)

    packed_in = dot(normed, ar_in_ref[...])
    low_in, gates_in, mixed_in, natural = single_gates(packed_in)

    def columns_of(index):
        return pl.ds(pl.multiple_of(index * CHUNK, CHUNK), CHUNK)

    def hidden_of(chunk):
        return dot(normed, w_in_ref[:, chunk]) + dot(natural, b_in_ref[:, chunk])

    def activate(chunk, values):
        grad_dense = dot_nt(cot, w_down_ref[chunk])
        square = values * values
        tangent = jnp.tanh(values * (GELU_SCALE + (GELU_SCALE * GELU_CUBIC) * square))
        half = 0.5 + 0.5 * tangent
        smooth = values * half
        active[:, chunk] = smooth.astype(BF16)
        steep = half + smooth * (1.0 - tangent) * (
            GELU_SCALE + (3.0 * GELU_SCALE * GELU_CUBIC) * square
        )
        slope[:, chunk] = steep.astype(BF16)
        sloped[:, chunk] = grad_dense * steep

    def forward_pair(pair, _):
        chunk_a = columns_of(2 * pair)
        chunk_b = columns_of(2 * pair + 1)
        hidden_a = hidden_of(chunk_a)
        hidden_b = hidden_of(chunk_b)
        activate(chunk_a, hidden_a)
        activate(chunk_b, hidden_b)
        return 0

    @pl.when(step == 0)
    def _():
        for load in loads:
            load.wait()

    lax.fori_loop(0, FF // (2 * CHUNK), forward_pair, 0)

    packed_down = dot(active[...], ar_down_ref[...])
    def feed_part(index, _):
        part = pl.ds(pl.multiple_of(index * 256, 256), 256)
        feeds[:, part] = dot(active[...], w_down_ref[:, part])
        return 0

    lax.fori_loop(0, 3, feed_part, 0)
    feed = feeds[...]
    low_down, gates_down, mixed_down, natural = single_gates(packed_down)
    delta_down, natural_delta = single_deltas(grad_mixed_down, low_down, gates_down)
    db_down_ref[...] += dot(mixed_down[:UP_ROWS], cot)
    feed = feed + dot(natural, b_down_ref[...])
    output = middle + feed
    out_ref[...] = output.astype(BF16)

    def backward_chunk(index, _):
        chunk = columns_of(index)
        grad_low = dot_nt(natural_delta, ar_down_ref[chunk])
        grad_hidden[:, chunk] = (
            sloped[:, chunk] + grad_low * slope[:, chunk].astype(F32)
        ).astype(BF16)
        return 0

    lax.fori_loop(0, FF // CHUNK, backward_chunk, 0)
    dar_down_ref[...] += dot(delta_down[:DOWN_ROWS], active[...])

    rows = row_iota((MIDDLE_ROWS, 1)) + step * MIDDLE_ROWS
    valid = (rows < length_ref[0]).astype(F32)
    lane = lane_iota((8, LANES))
    totals = jnp.where((lane == 4) & (step == 0), length_ref[0].astype(F32), 0.0)
    for place, member in enumerate((inputs, branch, feed, output)):
        kept = member * valid
        totals = jnp.where(lane == place, jnp.sum(kept * kept), totals)
    sums_ref[...] += totals

    grad_mixed = dot_nt(grad_hidden[...], b_in_ref[...])
    def back_part(index, _):
        part = pl.ds(pl.multiple_of(index * 256, 256), 256)
        feeds[:, part] = dot_nt(grad_hidden[...], w_in_ref[part])
        return 0

    lax.fori_loop(0, 3, back_part, 0)
    grad_normed = feeds[...]
    delta_in, natural_delta = single_deltas(grad_mixed, low_in, gates_in)
    db_in_ref[...] += dot(mixed_in[:UP_ROWS], grad_hidden[...])
    grad_normed = grad_normed + dot_nt(natural_delta, ar_in_ref[...])
    dar_in_ref[...] += dot(delta_in[:DOWN_ROWS], normed)

    grad_middle = cot.astype(F32) + rms_backward(middle, gain, inverse, grad_normed)
    dmid_ref[...] = grad_middle
    grad_branch = grad_middle.astype(BF16)
    grad_mixed = dot_nt(grad_branch, b_out_ref[...])
    grad_attended = dot_nt(grad_branch, w_out_ref[...])
    delta_out, natural_delta = single_deltas(grad_mixed, low_out, gates_out)
    grad_attended = grad_attended + dot_nt(natural_delta, ar_out_ref[...])
    gt_ref[...] = grad_attended.astype(BF16).T
    dar_out_ref[...] += dot(delta_out[:DOWN_ROWS], attended)
    db_out_ref[...] += dot(mixed_out[:UP_ROWS], grad_branch)


def middle_part(length_valid, ot, x, cot, gain, w_out, w_in, w_down, adapters):
    length = x.shape[0]
    tile = pl.BlockSpec((MIDDLE_ROWS, D), lambda i: (i, 0))
    turned = pl.BlockSpec((D, MIDDLE_ROWS), lambda i: (0, i))
    grad_shapes = [
        jax.ShapeDtypeStruct(shape, F32)
        for fan_in, fan_out in FANS[3:]
        for shape in ((DOWN_ROWS, fan_in), (UP_ROWS, fan_out))
    ]
    out_shape = [
        jax.ShapeDtypeStruct((length, D), BF16),
        jax.ShapeDtypeStruct((length, D), F32),
        jax.ShapeDtypeStruct((D, length), BF16),
        jax.ShapeDtypeStruct((8, LANES), F32),
    ] + grad_shapes
    return pl.pallas_call(
        middle_kernel,
        grid=(length // MIDDLE_ROWS,),
        in_specs=[pl.BlockSpec(memory_space=pltpu.SMEM), turned, tile, tile]
        + [whole(gain.shape), whole(w_out.shape)]
        + [pl.BlockSpec(memory_space=pl.ANY)] * 2
        + [whole(member.shape) for member in adapters],
        out_specs=[tile, tile, turned] + [whole(member.shape) for member in out_shape[3:]],
        out_shape=out_shape,
        scratch_shapes=[
            pltpu.VMEM((MIDDLE_ROWS, FF), BF16),
            pltpu.VMEM((MIDDLE_ROWS, FF), BF16),
            pltpu.VMEM((MIDDLE_ROWS, FF), F32),
            pltpu.VMEM((MIDDLE_ROWS, FF), BF16),
            pltpu.VMEM((MIDDLE_ROWS, D), F32),
            pltpu.VMEM(w_in.shape, BF16),
            pltpu.VMEM(w_down.shape, BF16),
            pltpu.SemaphoreType.DMA((2,)),
        ],
        compiler_params=params(),
        name="middle_part",
    )(length_valid, ot, x, cot, gain, w_out, w_in, w_down, *adapters)


def attend_back(
    pair,
    length_ref,
    off_ref,
    qt_ref,
    k_ref,
    kt_ref,
    v_ref,
    ot_ref,
    gt_ref,
    lse_ref,
    grads_ref,
    table,
    key_more,
    weights_all,
    grads_all,
):
    length = k_ref.shape[0]
    lane = lane_iota((1, LANES))
    first_lanes = lane < HDIM
    grad_query_parts = []
    for odd in range(2):
        half = slice(odd * HDIM, (odd + 1) * HDIM)
        table[odd] = bias_table(off_ref[pl.ds(2 * pair + odd, 1), :], length)
        keys = k_ref[...] * head_lanes(odd) + key_more[odd]
        place = lane - (0 if odd else HDIM)
        value_more = ((place >= 0) & (place < 3)).astype(F32).astype(BF16)
        values = v_ref[...] * head_lanes(odd) + value_more
        ones = jnp.ones((1, length), F32)
        lse = lse_ref[0, odd : odd + 1, :]
        queries = join_rows(
            qt_ref[half, :], extra_rows([ones] + [-part for part in split_three(lse)]), odd
        )
        delta = jnp.sum(
            ot_ref[half, :].astype(F32) * gt_ref[half, :].astype(F32), axis=0, keepdims=True
        )
        grads = join_rows(
            gt_ref[half, :], extra_rows([-part for part in split_three(delta)]), odd
        )
        for start in range(0, length, QBLOCK):
            columns = slice(start, start + QBLOCK)
            scores = add_bias(dot(keys, queries[:, columns]), table.at[odd], start, length)
            weights = jnp.exp2(scores)
            weights_all[:, columns] = weights.astype(BF16)
            grad_scores = weights * dot(values, grads[:, columns])
            grads_all[:, columns] = grad_scores.astype(BF16)
        grad_query_parts.append(dot(kt_ref[half, :], grads_all[...]) * 0.125)
        grad_values = dot_nt(weights_all[...], gt_ref[...])
        grad_keys = dot_nt(grads_all[...], qt_ref[...]) * LN2
        if odd:
            grad_values = jnp.where(first_lanes, even_values, grad_values)
            grad_keys = jnp.where(first_lanes, even_keys, grad_keys)
        else:
            even_values, even_keys = grad_values, grad_keys
    columns = pl.ds(pl.multiple_of(pair * LANES, LANES), LANES)
    grads_ref[0, :, columns] = jnp.concatenate(grad_query_parts, axis=0).T.astype(BF16)
    grads_ref[1, :, columns] = grad_keys.astype(BF16)
    grads_ref[2, :, columns] = grad_values.astype(BF16)


def project_back(
    tile, x_ref, gain_ref, w_ref, ar_ref, b_ref, zg_ref, grads_ref, dmid_ref, out_ref, dar_ref, db_ref
):
    values = x_ref[...].astype(F32)
    gain = gain_ref[...].reshape(1, D)
    inverse = rms_inverse(values)
    normed = (values * inverse * gain).astype(BF16)
    lowrank = zg_ref[: 3 * COLS]
    gates = zg_ref[3 * COLS :]
    mixed = pad_rows(lowrank * gates, LANES).astype(BF16)
    rows = pl.ds(pl.multiple_of(tile * ROWS, ROWS), ROWS)
    grads = [grads_ref[index, rows] for index in range(3)]
    columns = [slice(index * D, (index + 1) * D) for index in range(3)]
    grad_mixed = jnp.zeros((ROWS, LANES), F32)
    for grad, lanes in zip(grads, columns):
        grad_mixed = grad_mixed + dot_nt(grad, b_ref[:, lanes])
    grad_normed = jnp.zeros((ROWS, D), F32)
    for grad, lanes in zip(grads, columns):
        grad_normed = grad_normed + dot_nt(grad, w_ref[:, lanes])
        db_ref[:, lanes] += dot(mixed, grad)
    turned = grad_mixed.T
    parts = []
    for first in range(0, 3 * COLS, COLS):
        place = slice(first, first + COLS)
        parts.append(gate_grads(turned[place], lowrank[place], gates[place]))
    delta = jnp.concatenate([part[0] for part in parts] + [part[1] for part in parts], axis=0)
    delta = pad_rows(delta, 2 * LANES).astype(BF16)
    grad_normed = grad_normed + dot_nt(delta.T, ar_ref[...])
    dar_ref[...] += dot(delta, normed)
    out_ref[...] = dmid_ref[...] + rms_backward(values, gain, inverse, grad_normed)


def back_kernel(*refs):
    length_ref = refs[0]
    heads_refs = refs[:9]
    x_ref, gain_ref, w_hbm, ar_ref, b_ref, zg_ref, dmid_ref = refs[9:16]
    out_ref, dar_ref, db_ref = refs[16:19]
    table, key_more, weights_all, grads_all, grads_ref, w_ref, loaded = refs[19:]
    step = pl.program_id(0)
    pairs = HEADS // 2
    load = pltpu.make_async_copy(w_hbm, w_ref, loaded)

    @pl.when(step == 0)
    def _():
        load.start()
        dar_ref[...] = jnp.zeros_like(dar_ref)
        db_ref[...] = jnp.zeros_like(db_ref)
        for odd in range(2):
            key_more[odd] = key_extras(length_ref, key_more.shape[1:], odd)

    @pl.when(step < pairs)
    def _():
        attend_back(step, *heads_refs, grads_ref, table, key_more, weights_all, grads_all)

    @pl.when(step == pairs)
    def _():
        load.wait()

    @pl.when(step >= pairs)
    def _():
        project_back(
            step - pairs,
            x_ref,
            gain_ref,
            w_ref,
            ar_ref,
            b_ref,
            zg_ref,
            grads_ref,
            dmid_ref,
            out_ref,
            dar_ref,
            db_ref,
        )


def back_part(
    length_valid, offsets, qt, k, kt, v, ot, gt, lse, x, gain, w_qkv, ar_qkv, b_qkv, zg, dmid
):
    length = k.shape[0]
    pairs = HEADS // 2

    def pair_of(i):
        return jnp.minimum(i, pairs - 1)

    def tile_of(i):
        return jnp.maximum(i - pairs, 0)

    turned = pl.BlockSpec((LANES, length), lambda i: (pair_of(i), 0))
    natural = pl.BlockSpec((length, LANES), lambda i: (0, pair_of(i)))
    tile = pl.BlockSpec((ROWS, D), lambda i: (tile_of(i), 0))
    out_shape = [
        jax.ShapeDtypeStruct((length, D), F32),
        jax.ShapeDtypeStruct((2 * LANES, D), F32),
        jax.ShapeDtypeStruct((LANES, 3 * D), F32),
    ]
    return pl.pallas_call(
        back_kernel,
        grid=(pairs + length // ROWS,),
        in_specs=[
            pl.BlockSpec(memory_space=pltpu.SMEM),
            whole(offsets.shape),
            turned,
            natural,
            turned,
            natural,
            turned,
            turned,
            pl.BlockSpec((1, 2, length), lambda i: (pair_of(i), 0, 0)),
            tile,
            whole((D,)),
            pl.BlockSpec(memory_space=pl.ANY),
            whole(ar_qkv.shape),
            whole(b_qkv.shape),
            pl.BlockSpec((6 * COLS, ROWS), lambda i: (0, tile_of(i))),
            tile,
        ],
        out_specs=[tile] + [whole(member.shape) for member in out_shape[1:]],
        out_shape=out_shape,
        scratch_shapes=[
            pltpu.VMEM((2, LANES, 2 * length), F32),
            pltpu.VMEM((2, length, LANES), BF16),
            pltpu.VMEM((length, length), BF16),
            pltpu.VMEM((length, length), BF16),
            pltpu.VMEM((3, length, D), BF16),
            pltpu.VMEM(w_qkv.shape, BF16),
            pltpu.SemaphoreType.DMA,
        ],
        compiler_params=params(),
        name="back_part",
    )(length_valid, offsets, qt, k, kt, v, ot, gt, lse, x, gain, w_qkv, ar_qkv, b_qkv, zg, dmid)


PARAM_ROWS = sum((COLS + EXPERTS) * fan_in + COLS * fan_out for fan_in, fan_out in FANS) // LANES


def piece_rows():
    result = []
    row = 0
    for fan_in, fan_out in FANS:
        starts = []
        for count in (fan_in * COLS, COLS * fan_out, fan_in * EXPERTS):
            starts.append(row)
            row += count // LANES
        result.append(tuple(starts))
    return result


def shard_rows(count):
    return -(-count // (LANES * 16)) * 16


def align_in(flat_ref, shard, start):
    first, shift = divmod(start, LANES)
    rows = shard.shape[0]
    if shift == 0:
        flat_ref[first : first + rows] = shard
        return
    turned = pltpu.roll(shard, shift, 1)
    lane = lane_iota((1, LANES))
    zeros = jnp.zeros((8, LANES), F32)
    upper = jnp.concatenate([turned, zeros], axis=0)
    lower = pltpu.roll(upper, 1, 0)
    kept = flat_ref[first : first + 8]
    merged = jnp.where(lane >= shift, upper, lower)
    inside = (row_iota((8, LANES)) == 0) & (lane_iota((8, LANES)) < shift)
    flat_ref[first : first + 8] = jnp.where(inside, kept, merged[:8])
    flat_ref[first + 8 : first + 8 + rows] = merged[8:]


def align_out(flat_ref, rows, start):
    first, shift = divmod(start, LANES)
    if shift == 0:
        return flat_ref[first : first + rows]
    block = flat_ref[first : first + rows + 8]
    turned = pltpu.roll(block, LANES - shift, 1)
    below = pltpu.roll(turned, rows + 7, 0)
    lane = lane_iota((1, LANES))
    return jnp.where(lane < LANES - shift, turned, below)[:rows]


GROUP = 64


def narrow_to_rows(flat_ref, fan_in, items, out_ref):
    groups = fan_in // GROUP
    lane = lane_iota((1, LANES))
    lines = [
        [
            flat_ref[pl.ds(base + k, groups, stride=width * GROUP // LANES), :]
            for k in range(width * GROUP // LANES)
        ]
        for base, width, _ in items
    ]
    for b in range(GROUP):
        result = jnp.zeros((groups, LANES), F32)
        for line, (_, width, place) in zip(lines, items):
            first, shift = divmod(width * b, LANES)
            amount = (place - shift) % LANES
            value = line[first] if amount == 0 else pltpu.roll(line[first], amount, 1)
            if shift + width > LANES:
                value = jnp.where(
                    lane < place + LANES - shift, value, pltpu.roll(line[first + 1], amount, 1)
                )
            inside = (lane >= place) & (lane < place + width)
            result = jnp.where(inside, value, result)
        out_ref[pl.ds(b, groups, stride=GROUP), :] = result


def rows_to_narrow(in_ref, fan_in, items, flat_ref):
    groups = fan_in // GROUP
    lane = lane_iota((1, LANES))
    lines = [
        [jnp.zeros((groups, LANES), F32) for _ in range(width * GROUP // LANES)]
        for _, width, _ in items
    ]
    for b in range(GROUP):
        source = in_ref[pl.ds(b, groups, stride=GROUP), :]
        for line, (_, width, place) in zip(lines, items):
            first, shift = divmod(width * b, LANES)
            amount = (shift - place) % LANES
            value = source if amount == 0 else pltpu.roll(source, amount, 1)
            inside = (lane >= shift) & (lane < shift + width)
            line[first] = jnp.where(inside, value, line[first])
            if shift + width > LANES:
                line[first + 1] = jnp.where(lane < shift + width - LANES, value, line[first + 1])
    for line, (base, width, _) in zip(lines, items):
        for k, value in enumerate(line):
            flat_ref[pl.ds(base + k, groups, stride=width * GROUP // LANES), :] = value


def spread_matrix(experts, source, place):
    row = row_iota((LANES, LANES)) - source
    lane = lane_iota((LANES, LANES)) - place
    hit = (lane >= RANK * row) & (lane < RANK * row + RANK) & (row >= 0) & (row < experts)
    return jnp.where(hit, 1.0, 0.0)


def keep_matrix():
    row = row_iota((LANES, LANES))
    return jnp.where((row == lane_iota((LANES, LANES))) & (row < COLS), 1.0, 0.0)


FIRST_COUNT = sum((COLS + EXPERTS) * fan_in + COLS * fan_out for fan_in, fan_out in FANS[:3])


def unpack_ups(flat, base, fan_out, first, out_ref, column):
    width = fan_out // LANES
    above = jnp.zeros((first, LANES), F32)
    below = jnp.zeros((LANES - COLS - first, LANES), F32)
    for k in range(width):
        part = flat[pl.ds(base + k, COLS, stride=width), :]
        parts = [part, below] if first == 0 else [above, part, below]
        lanes = slice(column + k * LANES, column + (k + 1) * LANES)
        out_ref[:, lanes] = jnp.concatenate(parts, axis=0).astype(BF16)


def unpack_first(flat, ar_ref, b_ref, down, router):
    starts = piece_rows()
    narrow_to_rows(flat, D, [(starts[k][0], COLS, k * COLS) for k in range(3)], down)
    narrow_to_rows(flat, D, [(starts[k][2], EXPERTS, k * EXPERTS) for k in range(3)], router)
    routers = router[...].astype(BF16)
    for half in range(2):
        matrix = spread_matrix(3 * EXPERTS, 0, 3 * COLS - half * LANES).astype(BF16)
        packed = dot(routers, matrix)
        packed = packed if half else packed + down[...]
        ar_ref[:, half * LANES : (half + 1) * LANES] = packed.astype(BF16)
    for index in range(3):
        unpack_ups(flat, starts[index][1], D, index * COLS, b_ref, index * D)


def flat_rows(count):
    return PARAM_ROWS + shard_rows(count) + 20


def unpack_rest(flat, outs, work):
    starts = piece_rows()
    matrix = (keep_matrix() + spread_matrix(EXPERTS, COLS, COLS)).astype(BF16)
    for index in range(3, 6):
        base_a, base_b, base_r = starts[index]
        fan_in, fan_out = FANS[index]
        ar_ref, b_ref = outs[2 * index - 6], outs[2 * index - 5]
        narrow_to_rows(flat, fan_in, [(base_a, COLS, 0), (base_r, EXPERTS, COLS)], work)
        ar_ref[...] = dot(work[:fan_in].astype(BF16), matrix).astype(BF16)
        unpack_ups(flat, base_b, fan_out, 0, b_ref, 0)


def split_dot(value, matrix):
    high = value.astype(BF16)
    return dot(high, matrix) + dot((value - high.astype(F32)).astype(BF16), matrix)


def first_of_four(experts, source, place):
    row = row_iota((LANES, LANES)) - source
    lane = lane_iota((LANES, LANES)) - place
    hit = (row == RANK * lane) & (lane >= 0) & (lane < experts)
    return jnp.where(hit, 1.0, 0.0)


def assemble_ups(flat, base, fan_out, first, grad_ref, column):
    width = fan_out // LANES
    for k in range(width):
        lanes = slice(column + k * LANES, column + (k + 1) * LANES)
        flat[pl.ds(base + k, COLS, stride=width), :] = grad_ref[first : first + COLS, lanes]


def assemble_rest(flat, grads, work):
    starts = piece_rows()
    matrix = (keep_matrix() + first_of_four(EXPERTS, COLS, COLS)).astype(BF16)
    for index in range(3, 6):
        base_a, base_b, base_r = starts[index]
        fan_in, fan_out = FANS[index]
        dar_ref, db_ref = grads[2 * index - 6], grads[2 * index - 5]
        work[:fan_in] = split_dot(pad_rows(dar_ref[...], LANES).T, matrix)
        rows_to_narrow(work, fan_in, [(base_a, COLS, 0), (base_r, EXPERTS, COLS)], flat)
        assemble_ups(flat, base_b, fan_out, 0, db_ref, 0)


def assemble_first(flat, dar_ref, db_ref, down, router):
    starts = piece_rows()
    down[...] = dar_ref[:LANES].T
    rows_to_narrow(down, D, [(starts[k][0], COLS, k * COLS) for k in range(3)], flat)
    first_router = 3 * COLS
    turned = dar_ref[first_router : first_router + LANES].T
    router[...] = split_dot(turned, first_of_four(3 * EXPERTS, 0, 0).astype(BF16))
    rows_to_narrow(router, D, [(starts[k][2], EXPERTS, k * EXPERTS) for k in range(3)], flat)
    for index in range(3):
        assemble_ups(flat, starts[index][1], D, index * COLS, db_ref, index * D)


MESH = pl.DeviceIdType.MESH


def place_of(axes, sizes):
    me = lax.axis_index(axes[0]) * sizes[1] + lax.axis_index(axes[1])

    def coordinates(number):
        return (number // sizes[1], number % sizes[1])

    return me, coordinates


def partners_of(me):
    low = me % 8
    core = low % 2
    y = (low // 2) % 2
    x = low // 4
    over_x = low + 4 * (1 - 2 * x)
    over_y = low + 2 * (1 - 2 * y)
    first = over_x * (1 - core) + over_y * core
    second = over_y * (1 - core) + over_x * core
    both = first + second - low
    other = 1 - 2 * core
    return low, first, second, both, other, over_x, over_y


def greet(peers):
    barrier = pltpu.get_barrier_semaphore()
    for peer in peers:
        pl.semaphore_signal(barrier, inc=1, device_id=peer, device_id_type=MESH)
    pl.semaphore_wait(barrier, len(peers))


class Ring:
    def __init__(self, axes, sizes, send, receive):
        self.me, self.coordinates = place_of(axes, sizes)
        self.groups = sizes[0] * sizes[1] // 8
        self.group = self.me // 8
        places = partners_of(self.me)
        self.low, self.first, self.second, self.both, self.other, self.over_x, self.over_y = places
        self.mate = self.low + self.other
        self.send, self.receive = send, receive
        self.copies = {}

    def device(self, group, low):
        return self.coordinates(group * 8 + low)

    def greet(self):
        peers = [
            self.device((self.group + step) % self.groups, self.low)
            for step in range(1, self.groups)
        ]
        peers += [self.device(self.group, low) for low in (self.first, self.second, self.mate)]
        greet(peers)

    def copy(self, slot, source, target, peer, arrival=None):
        return pltpu.make_async_remote_copy(
            src_ref=source,
            dst_ref=target,
            send_sem=self.send.at[slot],
            recv_sem=self.receive.at[slot if arrival is None else arrival],
            device_id=peer,
            device_id_type=MESH,
        )


def gather_phases(ring, span, shard_ref, out_ref, local, greets):
    begin, end = span
    base = ring.groups
    inside = (ring.group >= begin) & (ring.group < end)

    def around(step):
        target = (ring.group + step) % ring.groups
        return ring.copy(
            step,
            shard_ref,
            out_ref.at[ring.group - begin, ring.low],
            ring.device(target, ring.low),
            base + 7 + ring.group,
        )

    def arrived(group):
        return ring.copy(
            0,
            shard_ref,
            out_ref.at[group - begin, ring.low],
            ring.device(group, ring.low),
            base + 7 + group,
        )

    def push(slot, part, partner):
        return ring.copy(
            base + slot, out_ref.at[:, part], out_ref.at[:, part], ring.device(ring.group, partner)
        )

    one = push(0, ring.low, ring.first)
    two = push(1, ring.low, ring.second)
    three = push(2, ring.first, ring.second)
    cores = [
        push(3 + index, part, ring.mate)
        for index, part in enumerate((ring.low, ring.first, ring.second, ring.both))
    ]

    def own():
        return pltpu.make_async_copy(
            shard_ref, out_ref.at[ring.group - begin, ring.low], local
        )

    def phase0():
        if greets:
            ring.greet()

        @pl.when(inside)
        def _():
            own().start()
            for step in range(1, ring.groups):
                around(step).start()

    def phase1():
        @pl.when(inside)
        def _():
            own().wait()
            for step in range(1, ring.groups):
                around(step).wait_send()

        for group in range(begin, end):

            @pl.when(ring.group != group)
            def _():
                arrived(group).wait_recv()

        for copy in (one, two, cores[0]):
            copy.start()

    def phase2():
        one.wait()
        three.start()
        cores[1].start()

    def phase3():
        two.wait()
        cores[2].start()
        three.wait()
        cores[3].start()

    def phase4():
        for copy in cores:
            copy.wait()

    return phase0, phase1, phase2, phase3, phase4


def gather_semaphores(groups):
    return [
        pltpu.SemaphoreType.DMA((groups + 7,)),
        pltpu.SemaphoreType.DMA((2 * groups + 7,)),
        pltpu.SemaphoreType.DMA,
    ]


def start_kernel(
    link,
    count,
    shard_ref,
    buckets_ref,
    table_ref,
    gain_ref,
    x_hbm,
    w_hbm,
    *refs,
):
    hbm_outs, off_ref, ar_ref, b_ref = refs[:6], refs[6], refs[7], refs[8]
    rest_refs = refs[9:15]
    x_ref, w_ref, normed, dense = refs[15:19]
    outs = refs[19:25]
    qt_ref, k_ref, kt_ref, v_ref, vt_ref, zg_ref = outs
    flat, down, router, work, loaded, stored, *more = refs[25:]
    loads = [
        pltpu.make_async_copy(x_hbm, x_ref, loaded.at[0]),
        pltpu.make_async_copy(w_hbm, w_ref, loaded.at[1]),
    ]
    stores = [
        pltpu.make_async_copy(source, target, stored.at[index])
        for index, (source, target) in enumerate(zip(outs, hbm_outs))
    ]
    for load in loads:
        load.start()
    if link is None:
        first = [lambda: None] * 5
        rest = first

        def shard_of(index):
            return shard_ref[...]
    else:
        axes, sizes, spans = link
        land_a, land_b, *sems = more
        first = gather_phases(
            Ring(axes, sizes, *sems[:2]), spans[0], shard_ref, land_a, sems[2], True
        )
        rest = gather_phases(
            Ring(axes, sizes, *sems[3:5]), spans[1], shard_ref, land_b, sems[5], False
        )

        def shard_of(index):
            group, low = divmod(index, 8)
            begin = spans[1][0]
            return land_a[group, low] if group < begin else land_b[group - begin, low]

    def rows_of(index):
        return pl.ds(pl.multiple_of(index * ROWS, ROWS), ROWS)

    def dense_tile(index, _):
        rows = rows_of(index)
        values = x_ref[rows].astype(F32)
        low = (values * rms_inverse(values) * gain_ref[...].reshape(1, D)).astype(BF16)
        normed[rows] = low
        dense[rows] = dot(low, w_ref[...])
        return 0

    def project_tile(index, _):
        rows = rows_of(index)
        packed = dot(normed[rows], ar_ref[...]).T
        lowrank = packed[: 3 * COLS]
        gates = jnp.concatenate(
            [gates_of(packed[place : place + COLS]) for place in range(3 * COLS, 6 * COLS, COLS)],
            axis=0,
        )
        zg_ref[: 3 * COLS, rows] = lowrank
        zg_ref[3 * COLS :, rows] = gates
        mixed = pad_rows(lowrank * gates, LANES).astype(BF16).T
        for part in range(3):
            columns = slice(part * D, (part + 1) * D)
            value = dense[rows, columns] + dot(mixed, b_ref[:, columns])
            if part == 0:
                qt_ref[:, rows] = (value * QUERY_SCALE).astype(BF16).T
            else:
                low = value.astype(BF16)
                natural, turned = ((k_ref, kt_ref), (v_ref, vt_ref))[part - 1]
                natural[rows] = low
                turned[:, rows] = low.T
        return 0

    tiles = x_ref.shape[0] // ROWS
    first[0]()
    rest[0]()
    for load in loads:
        load.wait()
    lax.fori_loop(0, tiles // 2, dense_tile, 0)
    first[1]()
    rest[1]()
    lax.fori_loop(tiles // 2, tiles, dense_tile, 0)
    buckets = buckets_ref[...]
    hits = jnp.where(row_iota((table_ref.shape[1], buckets.shape[1])) == buckets, LOG2E, 0.0)
    off_ref[...] = lax.dot_general(
        table_ref[...],
        hits,
        (((1,), (0,)), ((), ())),
        preferred_element_type=F32,
        precision=lax.Precision.HIGHEST,
    )
    for step in range(2, 5):
        first[step]()
        if step < 4:
            rest[step]()

    for index in range(-(-FIRST_COUNT // count)):
        align_in(flat, shard_of(index).astype(F32), index * count)
    unpack_first(flat, ar_ref, b_ref, down, router)
    lax.fori_loop(0, tiles, project_tile, 0)
    for store in stores:
        store.start()
    rest[4]()
    for index in range(FIRST_COUNT // count, PARAM_ROWS * LANES // count):
        align_in(flat, shard_of(index).astype(F32), index * count)
    unpack_rest(flat, rest_refs, work)
    for store in stores:
        store.wait()


def start(x, gain, w_qkv, shard, buckets, rel_table, count, axes, sizes, spans):
    length = x.shape[0]
    groups = sizes[0] * sizes[1] // 8
    link = (axes, sizes, spans) if groups else None
    rest_shapes = [
        shape for fan_in, fan_out in FANS[3:] for shape in ((fan_in, LANES), (LANES, fan_out))
    ]
    wide = [
        ((D, length), BF16),
        ((length, D), BF16),
        ((D, length), BF16),
        ((length, D), BF16),
        ((D, length), BF16),
        ((6 * COLS, length), F32),
    ]
    small = [
        ((HEADS, buckets.shape[1]), F32),
        ((D, 2 * LANES), BF16),
        ((LANES, 3 * D), BF16),
    ] + [(shape, BF16) for shape in rest_shapes]
    scratch = [
        pltpu.VMEM(x.shape, BF16),
        pltpu.VMEM(w_qkv.shape, BF16),
        pltpu.VMEM(x.shape, BF16),
        pltpu.VMEM((length, 3 * D), F32),
    ]
    scratch += [pltpu.VMEM(*member) for member in wide]
    scratch += [
        pltpu.VMEM((flat_rows(count), LANES), F32),
        pltpu.VMEM((D, LANES), F32),
        pltpu.VMEM((D, LANES), F32),
        pltpu.VMEM((FF, LANES), F32),
        pltpu.SemaphoreType.DMA((2,)),
        pltpu.SemaphoreType.DMA((len(wide),)),
    ]
    if link:
        scratch += [pltpu.VMEM((end - begin, 8, *shard.shape), BF16) for begin, end in spans]
        scratch += gather_semaphores(groups) * 2
    vmem = pl.BlockSpec(memory_space=pltpu.VMEM)
    anywhere = pl.BlockSpec(memory_space=pl.ANY)
    return pl.pallas_call(
        functools.partial(start_kernel, link, count),
        in_specs=[vmem] * 4 + [anywhere] * 2,
        out_specs=[anywhere] * len(wide) + [vmem] * len(small),
        out_shape=[jax.ShapeDtypeStruct(*member) for member in wide + small],
        scratch_shapes=scratch,
        compiler_params=params(collective_id=0, has_side_effects=True) if link else params(),
        name="start",
    )(shard, buckets, rel_table, gain, x, w_qkv)


def reduce_phases(ring, span, parts_ref, boxes, greets, sums_ref=None, sum_boxes=None):
    begin, end = span
    outbox, inbox, half, own, far_out, far_in, out_ref = boxes
    groups = ring.groups
    inside = (ring.group >= begin) & (ring.group < end)
    core_parts = (ring.first, ring.both, ring.second, ring.low)
    near = [ring.mate] * 4 + [ring.second, ring.second, ring.first]

    def push(slot):
        return ring.copy(slot, outbox.at[slot], inbox.at[slot], ring.device(ring.group, near[slot]))

    def fill(slot, value):
        outbox[slot] = value.astype(BF16)
        push(slot).start()

    def around(group):
        return ring.copy(
            7 + group - begin,
            far_out.at[group - begin],
            far_in.at[ring.group],
            ring.device(group, ring.low),
            7 + ring.group,
        )

    def arrived(group):
        return ring.copy(
            7,
            far_out.at[0],
            far_in.at[group],
            ring.device(group, ring.low),
            7 + group,
        )

    base = 7 + groups
    sum_peers = (ring.mate, ring.over_x, ring.over_y)

    def push_sums(slot):
        near_out, near_in = sum_boxes
        return ring.copy(
            base + slot,
            near_out.at[slot],
            near_in.at[slot],
            ring.device(ring.group, sum_peers[slot]),
        )

    def around_sums(step):
        near_out, near_in = sum_boxes
        target = (ring.group + step) % groups
        return ring.copy(
            base + 2 + step,
            near_out.at[3],
            near_in.at[3 + ring.group],
            ring.device(target, ring.low),
        )

    def start_sums(slot, value):
        if sum_boxes is not None:
            sum_boxes[0][slot] = value
            push_sums(slot).start()

    def phase0():
        if greets:
            ring.greet()
        if sum_boxes is not None:
            start_sums(0, sums_ref[...])
        for slot, part in enumerate(core_parts):
            fill(slot, parts_ref[:, part + ring.other])

    def phase1():
        push(0).wait()
        fill(4, parts_ref[:, ring.second] + inbox[0].astype(F32))
        push(1).wait()
        fill(5, parts_ref[:, ring.both] + inbox[1].astype(F32))
        if sum_boxes is not None:
            push_sums(0).wait()
            start_sums(1, sum_boxes[0][0] + sum_boxes[1][0])
        push(2).wait()
        half[...] = parts_ref[:, ring.first] + inbox[2].astype(F32)
        push(3).wait()
        own[...] = parts_ref[:, ring.low] + inbox[3].astype(F32)

    def phase2():
        push(5).wait()
        fill(6, half[...] + inbox[5].astype(F32))
        if sum_boxes is not None:
            push_sums(1).wait()
            start_sums(2, sum_boxes[0][1] + sum_boxes[1][1])
        push(4).wait()
        own[...] = own[...] + inbox[4].astype(F32)

    def phase3():
        push(6).wait()
        own[...] = own[...] + inbox[6].astype(F32)
        far_out[...] = own[...].astype(BF16)
        for group in range(begin, end):

            @pl.when(ring.group != group)
            def _():
                around(group).start()

        if sum_boxes is not None:
            near_out, near_in = sum_boxes
            push_sums(2).wait()
            near_out[3] = near_out[2] + near_in[2]
            for step in range(1, groups):
                around_sums(step).start()
            near_in[3 + ring.group] = near_out[3]

    def phase4(finish_sums=None):
        for group in range(begin, end):

            @pl.when(ring.group != group)
            def _():
                around(group).wait_send()

        @pl.when(inside)
        def _():
            for group in range(groups):

                @pl.when(ring.group != group)
                def _():
                    arrived(group).wait_recv()

            total = own[ring.group - begin]
            for step in range(1, groups):
                total = total + far_in[(ring.group + step) % groups].astype(F32)
            out_ref[...] = total

        if sum_boxes is not None:
            near_out, near_in = sum_boxes
            for step in range(1, groups):
                around_sums(step).wait()
            whole_sum = near_in[3]
            for index in range(1, groups):
                whole_sum = whole_sum + near_in[3 + index]
            finish_sums(whole_sum)

    return phase0, phase1, phase2, phase3, phase4


def reduce_scratch(groups, count, rows):
    return [
        pltpu.VMEM((7, count, rows, LANES), BF16),
        pltpu.VMEM((7, count, rows, LANES), BF16),
        pltpu.VMEM((count, rows, LANES), F32),
        pltpu.VMEM((count, rows, LANES), F32),
        pltpu.VMEM((count, rows, LANES), BF16),
        pltpu.VMEM((groups, rows, LANES), BF16),
    ]


def finish_kernel(link, count, dar_ref, db_ref, *refs):
    grads, sums_ref = refs[:6], refs[6]
    out_ref, roots_ref, flat, down, router, work, *more = refs[7:]

    def finish_sums(total):
        roots_ref[...] = jnp.sqrt(total / (total[:, 4:5] * D))

    assemble_rest(flat, grads, work)
    if link is None:
        assemble_first(flat, dar_ref, db_ref, down, router)
        out_ref[...] = align_out(flat, out_ref.shape[0], 0)
        finish_sums(sums_ref[...])
        return
    axes, sizes, spans = link
    parts_a, parts_b, near_out, near_in, *more = more
    boxes_a, boxes_b, sems = more[:7], more[7:14], more[14:]
    rows = out_ref.shape[0]
    split = spans[1][0]

    def align(parts, span):
        for group in range(*span):
            for low in range(8):
                parts[group - span[0], low] = align_out(flat, rows, (8 * group + low) * count)

    ring = Ring(axes, sizes, sems[0], sems[1])
    rest = reduce_phases(ring, spans[1], parts_b, boxes_b, True, sums_ref, (near_out, near_in))
    first = reduce_phases(
        Ring(axes, sizes, sems[2], sems[3]), spans[0], parts_a, boxes_a, False
    )
    align(parts_b, spans[1])
    rest[0]()
    assemble_first(flat, dar_ref, db_ref, down, router)
    align(parts_a, spans[0])
    first[0]()
    for step in range(1, 4):
        rest[step]()
        first[step]()
    rest[4](finish_sums)
    first[4]()

    @pl.when(ring.group < split)
    def _():
        out_ref[...] = boxes_a[6][...]

    @pl.when(ring.group >= split)
    def _():
        out_ref[...] = boxes_b[6][...]


def finish(dar, db, grads, sums, count, axes, sizes, spans):
    rows = shard_rows(count)
    groups = sizes[0] * sizes[1] // 8
    link = (axes, sizes, spans) if groups else None
    scratch = [
        pltpu.VMEM((flat_rows(count), LANES), F32),
        pltpu.VMEM((D, LANES), F32),
        pltpu.VMEM((D, LANES), F32),
        pltpu.VMEM((FF, LANES), F32),
    ]
    if link:
        widths = [end - begin for begin, end in spans]
        scratch += [pltpu.VMEM((width, 8, rows, LANES), F32) for width in widths]
        scratch += [
            pltpu.VMEM((4, *sums.shape), F32),
            pltpu.VMEM((3 + groups, *sums.shape), F32),
        ]
        for width in widths:
            scratch += reduce_scratch(groups, width, rows) + [pltpu.VMEM((rows, LANES), F32)]
        scratch += [pltpu.SemaphoreType.DMA((10 + 2 * groups,))] * 4
    vmem = pl.BlockSpec(memory_space=pltpu.VMEM)
    return pl.pallas_call(
        functools.partial(finish_kernel, link, count),
        in_specs=[vmem] * (3 + len(grads)),
        out_specs=[vmem] * 2,
        out_shape=[
            jax.ShapeDtypeStruct((rows, LANES), F32),
            jax.ShapeDtypeStruct(sums.shape, F32),
        ],
        scratch_shapes=scratch,
        compiler_params=params(collective_id=1, has_side_effects=True) if link else params(),
        name="finish",
    )(dar, db, *grads, sums)


def per_device(
    tokens,
    lengths,
    buckets,
    rel_table,
    gain_attn,
    gain_ff,
    w_qkv,
    w_out,
    w_in,
    w_down,
    adapters,
    cotangent,
    axes,
    sizes,
):
    seq_count, length, width = tokens.shape
    x = tokens.reshape(length, width)
    cot = cotangent.reshape(length, width)
    devices = sizes[0] * sizes[1]
    count = adapters.shape[0]
    rows = shard_rows(count)
    shard = jnp.pad(adapters, (0, rows * LANES - count)).reshape(rows, LANES)
    groups = devices // 8
    split_groups = min(-(-FIRST_COUNT // (8 * count)), max(groups - 1, 1))
    spans = ((0, split_groups), (split_groups, groups))
    reversed_buckets = jnp.pad(buckets[::-1], (0, 1)).reshape(1, 2 * length)
    qt, k, kt, v, vt, zg, offsets, ar_qkv, b_qkv, *packed = start(
        x, gain_attn, w_qkv, shard, reversed_buckets, rel_table.T, count, axes, sizes, spans
    )
    ot, lse = attend(lengths, offsets, qt, k, kt, vt)
    block_out, dmid, gt, sums, *grads = middle_part(
        lengths, ot, x, cot, gain_ff, w_out, w_in, w_down, packed
    )
    tokens_grad, dar_qkv, db_qkv = back_part(
        lengths,
        offsets,
        qt,
        k,
        kt,
        v,
        ot,
        gt,
        lse,
        x,
        gain_attn,
        w_qkv,
        ar_qkv,
        b_qkv,
        zg,
        dmid,
    )
    mine, roots = finish(dar_qkv, db_qkv, grads, sums, count, axes, sizes, spans)
    grad_shard = mine.reshape(-1)[:count]
    root_squares = roots[0, :4]
    return (
        block_out.reshape(tokens.shape),
        tokens_grad.reshape(tokens.shape),
        grad_shard,
        root_squares,
    )


def solution(mesh):
    axes = tuple(mesh.axis_names)
    sizes = tuple(mesh.shape[axis] for axis in axes)
    sequence = P(axes, None, None)
    placed = (
        sequence,
        P(axes),
        P(),
        P(),
        P(),
        P(),
        P(),
        P(),
        P(),
        P(),
        P(axes),
        sequence,
    )
    return jax.shard_map(
        functools.partial(per_device, axes=axes, sizes=sizes),
        mesh=mesh,
        in_specs=placed,
        out_specs=(sequence, sequence, P(axes), P()),
        check_vma=False,
    )
```

```python
import functools

import jax
import jax.numpy as jnp
from jax import lax
from jax.experimental import pallas as pl
from jax.experimental.pallas import tpu as pltpu
from jax.sharding import PartitionSpec as P

D = 768
FF = 3072
HEADS = 12
HDIM = 64
EXPERTS = 10
RANK = 4
FANS = ((D, D), (D, D), (D, D), (D, D), (D, FF), (FF, D))
COLS = EXPERTS * RANK
LANES = 128

EPSILON = 1e-06
MASKED = -1000000000.0
GELU_SCALE = 0.7978845608028654
GELU_CUBIC = 0.044715
LOG2E = 1.4426950408889634
LN2 = 0.6931471805599453
QUERY_SCALE = 0.125 * LOG2E

ROWS = 256
MIDDLE_ROWS = 512
CHUNK = 768
QBLOCK = 256
UP_ROWS = 48
DOWN_ROWS = 2 * COLS
VMEM_BYTES = 60 * 1024 * 1024

F32 = jnp.float32
BF16 = jnp.bfloat16


def dot(a, b):
    return lax.dot_general(a, b, (((1,), (0,)), ((), ())), preferred_element_type=F32)


def dot_nt(a, b):
    return lax.dot_general(a, b, (((1,), (1,)), ((), ())), preferred_element_type=F32)


def dot_tn(a, b):
    return lax.dot_general(a, b, (((0,), (0,)), ((), ())), preferred_element_type=F32)


def lane_iota(shape):
    return lax.broadcasted_iota(jnp.int32, shape, 1)


def row_iota(shape):
    return lax.broadcasted_iota(jnp.int32, shape, 0)


def gates_of(logits):
    weights = jnp.exp(logits - jnp.max(logits, axis=0, keepdims=True))
    return weights * (4.0 / jnp.sum(weights, axis=0, keepdims=True))


def gate_grads(grad_mixed, lowrank, gates):
    product = grad_mixed * lowrank
    summed = product
    for step in range(1, RANK):
        summed = summed + pltpu.roll(product, COLS - step, 0)
    centre = jnp.sum(gates * product, axis=0, keepdims=True)
    first = row_iota(gates.shape) % RANK == 0
    return grad_mixed * gates, jnp.where(first, gates * (summed - centre), 0.0)


def pad_rows(value, rows):
    return jnp.concatenate([value, jnp.zeros((rows - value.shape[0], value.shape[1]), F32)], axis=0)


def single_gates(packed):
    turned = packed.T
    lowrank = turned[:COLS]
    gates = gates_of(turned[COLS : 2 * COLS])
    mixed = pad_rows(lowrank * gates, LANES).astype(BF16)
    return lowrank, gates, mixed, mixed.T


def single_deltas(grad_mixed, lowrank, gates):
    parts = gate_grads(grad_mixed.T[:COLS], lowrank, gates)
    delta = pad_rows(jnp.concatenate(parts, axis=0), LANES).astype(BF16)
    return delta, delta.T


def rms_inverse(values):
    return lax.rsqrt(jnp.mean(values * values, axis=-1, keepdims=True) + EPSILON)


def rms_backward(values, gain, inverse, grad_normed):
    weighted = grad_normed * gain
    return inverse * weighted - values * (
        inverse * inverse * inverse * jnp.mean(values * weighted, axis=-1, keepdims=True)
    )


def params(**more):
    return pltpu.CompilerParams(vmem_limit_bytes=VMEM_BYTES, **more)


def whole(shape):
    zeros = (0,) * len(shape)
    return pl.BlockSpec(shape, lambda *_: zeros, pipeline_mode=pl.Buffered(1))


def bias_table(offset_row, length):
    spread = jnp.broadcast_to(offset_row, (LANES, 2 * length))
    return pltpu.roll(spread, 2 * length - (LANES - 1), 1, stride=1, stride_axis=0)


def add_bias(scores, table_ref, start, length):
    width = scores.shape[1]
    parts = []
    for block in range(length // LANES):
        offset = start - LANES * block + (length - LANES)
        parts.append(
            scores[block * LANES : (block + 1) * LANES] + table_ref[:, offset : offset + width]
        )
    return jnp.concatenate(parts, axis=0)


def key_extras(length_ref, shape, odd):
    lane = lane_iota(shape) - (0 if odd else HDIM)
    invalid = row_iota(shape) >= length_ref[0]
    extras = jnp.where((lane == 0) & invalid, MASKED, 0.0)
    return jnp.where((lane >= 1) & (lane <= 3), 1.0, extras).astype(BF16)


def head_lanes(odd):
    lane = lane_iota((1, LANES))
    return ((lane >= HDIM) if odd else (lane < HDIM)).astype(F32).astype(BF16)


def extra_rows(rows):
    width = rows[0].shape[1]
    index = row_iota((8, width))
    block = jnp.zeros((8, width), F32)
    for place, row in enumerate(rows):
        block = jnp.where(index == place, row, block)
    return jnp.concatenate([block, jnp.zeros((HDIM - 8, width), F32)], axis=0).astype(BF16)


def split_three(row):
    high = row.astype(BF16).astype(F32)
    middle = (row - high).astype(BF16).astype(F32)
    return high, middle, row - high - middle


def join_rows(rows, extras, odd):
    return jnp.concatenate([extras, rows] if odd else [rows, extras], axis=0)


def attend_kernel(
    length_ref, off_ref, qt_ref, k_ref, kt_ref, vt_ref, o_ref, lse_ref, table, key_more
):
    length = k_ref.shape[0]
    step = pl.program_id(0)

    @pl.when(step == 0)
    def _():
        for odd in range(2):
            key_more[odd] = key_extras(length_ref, k_ref.shape, odd)

    starts = range(0, length, QBLOCK)
    ones = jnp.ones((1, length), F32)

    def half_of(odd):
        return slice(odd * HDIM, (odd + 1) * HDIM)

    def keys_of(odd):
        return k_ref[...] * head_lanes(odd) + key_more[odd]

    def values_of(odd):
        return jnp.concatenate([vt_ref[half_of(odd), :], jnp.ones((16, length), BF16)], axis=0)

    def finish(odd, start, shift, weights):
        columns = slice(start, start + QBLOCK)
        summed = dot(values_of(odd), weights)
        total = summed[HDIM : HDIM + 1]
        o_ref[half_of(odd), columns] = (summed[:HDIM] / total).astype(BF16)
        lse_ref[0, odd : odd + 1, columns] = shift + jnp.log2(total)
        return total

    def bounded(odd):
        offsets = off_ref[pl.ds(2 * step + odd, 1), :]
        table[odd] = bias_table(offsets, length)
        squares = jnp.square(kt_ref[half_of(odd), :].astype(F32))
        sizes = jnp.sum(squares, axis=0, keepdims=True)
        sizes = jnp.where(lane_iota(sizes.shape) < length_ref[0], sizes, 0.0)
        largest = jnp.max(sizes, axis=1, keepdims=True)
        rows = qt_ref[half_of(odd), :].astype(F32)
        norms = jnp.sqrt(jnp.sum(rows * rows, axis=0, keepdims=True) * largest)
        bound = 1.001 * norms + jnp.max(offsets, axis=1, keepdims=True)
        queries = join_rows(
            qt_ref[half_of(odd), :],
            extra_rows([ones] + [-part for part in split_three(bound)]),
            odd,
        )
        keys = keys_of(odd)
        scores = [dot(keys, queries[:, start : start + QBLOCK]) for start in starts]
        weights = [
            jnp.exp2(add_bias(part, table.at[odd], start, length)).astype(BF16)
            for part, start in zip(scores, starts)
        ]
        least = None
        for start, part in zip(starts, weights):
            total = finish(odd, start, bound[:, start : start + QBLOCK], part)
            least = total if least is None else jnp.minimum(least, total)
        return least

    def exact(odd):
        queries = join_rows(qt_ref[half_of(odd), :], extra_rows([ones]), odd)
        keys = keys_of(odd)
        for start in starts:
            columns = slice(start, start + QBLOCK)
            scores = add_bias(dot(keys, queries[:, columns]), table.at[odd], start, length)
            peak = jnp.max(scores, axis=0, keepdims=True)
            finish(odd, start, peak, jnp.exp2(scores - peak).astype(BF16))

    least = jnp.minimum(bounded(0), bounded(1))

    @pl.when(jnp.logical_not(jnp.min(least) > 2.0**-100))
    def _():
        for odd in range(2):
            exact(odd)


def attend(length_valid, offsets, qt, k, kt, vt):
    length = k.shape[0]
    turned = pl.BlockSpec((LANES, length), lambda p: (p, 0))
    natural = pl.BlockSpec((length, LANES), lambda p: (0, p))
    return pl.pallas_call(
        attend_kernel,
        grid=(HEADS // 2,),
        in_specs=[
            pl.BlockSpec(memory_space=pltpu.SMEM),
            whole(offsets.shape),
            turned,
            natural,
            turned,
            turned,
        ],
        out_specs=[turned, pl.BlockSpec((1, 2, length), lambda p: (p, 0, 0))],
        out_shape=[
            jax.ShapeDtypeStruct((D, length), BF16),
            jax.ShapeDtypeStruct((HEADS // 2, 2, length), F32),
        ],
        scratch_shapes=[
            pltpu.VMEM((2, LANES, 2 * length), F32),
            pltpu.VMEM((2, length, LANES), BF16),
        ],
        compiler_params=params(),
        name="attend",
    )(length_valid, offsets, qt, k, kt, vt)


def middle_kernel(
    length_ref,
    ot_ref,
    x_ref,
    cot_ref,
    gain_ref,
    w_out_ref,
    w_in_hbm,
    w_down_hbm,
    ar_out_ref,
    b_out_ref,
    ar_in_ref,
    b_in_ref,
    ar_down_ref,
    b_down_ref,
    out_ref,
    dmid_ref,
    gt_ref,
    sums_ref,
    dar_out_ref,
    db_out_ref,
    dar_in_ref,
    db_in_ref,
    dar_down_ref,
    db_down_ref,
    active,
    slope,
    sloped,
    grad_hidden,
    feeds,
    w_in_ref,
    w_down_ref,
    loaded,
):
    step = pl.program_id(0)
    loads = [
        pltpu.make_async_copy(w_in_hbm, w_in_ref, loaded.at[0]),
        pltpu.make_async_copy(w_down_hbm, w_down_ref, loaded.at[1]),
    ]

    @pl.when(step == 0)
    def _():
        for load in loads:
            load.start()
        for ref in (
            sums_ref,
            dar_out_ref,
            db_out_ref,
            dar_in_ref,
            db_in_ref,
            dar_down_ref,
            db_down_ref,
        ):
            ref[...] = jnp.zeros_like(ref)

    attended = ot_ref[...].T
    inputs = x_ref[...].astype(F32)
    gain = gain_ref[...].reshape(1, D)
    cot = cot_ref[...]

    packed_out = dot(attended, ar_out_ref[...])
    branch = dot(attended, w_out_ref[...])
    low_out, gates_out, mixed_out, natural = single_gates(packed_out)
    grad_mixed_down = dot_nt(cot, b_down_ref[...])
    branch = branch + dot(natural, b_out_ref[...])
    middle = inputs + branch
    inverse = rms_inverse(middle)
    normed = (middle * inverse * gain).astype(BF16)

    packed_in = dot(normed, ar_in_ref[...])
    low_in, gates_in, mixed_in, natural = single_gates(packed_in)

    def columns_of(index):
        return pl.ds(pl.multiple_of(index * CHUNK, CHUNK), CHUNK)

    def hidden_of(chunk):
        return dot(normed, w_in_ref[:, chunk]) + dot(natural, b_in_ref[:, chunk])

    def activate(chunk, values):
        grad_dense = dot_nt(cot, w_down_ref[chunk])
        square = values * values
        tangent = jnp.tanh(values * (GELU_SCALE + (GELU_SCALE * GELU_CUBIC) * square))
        half = 0.5 + 0.5 * tangent
        smooth = values * half
        active[:, chunk] = smooth.astype(BF16)
        steep = half + smooth * (1.0 - tangent) * (
            GELU_SCALE + (3.0 * GELU_SCALE * GELU_CUBIC) * square
        )
        slope[:, chunk] = steep.astype(BF16)
        sloped[:, chunk] = grad_dense * steep

    def forward_pair(pair, _):
        chunk_a = columns_of(2 * pair)
        chunk_b = columns_of(2 * pair + 1)
        hidden_a = hidden_of(chunk_a)
        hidden_b = hidden_of(chunk_b)
        activate(chunk_a, hidden_a)
        activate(chunk_b, hidden_b)
        return 0

    @pl.when(step == 0)
    def _():
        for load in loads:
            load.wait()

    lax.fori_loop(0, FF // (2 * CHUNK), forward_pair, 0)

    packed_down = dot(active[...], ar_down_ref[...])
    for first in range(0, D, 256):
        part = slice(first, first + 256)
        feeds[:, part] = dot(active[...], w_down_ref[:, part])
    feed = feeds[...]
    low_down, gates_down, mixed_down, natural = single_gates(packed_down)
    delta_down, natural_delta = single_deltas(grad_mixed_down, low_down, gates_down)
    db_down_ref[...] += dot(mixed_down[:UP_ROWS], cot)
    feed = feed + dot(natural, b_down_ref[...])
    output = middle + feed
    out_ref[...] = output.astype(BF16)

    for first in range(0, FF, CHUNK):
        chunk = slice(first, first + CHUNK)
        grad_low = dot_nt(natural_delta, ar_down_ref[chunk])
        grad_hidden[:, chunk] = (
            sloped[:, chunk] + grad_low * slope[:, chunk].astype(F32)
        ).astype(BF16)

    rows = row_iota((MIDDLE_ROWS, 1)) + step * MIDDLE_ROWS
    valid = (rows < length_ref[0]).astype(F32)
    lane = lane_iota((8, LANES))
    totals = jnp.where((lane == 4) & (step == 0), length_ref[0].astype(F32), 0.0)
    for place, member in enumerate((inputs, branch, feed, output)):
        kept = member * valid
        totals = jnp.where(lane == place, jnp.sum(kept * kept), totals)
    sums_ref[...] += totals

    grad_mixed = dot_nt(grad_hidden[...], b_in_ref[...])
    for first in range(0, D, 256):
        part = slice(first, first + 256)
        feeds[:, part] = dot_nt(grad_hidden[...], w_in_ref[part])
    grad_normed = feeds[...]
    delta_in, natural_delta = single_deltas(grad_mixed, low_in, gates_in)
    grad_normed = grad_normed + dot_nt(natural_delta, ar_in_ref[...])
    dar_in_ref[...] += dot(delta_in[:DOWN_ROWS], normed)

    grad_middle = cot.astype(F32) + rms_backward(middle, gain, inverse, grad_normed)
    dmid_ref[...] = grad_middle
    grad_branch = grad_middle.astype(BF16)
    grad_mixed = dot_nt(grad_branch, b_out_ref[...])
    grad_attended = dot_nt(grad_branch, w_out_ref[...])
    dar_down_ref[...] += dot(delta_down[:DOWN_ROWS], active[...])
    db_in_ref[...] += dot(mixed_in[:UP_ROWS], grad_hidden[...])
    delta_out, natural_delta = single_deltas(grad_mixed, low_out, gates_out)
    grad_attended = grad_attended + dot_nt(natural_delta, ar_out_ref[...])
    gt_ref[...] = grad_attended.astype(BF16).T
    dar_out_ref[...] += dot(delta_out[:DOWN_ROWS], attended)
    db_out_ref[...] += dot(mixed_out[:UP_ROWS], grad_branch)


def middle_part(length_valid, ot, x, cot, gain, w_out, w_in, w_down, adapters):
    length = x.shape[0]
    tile = pl.BlockSpec((MIDDLE_ROWS, D), lambda i: (i, 0))
    turned = pl.BlockSpec((D, MIDDLE_ROWS), lambda i: (0, i))
    grad_shapes = [
        jax.ShapeDtypeStruct(shape, F32)
        for fan_in, fan_out in FANS[3:]
        for shape in ((DOWN_ROWS, fan_in), (UP_ROWS, fan_out))
    ]
    out_shape = [
        jax.ShapeDtypeStruct((length, D), BF16),
        jax.ShapeDtypeStruct((length, D), F32),
        jax.ShapeDtypeStruct((D, length), BF16),
        jax.ShapeDtypeStruct((8, LANES), F32),
    ] + grad_shapes
    return pl.pallas_call(
        middle_kernel,
        grid=(length // MIDDLE_ROWS,),
        in_specs=[pl.BlockSpec(memory_space=pltpu.SMEM), turned, tile, tile]
        + [whole(gain.shape), whole(w_out.shape)]
        + [pl.BlockSpec(memory_space=pl.ANY)] * 2
        + [whole(member.shape) for member in adapters],
        out_specs=[tile, tile, turned] + [whole(member.shape) for member in out_shape[3:]],
        out_shape=out_shape,
        scratch_shapes=[
            pltpu.VMEM((MIDDLE_ROWS, FF), BF16),
            pltpu.VMEM((MIDDLE_ROWS, FF), BF16),
            pltpu.VMEM((MIDDLE_ROWS, FF), F32),
            pltpu.VMEM((MIDDLE_ROWS, FF), BF16),
            pltpu.VMEM((MIDDLE_ROWS, D), F32),
            pltpu.VMEM(w_in.shape, BF16),
            pltpu.VMEM(w_down.shape, BF16),
            pltpu.SemaphoreType.DMA((2,)),
        ],
        compiler_params=params(),
        name="middle_part",
    )(length_valid, ot, x, cot, gain, w_out, w_in, w_down, *adapters)


def attend_back(
    pair,
    length_ref,
    off_ref,
    qt_ref,
    k_ref,
    kt_ref,
    v_ref,
    ot_ref,
    gt_ref,
    lse_ref,
    grads_ref,
    table,
    key_more,
    weights_all,
    grads_all,
):
    length = k_ref.shape[0]
    lane = lane_iota((1, LANES))
    first_lanes = lane < HDIM
    grad_query_parts = []
    for odd in range(2):
        half = slice(odd * HDIM, (odd + 1) * HDIM)
        table[odd] = bias_table(off_ref[pl.ds(2 * pair + odd, 1), :], length)
        keys = k_ref[...] * head_lanes(odd) + key_more[odd]
        place = lane - (0 if odd else HDIM)
        value_more = ((place >= 0) & (place < 3)).astype(F32).astype(BF16)
        values = v_ref[...] * head_lanes(odd) + value_more
        ones = jnp.ones((1, length), F32)
        lse = lse_ref[0, odd : odd + 1, :]
        queries = join_rows(
            qt_ref[half, :], extra_rows([ones] + [-part for part in split_three(lse)]), odd
        )
        delta = jnp.sum(
            ot_ref[half, :].astype(F32) * gt_ref[half, :].astype(F32), axis=0, keepdims=True
        )
        grads = join_rows(
            gt_ref[half, :], extra_rows([-part for part in split_three(delta)]), odd
        )
        for start in range(0, length, QBLOCK):
            columns = slice(start, start + QBLOCK)
            scores = add_bias(dot(keys, queries[:, columns]), table.at[odd], start, length)
            weights = jnp.exp2(scores)
            weights_all[:, columns] = weights.astype(BF16)
            grad_scores = weights * dot(values, grads[:, columns])
            grads_all[:, columns] = grad_scores.astype(BF16)
        grad_query_parts.append(dot(kt_ref[half, :], grads_all[...]) * 0.125)
        grad_values = dot_nt(weights_all[...], gt_ref[...])
        grad_keys = dot_nt(grads_all[...], qt_ref[...]) * LN2
        if odd:
            grad_values = jnp.where(first_lanes, even_values, grad_values)
            grad_keys = jnp.where(first_lanes, even_keys, grad_keys)
        else:
            even_values, even_keys = grad_values, grad_keys
    columns = pl.ds(pl.multiple_of(pair * LANES, LANES), LANES)
    grads_ref[0, :, columns] = jnp.concatenate(grad_query_parts, axis=0).T.astype(BF16)
    grads_ref[1, :, columns] = grad_keys.astype(BF16)
    grads_ref[2, :, columns] = grad_values.astype(BF16)


def project_back(
    tile, x_ref, gain_ref, w_ref, ar_ref, b_ref, zg_ref, grads_ref, dmid_ref, out_ref, dar_ref, db_ref
):
    values = x_ref[...].astype(F32)
    gain = gain_ref[...].reshape(1, D)
    inverse = rms_inverse(values)
    normed = (values * inverse * gain).astype(BF16)
    lowrank = zg_ref[: 3 * COLS]
    gates = zg_ref[3 * COLS :]
    mixed = pad_rows(lowrank * gates, LANES).astype(BF16)
    rows = pl.ds(pl.multiple_of(tile * ROWS, ROWS), ROWS)
    grads = [grads_ref[index, rows] for index in range(3)]
    columns = [slice(index * D, (index + 1) * D) for index in range(3)]
    grad_mixed = jnp.zeros((ROWS, LANES), F32)
    for grad, lanes in zip(grads, columns):
        grad_mixed = grad_mixed + dot_nt(grad, b_ref[:, lanes])
    grad_normed = jnp.zeros((ROWS, D), F32)
    for grad, lanes in zip(grads, columns):
        grad_normed = grad_normed + dot_nt(grad, w_ref[:, lanes])
        db_ref[:, lanes] += dot(mixed, grad)
    turned = grad_mixed.T
    parts = []
    for first in range(0, 3 * COLS, COLS):
        place = slice(first, first + COLS)
        parts.append(gate_grads(turned[place], lowrank[place], gates[place]))
    delta = jnp.concatenate([part[0] for part in parts] + [part[1] for part in parts], axis=0)
    delta = pad_rows(delta, 2 * LANES).astype(BF16)
    grad_normed = grad_normed + dot_nt(delta.T, ar_ref[...])
    dar_ref[...] += dot(delta, normed)
    out_ref[...] = dmid_ref[...] + rms_backward(values, gain, inverse, grad_normed)


def back_kernel(*refs):
    length_ref = refs[0]
    heads_refs = refs[:9]
    x_ref, gain_ref, w_hbm, ar_ref, b_ref, zg_ref, dmid_ref = refs[9:16]
    out_ref, dar_ref, db_ref = refs[16:19]
    table, key_more, weights_all, grads_all, grads_ref, w_ref, loaded = refs[19:]
    step = pl.program_id(0)
    pairs = HEADS // 2
    load = pltpu.make_async_copy(w_hbm, w_ref, loaded)

    @pl.when(step == 0)
    def _():
        load.start()
        dar_ref[...] = jnp.zeros_like(dar_ref)
        db_ref[...] = jnp.zeros_like(db_ref)
        for odd in range(2):
            key_more[odd] = key_extras(length_ref, key_more.shape[1:], odd)

    @pl.when(step < pairs)
    def _():
        attend_back(step, *heads_refs, grads_ref, table, key_more, weights_all, grads_all)

    @pl.when(step == pairs)
    def _():
        load.wait()

    @pl.when(step >= pairs)
    def _():
        project_back(
            step - pairs,
            x_ref,
            gain_ref,
            w_ref,
            ar_ref,
            b_ref,
            zg_ref,
            grads_ref,
            dmid_ref,
            out_ref,
            dar_ref,
            db_ref,
        )


def back_part(
    length_valid, offsets, qt, k, kt, v, ot, gt, lse, x, gain, w_qkv, ar_qkv, b_qkv, zg, dmid
):
    length = k.shape[0]
    pairs = HEADS // 2

    def pair_of(i):
        return jnp.minimum(i, pairs - 1)

    def tile_of(i):
        return jnp.maximum(i - pairs, 0)

    turned = pl.BlockSpec((LANES, length), lambda i: (pair_of(i), 0))
    natural = pl.BlockSpec((length, LANES), lambda i: (0, pair_of(i)))
    tile = pl.BlockSpec((ROWS, D), lambda i: (tile_of(i), 0))
    out_shape = [
        jax.ShapeDtypeStruct((length, D), F32),
        jax.ShapeDtypeStruct((2 * LANES, D), F32),
        jax.ShapeDtypeStruct((LANES, 3 * D), F32),
    ]
    return pl.pallas_call(
        back_kernel,
        grid=(pairs + length // ROWS,),
        in_specs=[
            pl.BlockSpec(memory_space=pltpu.SMEM),
            whole(offsets.shape),
            turned,
            natural,
            turned,
            natural,
            turned,
            turned,
            pl.BlockSpec((1, 2, length), lambda i: (pair_of(i), 0, 0)),
            tile,
            whole((D,)),
            pl.BlockSpec(memory_space=pl.ANY),
            whole(ar_qkv.shape),
            whole(b_qkv.shape),
            pl.BlockSpec((6 * COLS, ROWS), lambda i: (0, tile_of(i))),
            tile,
        ],
        out_specs=[tile] + [whole(member.shape) for member in out_shape[1:]],
        out_shape=out_shape,
        scratch_shapes=[
            pltpu.VMEM((2, LANES, 2 * length), F32),
            pltpu.VMEM((2, length, LANES), BF16),
            pltpu.VMEM((length, length), BF16),
            pltpu.VMEM((length, length), BF16),
            pltpu.VMEM((3, length, D), BF16),
            pltpu.VMEM(w_qkv.shape, BF16),
            pltpu.SemaphoreType.DMA,
        ],
        compiler_params=params(),
        name="back_part",
    )(length_valid, offsets, qt, k, kt, v, ot, gt, lse, x, gain, w_qkv, ar_qkv, b_qkv, zg, dmid)


PARAM_ROWS = sum((COLS + EXPERTS) * fan_in + COLS * fan_out for fan_in, fan_out in FANS) // LANES


def piece_rows():
    result = []
    row = 0
    for fan_in, fan_out in FANS:
        starts = []
        for count in (fan_in * COLS, COLS * fan_out, fan_in * EXPERTS):
            starts.append(row)
            row += count // LANES
        result.append(tuple(starts))
    return result


def shard_rows(count):
    return -(-count // (LANES * 16)) * 16


def align_in(flat_ref, shard, start):
    first, shift = divmod(start, LANES)
    rows = shard.shape[0]
    if shift == 0:
        flat_ref[first : first + rows] = shard
        return
    turned = pltpu.roll(shard, shift, 1)
    lane = lane_iota((1, LANES))
    zeros = jnp.zeros((8, LANES), F32)
    upper = jnp.concatenate([turned, zeros], axis=0)
    lower = pltpu.roll(upper, 1, 0)
    kept = flat_ref[first : first + 8]
    merged = jnp.where(lane >= shift, upper, lower)
    inside = (row_iota((8, LANES)) == 0) & (lane_iota((8, LANES)) < shift)
    flat_ref[first : first + 8] = jnp.where(inside, kept, merged[:8])
    flat_ref[first + 8 : first + 8 + rows] = merged[8:]


def align_out(flat_ref, rows, start):
    first, shift = divmod(start, LANES)
    if shift == 0:
        return flat_ref[first : first + rows]
    block = flat_ref[first : first + rows + 8]
    turned = pltpu.roll(block, LANES - shift, 1)
    below = pltpu.roll(turned, rows + 7, 0)
    lane = lane_iota((1, LANES))
    return jnp.where(lane < LANES - shift, turned, below)[:rows]


GROUP = 64


def narrow_to_rows(flat_ref, fan_in, items, out_ref):
    groups = fan_in // GROUP
    lane = lane_iota((1, LANES))
    lines = [
        [
            flat_ref[pl.ds(base + k, groups, stride=width * GROUP // LANES), :]
            for k in range(width * GROUP // LANES)
        ]
        for base, width, _ in items
    ]
    for b in range(GROUP):
        result = jnp.zeros((groups, LANES), F32)
        for line, (_, width, place) in zip(lines, items):
            first, shift = divmod(width * b, LANES)
            amount = (place - shift) % LANES
            value = line[first] if amount == 0 else pltpu.roll(line[first], amount, 1)
            if shift + width > LANES:
                value = jnp.where(
                    lane < place + LANES - shift, value, pltpu.roll(line[first + 1], amount, 1)
                )
            inside = (lane >= place) & (lane < place + width)
            result = jnp.where(inside, value, result)
        out_ref[pl.ds(b, groups, stride=GROUP), :] = result


def rows_to_narrow(in_ref, fan_in, items, flat_ref):
    groups = fan_in // GROUP
    lane = lane_iota((1, LANES))
    lines = [
        [jnp.zeros((groups, LANES), F32) for _ in range(width * GROUP // LANES)]
        for _, width, _ in items
    ]
    for b in range(GROUP):
        source = in_ref[pl.ds(b, groups, stride=GROUP), :]
        for line, (_, width, place) in zip(lines, items):
            first, shift = divmod(width * b, LANES)
            amount = (shift - place) % LANES
            value = source if amount == 0 else pltpu.roll(source, amount, 1)
            inside = (lane >= shift) & (lane < shift + width)
            line[first] = jnp.where(inside, value, line[first])
            if shift + width > LANES:
                line[first + 1] = jnp.where(lane < shift + width - LANES, value, line[first + 1])
    for line, (base, width, _) in zip(lines, items):
        for k, value in enumerate(line):
            flat_ref[pl.ds(base + k, groups, stride=width * GROUP // LANES), :] = value


def spread_matrix(experts, source, place):
    row = row_iota((LANES, LANES)) - source
    lane = lane_iota((LANES, LANES)) - place
    hit = (lane >= RANK * row) & (lane < RANK * row + RANK) & (row >= 0) & (row < experts)
    return jnp.where(hit, 1.0, 0.0)


def keep_matrix():
    row = row_iota((LANES, LANES))
    return jnp.where((row == lane_iota((LANES, LANES))) & (row < COLS), 1.0, 0.0)


FIRST_COUNT = sum((COLS + EXPERTS) * fan_in + COLS * fan_out for fan_in, fan_out in FANS[:3])


def unpack_ups(flat, base, fan_out, first, out_ref, column):
    width = fan_out // LANES
    above = jnp.zeros((first, LANES), F32)
    below = jnp.zeros((LANES - COLS - first, LANES), F32)
    for k in range(width):
        part = flat[pl.ds(base + k, COLS, stride=width), :]
        parts = [part, below] if first == 0 else [above, part, below]
        lanes = slice(column + k * LANES, column + (k + 1) * LANES)
        out_ref[:, lanes] = jnp.concatenate(parts, axis=0).astype(BF16)


def unpack_first(flat, ar_ref, b_ref, down, router):
    starts = piece_rows()
    narrow_to_rows(flat, D, [(starts[k][0], COLS, k * COLS) for k in range(3)], down)
    narrow_to_rows(flat, D, [(starts[k][2], EXPERTS, k * EXPERTS) for k in range(3)], router)
    routers = router[...].astype(BF16)
    for half in range(2):
        matrix = spread_matrix(3 * EXPERTS, 0, 3 * COLS - half * LANES).astype(BF16)
        packed = dot(routers, matrix)
        packed = packed if half else packed + down[...]
        ar_ref[:, half * LANES : (half + 1) * LANES] = packed.astype(BF16)
    for index in range(3):
        unpack_ups(flat, starts[index][1], D, index * COLS, b_ref, index * D)


def flat_rows(count):
    return PARAM_ROWS + shard_rows(count) + 20


def unpack_rest(flat, outs, work):
    starts = piece_rows()
    matrix = (keep_matrix() + spread_matrix(EXPERTS, COLS, COLS)).astype(BF16)
    for index in range(3, 6):
        base_a, base_b, base_r = starts[index]
        fan_in, fan_out = FANS[index]
        ar_ref, b_ref = outs[2 * index - 6], outs[2 * index - 5]
        narrow_to_rows(flat, fan_in, [(base_a, COLS, 0), (base_r, EXPERTS, COLS)], work)
        ar_ref[...] = dot(work[:fan_in].astype(BF16), matrix).astype(BF16)
        unpack_ups(flat, base_b, fan_out, 0, b_ref, 0)


def split_dot(value, matrix):
    high = value.astype(BF16)
    return dot(high, matrix) + dot((value - high.astype(F32)).astype(BF16), matrix)


def first_of_four(experts, source, place):
    row = row_iota((LANES, LANES)) - source
    lane = lane_iota((LANES, LANES)) - place
    hit = (row == RANK * lane) & (lane >= 0) & (lane < experts)
    return jnp.where(hit, 1.0, 0.0)


def assemble_ups(flat, base, fan_out, first, grad_ref, column):
    width = fan_out // LANES
    for k in range(width):
        lanes = slice(column + k * LANES, column + (k + 1) * LANES)
        flat[pl.ds(base + k, COLS, stride=width), :] = grad_ref[first : first + COLS, lanes]


def assemble_rest(flat, grads, work):
    starts = piece_rows()
    matrix = (keep_matrix() + first_of_four(EXPERTS, COLS, COLS)).astype(BF16)
    for index in range(3, 6):
        base_a, base_b, base_r = starts[index]
        fan_in, fan_out = FANS[index]
        dar_ref, db_ref = grads[2 * index - 6], grads[2 * index - 5]
        work[:fan_in] = split_dot(pad_rows(dar_ref[...], LANES).T, matrix)
        rows_to_narrow(work, fan_in, [(base_a, COLS, 0), (base_r, EXPERTS, COLS)], flat)
        assemble_ups(flat, base_b, fan_out, 0, db_ref, 0)


def assemble_first(flat, dar_ref, db_ref, down, router):
    starts = piece_rows()
    down[...] = dar_ref[:LANES].T
    rows_to_narrow(down, D, [(starts[k][0], COLS, k * COLS) for k in range(3)], flat)
    first_router = 3 * COLS
    turned = dar_ref[first_router : first_router + LANES].T
    router[...] = split_dot(turned, first_of_four(3 * EXPERTS, 0, 0).astype(BF16))
    rows_to_narrow(router, D, [(starts[k][2], EXPERTS, k * EXPERTS) for k in range(3)], flat)
    for index in range(3):
        assemble_ups(flat, starts[index][1], D, index * COLS, db_ref, index * D)


MESH = pl.DeviceIdType.MESH


def place_of(axes, sizes):
    me = lax.axis_index(axes[0]) * sizes[1] + lax.axis_index(axes[1])

    def coordinates(number):
        return (number // sizes[1], number % sizes[1])

    return me, coordinates


def partners_of(me):
    low = me % 8
    core = low % 2
    y = (low // 2) % 2
    x = low // 4
    over_x = low + 4 * (1 - 2 * x)
    over_y = low + 2 * (1 - 2 * y)
    first = over_x * (1 - core) + over_y * core
    second = over_y * (1 - core) + over_x * core
    both = first + second - low
    other = 1 - 2 * core
    return low, first, second, both, other, over_x, over_y


def greet(peers):
    barrier = pltpu.get_barrier_semaphore()
    for peer in peers:
        pl.semaphore_signal(barrier, inc=1, device_id=peer, device_id_type=MESH)
    pl.semaphore_wait(barrier, len(peers))


class Ring:
    def __init__(self, axes, sizes, send, receive):
        self.me, self.coordinates = place_of(axes, sizes)
        self.groups = sizes[0] * sizes[1] // 8
        self.group = self.me // 8
        places = partners_of(self.me)
        self.low, self.first, self.second, self.both, self.other, self.over_x, self.over_y = places
        self.mate = self.low + self.other
        self.send, self.receive = send, receive
        self.copies = {}

    def device(self, group, low):
        return self.coordinates(group * 8 + low)

    def greet(self):
        peers = [
            self.device((self.group + step) % self.groups, self.low)
            for step in range(1, self.groups)
        ]
        peers += [self.device(self.group, low) for low in (self.first, self.second, self.mate)]
        greet(peers)

    def copy(self, slot, source, target, peer, arrival=None):
        return pltpu.make_async_remote_copy(
            src_ref=source,
            dst_ref=target,
            send_sem=self.send.at[slot],
            recv_sem=self.receive.at[slot if arrival is None else arrival],
            device_id=peer,
            device_id_type=MESH,
        )


def gather_phases(ring, span, shard_ref, out_ref, local, greets):
    begin, end = span
    base = ring.groups
    inside = (ring.group >= begin) & (ring.group < end)

    def around(step):
        target = (ring.group + step) % ring.groups
        return ring.copy(
            step,
            shard_ref,
            out_ref.at[ring.group - begin, ring.low],
            ring.device(target, ring.low),
            base + 7 + ring.group,
        )

    def arrived(group):
        return ring.copy(
            0,
            shard_ref,
            out_ref.at[group - begin, ring.low],
            ring.device(group, ring.low),
            base + 7 + group,
        )

    def push(slot, part, partner):
        return ring.copy(
            base + slot, out_ref.at[:, part], out_ref.at[:, part], ring.device(ring.group, partner)
        )

    one = push(0, ring.low, ring.first)
    two = push(1, ring.low, ring.second)
    three = push(2, ring.first, ring.second)
    cores = [
        push(3 + index, part, ring.mate)
        for index, part in enumerate((ring.low, ring.first, ring.second, ring.both))
    ]

    def own():
        return pltpu.make_async_copy(
            shard_ref, out_ref.at[ring.group - begin, ring.low], local
        )

    def phase0():
        if greets:
            ring.greet()

        @pl.when(inside)
        def _():
            own().start()
            for step in range(1, ring.groups):
                around(step).start()

    def phase1():
        @pl.when(inside)
        def _():
            own().wait()
            for step in range(1, ring.groups):
                around(step).wait_send()

        for group in range(begin, end):

            @pl.when(ring.group != group)
            def _():
                arrived(group).wait_recv()

        for copy in (one, two, cores[0]):
            copy.start()

    def phase2():
        one.wait()
        three.start()
        cores[1].start()

    def phase3():
        two.wait()
        cores[2].start()
        three.wait()
        cores[3].start()

    def phase4():
        for copy in cores:
            copy.wait()

    return phase0, phase1, phase2, phase3, phase4


def gather_semaphores(groups):
    return [
        pltpu.SemaphoreType.DMA((groups + 7,)),
        pltpu.SemaphoreType.DMA((2 * groups + 7,)),
        pltpu.SemaphoreType.DMA,
    ]


def start_kernel(
    link,
    count,
    shard_ref,
    buckets_ref,
    table_ref,
    gain_ref,
    x_hbm,
    w_hbm,
    *refs,
):
    hbm_outs, off_ref, ar_ref, b_ref = refs[:6], refs[6], refs[7], refs[8]
    rest_refs = refs[9:15]
    x_ref, w_ref, normed, dense = refs[15:19]
    outs = refs[19:25]
    qt_ref, k_ref, kt_ref, v_ref, vt_ref, zg_ref = outs
    flat, down, router, work, loaded, stored, *more = refs[25:]
    loads = [
        pltpu.make_async_copy(x_hbm, x_ref, loaded.at[0]),
        pltpu.make_async_copy(w_hbm, w_ref, loaded.at[1]),
    ]
    stores = [
        pltpu.make_async_copy(source, target, stored.at[index])
        for index, (source, target) in enumerate(zip(outs, hbm_outs))
    ]
    for load in loads:
        load.start()
    if link is None:
        first = [lambda: None] * 5
        rest = first

        def shard_of(index):
            return shard_ref[...]
    else:
        axes, sizes, spans = link
        land_a, land_b, *sems = more
        first = gather_phases(
            Ring(axes, sizes, *sems[:2]), spans[0], shard_ref, land_a, sems[2], True
        )
        rest = gather_phases(
            Ring(axes, sizes, *sems[3:5]), spans[1], shard_ref, land_b, sems[5], False
        )

        def shard_of(index):
            group, low = divmod(index, 8)
            begin = spans[1][0]
            return land_a[group, low] if group < begin else land_b[group - begin, low]

    length = x_ref.shape[0]

    def dense_tile(index):
        rows = slice(index * length // 2, (index + 1) * length // 2)
        values = x_ref[rows].astype(F32)
        low = (values * rms_inverse(values) * gain_ref[...].reshape(1, D)).astype(BF16)
        normed[rows] = low
        dense[rows] = dot(low, w_ref[...])

    def project():
        packed = dot(normed[...], ar_ref[...]).T
        lowrank = packed[: 3 * COLS]
        gates = jnp.concatenate(
            [gates_of(packed[place : place + COLS]) for place in range(3 * COLS, 6 * COLS, COLS)],
            axis=0,
        )
        zg_ref[: 3 * COLS] = lowrank
        zg_ref[3 * COLS :] = gates
        stores[5].start()
        mixed = pad_rows(lowrank * gates, LANES).astype(BF16).T
        for part in range(3):
            columns = slice(part * D, (part + 1) * D)
            value = dense[:, columns] + dot(mixed, b_ref[:, columns])
            if part == 0:
                qt_ref[...] = (value * QUERY_SCALE).astype(BF16).T
                stores[0].start()
            else:
                low = value.astype(BF16)
                natural, turned = ((k_ref, kt_ref), (v_ref, vt_ref))[part - 1]
                natural[...] = low
                turned[...] = low.T
                stores[2 * part - 1].start()
                stores[2 * part].start()

    first[0]()
    rest[0]()
    for load in loads:
        load.wait()
    dense_tile(0)
    first[1]()
    rest[1]()
    dense_tile(1)
    first[2]()
    buckets = buckets_ref[...]
    hits = jnp.where(row_iota((table_ref.shape[1], buckets.shape[1])) == buckets, LOG2E, 0.0)
    off_ref[...] = lax.dot_general(
        table_ref[...],
        hits,
        (((1,), (0,)), ((), ())),
        preferred_element_type=F32,
        precision=lax.Precision.HIGHEST,
    )
    first[3]()
    rest[2]()
    first[4]()
    for index in range(-(-FIRST_COUNT // count)):
        align_in(flat, shard_of(index).astype(F32), index * count)
    unpack_first(flat, ar_ref, b_ref, down, router)
    rest[3]()
    project()
    rest[4]()
    for index in range(FIRST_COUNT // count, PARAM_ROWS * LANES // count):
        align_in(flat, shard_of(index).astype(F32), index * count)
    unpack_rest(flat, rest_refs, work)
    for store in stores:
        store.wait()


def start(x, gain, w_qkv, shard, buckets, rel_table, count, axes, sizes, spans):
    length = x.shape[0]
    groups = sizes[0] * sizes[1] // 8
    link = (axes, sizes, spans) if groups else None
    rest_shapes = [
        shape for fan_in, fan_out in FANS[3:] for shape in ((fan_in, LANES), (LANES, fan_out))
    ]
    wide = [
        ((D, length), BF16),
        ((length, D), BF16),
        ((D, length), BF16),
        ((length, D), BF16),
        ((D, length), BF16),
        ((6 * COLS, length), F32),
    ]
    small = [
        ((HEADS, buckets.shape[1]), F32),
        ((D, 2 * LANES), BF16),
        ((LANES, 3 * D), BF16),
    ] + [(shape, BF16) for shape in rest_shapes]
    scratch = [
        pltpu.VMEM(x.shape, BF16),
        pltpu.VMEM(w_qkv.shape, BF16),
        pltpu.VMEM(x.shape, BF16),
        pltpu.VMEM((length, 3 * D), F32),
    ]
    scratch += [pltpu.VMEM(*member) for member in wide]
    scratch += [
        pltpu.VMEM((flat_rows(count), LANES), F32),
        pltpu.VMEM((D, LANES), F32),
        pltpu.VMEM((D, LANES), F32),
        pltpu.VMEM((FF, LANES), F32),
        pltpu.SemaphoreType.DMA((2,)),
        pltpu.SemaphoreType.DMA((len(wide),)),
    ]
    if link:
        scratch += [pltpu.VMEM((end - begin, 8, *shard.shape), BF16) for begin, end in spans]
        scratch += gather_semaphores(groups) * 2
    vmem = pl.BlockSpec(memory_space=pltpu.VMEM)
    anywhere = pl.BlockSpec(memory_space=pl.ANY)
    return pl.pallas_call(
        functools.partial(start_kernel, link, count),
        in_specs=[vmem] * 4 + [anywhere] * 2,
        out_specs=[anywhere] * len(wide) + [vmem] * len(small),
        out_shape=[jax.ShapeDtypeStruct(*member) for member in wide + small],
        scratch_shapes=scratch,
        compiler_params=params(collective_id=0, has_side_effects=True) if link else params(),
        name="start",
    )(shard, buckets, rel_table, gain, x, w_qkv)


def reduce_phases(ring, span, parts_ref, boxes, greets, sums_ref=None, sum_boxes=None):
    begin, end = span
    outbox, inbox, half, own, far_out, far_in, out_ref = boxes
    groups = ring.groups
    inside = (ring.group >= begin) & (ring.group < end)
    core_parts = (ring.first, ring.both, ring.second, ring.low)
    near = [ring.mate] * 4 + [ring.second, ring.second, ring.first]

    def push(slot):
        return ring.copy(slot, outbox.at[slot], inbox.at[slot], ring.device(ring.group, near[slot]))

    def fill(slot, value):
        outbox[slot] = value.astype(BF16)
        push(slot).start()

    def around(group):
        return ring.copy(
            7 + group - begin,
            far_out.at[group - begin],
            far_in.at[ring.group],
            ring.device(group, ring.low),
            7 + ring.group,
        )

    def arrived(group):
        return ring.copy(
            7,
            far_out.at[0],
            far_in.at[group],
            ring.device(group, ring.low),
            7 + group,
        )

    base = 7 + groups
    sum_peers = (ring.mate, ring.over_x, ring.over_y)

    def push_sums(slot):
        near_out, near_in = sum_boxes
        return ring.copy(
            base + slot,
            near_out.at[slot],
            near_in.at[slot],
            ring.device(ring.group, sum_peers[slot]),
        )

    def around_sums(step):
        near_out, near_in = sum_boxes
        target = (ring.group + step) % groups
        return ring.copy(
            base + 2 + step,
            near_out.at[3],
            near_in.at[3 + ring.group],
            ring.device(target, ring.low),
        )

    def start_sums(slot, value):
        if sum_boxes is not None:
            sum_boxes[0][slot] = value
            push_sums(slot).start()

    def phase0():
        if greets:
            ring.greet()
        if sum_boxes is not None:
            start_sums(0, sums_ref[...])
        for slot, part in enumerate(core_parts):
            fill(slot, parts_ref[:, part + ring.other])

    def phase1():
        push(0).wait()
        fill(4, parts_ref[:, ring.second] + inbox[0].astype(F32))
        push(1).wait()
        fill(5, parts_ref[:, ring.both] + inbox[1].astype(F32))
        if sum_boxes is not None:
            push_sums(0).wait()
            start_sums(1, sum_boxes[0][0] + sum_boxes[1][0])
        push(2).wait()
        half[...] = parts_ref[:, ring.first] + inbox[2].astype(F32)
        push(3).wait()
        own[...] = parts_ref[:, ring.low] + inbox[3].astype(F32)

    def phase2():
        push(5).wait()
        fill(6, half[...] + inbox[5].astype(F32))
        if sum_boxes is not None:
            push_sums(1).wait()
            start_sums(2, sum_boxes[0][1] + sum_boxes[1][1])
        push(4).wait()
        own[...] = own[...] + inbox[4].astype(F32)

    def phase3():
        push(6).wait()
        own[...] = own[...] + inbox[6].astype(F32)
        far_out[...] = own[...].astype(BF16)
        for group in range(begin, end):

            @pl.when(ring.group != group)
            def _():
                around(group).start()

        if sum_boxes is not None:
            near_out, near_in = sum_boxes
            push_sums(2).wait()
            near_out[3] = near_out[2] + near_in[2]
            for step in range(1, groups):
                around_sums(step).start()
            near_in[3 + ring.group] = near_out[3]

    def phase4(finish_sums=None):
        for group in range(begin, end):

            @pl.when(ring.group != group)
            def _():
                around(group).wait_send()

        @pl.when(inside)
        def _():
            for group in range(groups):

                @pl.when(ring.group != group)
                def _():
                    arrived(group).wait_recv()

            total = own[ring.group - begin]
            for step in range(1, groups):
                total = total + far_in[(ring.group + step) % groups].astype(F32)
            out_ref[...] = total

        if sum_boxes is not None:
            near_out, near_in = sum_boxes
            for step in range(1, groups):
                around_sums(step).wait()
            whole_sum = near_in[3]
            for index in range(1, groups):
                whole_sum = whole_sum + near_in[3 + index]
            finish_sums(whole_sum)

    return phase0, phase1, phase2, phase3, phase4


def reduce_scratch(groups, count, rows):
    return [
        pltpu.VMEM((7, count, rows, LANES), BF16),
        pltpu.VMEM((7, count, rows, LANES), BF16),
        pltpu.VMEM((count, rows, LANES), F32),
        pltpu.VMEM((count, rows, LANES), F32),
        pltpu.VMEM((count, rows, LANES), BF16),
        pltpu.VMEM((groups, rows, LANES), BF16),
    ]


def finish_kernel(link, count, dar_ref, db_ref, *refs):
    grads, sums_ref = refs[:6], refs[6]
    out_ref, roots_ref, flat, down, router, work, *more = refs[7:]

    def finish_sums(total):
        roots_ref[...] = jnp.sqrt(total / (total[:, 4:5] * D))

    assemble_rest(flat, grads, work)
    if link is None:
        assemble_first(flat, dar_ref, db_ref, down, router)
        out_ref[...] = align_out(flat, out_ref.shape[0], 0)
        finish_sums(sums_ref[...])
        return
    axes, sizes, spans = link
    parts_a, parts_b, near_out, near_in, *more = more
    boxes_a, boxes_b, sems = more[:7], more[7:14], more[14:]
    rows = out_ref.shape[0]
    split = spans[1][0]

    def align(parts, span):
        for group in range(*span):
            for low in range(8):
                parts[group - span[0], low] = align_out(flat, rows, (8 * group + low) * count)

    ring = Ring(axes, sizes, sems[0], sems[1])
    rest = reduce_phases(ring, spans[1], parts_b, boxes_b, True, sums_ref, (near_out, near_in))
    first = reduce_phases(
        Ring(axes, sizes, sems[2], sems[3]), spans[0], parts_a, boxes_a, False
    )
    align(parts_b, spans[1])
    rest[0]()
    assemble_first(flat, dar_ref, db_ref, down, router)
    align(parts_a, spans[0])
    first[0]()
    for step in range(1, 4):
        rest[step]()
        first[step]()
    rest[4](finish_sums)
    first[4]()

    @pl.when(ring.group < split)
    def _():
        out_ref[...] = boxes_a[6][...]

    @pl.when(ring.group >= split)
    def _():
        out_ref[...] = boxes_b[6][...]


def finish(dar, db, grads, sums, count, axes, sizes, spans):
    rows = shard_rows(count)
    groups = sizes[0] * sizes[1] // 8
    link = (axes, sizes, spans) if groups else None
    scratch = [
        pltpu.VMEM((flat_rows(count), LANES), F32),
        pltpu.VMEM((D, LANES), F32),
        pltpu.VMEM((D, LANES), F32),
        pltpu.VMEM((FF, LANES), F32),
    ]
    if link:
        widths = [end - begin for begin, end in spans]
        scratch += [pltpu.VMEM((width, 8, rows, LANES), F32) for width in widths]
        scratch += [
            pltpu.VMEM((4, *sums.shape), F32),
            pltpu.VMEM((3 + groups, *sums.shape), F32),
        ]
        for width in widths:
            scratch += reduce_scratch(groups, width, rows) + [pltpu.VMEM((rows, LANES), F32)]
        scratch += [pltpu.SemaphoreType.DMA((10 + 2 * groups,))] * 4
    vmem = pl.BlockSpec(memory_space=pltpu.VMEM)
    return pl.pallas_call(
        functools.partial(finish_kernel, link, count),
        in_specs=[vmem] * (3 + len(grads)),
        out_specs=[vmem] * 2,
        out_shape=[
            jax.ShapeDtypeStruct((rows, LANES), F32),
            jax.ShapeDtypeStruct(sums.shape, F32),
        ],
        scratch_shapes=scratch,
        compiler_params=params(collective_id=1, has_side_effects=True) if link else params(),
        name="finish",
    )(dar, db, *grads, sums)


def per_device(
    tokens,
    lengths,
    buckets,
    rel_table,
    gain_attn,
    gain_ff,
    w_qkv,
    w_out,
    w_in,
    w_down,
    adapters,
    cotangent,
    axes,
    sizes,
):
    seq_count, length, width = tokens.shape
    x = tokens.reshape(length, width)
    cot = cotangent.reshape(length, width)
    devices = sizes[0] * sizes[1]
    count = adapters.shape[0]
    rows = shard_rows(count)
    shard = jnp.pad(adapters, (0, rows * LANES - count)).reshape(rows, LANES)
    groups = devices // 8
    split_groups = min(-(-FIRST_COUNT // (8 * count)), max(groups - 1, 1))
    spans = ((0, split_groups), (split_groups, groups))
    reversed_buckets = jnp.pad(buckets[::-1], (0, 1)).reshape(1, 2 * length)
    qt, k, kt, v, vt, zg, offsets, ar_qkv, b_qkv, *packed = start(
        x, gain_attn, w_qkv, shard, reversed_buckets, rel_table.T, count, axes, sizes, spans
    )
    ot, lse = attend(lengths, offsets, qt, k, kt, vt)
    block_out, dmid, gt, sums, *grads = middle_part(
        lengths, ot, x, cot, gain_ff, w_out, w_in, w_down, packed
    )
    tokens_grad, dar_qkv, db_qkv = back_part(
        lengths,
        offsets,
        qt,
        k,
        kt,
        v,
        ot,
        gt,
        lse,
        x,
        gain_attn,
        w_qkv,
        ar_qkv,
        b_qkv,
        zg,
        dmid,
    )
    mine, roots = finish(dar_qkv, db_qkv, grads, sums, count, axes, sizes, spans)
    grad_shard = mine.reshape(-1)[:count]
    root_squares = roots[0, :4]
    return (
        block_out.reshape(tokens.shape),
        tokens_grad.reshape(tokens.shape),
        grad_shard,
        root_squares,
    )


def solution(mesh):
    axes = tuple(mesh.axis_names)
    sizes = tuple(mesh.shape[axis] for axis in axes)
    sequence = P(axes, None, None)
    placed = (
        sequence,
        P(axes),
        P(),
        P(),
        P(),
        P(),
        P(),
        P(),
        P(),
        P(),
        P(axes),
        sequence,
    )
    return jax.shard_map(
        functools.partial(per_device, axes=axes, sizes=sizes),
        mesh=mesh,
        in_specs=placed,
        out_specs=(sequence, sequence, P(axes), P()),
        check_vma=False,
    )
```

```python
import functools

import jax
import jax.numpy as jnp
from jax import lax
from jax.experimental import pallas as pl
from jax.experimental.pallas import tpu as pltpu
from jax.sharding import PartitionSpec as P

D = 768
FF = 3072
HEADS = 12
HDIM = 64
EXPERTS = 10
RANK = 4
FANS = ((D, D), (D, D), (D, D), (D, D), (D, FF), (FF, D))
COLS = EXPERTS * RANK
LANES = 128

EPSILON = 1e-06
MASKED = -1000000000.0
GELU_SCALE = 0.7978845608028654
GELU_CUBIC = 0.044715
LOG2E = 1.4426950408889634
LN2 = 0.6931471805599453
QUERY_SCALE = 0.125 * LOG2E

ROWS = 256
MIDDLE_ROWS = 512
CHUNK = 512
QBLOCK = 256
UP_ROWS = 48
DOWN_ROWS = 2 * COLS
VMEM_BYTES = 60 * 1024 * 1024

F32 = jnp.float32
BF16 = jnp.bfloat16


def dot(a, b):
    return lax.dot_general(a, b, (((1,), (0,)), ((), ())), preferred_element_type=F32)


def dot_nt(a, b):
    return lax.dot_general(a, b, (((1,), (1,)), ((), ())), preferred_element_type=F32)


def dot_tn(a, b):
    return lax.dot_general(a, b, (((0,), (0,)), ((), ())), preferred_element_type=F32)


def lane_iota(shape):
    return lax.broadcasted_iota(jnp.int32, shape, 1)


def row_iota(shape):
    return lax.broadcasted_iota(jnp.int32, shape, 0)


def gates_of(logits):
    weights = jnp.exp(logits - jnp.max(logits, axis=0, keepdims=True))
    return weights * (4.0 / jnp.sum(weights, axis=0, keepdims=True))


def gate_grads(grad_mixed, lowrank, gates):
    product = grad_mixed * lowrank
    summed = product
    for step in range(1, RANK):
        summed = summed + pltpu.roll(product, COLS - step, 0)
    centre = jnp.sum(gates * product, axis=0, keepdims=True)
    first = row_iota(gates.shape) % RANK == 0
    return grad_mixed * gates, jnp.where(first, gates * (summed - centre), 0.0)


def pad_rows(value, rows):
    return jnp.concatenate([value, jnp.zeros((rows - value.shape[0], value.shape[1]), F32)], axis=0)


def single_gates(packed):
    turned = packed.T
    lowrank = turned[:COLS]
    gates = gates_of(turned[COLS : 2 * COLS])
    mixed = pad_rows(lowrank * gates, LANES).astype(BF16)
    return lowrank, gates, mixed, mixed.T


def single_deltas(grad_mixed, lowrank, gates):
    parts = gate_grads(grad_mixed.T[:COLS], lowrank, gates)
    delta = pad_rows(jnp.concatenate(parts, axis=0), LANES).astype(BF16)
    return delta, delta.T


def rms_inverse(values):
    return lax.rsqrt(jnp.mean(values * values, axis=-1, keepdims=True) + EPSILON)


def rms_backward(values, gain, inverse, grad_normed):
    weighted = grad_normed * gain
    return inverse * weighted - values * (
        inverse * inverse * inverse * jnp.mean(values * weighted, axis=-1, keepdims=True)
    )


def params(**more):
    return pltpu.CompilerParams(vmem_limit_bytes=VMEM_BYTES, **more)


def whole(shape):
    zeros = (0,) * len(shape)
    return pl.BlockSpec(shape, lambda *_: zeros, pipeline_mode=pl.Buffered(1))


def bias_table(offset_row, length):
    spread = jnp.broadcast_to(offset_row, (LANES, 2 * length))
    return pltpu.roll(spread, 2 * length - (LANES - 1), 1, stride=1, stride_axis=0)


def add_bias(scores, table_ref, start, length):
    width = scores.shape[1]
    parts = []
    for block in range(length // LANES):
        offset = start - LANES * block + (length - LANES)
        parts.append(
            scores[block * LANES : (block + 1) * LANES] + table_ref[:, offset : offset + width]
        )
    return jnp.concatenate(parts, axis=0)


def key_extras(length_ref, shape, odd):
    lane = lane_iota(shape) - (0 if odd else HDIM)
    invalid = row_iota(shape) >= length_ref[0]
    extras = jnp.where((lane == 0) & invalid, MASKED, 0.0)
    return jnp.where((lane >= 1) & (lane <= 3), 1.0, extras).astype(BF16)


def head_lanes(odd):
    lane = lane_iota((1, LANES))
    return ((lane >= HDIM) if odd else (lane < HDIM)).astype(F32).astype(BF16)


def extra_rows(rows):
    width = rows[0].shape[1]
    index = row_iota((8, width))
    block = jnp.zeros((8, width), F32)
    for place, row in enumerate(rows):
        block = jnp.where(index == place, row, block)
    return jnp.concatenate([block, jnp.zeros((HDIM - 8, width), F32)], axis=0).astype(BF16)


def split_three(row):
    high = row.astype(BF16).astype(F32)
    middle = (row - high).astype(BF16).astype(F32)
    return high, middle, row - high - middle


def join_rows(rows, extras, odd):
    return jnp.concatenate([extras, rows] if odd else [rows, extras], axis=0)


def attend_kernel(
    length_ref, off_ref, qt_ref, k_ref, kt_ref, vt_ref, o_ref, lse_ref, table, key_more, plain
):
    length = k_ref.shape[0]
    step = pl.program_id(0)

    @pl.when(step == 0)
    def _():
        for odd in range(2):
            key_more[odd] = key_extras(length_ref, k_ref.shape, odd)

    starts = range(0, length, QBLOCK)
    ones = jnp.ones((1, length), F32)

    def half_of(odd):
        return slice(odd * HDIM, (odd + 1) * HDIM)

    def keys_of(odd):
        return k_ref[...] * head_lanes(odd) + key_more[odd]

    def values_of(odd):
        return jnp.concatenate([vt_ref[half_of(odd), :], jnp.ones((16, length), BF16)], axis=0)

    def finish(odd, start, shift, weights):
        columns = slice(start, start + QBLOCK)
        summed = dot(values_of(odd), weights)
        total = summed[HDIM : HDIM + 1]
        o_ref[half_of(odd), columns] = (summed[:HDIM] / total).astype(BF16)
        lse_ref[0, odd : odd + 1, columns] = shift + jnp.log2(total)
        return total

    def bounded(odd):
        offsets = off_ref[pl.ds(2 * step + odd, 1), :]
        table[odd] = bias_table(offsets, length)
        squares = jnp.square(kt_ref[half_of(odd), :].astype(F32))
        sizes = jnp.sum(squares, axis=0, keepdims=True)
        sizes = jnp.where(lane_iota(sizes.shape) < length_ref[0], sizes, 0.0)
        largest = jnp.max(sizes, axis=1, keepdims=True)
        rows = qt_ref[half_of(odd), :].astype(F32)
        norms = jnp.sqrt(jnp.sum(rows * rows, axis=0, keepdims=True) * largest)
        bound = 1.001 * norms + jnp.max(offsets, axis=1, keepdims=True)
        queries = join_rows(
            qt_ref[half_of(odd), :],
            extra_rows([ones] + [-part for part in split_three(bound)]),
            odd,
        )
        keys = keys_of(odd)
        scores = [dot(keys, queries[:, start : start + QBLOCK]) for start in starts]
        weights = [
            jnp.exp2(add_bias(part, table.at[odd], start, length)).astype(BF16)
            for part, start in zip(scores, starts)
        ]
        least = None
        for start, part in zip(starts, weights):
            total = finish(odd, start, bound[:, start : start + QBLOCK], part)
            least = total if least is None else jnp.minimum(least, total)
        return least

    def exact(odd):
        plain[...] = join_rows(qt_ref[half_of(odd), :], extra_rows([ones]), odd)
        keys = keys_of(odd)

        def block(index, _):
            columns = pl.ds(pl.multiple_of(index * LANES, LANES), LANES)
            raw = dot(keys, plain[:, columns])
            parts = []
            for row in range(0, length, LANES):
                place = pl.multiple_of(index * LANES - row + (length - LANES), LANES)
                parts.append(raw[row : row + LANES] + table[odd, :, pl.ds(place, LANES)])
            scores = jnp.concatenate(parts, axis=0)
            peak = jnp.max(scores, axis=0, keepdims=True)
            summed = dot(values_of(odd), jnp.exp2(scores - peak).astype(BF16))
            total = summed[HDIM : HDIM + 1]
            o_ref[half_of(odd), columns] = (summed[:HDIM] / total).astype(BF16)
            lse_ref[0, odd : odd + 1, columns] = peak + jnp.log2(total)
            return 0

        lax.fori_loop(0, length // LANES, block, 0)

    least = jnp.minimum(bounded(0), bounded(1))

    @pl.when(jnp.logical_not(jnp.min(least) > 2.0**-100))
    def _():
        for odd in range(2):
            exact(odd)


def attend(length_valid, offsets, qt, k, kt, vt):
    length = k.shape[0]
    turned = pl.BlockSpec((LANES, length), lambda p: (p, 0))
    natural = pl.BlockSpec((length, LANES), lambda p: (0, p))
    return pl.pallas_call(
        attend_kernel,
        grid=(HEADS // 2,),
        in_specs=[
            pl.BlockSpec(memory_space=pltpu.SMEM),
            whole(offsets.shape),
            turned,
            natural,
            turned,
            turned,
        ],
        out_specs=[turned, pl.BlockSpec((1, 2, length), lambda p: (p, 0, 0))],
        out_shape=[
            jax.ShapeDtypeStruct((D, length), BF16),
            jax.ShapeDtypeStruct((HEADS // 2, 2, length), F32),
        ],
        scratch_shapes=[
            pltpu.VMEM((2, LANES, 2 * length), F32),
            pltpu.VMEM((2, length, LANES), BF16),
            pltpu.VMEM((LANES, length), BF16),
        ],
        compiler_params=params(),
        name="attend",
    )(length_valid, offsets, qt, k, kt, vt)


def middle_kernel(
    length_ref,
    ot_ref,
    x_ref,
    cot_ref,
    gain_ref,
    w_out_ref,
    w_in_hbm,
    w_down_hbm,
    ar_out_ref,
    b_out_ref,
    ar_in_ref,
    b_in_ref,
    ar_down_ref,
    b_down_ref,
    out_ref,
    dmid_ref,
    gt_ref,
    sums_ref,
    dar_out_ref,
    db_out_ref,
    dar_in_ref,
    db_in_ref,
    dar_down_ref,
    db_down_ref,
    active,
    slope,
    sloped,
    grad_hidden,
    feeds,
    w_in_ref,
    w_down_ref,
    loaded,
):
    step = pl.program_id(0)
    loads = [
        pltpu.make_async_copy(w_in_hbm, w_in_ref, loaded.at[0]),
        pltpu.make_async_copy(w_down_hbm, w_down_ref, loaded.at[1]),
    ]

    @pl.when(step == 0)
    def _():
        for load in loads:
            load.start()
        for ref in (
            sums_ref,
            dar_out_ref,
            db_out_ref,
            dar_in_ref,
            db_in_ref,
            dar_down_ref,
            db_down_ref,
        ):
            ref[...] = jnp.zeros_like(ref)

    attended = ot_ref[...].T
    inputs = x_ref[...].astype(F32)
    gain = gain_ref[...].reshape(1, D)
    cot = cot_ref[...]

    packed_out = dot(attended, ar_out_ref[...])
    branch = dot(attended, w_out_ref[...])
    low_out, gates_out, mixed_out, natural = single_gates(packed_out)
    grad_mixed_down = dot_nt(cot, b_down_ref[...])
    branch = branch + dot(natural, b_out_ref[...])
    middle = inputs + branch
    inverse = rms_inverse(middle)
    normed = (middle * inverse * gain).astype(BF16)

    packed_in = dot(normed, ar_in_ref[...])
    low_in, gates_in, mixed_in, natural = single_gates(packed_in)

    def columns_of(index):
        return pl.ds(pl.multiple_of(index * CHUNK, CHUNK), CHUNK)

    def hidden_of(chunk):
        return dot(normed, w_in_ref[:, chunk]) + dot(natural, b_in_ref[:, chunk])

    def activate(chunk, values):
        grad_dense = dot_nt(cot, w_down_ref[chunk])
        square = values * values
        tangent = jnp.tanh(values * (GELU_SCALE + (GELU_SCALE * GELU_CUBIC) * square))
        half = 0.5 + 0.5 * tangent
        smooth = values * half
        active[:, chunk] = smooth.astype(BF16)
        steep = half + smooth * (1.0 - tangent) * (
            GELU_SCALE + (3.0 * GELU_SCALE * GELU_CUBIC) * square
        )
        slope[:, chunk] = steep.astype(BF16)
        sloped[:, chunk] = grad_dense * steep

    def forward_pair(pair, _):
        chunk_a = columns_of(2 * pair)
        chunk_b = columns_of(2 * pair + 1)
        hidden_a = hidden_of(chunk_a)
        hidden_b = hidden_of(chunk_b)
        activate(chunk_a, hidden_a)
        activate(chunk_b, hidden_b)
        return 0

    @pl.when(step == 0)
    def _():
        for load in loads:
            load.wait()

    lax.fori_loop(0, FF // (2 * CHUNK), forward_pair, 0)

    packed_down = dot(active[...], ar_down_ref[...])
    for first in range(0, D, 256):
        part = slice(first, first + 256)
        feeds[:, part] = dot(active[...], w_down_ref[:, part])
    feed = feeds[...]
    low_down, gates_down, mixed_down, natural = single_gates(packed_down)
    delta_down, natural_delta = single_deltas(grad_mixed_down, low_down, gates_down)
    db_down_ref[...] += dot(mixed_down[:UP_ROWS], cot)
    feed = feed + dot(natural, b_down_ref[...])
    output = middle + feed
    out_ref[...] = output.astype(BF16)

    for first in range(0, FF, CHUNK):
        chunk = slice(first, first + CHUNK)
        grad_low = dot_nt(natural_delta, ar_down_ref[chunk])
        grad_hidden[:, chunk] = (
            sloped[:, chunk] + grad_low * slope[:, chunk].astype(F32)
        ).astype(BF16)

    rows = row_iota((MIDDLE_ROWS, 1)) + step * MIDDLE_ROWS
    valid = (rows < length_ref[0]).astype(F32)
    lane = lane_iota((8, LANES))
    totals = jnp.where((lane == 4) & (step == 0), length_ref[0].astype(F32), 0.0)
    for place, member in enumerate((inputs, branch, feed, output)):
        kept = member * valid
        totals = jnp.where(lane == place, jnp.sum(kept * kept), totals)
    sums_ref[...] += totals

    grad_mixed = dot_nt(grad_hidden[...], b_in_ref[...])
    for first in range(0, D, 256):
        part = slice(first, first + 256)
        feeds[:, part] = dot_nt(grad_hidden[...], w_in_ref[part])
    grad_normed = feeds[...]
    delta_in, natural_delta = single_deltas(grad_mixed, low_in, gates_in)
    grad_normed = grad_normed + dot_nt(natural_delta, ar_in_ref[...])
    dar_in_ref[...] += dot(delta_in[:DOWN_ROWS], normed)

    grad_middle = cot.astype(F32) + rms_backward(middle, gain, inverse, grad_normed)
    dmid_ref[...] = grad_middle
    grad_branch = grad_middle.astype(BF16)
    grad_mixed = dot_nt(grad_branch, b_out_ref[...])
    grad_attended = dot_nt(grad_branch, w_out_ref[...])
    dar_down_ref[...] += dot(delta_down[:DOWN_ROWS], active[...])
    db_in_ref[...] += dot(mixed_in[:UP_ROWS], grad_hidden[...])
    delta_out, natural_delta = single_deltas(grad_mixed, low_out, gates_out)
    grad_attended = grad_attended + dot_nt(natural_delta, ar_out_ref[...])
    gt_ref[...] = grad_attended.astype(BF16).T
    dar_out_ref[...] += dot(delta_out[:DOWN_ROWS], attended)
    db_out_ref[...] += dot(mixed_out[:UP_ROWS], grad_branch)


def middle_part(length_valid, ot, x, cot, gain, w_out, w_in, w_down, adapters):
    length = x.shape[0]
    tile = pl.BlockSpec((MIDDLE_ROWS, D), lambda i: (i, 0))
    turned = pl.BlockSpec((D, MIDDLE_ROWS), lambda i: (0, i))
    grad_shapes = [
        jax.ShapeDtypeStruct(shape, F32)
        for fan_in, fan_out in FANS[3:]
        for shape in ((DOWN_ROWS, fan_in), (UP_ROWS, fan_out))
    ]
    out_shape = [
        jax.ShapeDtypeStruct((length, D), BF16),
        jax.ShapeDtypeStruct((length, D), F32),
        jax.ShapeDtypeStruct((D, length), BF16),
        jax.ShapeDtypeStruct((8, LANES), F32),
    ] + grad_shapes
    return pl.pallas_call(
        middle_kernel,
        grid=(length // MIDDLE_ROWS,),
        in_specs=[pl.BlockSpec(memory_space=pltpu.SMEM), turned, tile, tile]
        + [whole(gain.shape), whole(w_out.shape)]
        + [pl.BlockSpec(memory_space=pl.ANY)] * 2
        + [whole(member.shape) for member in adapters],
        out_specs=[tile, tile, turned] + [whole(member.shape) for member in out_shape[3:]],
        out_shape=out_shape,
        scratch_shapes=[
            pltpu.VMEM((MIDDLE_ROWS, FF), BF16),
            pltpu.VMEM((MIDDLE_ROWS, FF), BF16),
            pltpu.VMEM((MIDDLE_ROWS, FF), F32),
            pltpu.VMEM((MIDDLE_ROWS, FF), BF16),
            pltpu.VMEM((MIDDLE_ROWS, D), F32),
            pltpu.VMEM(w_in.shape, BF16),
            pltpu.VMEM(w_down.shape, BF16),
            pltpu.SemaphoreType.DMA((2,)),
        ],
        compiler_params=params(),
        name="middle_part",
    )(length_valid, ot, x, cot, gain, w_out, w_in, w_down, *adapters)


def attend_back(
    pair,
    length_ref,
    off_ref,
    qt_ref,
    k_ref,
    kt_ref,
    v_ref,
    ot_ref,
    gt_ref,
    lse_ref,
    grads_ref,
    table,
    key_more,
    weights_all,
    grads_all,
):
    length = k_ref.shape[0]
    lane = lane_iota((1, LANES))
    first_lanes = lane < HDIM
    grad_query_parts = []
    for odd in range(2):
        half = slice(odd * HDIM, (odd + 1) * HDIM)
        table[odd] = bias_table(off_ref[pl.ds(2 * pair + odd, 1), :], length)
        keys = k_ref[...] * head_lanes(odd) + key_more[odd]
        place = lane - (0 if odd else HDIM)
        value_more = ((place >= 0) & (place < 3)).astype(F32).astype(BF16)
        values = v_ref[...] * head_lanes(odd) + value_more
        ones = jnp.ones((1, length), F32)
        lse = lse_ref[0, odd : odd + 1, :]
        queries = join_rows(
            qt_ref[half, :], extra_rows([ones] + [-part for part in split_three(lse)]), odd
        )
        delta = jnp.sum(
            ot_ref[half, :].astype(F32) * gt_ref[half, :].astype(F32), axis=0, keepdims=True
        )
        grads = join_rows(
            gt_ref[half, :], extra_rows([-part for part in split_three(delta)]), odd
        )
        for start in range(0, length, QBLOCK):
            columns = slice(start, start + QBLOCK)
            scores = add_bias(dot(keys, queries[:, columns]), table.at[odd], start, length)
            weights = jnp.exp2(scores)
            weights_all[:, columns] = weights.astype(BF16)
            grad_scores = weights * dot(values, grads[:, columns])
            grads_all[:, columns] = grad_scores.astype(BF16)
        grad_query_parts.append(dot(kt_ref[half, :], grads_all[...]) * 0.125)
        grad_values = dot_nt(weights_all[...], gt_ref[...])
        grad_keys = dot_nt(grads_all[...], qt_ref[...]) * LN2
        if odd:
            grad_values = jnp.where(first_lanes, even_values, grad_values)
            grad_keys = jnp.where(first_lanes, even_keys, grad_keys)
        else:
            even_values, even_keys = grad_values, grad_keys
    columns = pl.ds(pl.multiple_of(pair * LANES, LANES), LANES)
    grads_ref[0, :, columns] = jnp.concatenate(grad_query_parts, axis=0).T.astype(BF16)
    grads_ref[1, :, columns] = grad_keys.astype(BF16)
    grads_ref[2, :, columns] = grad_values.astype(BF16)


def project_back(
    tile, x_ref, gain_ref, w_ref, ar_ref, b_ref, zg_ref, grads_ref, dmid_ref, out_ref, dar_ref, db_ref
):
    values = x_ref[...].astype(F32)
    gain = gain_ref[...].reshape(1, D)
    inverse = rms_inverse(values)
    normed = (values * inverse * gain).astype(BF16)
    lowrank = zg_ref[: 3 * COLS]
    gates = zg_ref[3 * COLS :]
    mixed = pad_rows(lowrank * gates, LANES).astype(BF16)
    rows = pl.ds(pl.multiple_of(tile * ROWS, ROWS), ROWS)
    grads = [grads_ref[index, rows] for index in range(3)]
    columns = [slice(index * D, (index + 1) * D) for index in range(3)]
    grad_mixed = jnp.zeros((ROWS, LANES), F32)
    for grad, lanes in zip(grads, columns):
        grad_mixed = grad_mixed + dot_nt(grad, b_ref[:, lanes])
    grad_normed = jnp.zeros((ROWS, D), F32)
    for grad, lanes in zip(grads, columns):
        grad_normed = grad_normed + dot_nt(grad, w_ref[:, lanes])
        db_ref[:, lanes] += dot(mixed, grad)
    turned = grad_mixed.T
    parts = []
    for first in range(0, 3 * COLS, COLS):
        place = slice(first, first + COLS)
        parts.append(gate_grads(turned[place], lowrank[place], gates[place]))
    delta = jnp.concatenate([part[0] for part in parts] + [part[1] for part in parts], axis=0)
    delta = pad_rows(delta, 2 * LANES).astype(BF16)
    grad_normed = grad_normed + dot_nt(delta.T, ar_ref[...])
    dar_ref[...] += dot(delta, normed)
    out_ref[...] = dmid_ref[...] + rms_backward(values, gain, inverse, grad_normed)


def back_kernel(*refs):
    length_ref = refs[0]
    heads_refs = refs[:9]
    x_ref, gain_ref, w_hbm, ar_ref, b_ref, zg_ref, dmid_ref = refs[9:16]
    out_ref, dar_ref, db_ref = refs[16:19]
    table, key_more, weights_all, grads_all, grads_ref, w_ref, loaded = refs[19:]
    step = pl.program_id(0)
    pairs = HEADS // 2
    load = pltpu.make_async_copy(w_hbm, w_ref, loaded)

    @pl.when(step == 0)
    def _():
        load.start()
        dar_ref[...] = jnp.zeros_like(dar_ref)
        db_ref[...] = jnp.zeros_like(db_ref)
        for odd in range(2):
            key_more[odd] = key_extras(length_ref, key_more.shape[1:], odd)

    @pl.when(step < pairs)
    def _():
        attend_back(step, *heads_refs, grads_ref, table, key_more, weights_all, grads_all)

    @pl.when(step == pairs)
    def _():
        load.wait()

    @pl.when(step >= pairs)
    def _():
        project_back(
            step - pairs,
            x_ref,
            gain_ref,
            w_ref,
            ar_ref,
            b_ref,
            zg_ref,
            grads_ref,
            dmid_ref,
            out_ref,
            dar_ref,
            db_ref,
        )


def back_part(
    length_valid, offsets, qt, k, kt, v, ot, gt, lse, x, gain, w_qkv, ar_qkv, b_qkv, zg, dmid
):
    length = k.shape[0]
    pairs = HEADS // 2

    def pair_of(i):
        return jnp.minimum(i, pairs - 1)

    def tile_of(i):
        return jnp.maximum(i - pairs, 0)

    turned = pl.BlockSpec((LANES, length), lambda i: (pair_of(i), 0))
    natural = pl.BlockSpec((length, LANES), lambda i: (0, pair_of(i)))
    tile = pl.BlockSpec((ROWS, D), lambda i: (tile_of(i), 0))
    out_shape = [
        jax.ShapeDtypeStruct((length, D), F32),
        jax.ShapeDtypeStruct((2 * LANES, D), F32),
        jax.ShapeDtypeStruct((LANES, 3 * D), F32),
    ]
    return pl.pallas_call(
        back_kernel,
        grid=(pairs + length // ROWS,),
        in_specs=[
            pl.BlockSpec(memory_space=pltpu.SMEM),
            whole(offsets.shape),
            turned,
            natural,
            turned,
            natural,
            turned,
            turned,
            pl.BlockSpec((1, 2, length), lambda i: (pair_of(i), 0, 0)),
            tile,
            whole((D,)),
            pl.BlockSpec(memory_space=pl.ANY),
            whole(ar_qkv.shape),
            whole(b_qkv.shape),
            pl.BlockSpec((6 * COLS, ROWS), lambda i: (0, tile_of(i))),
            tile,
        ],
        out_specs=[tile] + [whole(member.shape) for member in out_shape[1:]],
        out_shape=out_shape,
        scratch_shapes=[
            pltpu.VMEM((2, LANES, 2 * length), F32),
            pltpu.VMEM((2, length, LANES), BF16),
            pltpu.VMEM((length, length), BF16),
            pltpu.VMEM((length, length), BF16),
            pltpu.VMEM((3, length, D), BF16),
            pltpu.VMEM(w_qkv.shape, BF16),
            pltpu.SemaphoreType.DMA,
        ],
        compiler_params=params(),
        name="back_part",
    )(length_valid, offsets, qt, k, kt, v, ot, gt, lse, x, gain, w_qkv, ar_qkv, b_qkv, zg, dmid)


PARAM_ROWS = sum((COLS + EXPERTS) * fan_in + COLS * fan_out for fan_in, fan_out in FANS) // LANES


def piece_rows():
    result = []
    row = 0
    for fan_in, fan_out in FANS:
        starts = []
        for count in (fan_in * COLS, COLS * fan_out, fan_in * EXPERTS):
            starts.append(row)
            row += count // LANES
        result.append(tuple(starts))
    return result


def shard_rows(count):
    return -(-count // (LANES * 16)) * 16


def align_in(flat_ref, shard, start):
    first, shift = divmod(start, LANES)
    rows = shard.shape[0]
    if shift == 0:
        flat_ref[first : first + rows] = shard
        return
    turned = pltpu.roll(shard, shift, 1)
    lane = lane_iota((1, LANES))
    zeros = jnp.zeros((8, LANES), F32)
    upper = jnp.concatenate([turned, zeros], axis=0)
    lower = pltpu.roll(upper, 1, 0)
    kept = flat_ref[first : first + 8]
    merged = jnp.where(lane >= shift, upper, lower)
    inside = (row_iota((8, LANES)) == 0) & (lane_iota((8, LANES)) < shift)
    flat_ref[first : first + 8] = jnp.where(inside, kept, merged[:8])
    flat_ref[first + 8 : first + 8 + rows] = merged[8:]


def align_out(flat_ref, rows, start):
    first, shift = divmod(start, LANES)
    if shift == 0:
        return flat_ref[first : first + rows]
    block = flat_ref[first : first + rows + 8]
    turned = pltpu.roll(block, LANES - shift, 1)
    below = pltpu.roll(turned, rows + 7, 0)
    lane = lane_iota((1, LANES))
    return jnp.where(lane < LANES - shift, turned, below)[:rows]


GROUP = 64


def narrow_to_rows(flat_ref, fan_in, items, out_ref, begin=0):
    groups = fan_in // GROUP
    lane = lane_iota((1, LANES))
    lines = [
        [
            flat_ref[pl.ds(base + k, groups, stride=width * GROUP // LANES), :]
            for k in range(width * GROUP // LANES)
        ]
        for base, width, _ in items
    ]
    for b in range(GROUP):
        result = jnp.zeros((groups, LANES), F32)
        for line, (_, width, place) in zip(lines, items):
            first, shift = divmod(width * b, LANES)
            amount = (place - shift) % LANES
            value = line[first] if amount == 0 else pltpu.roll(line[first], amount, 1)
            if shift + width > LANES:
                value = jnp.where(
                    lane < place + LANES - shift, value, pltpu.roll(line[first + 1], amount, 1)
                )
            inside = (lane >= place) & (lane < place + width)
            result = jnp.where(inside, value, result)
        out_ref[pl.ds(begin + b, groups, stride=GROUP), :] = result


def rows_to_narrow(in_ref, fan_in, items, flat_ref, begin=0):
    groups = fan_in // GROUP
    lane = lane_iota((1, LANES))
    lines = [
        [jnp.zeros((groups, LANES), F32) for _ in range(width * GROUP // LANES)]
        for _, width, _ in items
    ]
    for b in range(GROUP):
        source = in_ref[pl.ds(begin + b, groups, stride=GROUP), :]
        for line, (_, width, place) in zip(lines, items):
            first, shift = divmod(width * b, LANES)
            amount = (shift - place) % LANES
            value = source if amount == 0 else pltpu.roll(source, amount, 1)
            inside = (lane >= shift) & (lane < shift + width)
            line[first] = jnp.where(inside, value, line[first])
            if shift + width > LANES:
                line[first + 1] = jnp.where(lane < shift + width - LANES, value, line[first + 1])
    for line, (base, width, _) in zip(lines, items):
        for k, value in enumerate(line):
            flat_ref[pl.ds(base + k, groups, stride=width * GROUP // LANES), :] = value


def single_items(block):
    starts = piece_rows()
    after_out, after_in = (block + 4) // 5, (block + 2) // 4
    down = (block - 2) * after_in
    bases = []
    for piece, width in ((0, COLS), (2, EXPERTS)):
        out, inner, outer = (starts[index][piece] for index in range(3, 6))
        base = out + (inner - out) * after_out + (outer - inner) * after_in
        bases.append(base + down * (D * width // LANES))
    return [(bases[0], COLS, 0), (bases[1], EXPERTS, COLS)]


SINGLE_BLOCKS = 2 + FF // D


def spread_matrix(experts, source, place):
    row = row_iota((LANES, LANES)) - source
    lane = lane_iota((LANES, LANES)) - place
    hit = (lane >= RANK * row) & (lane < RANK * row + RANK) & (row >= 0) & (row < experts)
    return jnp.where(hit, 1.0, 0.0)


def keep_matrix():
    row = row_iota((LANES, LANES))
    return jnp.where((row == lane_iota((LANES, LANES))) & (row < COLS), 1.0, 0.0)


FIRST_COUNT = sum((COLS + EXPERTS) * fan_in + COLS * fan_out for fan_in, fan_out in FANS[:3])


def unpack_ups(flat, base, fan_out, first, out_ref, column):
    width = fan_out // LANES
    above = jnp.zeros((first, LANES), F32)
    below = jnp.zeros((LANES - COLS - first, LANES), F32)
    for k in range(width):
        part = flat[pl.ds(base + k, COLS, stride=width), :]
        parts = [part, below] if first == 0 else [above, part, below]
        lanes = slice(column + k * LANES, column + (k + 1) * LANES)
        out_ref[:, lanes] = jnp.concatenate(parts, axis=0).astype(BF16)


def unpack_first(flat, ar_ref, b_ref, down, router):
    starts = piece_rows()
    narrow_to_rows(flat, D, [(starts[k][0], COLS, k * COLS) for k in range(3)], down)
    narrow_to_rows(flat, D, [(starts[k][2], EXPERTS, k * EXPERTS) for k in range(3)], router)
    routers = router[...].astype(BF16)
    for half in range(2):
        matrix = spread_matrix(3 * EXPERTS, 0, 3 * COLS - half * LANES).astype(BF16)
        packed = dot(routers, matrix)
        packed = packed if half else packed + down[...]
        ar_ref[:, half * LANES : (half + 1) * LANES] = packed.astype(BF16)
    for index in range(3):
        unpack_ups(flat, starts[index][1], D, index * COLS, b_ref, index * D)


def flat_rows(count):
    return PARAM_ROWS + shard_rows(count) + 20


def unpack_rest(flat, outs, work):
    starts = piece_rows()
    matrix = (keep_matrix() + spread_matrix(EXPERTS, COLS, COLS)).astype(BF16)

    def block(index, _):
        narrow_to_rows(flat, D, single_items(index), work, index * D)
        return 0

    lax.fori_loop(0, SINGLE_BLOCKS, block, 0)
    begin = 0
    for index in range(3, 6):
        fan_in, fan_out = FANS[index]
        ar_ref, b_ref = outs[2 * index - 6], outs[2 * index - 5]
        ar_ref[...] = dot(work[begin : begin + fan_in].astype(BF16), matrix).astype(BF16)
        unpack_ups(flat, starts[index][1], fan_out, 0, b_ref, 0)
        begin += fan_in


def split_dot(value, matrix):
    high = value.astype(BF16)
    return dot(high, matrix) + dot((value - high.astype(F32)).astype(BF16), matrix)


def first_of_four(experts, source, place):
    row = row_iota((LANES, LANES)) - source
    lane = lane_iota((LANES, LANES)) - place
    hit = (row == RANK * lane) & (lane >= 0) & (lane < experts)
    return jnp.where(hit, 1.0, 0.0)


def assemble_ups(flat, base, fan_out, first, grad_ref, column):
    width = fan_out // LANES
    for k in range(width):
        lanes = slice(column + k * LANES, column + (k + 1) * LANES)
        flat[pl.ds(base + k, COLS, stride=width), :] = grad_ref[first : first + COLS, lanes]


def assemble_rest(flat, grads, work):
    starts = piece_rows()
    matrix = (keep_matrix() + first_of_four(EXPERTS, COLS, COLS)).astype(BF16)
    begin = 0
    for index in range(3, 6):
        fan_in, fan_out = FANS[index]
        dar_ref, db_ref = grads[2 * index - 6], grads[2 * index - 5]
        work[begin : begin + fan_in] = split_dot(pad_rows(dar_ref[...], LANES).T, matrix)
        assemble_ups(flat, starts[index][1], fan_out, 0, db_ref, 0)
        begin += fan_in

    def block(index, _):
        rows_to_narrow(work, D, single_items(index), flat, index * D)
        return 0

    lax.fori_loop(0, SINGLE_BLOCKS, block, 0)


def assemble_first(flat, dar_ref, db_ref, down, router):
    starts = piece_rows()
    down[...] = dar_ref[:LANES].T
    rows_to_narrow(down, D, [(starts[k][0], COLS, k * COLS) for k in range(3)], flat)
    first_router = 3 * COLS
    turned = dar_ref[first_router : first_router + LANES].T
    router[...] = split_dot(turned, first_of_four(3 * EXPERTS, 0, 0).astype(BF16))
    rows_to_narrow(router, D, [(starts[k][2], EXPERTS, k * EXPERTS) for k in range(3)], flat)
    for index in range(3):
        assemble_ups(flat, starts[index][1], D, index * COLS, db_ref, index * D)


MESH = pl.DeviceIdType.MESH


def place_of(axes, sizes):
    me = lax.axis_index(axes[0]) * sizes[1] + lax.axis_index(axes[1])

    def coordinates(number):
        return (number // sizes[1], number % sizes[1])

    return me, coordinates


def partners_of(me):
    low = me % 8
    core = low % 2
    y = (low // 2) % 2
    x = low // 4
    over_x = low + 4 * (1 - 2 * x)
    over_y = low + 2 * (1 - 2 * y)
    first = over_x * (1 - core) + over_y * core
    second = over_y * (1 - core) + over_x * core
    both = first + second - low
    other = 1 - 2 * core
    return low, first, second, both, other, over_x, over_y


def greet(peers):
    barrier = pltpu.get_barrier_semaphore()
    for peer in peers:
        pl.semaphore_signal(barrier, inc=1, device_id=peer, device_id_type=MESH)
    pl.semaphore_wait(barrier, len(peers))


class Ring:
    def __init__(self, axes, sizes, send, receive):
        self.me, self.coordinates = place_of(axes, sizes)
        self.groups = sizes[0] * sizes[1] // 8
        self.group = self.me // 8
        places = partners_of(self.me)
        self.low, self.first, self.second, self.both, self.other, self.over_x, self.over_y = places
        self.mate = self.low + self.other
        self.send, self.receive = send, receive
        self.copies = {}

    def device(self, group, low):
        return self.coordinates(group * 8 + low)

    def greet(self):
        peers = [
            self.device((self.group + step) % self.groups, self.low)
            for step in range(1, self.groups)
        ]
        peers += [self.device(self.group, low) for low in (self.first, self.second, self.mate)]
        greet(peers)

    def copy(self, slot, source, target, peer, arrival=None):
        return pltpu.make_async_remote_copy(
            src_ref=source,
            dst_ref=target,
            send_sem=self.send.at[slot],
            recv_sem=self.receive.at[slot if arrival is None else arrival],
            device_id=peer,
            device_id_type=MESH,
        )


def gather_phases(ring, span, shard_ref, out_ref, local, greets):
    begin, end = span
    base = ring.groups
    inside = (ring.group >= begin) & (ring.group < end)

    def around(step):
        target = (ring.group + step) % ring.groups
        return ring.copy(
            step,
            shard_ref,
            out_ref.at[ring.group - begin, ring.low],
            ring.device(target, ring.low),
            base + 7 + ring.group,
        )

    def arrived(group):
        return ring.copy(
            0,
            shard_ref,
            out_ref.at[group - begin, ring.low],
            ring.device(group, ring.low),
            base + 7 + group,
        )

    def push(slot, part, partner):
        return ring.copy(
            base + slot, out_ref.at[:, part], out_ref.at[:, part], ring.device(ring.group, partner)
        )

    one = push(0, ring.low, ring.first)
    two = push(1, ring.low, ring.second)
    three = push(2, ring.first, ring.second)
    cores = [
        push(3 + index, part, ring.mate)
        for index, part in enumerate((ring.low, ring.first, ring.second, ring.both))
    ]

    def own():
        return pltpu.make_async_copy(
            shard_ref, out_ref.at[ring.group - begin, ring.low], local
        )

    def phase0():
        if greets:
            ring.greet()

        @pl.when(inside)
        def _():
            own().start()
            for step in range(1, ring.groups):
                around(step).start()

    def phase1():
        @pl.when(inside)
        def _():
            own().wait()
            for step in range(1, ring.groups):
                around(step).wait_send()

        for group in range(begin, end):

            @pl.when(ring.group != group)
            def _():
                arrived(group).wait_recv()

        for copy in (one, two, cores[0]):
            copy.start()

    def phase2():
        one.wait()
        three.start()
        cores[1].start()

    def phase3():
        two.wait()
        cores[2].start()
        three.wait()
        cores[3].start()

    def phase4():
        for copy in cores:
            copy.wait()

    return phase0, phase1, phase2, phase3, phase4


def gather_semaphores(groups):
    return [
        pltpu.SemaphoreType.DMA((groups + 7,)),
        pltpu.SemaphoreType.DMA((2 * groups + 7,)),
        pltpu.SemaphoreType.DMA,
    ]


def start_kernel(
    link,
    count,
    shard_ref,
    buckets_ref,
    table_ref,
    gain_ref,
    x_hbm,
    w_hbm,
    *refs,
):
    hbm_outs, off_ref, ar_ref, b_ref = refs[:6], refs[6], refs[7], refs[8]
    rest_refs = refs[9:15]
    x_ref, w_ref, normed, dense = refs[15:19]
    outs = refs[19:25]
    qt_ref, k_ref, kt_ref, v_ref, vt_ref, zg_ref = outs
    flat, down, router, work, loaded, stored, *more = refs[25:]
    loads = [
        pltpu.make_async_copy(x_hbm, x_ref, loaded.at[0]),
        pltpu.make_async_copy(w_hbm, w_ref, loaded.at[1]),
    ]
    stores = [
        pltpu.make_async_copy(source, target, stored.at[index])
        for index, (source, target) in enumerate(zip(outs, hbm_outs))
    ]
    for load in loads:
        load.start()
    if link is None:
        first = [lambda: None] * 5
        rest = first

        def shard_of(index):
            return shard_ref[...]
    else:
        axes, sizes, spans = link
        land_a, land_b, *sems = more
        first = gather_phases(
            Ring(axes, sizes, *sems[:2]), spans[0], shard_ref, land_a, sems[2], True
        )
        rest = gather_phases(
            Ring(axes, sizes, *sems[3:5]), spans[1], shard_ref, land_b, sems[5], False
        )

        def shard_of(index):
            group, low = divmod(index, 8)
            begin = spans[1][0]
            return land_a[group, low] if group < begin else land_b[group - begin, low]

    length = x_ref.shape[0]

    def dense_tile(index):
        rows = slice(index * length // 2, (index + 1) * length // 2)
        values = x_ref[rows].astype(F32)
        low = (values * rms_inverse(values) * gain_ref[...].reshape(1, D)).astype(BF16)
        normed[rows] = low

        def columns(part, _):
            lanes = pl.ds(pl.multiple_of(part * D, D), D)
            dense[rows, lanes] = dot(normed[rows], w_ref[:, lanes])
            return 0

        lax.fori_loop(0, 3, columns, 0)

    def project():
        packed = dot(normed[...], ar_ref[...]).T
        lowrank = packed[: 3 * COLS]
        gates = jnp.concatenate(
            [gates_of(packed[place : place + COLS]) for place in range(3 * COLS, 6 * COLS, COLS)],
            axis=0,
        )
        zg_ref[: 3 * COLS] = lowrank
        zg_ref[3 * COLS :] = gates
        stores[5].start()
        mixed = pad_rows(lowrank * gates, LANES).astype(BF16).T
        for part in range(3):
            columns = slice(part * D, (part + 1) * D)
            value = dense[:, columns] + dot(mixed, b_ref[:, columns])
            if part == 0:
                qt_ref[...] = (value * QUERY_SCALE).astype(BF16).T
                stores[0].start()
            else:
                low = value.astype(BF16)
                natural, turned = ((k_ref, kt_ref), (v_ref, vt_ref))[part - 1]
                natural[...] = low
                turned[...] = low.T
                stores[2 * part - 1].start()
                stores[2 * part].start()

    first[0]()
    rest[0]()
    for load in loads:
        load.wait()
    dense_tile(0)
    first[1]()
    rest[1]()
    dense_tile(1)
    first[2]()
    buckets = buckets_ref[...]
    hits = jnp.where(row_iota((table_ref.shape[1], buckets.shape[1])) == buckets, LOG2E, 0.0)
    off_ref[...] = lax.dot_general(
        table_ref[...],
        hits,
        (((1,), (0,)), ((), ())),
        preferred_element_type=F32,
        precision=lax.Precision.HIGHEST,
    )
    first[3]()
    rest[2]()
    first[4]()
    for index in range(-(-FIRST_COUNT // count)):
        align_in(flat, shard_of(index).astype(F32), index * count)
    unpack_first(flat, ar_ref, b_ref, down, router)
    rest[3]()
    project()
    rest[4]()
    for index in range(FIRST_COUNT // count, PARAM_ROWS * LANES // count):
        align_in(flat, shard_of(index).astype(F32), index * count)
    unpack_rest(flat, rest_refs, work)
    for store in stores:
        store.wait()


def start(x, gain, w_qkv, shard, buckets, rel_table, count, axes, sizes, spans):
    length = x.shape[0]
    groups = sizes[0] * sizes[1] // 8
    link = (axes, sizes, spans) if groups else None
    rest_shapes = [
        shape for fan_in, fan_out in FANS[3:] for shape in ((fan_in, LANES), (LANES, fan_out))
    ]
    wide = [
        ((D, length), BF16),
        ((length, D), BF16),
        ((D, length), BF16),
        ((length, D), BF16),
        ((D, length), BF16),
        ((6 * COLS, length), F32),
    ]
    small = [
        ((HEADS, buckets.shape[1]), F32),
        ((D, 2 * LANES), BF16),
        ((LANES, 3 * D), BF16),
    ] + [(shape, BF16) for shape in rest_shapes]
    scratch = [
        pltpu.VMEM(x.shape, BF16),
        pltpu.VMEM(w_qkv.shape, BF16),
        pltpu.VMEM(x.shape, BF16),
        pltpu.VMEM((length, 3 * D), F32),
    ]
    scratch += [pltpu.VMEM(*member) for member in wide]
    scratch += [
        pltpu.VMEM((flat_rows(count), LANES), F32),
        pltpu.VMEM((D, LANES), F32),
        pltpu.VMEM((D, LANES), F32),
        pltpu.VMEM((SINGLE_BLOCKS * D, LANES), F32),
        pltpu.SemaphoreType.DMA((2,)),
        pltpu.SemaphoreType.DMA((len(wide),)),
    ]
    if link:
        scratch += [pltpu.VMEM((end - begin, 8, *shard.shape), BF16) for begin, end in spans]
        scratch += gather_semaphores(groups) * 2
    vmem = pl.BlockSpec(memory_space=pltpu.VMEM)
    anywhere = pl.BlockSpec(memory_space=pl.ANY)
    return pl.pallas_call(
        functools.partial(start_kernel, link, count),
        in_specs=[vmem] * 4 + [anywhere] * 2,
        out_specs=[anywhere] * len(wide) + [vmem] * len(small),
        out_shape=[jax.ShapeDtypeStruct(*member) for member in wide + small],
        scratch_shapes=scratch,
        compiler_params=params(collective_id=0, has_side_effects=True) if link else params(),
        name="start",
    )(shard, buckets, rel_table, gain, x, w_qkv)


def reduce_phases(ring, span, parts_ref, boxes, greets, sums_ref=None, sum_boxes=None):
    begin, end = span
    outbox, inbox, half, own, far_out, far_in, out_ref = boxes
    groups = ring.groups
    inside = (ring.group >= begin) & (ring.group < end)
    core_parts = (ring.first, ring.both, ring.second, ring.low)
    near = [ring.mate] * 4 + [ring.second, ring.second, ring.first]

    def push(slot):
        return ring.copy(slot, outbox.at[slot], inbox.at[slot], ring.device(ring.group, near[slot]))

    def fill(slot, value):
        outbox[slot] = value.astype(BF16)
        push(slot).start()

    def around(group):
        return ring.copy(
            7 + group - begin,
            far_out.at[group - begin],
            far_in.at[ring.group],
            ring.device(group, ring.low),
            7 + ring.group,
        )

    def arrived(group):
        return ring.copy(
            7,
            far_out.at[0],
            far_in.at[group],
            ring.device(group, ring.low),
            7 + group,
        )

    base = 7 + groups
    sum_peers = (ring.mate, ring.over_x, ring.over_y)

    def push_sums(slot):
        near_out, near_in = sum_boxes
        return ring.copy(
            base + slot,
            near_out.at[slot],
            near_in.at[slot],
            ring.device(ring.group, sum_peers[slot]),
        )

    def around_sums(step):
        near_out, near_in = sum_boxes
        target = (ring.group + step) % groups
        return ring.copy(
            base + 2 + step,
            near_out.at[3],
            near_in.at[3 + ring.group],
            ring.device(target, ring.low),
        )

    def start_sums(slot, value):
        if sum_boxes is not None:
            sum_boxes[0][slot] = value
            push_sums(slot).start()

    def phase0():
        if greets:
            ring.greet()
        if sum_boxes is not None:
            start_sums(0, sums_ref[...])
        for slot, part in enumerate(core_parts):
            fill(slot, parts_ref[:, part + ring.other])

    def phase1():
        push(0).wait()
        fill(4, parts_ref[:, ring.second] + inbox[0].astype(F32))
        push(1).wait()
        fill(5, parts_ref[:, ring.both] + inbox[1].astype(F32))
        if sum_boxes is not None:
            push_sums(0).wait()
            start_sums(1, sum_boxes[0][0] + sum_boxes[1][0])
        push(2).wait()
        half[...] = parts_ref[:, ring.first] + inbox[2].astype(F32)
        push(3).wait()
        own[...] = parts_ref[:, ring.low] + inbox[3].astype(F32)

    def phase2():
        push(5).wait()
        fill(6, half[...] + inbox[5].astype(F32))
        if sum_boxes is not None:
            push_sums(1).wait()
            start_sums(2, sum_boxes[0][1] + sum_boxes[1][1])
        push(4).wait()
        own[...] = own[...] + inbox[4].astype(F32)

    def phase3():
        push(6).wait()
        own[...] = own[...] + inbox[6].astype(F32)
        far_out[...] = own[...].astype(BF16)
        for group in range(begin, end):

            @pl.when(ring.group != group)
            def _():
                around(group).start()

        if sum_boxes is not None:
            near_out, near_in = sum_boxes
            push_sums(2).wait()
            near_out[3] = near_out[2] + near_in[2]
            for step in range(1, groups):
                around_sums(step).start()
            near_in[3 + ring.group] = near_out[3]

    def phase4(finish_sums=None):
        for group in range(begin, end):

            @pl.when(ring.group != group)
            def _():
                around(group).wait_send()

        @pl.when(inside)
        def _():
            for group in range(groups):

                @pl.when(ring.group != group)
                def _():
                    arrived(group).wait_recv()

            total = own[ring.group - begin]
            for step in range(1, groups):
                total = total + far_in[(ring.group + step) % groups].astype(F32)
            out_ref[...] = total

        if sum_boxes is not None:
            near_out, near_in = sum_boxes
            for step in range(1, groups):
                around_sums(step).wait()
            whole_sum = near_in[3]
            for index in range(1, groups):
                whole_sum = whole_sum + near_in[3 + index]
            finish_sums(whole_sum)

    return phase0, phase1, phase2, phase3, phase4


def reduce_scratch(groups, count, rows):
    return [
        pltpu.VMEM((7, count, rows, LANES), BF16),
        pltpu.VMEM((7, count, rows, LANES), BF16),
        pltpu.VMEM((count, rows, LANES), F32),
        pltpu.VMEM((count, rows, LANES), F32),
        pltpu.VMEM((count, rows, LANES), BF16),
        pltpu.VMEM((groups, rows, LANES), BF16),
    ]


def finish_kernel(link, count, dar_ref, db_ref, *refs):
    grads, sums_ref = refs[:6], refs[6]
    out_ref, roots_ref, flat, down, router, work, *more = refs[7:]

    def finish_sums(total):
        roots_ref[...] = jnp.sqrt(total / (total[:, 4:5] * D))

    assemble_rest(flat, grads, work)
    if link is None:
        assemble_first(flat, dar_ref, db_ref, down, router)
        out_ref[...] = align_out(flat, out_ref.shape[0], 0)
        finish_sums(sums_ref[...])
        return
    axes, sizes, spans = link
    parts_a, parts_b, near_out, near_in, *more = more
    boxes_a, boxes_b, sems = more[:7], more[7:14], more[14:]
    rows = out_ref.shape[0]
    split = spans[1][0]

    def align(parts, span):
        for group in range(*span):
            for low in range(8):
                parts[group - span[0], low] = align_out(flat, rows, (8 * group + low) * count)

    ring = Ring(axes, sizes, sems[0], sems[1])
    rest = reduce_phases(ring, spans[1], parts_b, boxes_b, True, sums_ref, (near_out, near_in))
    first = reduce_phases(
        Ring(axes, sizes, sems[2], sems[3]), spans[0], parts_a, boxes_a, False
    )
    align(parts_b, spans[1])
    rest[0]()
    assemble_first(flat, dar_ref, db_ref, down, router)
    align(parts_a, spans[0])
    first[0]()
    for step in range(1, 4):
        rest[step]()
        first[step]()
    rest[4](finish_sums)
    first[4]()

    @pl.when(ring.group < split)
    def _():
        out_ref[...] = boxes_a[6][...]

    @pl.when(ring.group >= split)
    def _():
        out_ref[...] = boxes_b[6][...]


def finish(dar, db, grads, sums, count, axes, sizes, spans):
    rows = shard_rows(count)
    groups = sizes[0] * sizes[1] // 8
    link = (axes, sizes, spans) if groups else None
    scratch = [
        pltpu.VMEM((flat_rows(count), LANES), F32),
        pltpu.VMEM((D, LANES), F32),
        pltpu.VMEM((D, LANES), F32),
        pltpu.VMEM((SINGLE_BLOCKS * D, LANES), F32),
    ]
    if link:
        widths = [end - begin for begin, end in spans]
        scratch += [pltpu.VMEM((width, 8, rows, LANES), F32) for width in widths]
        scratch += [
            pltpu.VMEM((4, *sums.shape), F32),
            pltpu.VMEM((3 + groups, *sums.shape), F32),
        ]
        for width in widths:
            scratch += reduce_scratch(groups, width, rows) + [pltpu.VMEM((rows, LANES), F32)]
        scratch += [pltpu.SemaphoreType.DMA((10 + 2 * groups,))] * 4
    vmem = pl.BlockSpec(memory_space=pltpu.VMEM)
    return pl.pallas_call(
        functools.partial(finish_kernel, link, count),
        in_specs=[vmem] * (3 + len(grads)),
        out_specs=[vmem] * 2,
        out_shape=[
            jax.ShapeDtypeStruct((rows, LANES), F32),
            jax.ShapeDtypeStruct(sums.shape, F32),
        ],
        scratch_shapes=scratch,
        compiler_params=params(collective_id=1, has_side_effects=True) if link else params(),
        name="finish",
    )(dar, db, *grads, sums)


def per_device(
    tokens,
    lengths,
    buckets,
    rel_table,
    gain_attn,
    gain_ff,
    w_qkv,
    w_out,
    w_in,
    w_down,
    adapters,
    cotangent,
    axes,
    sizes,
):
    seq_count, length, width = tokens.shape
    x = tokens.reshape(length, width)
    cot = cotangent.reshape(length, width)
    devices = sizes[0] * sizes[1]
    count = adapters.shape[0]
    rows = shard_rows(count)
    shard = jnp.pad(adapters, (0, rows * LANES - count)).reshape(rows, LANES)
    groups = devices // 8
    split_groups = min(-(-FIRST_COUNT // (8 * count)), max(groups - 1, 1))
    spans = ((0, split_groups), (split_groups, groups))
    reversed_buckets = jnp.pad(buckets[::-1], (0, 1)).reshape(1, 2 * length)
    qt, k, kt, v, vt, zg, offsets, ar_qkv, b_qkv, *packed = start(
        x, gain_attn, w_qkv, shard, reversed_buckets, rel_table.T, count, axes, sizes, spans
    )
    ot, lse = attend(lengths, offsets, qt, k, kt, vt)
    block_out, dmid, gt, sums, *grads = middle_part(
        lengths, ot, x, cot, gain_ff, w_out, w_in, w_down, packed
    )
    tokens_grad, dar_qkv, db_qkv = back_part(
        lengths,
        offsets,
        qt,
        k,
        kt,
        v,
        ot,
        gt,
        lse,
        x,
        gain_attn,
        w_qkv,
        ar_qkv,
        b_qkv,
        zg,
        dmid,
    )
    mine, roots = finish(dar_qkv, db_qkv, grads, sums, count, axes, sizes, spans)
    grad_shard = mine.reshape(-1)[:count]
    root_squares = roots[0, :4]
    return (
        block_out.reshape(tokens.shape),
        tokens_grad.reshape(tokens.shape),
        grad_shard,
        root_squares,
    )


def solution(mesh):
    axes = tuple(mesh.axis_names)
    sizes = tuple(mesh.shape[axis] for axis in axes)
    sequence = P(axes, None, None)
    placed = (
        sequence,
        P(axes),
        P(),
        P(),
        P(),
        P(),
        P(),
        P(),
        P(),
        P(),
        P(axes),
        sequence,
    )
    return jax.shard_map(
        functools.partial(per_device, axes=axes, sizes=sizes),
        mesh=mesh,
        in_specs=placed,
        out_specs=(sequence, sequence, P(axes), P()),
        check_vma=False,
    )
```

```python
import functools

import jax
import jax.numpy as jnp
from jax import lax
from jax.experimental import pallas as pl
from jax.experimental.pallas import tpu as pltpu
from jax.sharding import PartitionSpec as P

D = 768
FF = 3072
HEADS = 12
HDIM = 64
EXPERTS = 10
RANK = 4
FANS = ((D, D), (D, D), (D, D), (D, D), (D, FF), (FF, D))
COLS = EXPERTS * RANK
LANES = 128

EPSILON = 1e-06
MASKED = -1000000000.0
GELU_SCALE = 0.7978845608028654
GELU_CUBIC = 0.044715
LOG2E = 1.4426950408889634
LN2 = 0.6931471805599453
QUERY_SCALE = 0.125 * LOG2E

ROWS = 256
MIDDLE_ROWS = 512
CHUNK = 512
QBLOCK = 256
UP_ROWS = 48
DOWN_ROWS = 2 * COLS
VMEM_BYTES = 60 * 1024 * 1024

F32 = jnp.float32
BF16 = jnp.bfloat16


def dot(a, b):
    return lax.dot_general(a, b, (((1,), (0,)), ((), ())), preferred_element_type=F32)


def dot_nt(a, b):
    return lax.dot_general(a, b, (((1,), (1,)), ((), ())), preferred_element_type=F32)


def dot_tn(a, b):
    return lax.dot_general(a, b, (((0,), (0,)), ((), ())), preferred_element_type=F32)


def exact_dot(a, b):
    return lax.dot_general(
        a,
        b,
        (((1,), (0,)), ((), ())),
        preferred_element_type=F32,
        precision=lax.Precision.HIGHEST,
    )


def lane_iota(shape):
    return lax.broadcasted_iota(jnp.int32, shape, 1)


def row_iota(shape):
    return lax.broadcasted_iota(jnp.int32, shape, 0)


def gates_of(logits):
    weights = jnp.exp(logits - jnp.max(logits, axis=0, keepdims=True))
    return weights * (4.0 / jnp.sum(weights, axis=0, keepdims=True))


def gate_grads(grad_mixed, lowrank, gates):
    product = grad_mixed * lowrank
    summed = product
    for step in range(1, RANK):
        summed = summed + pltpu.roll(product, COLS - step, 0)
    centre = jnp.sum(gates * product, axis=0, keepdims=True)
    first = row_iota(gates.shape) % RANK == 0
    return grad_mixed * gates, jnp.where(first, gates * (summed - centre), 0.0)


def pad_rows(value, rows):
    return jnp.concatenate([value, jnp.zeros((rows - value.shape[0], value.shape[1]), F32)], axis=0)


def single_gates(packed):
    turned = packed.T
    lowrank = turned[:COLS]
    gates = gates_of(turned[COLS : 2 * COLS])
    mixed = pad_rows(lowrank * gates, LANES).astype(BF16)
    return lowrank, gates, mixed, mixed.T


def single_deltas(grad_mixed, lowrank, gates):
    parts = gate_grads(grad_mixed.T[:COLS], lowrank, gates)
    delta = pad_rows(jnp.concatenate(parts, axis=0), LANES).astype(BF16)
    return delta, delta.T


def rms_inverse(values):
    return lax.rsqrt(jnp.mean(values * values, axis=-1, keepdims=True) + EPSILON)


def rms_backward(values, gain, inverse, grad_normed):
    weighted = grad_normed * gain
    return inverse * weighted - values * (
        inverse * inverse * inverse * jnp.mean(values * weighted, axis=-1, keepdims=True)
    )


def params(**more):
    return pltpu.CompilerParams(vmem_limit_bytes=VMEM_BYTES, **more)


def whole(shape):
    zeros = (0,) * len(shape)
    return pl.BlockSpec(shape, lambda *_: zeros, pipeline_mode=pl.Buffered(1))


def bias_table(offset_row, length):
    spread = jnp.broadcast_to(offset_row, (LANES, 2 * length))
    return pltpu.roll(spread, 2 * length - (LANES - 1), 1, stride=1, stride_axis=0)


def add_bias(scores, table_ref, start, length):
    width = scores.shape[1]
    parts = []
    for block in range(length // LANES):
        offset = start - LANES * block + (length - LANES)
        parts.append(
            scores[block * LANES : (block + 1) * LANES] + table_ref[:, offset : offset + width]
        )
    return jnp.concatenate(parts, axis=0)


def key_extras(length_ref, shape, odd):
    lane = lane_iota(shape) - (0 if odd else HDIM)
    invalid = row_iota(shape) >= length_ref[0]
    extras = jnp.where((lane == 0) & invalid, MASKED, 0.0)
    return jnp.where((lane >= 1) & (lane <= 3), 1.0, extras).astype(BF16)


def head_lanes(odd):
    lane = lane_iota((1, LANES))
    return ((lane >= HDIM) if odd else (lane < HDIM)).astype(F32).astype(BF16)


def extra_rows(rows):
    width = rows[0].shape[1]
    index = row_iota((8, width))
    block = jnp.zeros((8, width), F32)
    for place, row in enumerate(rows):
        block = jnp.where(index == place, row, block)
    return jnp.concatenate([block, jnp.zeros((HDIM - 8, width), F32)], axis=0).astype(BF16)


def split_three(row):
    high = row.astype(BF16).astype(F32)
    middle = (row - high).astype(BF16).astype(F32)
    return high, middle, row - high - middle


def join_rows(rows, extras, odd):
    return jnp.concatenate([extras, rows] if odd else [rows, extras], axis=0)


def attend_kernel(
    length_ref, off_ref, qt_ref, k_ref, kt_ref, vt_ref, o_ref, lse_ref, table, key_more, plain
):
    length = k_ref.shape[0]
    step = pl.program_id(0)

    @pl.when(step == 0)
    def _():
        for odd in range(2):
            key_more[odd] = key_extras(length_ref, k_ref.shape, odd)

    starts = range(0, length, QBLOCK)
    ones = jnp.ones((1, length), F32)

    def half_of(odd):
        return slice(odd * HDIM, (odd + 1) * HDIM)

    def keys_of(odd):
        return k_ref[...] * head_lanes(odd) + key_more[odd]

    def values_of(odd):
        return jnp.concatenate([vt_ref[half_of(odd), :], jnp.ones((16, length), BF16)], axis=0)

    def finish(odd, start, shift, weights):
        columns = slice(start, start + QBLOCK)
        summed = dot(values_of(odd), weights)
        total = summed[HDIM : HDIM + 1]
        o_ref[half_of(odd), columns] = (summed[:HDIM] / total).astype(BF16)
        lse_ref[0, odd : odd + 1, columns] = shift + jnp.log2(total)
        return total

    def bounded(odd):
        offsets = off_ref[pl.ds(2 * step + odd, 1), :]
        table[odd] = bias_table(offsets, length)
        squares = jnp.square(kt_ref[half_of(odd), :].astype(F32))
        sizes = jnp.sum(squares, axis=0, keepdims=True)
        sizes = jnp.where(lane_iota(sizes.shape) < length_ref[0], sizes, 0.0)
        largest = jnp.max(sizes, axis=1, keepdims=True)
        rows = qt_ref[half_of(odd), :].astype(F32)
        norms = jnp.sqrt(jnp.sum(rows * rows, axis=0, keepdims=True) * largest)
        bound = 1.001 * norms + jnp.max(offsets, axis=1, keepdims=True)
        queries = join_rows(
            qt_ref[half_of(odd), :],
            extra_rows([ones] + [-part for part in split_three(bound)]),
            odd,
        )
        keys = keys_of(odd)
        scores = [dot(keys, queries[:, start : start + QBLOCK]) for start in starts]
        weights = [
            jnp.exp2(add_bias(part, table.at[odd], start, length)).astype(BF16)
            for part, start in zip(scores, starts)
        ]
        least = None
        for start, part in zip(starts, weights):
            total = finish(odd, start, bound[:, start : start + QBLOCK], part)
            least = total if least is None else jnp.minimum(least, total)
        return least

    def exact(odd):
        plain[...] = join_rows(qt_ref[half_of(odd), :], extra_rows([ones]), odd)
        keys = keys_of(odd)

        def block(index, _):
            columns = pl.ds(pl.multiple_of(index * LANES, LANES), LANES)
            raw = dot(keys, plain[:, columns])
            parts = []
            for row in range(0, length, LANES):
                place = pl.multiple_of(index * LANES - row + (length - LANES), LANES)
                parts.append(raw[row : row + LANES] + table[odd, :, pl.ds(place, LANES)])
            scores = jnp.concatenate(parts, axis=0)
            peak = jnp.max(scores, axis=0, keepdims=True)
            summed = dot(values_of(odd), jnp.exp2(scores - peak).astype(BF16))
            total = summed[HDIM : HDIM + 1]
            o_ref[half_of(odd), columns] = (summed[:HDIM] / total).astype(BF16)
            lse_ref[0, odd : odd + 1, columns] = peak + jnp.log2(total)
            return 0

        lax.fori_loop(0, length // LANES, block, 0)

    least = jnp.minimum(bounded(0), bounded(1))

    @pl.when(jnp.logical_not(jnp.min(least) > 2.0**-100))
    def _():
        for odd in range(2):
            exact(odd)


def attend(length_valid, offsets, qt, k, kt, vt):
    length = k.shape[0]
    turned = pl.BlockSpec((LANES, length), lambda p: (p, 0))
    natural = pl.BlockSpec((length, LANES), lambda p: (0, p))
    return pl.pallas_call(
        attend_kernel,
        grid=(HEADS // 2,),
        in_specs=[
            pl.BlockSpec(memory_space=pltpu.SMEM),
            whole(offsets.shape),
            turned,
            natural,
            turned,
            turned,
        ],
        out_specs=[turned, pl.BlockSpec((1, 2, length), lambda p: (p, 0, 0))],
        out_shape=[
            jax.ShapeDtypeStruct((D, length), BF16),
            jax.ShapeDtypeStruct((HEADS // 2, 2, length), F32),
        ],
        scratch_shapes=[
            pltpu.VMEM((2, LANES, 2 * length), F32),
            pltpu.VMEM((2, length, LANES), BF16),
            pltpu.VMEM((LANES, length), BF16),
        ],
        compiler_params=params(),
        name="attend",
    )(length_valid, offsets, qt, k, kt, vt)


def middle_kernel(
    length_ref,
    ot_ref,
    x_ref,
    cot_ref,
    gain_ref,
    w_out_ref,
    w_in_hbm,
    w_down_hbm,
    ar_out_ref,
    b_out_ref,
    ar_in_ref,
    b_in_ref,
    ar_down_ref,
    b_down_ref,
    out_ref,
    dmid_ref,
    gt_ref,
    sums_ref,
    dar_out_ref,
    db_out_ref,
    dar_in_ref,
    db_in_ref,
    dar_down_ref,
    db_down_ref,
    active,
    slope,
    sloped,
    grad_hidden,
    feeds,
    w_in_ref,
    w_down_ref,
    loaded,
):
    step = pl.program_id(0)
    loads = [
        pltpu.make_async_copy(w_in_hbm, w_in_ref, loaded.at[0]),
        pltpu.make_async_copy(w_down_hbm, w_down_ref, loaded.at[1]),
    ]

    @pl.when(step == 0)
    def _():
        for load in loads:
            load.start()
        for ref in (
            sums_ref,
            dar_out_ref,
            db_out_ref,
            dar_in_ref,
            db_in_ref,
            dar_down_ref,
            db_down_ref,
        ):
            ref[...] = jnp.zeros_like(ref)

    attended = ot_ref[...].T
    inputs = x_ref[...].astype(F32)
    gain = gain_ref[...].reshape(1, D)
    cot = cot_ref[...]

    packed_out = dot(attended, ar_out_ref[...])
    branch = dot(attended, w_out_ref[...])
    low_out, gates_out, mixed_out, natural = single_gates(packed_out)
    grad_mixed_down = dot_nt(cot, b_down_ref[...])
    branch = branch + dot(natural, b_out_ref[...])
    middle = inputs + branch
    inverse = rms_inverse(middle)
    normed = (middle * inverse * gain).astype(BF16)

    packed_in = dot(normed, ar_in_ref[...])
    low_in, gates_in, mixed_in, natural = single_gates(packed_in)

    def columns_of(index):
        return pl.ds(pl.multiple_of(index * CHUNK, CHUNK), CHUNK)

    def hidden_of(chunk):
        return dot(normed, w_in_ref[:, chunk]) + dot(natural, b_in_ref[:, chunk])

    def activate(chunk, values):
        grad_dense = dot_nt(cot, w_down_ref[chunk])
        square = values * values
        tangent = jnp.tanh(values * (GELU_SCALE + (GELU_SCALE * GELU_CUBIC) * square))
        half = 0.5 + 0.5 * tangent
        smooth = values * half
        active[:, chunk] = smooth.astype(BF16)
        steep = half + smooth * (1.0 - tangent) * (
            GELU_SCALE + (3.0 * GELU_SCALE * GELU_CUBIC) * square
        )
        slope[:, chunk] = steep.astype(BF16)
        sloped[:, chunk] = grad_dense * steep

    def forward_pair(pair, _):
        chunk_a = columns_of(2 * pair)
        chunk_b = columns_of(2 * pair + 1)
        hidden_a = hidden_of(chunk_a)
        hidden_b = hidden_of(chunk_b)
        activate(chunk_a, hidden_a)
        activate(chunk_b, hidden_b)
        return 0

    @pl.when(step == 0)
    def _():
        for load in loads:
            load.wait()

    lax.fori_loop(0, FF // (2 * CHUNK), forward_pair, 0)

    packed_down = dot(active[...], ar_down_ref[...])
    for first in range(0, D, 256):
        part = slice(first, first + 256)
        feeds[:, part] = dot(active[...], w_down_ref[:, part])
    feed = feeds[...]
    low_down, gates_down, mixed_down, natural = single_gates(packed_down)
    delta_down, natural_delta = single_deltas(grad_mixed_down, low_down, gates_down)
    db_down_ref[...] += dot(mixed_down[:UP_ROWS], cot)
    feed = feed + dot(natural, b_down_ref[...])
    output = middle + feed
    out_ref[...] = output.astype(BF16)

    for first in range(0, FF, CHUNK):
        chunk = slice(first, first + CHUNK)
        grad_low = dot_nt(natural_delta, ar_down_ref[chunk])
        grad_hidden[:, chunk] = (
            sloped[:, chunk] + grad_low * slope[:, chunk].astype(F32)
        ).astype(BF16)

    rows = row_iota((MIDDLE_ROWS, 1)) + step * MIDDLE_ROWS
    valid = (rows < length_ref[0]).astype(F32)
    lane = lane_iota((8, LANES))
    totals = jnp.where((lane == 4) & (step == 0), length_ref[0].astype(F32), 0.0)
    for place, member in enumerate((inputs, branch, feed, output)):
        kept = member * valid
        totals = jnp.where(lane == place, jnp.sum(kept * kept), totals)
    sums_ref[...] += totals

    grad_mixed = dot_nt(grad_hidden[...], b_in_ref[...])
    for first in range(0, D, 256):
        part = slice(first, first + 256)
        feeds[:, part] = dot_nt(grad_hidden[...], w_in_ref[part])
    grad_normed = feeds[...]
    delta_in, natural_delta = single_deltas(grad_mixed, low_in, gates_in)
    grad_normed = grad_normed + dot_nt(natural_delta, ar_in_ref[...])
    dar_in_ref[...] += dot(delta_in[:DOWN_ROWS], normed)

    grad_middle = cot.astype(F32) + rms_backward(middle, gain, inverse, grad_normed)
    dmid_ref[...] = grad_middle
    grad_branch = grad_middle.astype(BF16)
    grad_mixed = dot_nt(grad_branch, b_out_ref[...])
    grad_attended = dot_nt(grad_branch, w_out_ref[...])
    dar_down_ref[...] += dot(delta_down[:DOWN_ROWS], active[...])
    db_in_ref[...] += dot(mixed_in[:UP_ROWS], grad_hidden[...])
    delta_out, natural_delta = single_deltas(grad_mixed, low_out, gates_out)
    grad_attended = grad_attended + dot_nt(natural_delta, ar_out_ref[...])
    gt_ref[...] = grad_attended.astype(BF16).T
    dar_out_ref[...] += dot(delta_out[:DOWN_ROWS], attended)
    db_out_ref[...] += dot(mixed_out[:UP_ROWS], grad_branch)


def middle_part(length_valid, ot, x, cot, gain, w_out, w_in, w_down, adapters):
    length = x.shape[0]
    tile = pl.BlockSpec((MIDDLE_ROWS, D), lambda i: (i, 0))
    turned = pl.BlockSpec((D, MIDDLE_ROWS), lambda i: (0, i))
    grad_shapes = [
        jax.ShapeDtypeStruct(shape, F32)
        for fan_in, fan_out in FANS[3:]
        for shape in ((DOWN_ROWS, fan_in), (UP_ROWS, fan_out))
    ]
    out_shape = [
        jax.ShapeDtypeStruct((length, D), BF16),
        jax.ShapeDtypeStruct((length, D), F32),
        jax.ShapeDtypeStruct((D, length), BF16),
        jax.ShapeDtypeStruct((8, LANES), F32),
    ] + grad_shapes
    return pl.pallas_call(
        middle_kernel,
        grid=(length // MIDDLE_ROWS,),
        in_specs=[pl.BlockSpec(memory_space=pltpu.SMEM), turned, tile, tile]
        + [whole(gain.shape), whole(w_out.shape)]
        + [pl.BlockSpec(memory_space=pl.ANY)] * 2
        + [whole(member.shape) for member in adapters],
        out_specs=[tile, tile, turned] + [whole(member.shape) for member in out_shape[3:]],
        out_shape=out_shape,
        scratch_shapes=[
            pltpu.VMEM((MIDDLE_ROWS, FF), BF16),
            pltpu.VMEM((MIDDLE_ROWS, FF), BF16),
            pltpu.VMEM((MIDDLE_ROWS, FF), F32),
            pltpu.VMEM((MIDDLE_ROWS, FF), BF16),
            pltpu.VMEM((MIDDLE_ROWS, D), F32),
            pltpu.VMEM(w_in.shape, BF16),
            pltpu.VMEM(w_down.shape, BF16),
            pltpu.SemaphoreType.DMA((2,)),
        ],
        compiler_params=params(),
        name="middle_part",
    )(length_valid, ot, x, cot, gain, w_out, w_in, w_down, *adapters)


def attend_back(
    pair,
    length_ref,
    off_ref,
    qt_ref,
    k_ref,
    kt_ref,
    v_ref,
    ot_ref,
    gt_ref,
    lse_ref,
    grads_ref,
    table,
    key_more,
    weights_all,
    grads_all,
):
    length = k_ref.shape[0]
    lane = lane_iota((1, LANES))
    first_lanes = lane < HDIM
    grad_query_parts = []
    for odd in range(2):
        half = slice(odd * HDIM, (odd + 1) * HDIM)
        table[odd] = bias_table(off_ref[pl.ds(2 * pair + odd, 1), :], length)
        keys = k_ref[...] * head_lanes(odd) + key_more[odd]
        place = lane - (0 if odd else HDIM)
        value_more = ((place >= 0) & (place < 3)).astype(F32).astype(BF16)
        values = v_ref[...] * head_lanes(odd) + value_more
        ones = jnp.ones((1, length), F32)
        lse = lse_ref[0, odd : odd + 1, :]
        queries = join_rows(
            qt_ref[half, :], extra_rows([ones] + [-part for part in split_three(lse)]), odd
        )
        delta = jnp.sum(
            ot_ref[half, :].astype(F32) * gt_ref[half, :].astype(F32), axis=0, keepdims=True
        )
        grads = join_rows(
            gt_ref[half, :], extra_rows([-part for part in split_three(delta)]), odd
        )
        query_blocks = []
        previous = None
        for start in range(0, length, QBLOCK):
            columns = slice(start, start + QBLOCK)
            raw = dot(keys, queries[:, columns])
            grad_raw = dot(values, grads[:, columns])
            if previous is not None:
                query_blocks.append(dot(kt_ref[half, :], previous))
            weights = jnp.exp2(add_bias(raw, table.at[odd], start, length))
            weights_all[:, columns] = weights.astype(BF16)
            previous = (weights * grad_raw).astype(BF16)
            grads_all[:, columns] = previous
        query_blocks.append(dot(kt_ref[half, :], previous))
        grad_query_parts.append(jnp.concatenate(query_blocks, axis=1) * 0.125)
        grad_values = dot_nt(weights_all[...], gt_ref[...])
        grad_keys = dot_nt(grads_all[...], qt_ref[...]) * LN2
        if odd:
            grad_values = jnp.where(first_lanes, even_values, grad_values)
            grad_keys = jnp.where(first_lanes, even_keys, grad_keys)
        else:
            even_values, even_keys = grad_values, grad_keys
    columns = pl.ds(pl.multiple_of(pair * LANES, LANES), LANES)
    grads_ref[0, :, columns] = jnp.concatenate(grad_query_parts, axis=0).T.astype(BF16)
    grads_ref[1, :, columns] = grad_keys.astype(BF16)
    grads_ref[2, :, columns] = grad_values.astype(BF16)


def project_back(
    tile, x_ref, gain_ref, w_ref, ar_ref, b_ref, zg_ref, grads_ref, dmid_ref, out_ref, dar_ref, db_ref
):
    values = x_ref[...].astype(F32)
    gain = gain_ref[...].reshape(1, D)
    inverse = rms_inverse(values)
    normed = (values * inverse * gain).astype(BF16)
    lowrank = zg_ref[: 3 * COLS]
    gates = zg_ref[3 * COLS :]
    mixed = pad_rows(lowrank * gates, LANES).astype(BF16)
    rows = pl.ds(pl.multiple_of(tile * ROWS, ROWS), ROWS)
    grads = [grads_ref[index, rows] for index in range(3)]
    columns = [slice(index * D, (index + 1) * D) for index in range(3)]
    grad_mixed = jnp.zeros((ROWS, LANES), F32)
    for grad, lanes in zip(grads, columns):
        grad_mixed = grad_mixed + dot_nt(grad, b_ref[:, lanes])
    grad_normed = jnp.zeros((ROWS, D), F32)
    for grad, lanes in zip(grads, columns):
        grad_normed = grad_normed + dot_nt(grad, w_ref[:, lanes])
        db_ref[:, lanes] += dot(mixed, grad)
    turned = grad_mixed.T
    parts = []
    for first in range(0, 3 * COLS, COLS):
        place = slice(first, first + COLS)
        parts.append(gate_grads(turned[place], lowrank[place], gates[place]))
    delta = jnp.concatenate([part[0] for part in parts] + [part[1] for part in parts], axis=0)
    delta = pad_rows(delta, 2 * LANES).astype(BF16)
    grad_normed = grad_normed + dot_nt(delta.T, ar_ref[...])
    dar_ref[...] += dot(delta, normed)
    out_ref[...] = dmid_ref[...] + rms_backward(values, gain, inverse, grad_normed)


def back_kernel(*refs):
    length_ref = refs[0]
    heads_refs = refs[:9]
    x_ref, gain_ref, w_hbm, ar_ref, b_ref, zg_ref, dmid_ref = refs[9:16]
    out_ref, dar_ref, db_ref = refs[16:19]
    table, key_more, weights_all, grads_all, grads_ref, w_ref, loaded = refs[19:]
    step = pl.program_id(0)
    pairs = HEADS // 2
    load = pltpu.make_async_copy(w_hbm, w_ref, loaded)

    @pl.when(step == 0)
    def _():
        load.start()
        dar_ref[...] = jnp.zeros_like(dar_ref)
        db_ref[...] = jnp.zeros_like(db_ref)
        for odd in range(2):
            key_more[odd] = key_extras(length_ref, key_more.shape[1:], odd)

    @pl.when(step < pairs)
    def _():
        attend_back(step, *heads_refs, grads_ref, table, key_more, weights_all, grads_all)

    @pl.when(step == pairs)
    def _():
        load.wait()

    @pl.when(step >= pairs)
    def _():
        project_back(
            step - pairs,
            x_ref,
            gain_ref,
            w_ref,
            ar_ref,
            b_ref,
            zg_ref,
            grads_ref,
            dmid_ref,
            out_ref,
            dar_ref,
            db_ref,
        )


def back_part(
    length_valid, offsets, qt, k, kt, v, ot, gt, lse, x, gain, w_qkv, ar_qkv, b_qkv, zg, dmid
):
    length = k.shape[0]
    pairs = HEADS // 2

    def pair_of(i):
        return jnp.minimum(i, pairs - 1)

    def tile_of(i):
        return jnp.maximum(i - pairs, 0)

    turned = pl.BlockSpec((LANES, length), lambda i: (pair_of(i), 0))
    natural = pl.BlockSpec((length, LANES), lambda i: (0, pair_of(i)))
    tile = pl.BlockSpec((ROWS, D), lambda i: (tile_of(i), 0))
    out_shape = [
        jax.ShapeDtypeStruct((length, D), F32),
        jax.ShapeDtypeStruct((2 * LANES, D), F32),
        jax.ShapeDtypeStruct((LANES, 3 * D), F32),
    ]
    return pl.pallas_call(
        back_kernel,
        grid=(pairs + length // ROWS,),
        in_specs=[
            pl.BlockSpec(memory_space=pltpu.SMEM),
            whole(offsets.shape),
            turned,
            natural,
            turned,
            natural,
            turned,
            turned,
            pl.BlockSpec((1, 2, length), lambda i: (pair_of(i), 0, 0)),
            tile,
            whole((D,)),
            pl.BlockSpec(memory_space=pl.ANY),
            whole(ar_qkv.shape),
            whole(b_qkv.shape),
            pl.BlockSpec((6 * COLS, ROWS), lambda i: (0, tile_of(i))),
            tile,
        ],
        out_specs=[tile] + [whole(member.shape) for member in out_shape[1:]],
        out_shape=out_shape,
        scratch_shapes=[
            pltpu.VMEM((2, LANES, 2 * length), F32),
            pltpu.VMEM((2, length, LANES), BF16),
            pltpu.VMEM((length, length), BF16),
            pltpu.VMEM((length, length), BF16),
            pltpu.VMEM((3, length, D), BF16),
            pltpu.VMEM(w_qkv.shape, BF16),
            pltpu.SemaphoreType.DMA,
        ],
        compiler_params=params(),
        name="back_part",
    )(length_valid, offsets, qt, k, kt, v, ot, gt, lse, x, gain, w_qkv, ar_qkv, b_qkv, zg, dmid)


PARAM_ROWS = sum((COLS + EXPERTS) * fan_in + COLS * fan_out for fan_in, fan_out in FANS) // LANES


def piece_rows():
    result = []
    row = 0
    for fan_in, fan_out in FANS:
        starts = []
        for count in (fan_in * COLS, COLS * fan_out, fan_in * EXPERTS):
            starts.append(row)
            row += count // LANES
        result.append(tuple(starts))
    return result


def shard_rows(count):
    return -(-count // (LANES * 16)) * 16


def align_in(flat_ref, shard, start):
    first, shift = divmod(start, LANES)
    rows = shard.shape[0]
    if shift == 0:
        flat_ref[first : first + rows] = shard
        return
    turned = pltpu.roll(shard, shift, 1)
    lane = lane_iota((1, LANES))
    zeros = jnp.zeros((8, LANES), F32)
    upper = jnp.concatenate([turned, zeros], axis=0)
    lower = pltpu.roll(upper, 1, 0)
    kept = flat_ref[first : first + 8]
    merged = jnp.where(lane >= shift, upper, lower)
    inside = (row_iota((8, LANES)) == 0) & (lane_iota((8, LANES)) < shift)
    flat_ref[first : first + 8] = jnp.where(inside, kept, merged[:8])
    flat_ref[first + 8 : first + 8 + rows] = merged[8:]


def align_out(flat_ref, rows, start):
    first, shift = divmod(start, LANES)
    if shift == 0:
        return flat_ref[first : first + rows]
    block = flat_ref[first : first + rows + 8]
    turned = pltpu.roll(block, LANES - shift, 1)
    below = pltpu.roll(turned, rows + 7, 0)
    lane = lane_iota((1, LANES))
    return jnp.where(lane < LANES - shift, turned, below)[:rows]


GROUP = 64


def narrow_to_rows(flat_ref, fan_in, items, out_ref, begin=0):
    groups = fan_in // GROUP
    lane = lane_iota((1, LANES))
    lines = [
        [
            flat_ref[pl.ds(base + k, groups, stride=width * GROUP // LANES), :]
            for k in range(width * GROUP // LANES)
        ]
        for base, width, _ in items
    ]
    for b in range(GROUP):
        result = jnp.zeros((groups, LANES), F32)
        for line, (_, width, place) in zip(lines, items):
            first, shift = divmod(width * b, LANES)
            amount = (place - shift) % LANES
            value = line[first] if amount == 0 else pltpu.roll(line[first], amount, 1)
            if shift + width > LANES:
                value = jnp.where(
                    lane < place + LANES - shift, value, pltpu.roll(line[first + 1], amount, 1)
                )
            inside = (lane >= place) & (lane < place + width)
            result = jnp.where(inside, value, result)
        out_ref[pl.ds(begin + b, groups, stride=GROUP), :] = result


def rows_to_narrow(in_ref, fan_in, items, flat_ref, begin=0):
    groups = fan_in // GROUP
    lane = lane_iota((1, LANES))
    lines = [
        [jnp.zeros((groups, LANES), F32) for _ in range(width * GROUP // LANES)]
        for _, width, _ in items
    ]
    for b in range(GROUP):
        source = in_ref[pl.ds(begin + b, groups, stride=GROUP), :]
        for line, (_, width, place) in zip(lines, items):
            first, shift = divmod(width * b, LANES)
            amount = (shift - place) % LANES
            value = source if amount == 0 else pltpu.roll(source, amount, 1)
            inside = (lane >= shift) & (lane < shift + width)
            line[first] = jnp.where(inside, value, line[first])
            if shift + width > LANES:
                line[first + 1] = jnp.where(lane < shift + width - LANES, value, line[first + 1])
    for line, (base, width, _) in zip(lines, items):
        for k, value in enumerate(line):
            flat_ref[pl.ds(base + k, groups, stride=width * GROUP // LANES), :] = value


def single_items(block):
    starts = piece_rows()
    after_out, after_in = (block + 4) // 5, (block + 2) // 4
    down = (block - 2) * after_in
    bases = []
    for piece, width in ((0, COLS), (2, EXPERTS)):
        out, inner, outer = (starts[index][piece] for index in range(3, 6))
        base = out + (inner - out) * after_out + (outer - inner) * after_in
        bases.append(base + down * (D * width // LANES))
    return [(bases[0], COLS, 0), (bases[1], EXPERTS, COLS)]


SINGLE_BLOCKS = 2 + FF // D


def spread_matrix(experts, source, place):
    row = row_iota((LANES, LANES)) - source
    lane = lane_iota((LANES, LANES)) - place
    hit = (lane >= RANK * row) & (lane < RANK * row + RANK) & (row >= 0) & (row < experts)
    return jnp.where(hit, 1.0, 0.0)


def keep_matrix():
    row = row_iota((LANES, LANES))
    return jnp.where((row == lane_iota((LANES, LANES))) & (row < COLS), 1.0, 0.0)


FIRST_COUNT = sum((COLS + EXPERTS) * fan_in + COLS * fan_out for fan_in, fan_out in FANS[:3])


def unpack_ups(flat, base, fan_out, first, out_ref, column):
    width = fan_out // LANES
    above = jnp.zeros((first, LANES), F32)
    below = jnp.zeros((LANES - COLS - first, LANES), F32)
    for k in range(width):
        part = flat[pl.ds(base + k, COLS, stride=width), :]
        parts = [part, below] if first == 0 else [above, part, below]
        lanes = slice(column + k * LANES, column + (k + 1) * LANES)
        out_ref[:, lanes] = jnp.concatenate(parts, axis=0).astype(BF16)


def unpack_first(flat, ar_ref, b_ref, down, router):
    starts = piece_rows()
    narrow_to_rows(flat, D, [(starts[k][0], COLS, k * COLS) for k in range(3)], down)
    narrow_to_rows(flat, D, [(starts[k][2], EXPERTS, k * EXPERTS) for k in range(3)], router)
    routers = router[...].astype(BF16)
    for half in range(2):
        matrix = spread_matrix(3 * EXPERTS, 0, 3 * COLS - half * LANES).astype(BF16)
        packed = dot(routers, matrix)
        packed = packed if half else packed + down[...]
        ar_ref[:, half * LANES : (half + 1) * LANES] = packed.astype(BF16)
    for index in range(3):
        unpack_ups(flat, starts[index][1], D, index * COLS, b_ref, index * D)


def flat_rows(count):
    return PARAM_ROWS + shard_rows(count) + 20


def unpack_rest(flat, outs, work):
    starts = piece_rows()
    matrix = (keep_matrix() + spread_matrix(EXPERTS, COLS, COLS)).astype(BF16)

    def block(index, _):
        narrow_to_rows(flat, D, single_items(index), work, index * D)
        return 0

    lax.fori_loop(0, SINGLE_BLOCKS, block, 0)
    begin = 0
    for index in range(3, 6):
        fan_in, fan_out = FANS[index]
        ar_ref, b_ref = outs[2 * index - 6], outs[2 * index - 5]
        ar_ref[...] = dot(work[begin : begin + fan_in].astype(BF16), matrix).astype(BF16)
        unpack_ups(flat, starts[index][1], fan_out, 0, b_ref, 0)
        begin += fan_in


def split_dot(value, matrix):
    high = value.astype(BF16)
    return dot(high, matrix) + dot((value - high.astype(F32)).astype(BF16), matrix)


def first_of_four(experts, source, place):
    row = row_iota((LANES, LANES)) - source
    lane = lane_iota((LANES, LANES)) - place
    hit = (row == RANK * lane) & (lane >= 0) & (lane < experts)
    return jnp.where(hit, 1.0, 0.0)


def assemble_ups(flat, base, fan_out, first, grad_ref, column):
    width = fan_out // LANES
    for k in range(width):
        lanes = slice(column + k * LANES, column + (k + 1) * LANES)
        flat[pl.ds(base + k, COLS, stride=width), :] = grad_ref[first : first + COLS, lanes]


def assemble_rest(flat, grads, work):
    starts = piece_rows()
    matrix = (keep_matrix() + first_of_four(EXPERTS, COLS, COLS)).astype(BF16)
    begin = 0
    for index in range(3, 6):
        fan_in, fan_out = FANS[index]
        dar_ref, db_ref = grads[2 * index - 6], grads[2 * index - 5]
        work[begin : begin + fan_in] = split_dot(pad_rows(dar_ref[...], LANES).T, matrix)
        assemble_ups(flat, starts[index][1], fan_out, 0, db_ref, 0)
        begin += fan_in

    def block(index, _):
        rows_to_narrow(work, D, single_items(index), flat, index * D)
        return 0

    lax.fori_loop(0, SINGLE_BLOCKS, block, 0)


def assemble_first(flat, dar_ref, db_ref, down, router):
    starts = piece_rows()
    down[...] = dar_ref[:LANES].T
    rows_to_narrow(down, D, [(starts[k][0], COLS, k * COLS) for k in range(3)], flat)
    first_router = 3 * COLS
    turned = dar_ref[first_router : first_router + LANES].T
    router[...] = split_dot(turned, first_of_four(3 * EXPERTS, 0, 0).astype(BF16))
    rows_to_narrow(router, D, [(starts[k][2], EXPERTS, k * EXPERTS) for k in range(3)], flat)
    for index in range(3):
        assemble_ups(flat, starts[index][1], D, index * COLS, db_ref, index * D)


MESH = pl.DeviceIdType.MESH


def place_of(axes, sizes):
    me = lax.axis_index(axes[0]) * sizes[1] + lax.axis_index(axes[1])

    def coordinates(number):
        return (number // sizes[1], number % sizes[1])

    return me, coordinates


def partners_of(me):
    low = me % 8
    core = low % 2
    y = (low // 2) % 2
    x = low // 4
    over_x = low + 4 * (1 - 2 * x)
    over_y = low + 2 * (1 - 2 * y)
    first = over_x * (1 - core) + over_y * core
    second = over_y * (1 - core) + over_x * core
    both = first + second - low
    other = 1 - 2 * core
    return low, first, second, both, other, over_x, over_y


def greet(peers):
    for peer in peers:
        pl.semaphore_signal(
            pltpu.get_barrier_semaphore(), inc=1, device_id=peer, device_id_type=MESH
        )


def await_greetings(count):
    pl.semaphore_wait(pltpu.get_barrier_semaphore(), count)


class Ring:
    def __init__(self, axes, sizes, send, receive):
        self.me, self.coordinates = place_of(axes, sizes)
        self.groups = sizes[0] * sizes[1] // 8
        self.group = self.me // 8
        places = partners_of(self.me)
        self.low, self.first, self.second, self.both, self.other, self.over_x, self.over_y = places
        self.mate = self.low + self.other
        self.send, self.receive = send, receive
        self.copies = {}

    def device(self, group, low):
        return self.coordinates(group * 8 + low)

    def greet(self):
        peers = [
            self.device((self.group + step) % self.groups, self.low)
            for step in range(1, self.groups)
        ]
        peers += [self.device(self.group, low) for low in (self.first, self.second, self.mate)]
        greet(peers)

    def await_greetings(self):
        await_greetings(self.groups + 2)

    def copy(self, slot, source, target, peer, arrival=None):
        return pltpu.make_async_remote_copy(
            src_ref=source,
            dst_ref=target,
            send_sem=self.send.at[slot],
            recv_sem=self.receive.at[slot if arrival is None else arrival],
            device_id=peer,
            device_id_type=MESH,
        )


def gather_phases(ring, span, shard_ref, out_ref, local, greets):
    begin, end = span
    base = ring.groups
    inside = (ring.group >= begin) & (ring.group < end)

    def around(step):
        target = (ring.group + step) % ring.groups
        return ring.copy(
            step,
            shard_ref,
            out_ref.at[ring.group - begin, ring.low],
            ring.device(target, ring.low),
            base + 7 + ring.group,
        )

    def arrived(group):
        return ring.copy(
            0,
            shard_ref,
            out_ref.at[group - begin, ring.low],
            ring.device(group, ring.low),
            base + 7 + group,
        )

    def push(slot, part, partner):
        return ring.copy(
            base + slot, out_ref.at[:, part], out_ref.at[:, part], ring.device(ring.group, partner)
        )

    one = push(0, ring.low, ring.first)
    two = push(1, ring.low, ring.second)
    three = push(2, ring.first, ring.second)
    cores = [
        push(3 + index, part, ring.mate)
        for index, part in enumerate((ring.low, ring.first, ring.second, ring.both))
    ]

    def own():
        return pltpu.make_async_copy(
            shard_ref, out_ref.at[ring.group - begin, ring.low], local
        )

    def phase0():
        if greets:
            ring.greet()
            ring.await_greetings()

        @pl.when(inside)
        def _():
            own().start()
            for step in range(1, ring.groups):
                around(step).start()

    def phase1():
        @pl.when(inside)
        def _():
            own().wait()
            for step in range(1, ring.groups):
                around(step).wait_send()

        for group in range(begin, end):

            @pl.when(ring.group != group)
            def _():
                arrived(group).wait_recv()

        for copy in (one, two, cores[0]):
            copy.start()

    def phase2():
        one.wait()
        three.start()
        cores[1].start()

    def phase3():
        two.wait()
        cores[2].start()
        three.wait()
        cores[3].start()

    def phase4():
        for copy in cores:
            copy.wait()

    return phase0, phase1, phase2, phase3, phase4


def gather_semaphores(groups):
    return [
        pltpu.SemaphoreType.DMA((groups + 7,)),
        pltpu.SemaphoreType.DMA((2 * groups + 7,)),
        pltpu.SemaphoreType.DMA,
    ]


def start_kernel(
    link,
    count,
    shard_ref,
    buckets_ref,
    table_ref,
    gain_ref,
    x_hbm,
    w_hbm,
    *refs,
):
    hbm_outs, off_ref, ar_ref, b_ref = refs[:6], refs[6], refs[7], refs[8]
    rest_refs = refs[9:15]
    x_ref, w_ref, normed, dense = refs[15:19]
    outs = refs[19:25]
    qt_ref, k_ref, kt_ref, v_ref, vt_ref, zg_ref = outs
    flat, down, router, work, offsets_ref, loaded, stored, *more = refs[25:]
    loads = [
        pltpu.make_async_copy(x_hbm, x_ref, loaded.at[0]),
        pltpu.make_async_copy(w_hbm, w_ref, loaded.at[1]),
    ]
    stores = [
        pltpu.make_async_copy(source, target, stored.at[index])
        for index, (source, target) in enumerate(zip(outs, hbm_outs))
    ]
    for load in loads:
        load.start()
    if link is None:
        first = [lambda: None] * 5
        rest = first

        def shard_of(index):
            return shard_ref[...]
    else:
        axes, sizes, spans = link
        land_a, land_b, *sems = more
        first = gather_phases(
            Ring(axes, sizes, *sems[:2]), spans[0], shard_ref, land_a, sems[2], True
        )
        rest = gather_phases(
            Ring(axes, sizes, *sems[3:5]), spans[1], shard_ref, land_b, sems[5], False
        )

        def shard_of(index):
            group, low = divmod(index, 8)
            begin = spans[1][0]
            return land_a[group, low] if group < begin else land_b[group - begin, low]

    length = x_ref.shape[0]

    def dense_tile(index):
        rows = slice(index * length // 2, (index + 1) * length // 2)
        values = x_ref[rows].astype(F32)
        low = (values * rms_inverse(values) * gain_ref[...].reshape(1, D)).astype(BF16)
        normed[rows] = low

        def columns(part, _):
            lanes = pl.ds(pl.multiple_of(part * D, D), D)
            dense[rows, lanes] = dot(normed[rows], w_ref[:, lanes])
            return 0

        lax.fori_loop(0, 3, columns, 0)

    def project():
        packed = dot(normed[...], ar_ref[...]).T
        lowrank = packed[: 3 * COLS]
        gates = jnp.concatenate(
            [gates_of(packed[place : place + COLS]) for place in range(3 * COLS, 6 * COLS, COLS)],
            axis=0,
        )
        zg_ref[: 3 * COLS] = lowrank
        zg_ref[3 * COLS :] = gates
        stores[5].start()
        mixed = pad_rows(lowrank * gates, LANES).astype(BF16).T
        for part in range(3):
            columns = slice(part * D, (part + 1) * D)
            value = dense[:, columns] + dot(mixed, b_ref[:, columns])
            if part == 0:
                qt_ref[...] = (value * QUERY_SCALE).astype(BF16).T
                stores[0].start()
            else:
                low = value.astype(BF16)
                natural, turned = ((k_ref, kt_ref), (v_ref, vt_ref))[part - 1]
                natural[...] = low
                turned[...] = low.T
                stores[2 * part - 1].start()
                stores[2 * part].start()

    first[0]()
    rest[0]()
    for load in loads:
        load.wait()
    dense_tile(0)
    first[1]()
    rest[1]()
    dense_tile(1)
    first[2]()
    buckets = buckets_ref[...].reshape(1, buckets_ref.shape[0])
    hits = jnp.where(row_iota((table_ref.shape[1], buckets.shape[1])) == buckets, LOG2E, 0.0)
    offsets_ref[...] = jnp.zeros_like(offsets_ref)
    offsets_ref[:, : buckets.shape[1]] = exact_dot(table_ref[...], hits)
    flip = (row_iota((LANES, LANES)) + lane_iota((LANES, LANES)) == LANES - 1).astype(F32)
    blocks = offsets_ref.shape[1] // LANES
    for block in range(blocks):
        lanes = slice(block * LANES, (block + 1) * LANES)
        turned = slice((blocks - 1 - block) * LANES, (blocks - block) * LANES)
        off_ref[:, turned] = exact_dot(offsets_ref[:, lanes], flip)
    off_ref[...] = pltpu.roll(off_ref[...], offsets_ref.shape[1] - 1, 1)
    first[3]()
    rest[2]()
    first[4]()
    for index in range(-(-FIRST_COUNT // count)):
        align_in(flat, shard_of(index).astype(F32), index * count)
    unpack_first(flat, ar_ref, b_ref, down, router)
    rest[3]()
    project()
    rest[4]()
    for index in range(FIRST_COUNT // count, PARAM_ROWS * LANES // count):
        align_in(flat, shard_of(index).astype(F32), index * count)
    unpack_rest(flat, rest_refs, work)
    for store in stores:
        store.wait()


def start(x, gain, w_qkv, shard, buckets, rel_table, count, axes, sizes, spans):
    length = x.shape[0]
    groups = sizes[0] * sizes[1] // 8
    link = (axes, sizes, spans) if groups else None
    rest_shapes = [
        shape for fan_in, fan_out in FANS[3:] for shape in ((fan_in, LANES), (LANES, fan_out))
    ]
    wide = [
        ((D, length), BF16),
        ((length, D), BF16),
        ((D, length), BF16),
        ((length, D), BF16),
        ((D, length), BF16),
        ((6 * COLS, length), F32),
    ]
    small = [
        ((HEADS, 2 * length), F32),
        ((D, 2 * LANES), BF16),
        ((LANES, 3 * D), BF16),
    ] + [(shape, BF16) for shape in rest_shapes]
    scratch = [
        pltpu.VMEM(x.shape, BF16),
        pltpu.VMEM(w_qkv.shape, BF16),
        pltpu.VMEM(x.shape, BF16),
        pltpu.VMEM((length, 3 * D), F32),
    ]
    scratch += [pltpu.VMEM(*member) for member in wide]
    scratch += [
        pltpu.VMEM((flat_rows(count), LANES), F32),
        pltpu.VMEM((D, LANES), F32),
        pltpu.VMEM((D, LANES), F32),
        pltpu.VMEM((SINGLE_BLOCKS * D, LANES), F32),
        pltpu.VMEM((HEADS, 2 * length), F32),
        pltpu.SemaphoreType.DMA((2,)),
        pltpu.SemaphoreType.DMA((len(wide),)),
    ]
    if link:
        scratch += [pltpu.VMEM((end - begin, 8, *shard.shape), BF16) for begin, end in spans]
        scratch += gather_semaphores(groups) * 2
    vmem = pl.BlockSpec(memory_space=pltpu.VMEM)
    anywhere = pl.BlockSpec(memory_space=pl.ANY)
    return pl.pallas_call(
        functools.partial(start_kernel, link, count),
        in_specs=[vmem] * 4 + [anywhere] * 2,
        out_specs=[anywhere] * len(wide) + [vmem] * len(small),
        out_shape=[jax.ShapeDtypeStruct(*member) for member in wide + small],
        scratch_shapes=scratch,
        compiler_params=params(collective_id=0, has_side_effects=True) if link else params(),
        name="start",
    )(shard, buckets, rel_table, gain, x, w_qkv)


def reduce_phases(ring, span, parts_ref, boxes, greets, sums_ref=None, sum_boxes=None):
    begin, end = span
    outbox, inbox, half, own, far_out, far_in, out_ref = boxes
    groups = ring.groups
    inside = (ring.group >= begin) & (ring.group < end)
    core_parts = (ring.first, ring.both, ring.second, ring.low)
    near = [ring.mate] * 4 + [ring.second, ring.second, ring.first]

    def push(slot):
        return ring.copy(slot, outbox.at[slot], inbox.at[slot], ring.device(ring.group, near[slot]))

    def fill(slot, value):
        outbox[slot] = value.astype(BF16)
        push(slot).start()

    def around(group):
        return ring.copy(
            7 + group - begin,
            far_out.at[group - begin],
            far_in.at[ring.group],
            ring.device(group, ring.low),
            7 + ring.group,
        )

    def arrived(group):
        return ring.copy(
            7,
            far_out.at[0],
            far_in.at[group],
            ring.device(group, ring.low),
            7 + group,
        )

    base = 7 + groups
    sum_peers = (ring.mate, ring.over_x, ring.over_y)

    def push_sums(slot):
        near_out, near_in = sum_boxes
        return ring.copy(
            base + slot,
            near_out.at[slot],
            near_in.at[slot],
            ring.device(ring.group, sum_peers[slot]),
        )

    def around_sums(step):
        near_out, near_in = sum_boxes
        target = (ring.group + step) % groups
        return ring.copy(
            base + 2 + step,
            near_out.at[3],
            near_in.at[3 + ring.group],
            ring.device(target, ring.low),
        )

    def start_sums(slot, value):
        if sum_boxes is not None:
            sum_boxes[0][slot] = value
            push_sums(slot).start()

    def phase0():
        if greets:
            ring.await_greetings()
        if sum_boxes is not None:
            start_sums(0, sums_ref[...])
        for slot, part in enumerate(core_parts):
            fill(slot, parts_ref[:, part + ring.other])

    def phase1():
        push(0).wait()
        fill(4, parts_ref[:, ring.second] + inbox[0].astype(F32))
        push(1).wait()
        fill(5, parts_ref[:, ring.both] + inbox[1].astype(F32))
        if sum_boxes is not None:
            push_sums(0).wait()
            start_sums(1, sum_boxes[0][0] + sum_boxes[1][0])

    def add1():
        push(2).wait()
        half[...] = parts_ref[:, ring.first] + inbox[2].astype(F32)
        push(3).wait()
        own[...] = parts_ref[:, ring.low] + inbox[3].astype(F32)

    def phase2():
        push(5).wait()
        fill(6, half[...] + inbox[5].astype(F32))
        if sum_boxes is not None:
            push_sums(1).wait()
            start_sums(2, sum_boxes[0][1] + sum_boxes[1][1])

    def add2():
        push(4).wait()
        own[...] = own[...] + inbox[4].astype(F32)

    def phase3():
        push(6).wait()
        own[...] = own[...] + inbox[6].astype(F32)
        far_out[...] = own[...].astype(BF16)
        for group in range(begin, end):

            @pl.when(ring.group != group)
            def _():
                around(group).start()

        if sum_boxes is not None:
            near_out, near_in = sum_boxes
            push_sums(2).wait()
            near_out[3] = near_out[2] + near_in[2]
            for step in range(1, groups):
                around_sums(step).start()
            near_in[3 + ring.group] = near_out[3]

    def phase4(finish_sums=None):
        for group in range(begin, end):

            @pl.when(ring.group != group)
            def _():
                around(group).wait_send()

        @pl.when(inside)
        def _():
            for group in range(groups):

                @pl.when(ring.group != group)
                def _():
                    arrived(group).wait_recv()

            total = own[ring.group - begin]
            for step in range(1, groups):
                total = total + far_in[(ring.group + step) % groups].astype(F32)
            out_ref[...] = total

        if sum_boxes is not None:
            near_out, near_in = sum_boxes
            for step in range(1, groups):
                around_sums(step).wait()
            whole_sum = near_in[3]
            for index in range(1, groups):
                whole_sum = whole_sum + near_in[3 + index]
            finish_sums(whole_sum)

    return phase0, phase1, add1, phase2, add2, phase3, phase4


def reduce_scratch(groups, count, rows):
    return [
        pltpu.VMEM((7, count, rows, LANES), BF16),
        pltpu.VMEM((7, count, rows, LANES), BF16),
        pltpu.VMEM((count, rows, LANES), F32),
        pltpu.VMEM((count, rows, LANES), F32),
        pltpu.VMEM((count, rows, LANES), BF16),
        pltpu.VMEM((groups, rows, LANES), BF16),
    ]


def finish_kernel(link, count, dar_ref, db_ref, *refs):
    grads, sums_ref = refs[:6], refs[6]
    out_ref, roots_ref, flat, down, router, work, *more = refs[7:]

    def finish_sums(total):
        roots_ref[...] = jnp.sqrt(total / (total[:, 4:5] * D))

    if link is not None:
        axes, sizes, spans = link
        parts_a, parts_b, near_out, near_in, *more = more
        boxes_a, boxes_b, sems = more[:7], more[7:14], more[14:]
        ring = Ring(axes, sizes, sems[0], sems[1])
        ring.greet()
    assemble_rest(flat, grads, work)
    if link is None:
        assemble_first(flat, dar_ref, db_ref, down, router)
        out_ref[...] = align_out(flat, out_ref.shape[0], 0)
        finish_sums(sums_ref[...])
        return
    rows = out_ref.shape[0]
    split = spans[1][0]

    def align(parts, span):
        for group in range(*span):
            for low in range(8):
                parts[group - span[0], low] = align_out(flat, rows, (8 * group + low) * count)

    rest = reduce_phases(ring, spans[1], parts_b, boxes_b, True, sums_ref, (near_out, near_in))
    first = reduce_phases(
        Ring(axes, sizes, sems[2], sems[3]), spans[0], parts_a, boxes_a, False
    )
    align(parts_b, spans[1])
    rest[0]()
    assemble_first(flat, dar_ref, db_ref, down, router)
    rest[1]()
    align(parts_a, spans[0])
    first[0]()
    rest[2]()
    for step in (1, 2):
        first[step]()
    for step in (3, 4, 5):
        rest[step]()
        first[step]()
    rest[6](finish_sums)
    first[6]()

    @pl.when(ring.group < split)
    def _():
        out_ref[...] = boxes_a[6][...]

    @pl.when(ring.group >= split)
    def _():
        out_ref[...] = boxes_b[6][...]


def finish(dar, db, grads, sums, count, axes, sizes, spans):
    rows = shard_rows(count)
    groups = sizes[0] * sizes[1] // 8
    link = (axes, sizes, spans) if groups else None
    scratch = [
        pltpu.VMEM((flat_rows(count), LANES), F32),
        pltpu.VMEM((D, LANES), F32),
        pltpu.VMEM((D, LANES), F32),
        pltpu.VMEM((SINGLE_BLOCKS * D, LANES), F32),
    ]
    if link:
        widths = [end - begin for begin, end in spans]
        scratch += [pltpu.VMEM((width, 8, rows, LANES), F32) for width in widths]
        scratch += [
            pltpu.VMEM((4, *sums.shape), F32),
            pltpu.VMEM((3 + groups, *sums.shape), F32),
        ]
        for width in widths:
            scratch += reduce_scratch(groups, width, rows) + [pltpu.VMEM((rows, LANES), F32)]
        scratch += [pltpu.SemaphoreType.DMA((10 + 2 * groups,))] * 4
    vmem = pl.BlockSpec(memory_space=pltpu.VMEM)
    return pl.pallas_call(
        functools.partial(finish_kernel, link, count),
        in_specs=[vmem] * (3 + len(grads)),
        out_specs=[vmem] * 2,
        out_shape=[
            jax.ShapeDtypeStruct((rows, LANES), F32),
            jax.ShapeDtypeStruct(sums.shape, F32),
        ],
        scratch_shapes=scratch,
        compiler_params=params(collective_id=1, has_side_effects=True) if link else params(),
        name="finish",
    )(dar, db, *grads, sums)


def per_device(
    tokens,
    lengths,
    buckets,
    rel_table,
    gain_attn,
    gain_ff,
    w_qkv,
    w_out,
    w_in,
    w_down,
    adapters,
    cotangent,
    axes,
    sizes,
):
    seq_count, length, width = tokens.shape
    x = tokens.reshape(length, width)
    cot = cotangent.reshape(length, width)
    devices = sizes[0] * sizes[1]
    count = adapters.shape[0]
    rows = shard_rows(count)
    shard = jnp.pad(adapters, (0, rows * LANES - count)).reshape(rows, LANES)
    groups = devices // 8
    split_groups = min(-(-FIRST_COUNT // (8 * count)), max(groups - 1, 1))
    spans = ((0, split_groups), (split_groups, groups))
    qt, k, kt, v, vt, zg, offsets, ar_qkv, b_qkv, *packed = start(
        x, gain_attn, w_qkv, shard, buckets, rel_table.T, count, axes, sizes, spans
    )
    ot, lse = attend(lengths, offsets, qt, k, kt, vt)
    block_out, dmid, gt, sums, *grads = middle_part(
        lengths, ot, x, cot, gain_ff, w_out, w_in, w_down, packed
    )
    tokens_grad, dar_qkv, db_qkv = back_part(
        lengths,
        offsets,
        qt,
        k,
        kt,
        v,
        ot,
        gt,
        lse,
        x,
        gain_attn,
        w_qkv,
        ar_qkv,
        b_qkv,
        zg,
        dmid,
    )
    mine, roots = finish(dar_qkv, db_qkv, grads, sums, count, axes, sizes, spans)
    grad_shard = mine.reshape(-1)[:count]
    root_squares = roots[0, :4]
    return (
        block_out.reshape(tokens.shape),
        tokens_grad.reshape(tokens.shape),
        grad_shard,
        root_squares,
    )


def solution(mesh):
    axes = tuple(mesh.axis_names)
    sizes = tuple(mesh.shape[axis] for axis in axes)
    sequence = P(axes, None, None)
    placed = (
        sequence,
        P(axes),
        P(),
        P(),
        P(),
        P(),
        P(),
        P(),
        P(),
        P(),
        P(axes),
        sequence,
    )
    return jax.shard_map(
        functools.partial(per_device, axes=axes, sizes=sizes),
        mesh=mesh,
        in_specs=placed,
        out_specs=(sequence, sequence, P(axes), P()),
        check_vma=False,
    )
```

```python
import functools

import jax
import jax.numpy as jnp
from jax import lax
from jax.experimental import pallas as pl
from jax.experimental.pallas import tpu as pltpu
from jax.sharding import PartitionSpec as P

D = 768
FF = 3072
HEADS = 12
HDIM = 64
EXPERTS = 10
RANK = 4
FANS = ((D, D), (D, D), (D, D), (D, D), (D, FF), (FF, D))
COLS = EXPERTS * RANK
LANES = 128

EPSILON = 1e-06
MASKED = -1000000000.0
GELU_SCALE = 0.7978845608028654
GELU_CUBIC = 0.044715
LOG2E = 1.4426950408889634
LN2 = 0.6931471805599453
QUERY_SCALE = 0.125 * LOG2E

ROWS = 256
MIDDLE_ROWS = 512
CHUNK = 512
QBLOCK = 256
UP_ROWS = 48
DOWN_ROWS = 2 * COLS
VMEM_BYTES = 60 * 1024 * 1024

F32 = jnp.float32
BF16 = jnp.bfloat16


def dot(a, b):
    return lax.dot_general(a, b, (((1,), (0,)), ((), ())), preferred_element_type=F32)


def dot_nt(a, b):
    return lax.dot_general(a, b, (((1,), (1,)), ((), ())), preferred_element_type=F32)


def dot_tn(a, b):
    return lax.dot_general(a, b, (((0,), (0,)), ((), ())), preferred_element_type=F32)


def exact_dot(a, b):
    return lax.dot_general(
        a,
        b,
        (((1,), (0,)), ((), ())),
        preferred_element_type=F32,
        precision=lax.Precision.HIGHEST,
    )


def lane_iota(shape):
    return lax.broadcasted_iota(jnp.int32, shape, 1)


def row_iota(shape):
    return lax.broadcasted_iota(jnp.int32, shape, 0)


def gates_of(logits):
    weights = jnp.exp(logits - jnp.max(logits, axis=0, keepdims=True))
    return weights * (4.0 / jnp.sum(weights, axis=0, keepdims=True))


def gate_grads(grad_mixed, lowrank, gates):
    product = grad_mixed * lowrank
    summed = product
    for step in range(1, RANK):
        summed = summed + pltpu.roll(product, COLS - step, 0)
    centre = jnp.sum(gates * product, axis=0, keepdims=True)
    first = row_iota(gates.shape) % RANK == 0
    return grad_mixed * gates, jnp.where(first, gates * (summed - centre), 0.0)


def pad_rows(value, rows):
    return jnp.concatenate([value, jnp.zeros((rows - value.shape[0], value.shape[1]), F32)], axis=0)


def single_gates(packed):
    turned = packed.T
    lowrank = turned[:COLS]
    gates = gates_of(turned[COLS : 2 * COLS])
    mixed = pad_rows(lowrank * gates, LANES).astype(BF16)
    return lowrank, gates, mixed, mixed.T


def single_deltas(grad_mixed, lowrank, gates):
    parts = gate_grads(grad_mixed.T[:COLS], lowrank, gates)
    delta = pad_rows(jnp.concatenate(parts, axis=0), LANES).astype(BF16)
    return delta, delta.T


def rms_inverse(values):
    return lax.rsqrt(jnp.mean(values * values, axis=-1, keepdims=True) + EPSILON)


def rms_backward(values, gain, inverse, grad_normed):
    weighted = grad_normed * gain
    return inverse * weighted - values * (
        inverse * inverse * inverse * jnp.mean(values * weighted, axis=-1, keepdims=True)
    )


def params(**more):
    return pltpu.CompilerParams(vmem_limit_bytes=VMEM_BYTES, **more)


def whole(shape):
    zeros = (0,) * len(shape)
    return pl.BlockSpec(shape, lambda *_: zeros, pipeline_mode=pl.Buffered(1))


def bias_table(offset_row, length):
    spread = jnp.broadcast_to(offset_row, (LANES, 2 * length))
    return pltpu.roll(spread, 2 * length - (LANES - 1), 1, stride=1, stride_axis=0)


def add_bias(scores, table_ref, start, length):
    width = scores.shape[1]
    parts = []
    for block in range(length // LANES):
        offset = start - LANES * block + (length - LANES)
        parts.append(
            scores[block * LANES : (block + 1) * LANES] + table_ref[:, offset : offset + width]
        )
    return jnp.concatenate(parts, axis=0)


def key_extras(length_ref, shape, odd):
    lane = lane_iota(shape) - (0 if odd else HDIM)
    invalid = row_iota(shape) >= length_ref[0]
    extras = jnp.where((lane == 0) & invalid, MASKED, 0.0)
    return jnp.where((lane >= 1) & (lane <= 3), 1.0, extras).astype(BF16)


def head_lanes(odd):
    lane = lane_iota((1, LANES))
    return ((lane >= HDIM) if odd else (lane < HDIM)).astype(F32).astype(BF16)


def extra_rows(rows):
    width = rows[0].shape[1]
    index = row_iota((8, width))
    block = jnp.zeros((8, width), F32)
    for place, row in enumerate(rows):
        block = jnp.where(index == place, row, block)
    return jnp.concatenate([block, jnp.zeros((HDIM - 8, width), F32)], axis=0).astype(BF16)


def split_three(row):
    high = row.astype(BF16).astype(F32)
    middle = (row - high).astype(BF16).astype(F32)
    return high, middle, row - high - middle


def join_rows(rows, extras, odd):
    return jnp.concatenate([extras, rows] if odd else [rows, extras], axis=0)


def attend_kernel(
    length_ref, off_ref, qt_ref, k_ref, kt_ref, vt_ref, o_ref, lse_ref, table, key_more, plain
):
    length = k_ref.shape[0]
    step = pl.program_id(0)

    @pl.when(step == 0)
    def _():
        for odd in range(2):
            key_more[odd] = key_extras(length_ref, k_ref.shape, odd)

    starts = range(0, length, QBLOCK)
    ones = jnp.ones((1, length), F32)

    def half_of(odd):
        return slice(odd * HDIM, (odd + 1) * HDIM)

    def keys_of(odd):
        return k_ref[...] * head_lanes(odd) + key_more[odd]

    def values_of(odd):
        return jnp.concatenate([vt_ref[half_of(odd), :], jnp.ones((16, length), BF16)], axis=0)

    def finish(odd, start, shift, weights):
        columns = slice(start, start + QBLOCK)
        summed = dot(values_of(odd), weights)
        total = summed[HDIM : HDIM + 1]
        o_ref[half_of(odd), columns] = (summed[:HDIM] / total).astype(BF16)
        lse_ref[0, odd : odd + 1, columns] = shift + jnp.log2(total)
        return total

    def bounded(odd):
        offsets = off_ref[pl.ds(2 * step + odd, 1), :]
        table[odd] = bias_table(offsets, length)
        squares = jnp.square(kt_ref[half_of(odd), :].astype(F32))
        sizes = jnp.sum(squares, axis=0, keepdims=True)
        sizes = jnp.where(lane_iota(sizes.shape) < length_ref[0], sizes, 0.0)
        largest = jnp.max(sizes, axis=1, keepdims=True)
        rows = qt_ref[half_of(odd), :].astype(F32)
        norms = jnp.sqrt(jnp.sum(rows * rows, axis=0, keepdims=True) * largest)
        bound = 1.001 * norms + jnp.max(offsets, axis=1, keepdims=True)
        queries = join_rows(
            qt_ref[half_of(odd), :],
            extra_rows([ones] + [-part for part in split_three(bound)]),
            odd,
        )
        keys = keys_of(odd)
        scores = [dot(keys, queries[:, start : start + QBLOCK]) for start in starts]
        weights = [
            jnp.exp2(add_bias(part, table.at[odd], start, length)).astype(BF16)
            for part, start in zip(scores, starts)
        ]
        least = None
        for start, part in zip(starts, weights):
            total = finish(odd, start, bound[:, start : start + QBLOCK], part)
            least = total if least is None else jnp.minimum(least, total)
        return least

    def exact(odd):
        plain[...] = join_rows(qt_ref[half_of(odd), :], extra_rows([ones]), odd)
        keys = keys_of(odd)

        def block(index, _):
            columns = pl.ds(pl.multiple_of(index * LANES, LANES), LANES)
            raw = dot(keys, plain[:, columns])
            parts = []
            for row in range(0, length, LANES):
                place = pl.multiple_of(index * LANES - row + (length - LANES), LANES)
                parts.append(raw[row : row + LANES] + table[odd, :, pl.ds(place, LANES)])
            scores = jnp.concatenate(parts, axis=0)
            peak = jnp.max(scores, axis=0, keepdims=True)
            summed = dot(values_of(odd), jnp.exp2(scores - peak).astype(BF16))
            total = summed[HDIM : HDIM + 1]
            o_ref[half_of(odd), columns] = (summed[:HDIM] / total).astype(BF16)
            lse_ref[0, odd : odd + 1, columns] = peak + jnp.log2(total)
            return 0

        lax.fori_loop(0, length // LANES, block, 0)

    least = jnp.minimum(bounded(0), bounded(1))

    @pl.when(jnp.logical_not(jnp.min(least) > 2.0**-100))
    def _():
        for odd in range(2):
            exact(odd)


def attend(length_valid, offsets, qt, k, kt, vt):
    length = k.shape[0]
    turned = pl.BlockSpec((LANES, length), lambda p: (p, 0))
    natural = pl.BlockSpec((length, LANES), lambda p: (0, p))
    return pl.pallas_call(
        attend_kernel,
        grid=(HEADS // 2,),
        in_specs=[
            pl.BlockSpec(memory_space=pltpu.SMEM),
            whole(offsets.shape),
            turned,
            natural,
            turned,
            turned,
        ],
        out_specs=[turned, pl.BlockSpec((1, 2, length), lambda p: (p, 0, 0))],
        out_shape=[
            jax.ShapeDtypeStruct((D, length), BF16),
            jax.ShapeDtypeStruct((HEADS // 2, 2, length), F32),
        ],
        scratch_shapes=[
            pltpu.VMEM((2, LANES, 2 * length), F32),
            pltpu.VMEM((2, length, LANES), BF16),
            pltpu.VMEM((LANES, length), BF16),
        ],
        compiler_params=params(),
        name="attend",
    )(length_valid, offsets, qt, k, kt, vt)


def middle_kernel(
    length_ref,
    ot_ref,
    x_ref,
    cot_ref,
    gain_ref,
    w_out_ref,
    w_in_hbm,
    w_down_hbm,
    ar_out_ref,
    b_out_ref,
    ar_in_ref,
    b_in_ref,
    ar_down_ref,
    b_down_ref,
    out_ref,
    dmid_ref,
    gt_ref,
    sums_ref,
    dar_out_ref,
    db_out_ref,
    dar_in_ref,
    db_in_ref,
    dar_down_ref,
    db_down_ref,
    active,
    slope,
    sloped,
    grad_hidden,
    feeds,
    w_in_ref,
    w_down_ref,
    loaded,
):
    step = pl.program_id(0)
    loads = [
        pltpu.make_async_copy(w_in_hbm, w_in_ref, loaded.at[0]),
        pltpu.make_async_copy(w_down_hbm, w_down_ref, loaded.at[1]),
    ]

    @pl.when(step == 0)
    def _():
        for load in loads:
            load.start()
        for ref in (
            sums_ref,
            dar_out_ref,
            db_out_ref,
            dar_in_ref,
            db_in_ref,
            dar_down_ref,
            db_down_ref,
        ):
            ref[...] = jnp.zeros_like(ref)

    attended = ot_ref[...].T
    inputs = x_ref[...].astype(F32)
    gain = gain_ref[...].reshape(1, D)
    cot = cot_ref[...]

    packed_out = dot(attended, ar_out_ref[...])
    branch = dot(attended, w_out_ref[...])
    low_out, gates_out, mixed_out, natural = single_gates(packed_out)
    grad_mixed_down = dot_nt(cot, b_down_ref[...])
    branch = branch + dot(natural, b_out_ref[...])
    middle = inputs + branch
    inverse = rms_inverse(middle)
    normed = (middle * inverse * gain).astype(BF16)

    packed_in = dot(normed, ar_in_ref[...])
    low_in, gates_in, mixed_in, natural = single_gates(packed_in)

    def columns_of(index):
        return pl.ds(pl.multiple_of(index * CHUNK, CHUNK), CHUNK)

    def hidden_of(chunk):
        return dot(normed, w_in_ref[:, chunk]) + dot(natural, b_in_ref[:, chunk])

    def activate(chunk, values):
        grad_dense = dot_nt(cot, w_down_ref[chunk])
        square = values * values
        tangent = jnp.tanh(values * (GELU_SCALE + (GELU_SCALE * GELU_CUBIC) * square))
        half = 0.5 + 0.5 * tangent
        smooth = values * half
        active[:, chunk] = smooth.astype(BF16)
        steep = half + smooth * (1.0 - tangent) * (
            GELU_SCALE + (3.0 * GELU_SCALE * GELU_CUBIC) * square
        )
        slope[:, chunk] = steep.astype(BF16)
        sloped[:, chunk] = grad_dense * steep

    def forward_pair(pair, _):
        chunk_a = columns_of(2 * pair)
        chunk_b = columns_of(2 * pair + 1)
        hidden_a = hidden_of(chunk_a)
        hidden_b = hidden_of(chunk_b)
        activate(chunk_a, hidden_a)
        activate(chunk_b, hidden_b)
        return 0

    @pl.when(step == 0)
    def _():
        for load in loads:
            load.wait()

    lax.fori_loop(0, FF // (2 * CHUNK), forward_pair, 0)

    packed_down = dot(active[...], ar_down_ref[...])
    for first in range(0, D, 256):
        part = slice(first, first + 256)
        feeds[:, part] = dot(active[...], w_down_ref[:, part])
    feed = feeds[...]
    low_down, gates_down, mixed_down, natural = single_gates(packed_down)
    delta_down, natural_delta = single_deltas(grad_mixed_down, low_down, gates_down)
    db_down_ref[...] += dot(mixed_down[:UP_ROWS], cot)
    feed = feed + dot(natural, b_down_ref[...])
    output = middle + feed
    out_ref[...] = output.astype(BF16)

    for first in range(0, FF, CHUNK):
        chunk = slice(first, first + CHUNK)
        grad_low = dot_nt(natural_delta, ar_down_ref[chunk])
        grad_hidden[:, chunk] = (
            sloped[:, chunk] + grad_low * slope[:, chunk].astype(F32)
        ).astype(BF16)

    rows = row_iota((MIDDLE_ROWS, 1)) + step * MIDDLE_ROWS
    valid = (rows < length_ref[0]).astype(F32)
    lane = lane_iota((8, LANES))
    totals = jnp.where((lane == 4) & (step == 0), length_ref[0].astype(F32), 0.0)
    for place, member in enumerate((inputs, branch, feed, output)):
        kept = member * valid
        totals = jnp.where(lane == place, jnp.sum(kept * kept), totals)
    sums_ref[...] += totals

    grad_mixed = dot_nt(grad_hidden[...], b_in_ref[...])
    for first in range(0, D, 256):
        part = slice(first, first + 256)
        feeds[:, part] = dot_nt(grad_hidden[...], w_in_ref[part])
    grad_normed = feeds[...]
    delta_in, natural_delta = single_deltas(grad_mixed, low_in, gates_in)
    grad_normed = grad_normed + dot_nt(natural_delta, ar_in_ref[...])
    dar_in_ref[...] += dot(delta_in[:DOWN_ROWS], normed)

    grad_middle = cot.astype(F32) + rms_backward(middle, gain, inverse, grad_normed)
    dmid_ref[...] = grad_middle
    grad_branch = grad_middle.astype(BF16)
    grad_mixed = dot_nt(grad_branch, b_out_ref[...])
    grad_attended = dot_nt(grad_branch, w_out_ref[...])
    dar_down_ref[...] += dot(delta_down[:DOWN_ROWS], active[...])
    db_in_ref[...] += dot(mixed_in[:UP_ROWS], grad_hidden[...])
    delta_out, natural_delta = single_deltas(grad_mixed, low_out, gates_out)
    grad_attended = grad_attended + dot_nt(natural_delta, ar_out_ref[...])
    gt_ref[...] = grad_attended.astype(BF16).T
    dar_out_ref[...] += dot(delta_out[:DOWN_ROWS], attended)
    db_out_ref[...] += dot(mixed_out[:UP_ROWS], grad_branch)


def middle_part(length_valid, ot, x, cot, gain, w_out, w_in, w_down, adapters):
    length = x.shape[0]
    tile = pl.BlockSpec((MIDDLE_ROWS, D), lambda i: (i, 0))
    turned = pl.BlockSpec((D, MIDDLE_ROWS), lambda i: (0, i))
    grad_shapes = [
        jax.ShapeDtypeStruct(shape, F32)
        for fan_in, fan_out in FANS[3:]
        for shape in ((DOWN_ROWS, fan_in), (UP_ROWS, fan_out))
    ]
    out_shape = [
        jax.ShapeDtypeStruct((length, D), BF16),
        jax.ShapeDtypeStruct((length, D), F32),
        jax.ShapeDtypeStruct((D, length), BF16),
        jax.ShapeDtypeStruct((8, LANES), F32),
    ] + grad_shapes
    return pl.pallas_call(
        middle_kernel,
        grid=(length // MIDDLE_ROWS,),
        in_specs=[pl.BlockSpec(memory_space=pltpu.SMEM), turned, tile, tile]
        + [whole(gain.shape), whole(w_out.shape)]
        + [pl.BlockSpec(memory_space=pl.ANY)] * 2
        + [whole(member.shape) for member in adapters],
        out_specs=[tile, tile, turned] + [whole(member.shape) for member in out_shape[3:]],
        out_shape=out_shape,
        scratch_shapes=[
            pltpu.VMEM((MIDDLE_ROWS, FF), BF16),
            pltpu.VMEM((MIDDLE_ROWS, FF), BF16),
            pltpu.VMEM((MIDDLE_ROWS, FF), F32),
            pltpu.VMEM((MIDDLE_ROWS, FF), BF16),
            pltpu.VMEM((MIDDLE_ROWS, D), F32),
            pltpu.VMEM(w_in.shape, BF16),
            pltpu.VMEM(w_down.shape, BF16),
            pltpu.SemaphoreType.DMA((2,)),
        ],
        compiler_params=params(),
        name="middle_part",
    )(length_valid, ot, x, cot, gain, w_out, w_in, w_down, *adapters)


def attend_back(
    pair,
    length_ref,
    off_ref,
    qt_ref,
    k_ref,
    kt_ref,
    v_ref,
    ot_ref,
    gt_ref,
    lse_ref,
    grads_ref,
    table,
    key_more,
    weights_all,
    grads_all,
):
    length = k_ref.shape[0]
    lane = lane_iota((1, LANES))
    first_lanes = lane < HDIM
    grad_query_parts = []
    for odd in range(2):
        half = slice(odd * HDIM, (odd + 1) * HDIM)
        table[odd] = bias_table(off_ref[pl.ds(2 * pair + odd, 1), :], length)
        keys = k_ref[...] * head_lanes(odd) + key_more[odd]
        place = lane - (0 if odd else HDIM)
        value_more = ((place >= 0) & (place < 3)).astype(F32).astype(BF16)
        values = v_ref[...] * head_lanes(odd) + value_more
        ones = jnp.ones((1, length), F32)
        lse = lse_ref[0, odd : odd + 1, :]
        queries = join_rows(
            qt_ref[half, :], extra_rows([ones] + [-part for part in split_three(lse)]), odd
        )
        delta = jnp.sum(
            ot_ref[half, :].astype(F32) * gt_ref[half, :].astype(F32), axis=0, keepdims=True
        )
        grads = join_rows(
            gt_ref[half, :], extra_rows([-part for part in split_three(delta)]), odd
        )
        query_blocks = []
        previous = None
        for start in range(0, length, QBLOCK):
            columns = slice(start, start + QBLOCK)
            raw = dot(keys, queries[:, columns])
            grad_raw = dot(values, grads[:, columns])
            if previous is not None:
                query_blocks.append(dot(kt_ref[half, :], previous))
            weights = jnp.exp2(add_bias(raw, table.at[odd], start, length))
            weights_all[:, columns] = weights.astype(BF16)
            previous = (weights * grad_raw).astype(BF16)
            grads_all[:, columns] = previous
        query_blocks.append(dot(kt_ref[half, :], previous))
        grad_query_parts.append(jnp.concatenate(query_blocks, axis=1) * 0.125)
        grad_values = dot_nt(weights_all[...], gt_ref[...])
        grad_keys = dot_nt(grads_all[...], qt_ref[...]) * LN2
        if odd:
            grad_values = jnp.where(first_lanes, even_values, grad_values)
            grad_keys = jnp.where(first_lanes, even_keys, grad_keys)
        else:
            even_values, even_keys = grad_values, grad_keys
    columns = pl.ds(pl.multiple_of(pair * LANES, LANES), LANES)
    grads_ref[0, :, columns] = jnp.concatenate(grad_query_parts, axis=0).T.astype(BF16)
    grads_ref[1, :, columns] = grad_keys.astype(BF16)
    grads_ref[2, :, columns] = grad_values.astype(BF16)


def project_back(
    tile, x_ref, gain_ref, w_ref, ar_ref, b_ref, zg_ref, grads_ref, dmid_ref, out_ref, dar_ref, db_ref
):
    values = x_ref[...].astype(F32)
    gain = gain_ref[...].reshape(1, D)
    inverse = rms_inverse(values)
    normed = (values * inverse * gain).astype(BF16)
    lowrank = zg_ref[: 3 * COLS]
    gates = zg_ref[3 * COLS :]
    mixed = pad_rows(lowrank * gates, LANES).astype(BF16)
    rows = pl.ds(pl.multiple_of(tile * ROWS, ROWS), ROWS)
    grads = [grads_ref[index, rows] for index in range(3)]
    columns = [slice(index * D, (index + 1) * D) for index in range(3)]
    grad_mixed = jnp.zeros((ROWS, LANES), F32)
    for grad, lanes in zip(grads, columns):
        grad_mixed = grad_mixed + dot_nt(grad, b_ref[:, lanes])
    grad_normed = jnp.zeros((ROWS, D), F32)
    for grad, lanes in zip(grads, columns):
        grad_normed = grad_normed + dot_nt(grad, w_ref[:, lanes])
        db_ref[:, lanes] += dot(mixed, grad)
    turned = grad_mixed.T
    parts = []
    for first in range(0, 3 * COLS, COLS):
        place = slice(first, first + COLS)
        parts.append(gate_grads(turned[place], lowrank[place], gates[place]))
    delta = jnp.concatenate([part[0] for part in parts] + [part[1] for part in parts], axis=0)
    delta = pad_rows(delta, 2 * LANES).astype(BF16)
    grad_normed = grad_normed + dot_nt(delta.T, ar_ref[...])
    dar_ref[...] += dot(delta, normed)
    out_ref[...] = dmid_ref[...] + rms_backward(values, gain, inverse, grad_normed)


def back_kernel(*refs):
    length_ref = refs[0]
    heads_refs = refs[:9]
    x_ref, gain_ref, w_hbm, ar_ref, b_ref, zg_ref, dmid_ref = refs[9:16]
    out_ref, dar_ref, db_ref = refs[16:19]
    table, key_more, weights_all, grads_all, grads_ref, w_ref, loaded = refs[19:]
    step = pl.program_id(0)
    pairs = HEADS // 2
    load = pltpu.make_async_copy(w_hbm, w_ref, loaded)

    @pl.when(step == 0)
    def _():
        load.start()
        dar_ref[...] = jnp.zeros_like(dar_ref)
        db_ref[...] = jnp.zeros_like(db_ref)
        for odd in range(2):
            key_more[odd] = key_extras(length_ref, key_more.shape[1:], odd)

    @pl.when(step < pairs)
    def _():
        attend_back(step, *heads_refs, grads_ref, table, key_more, weights_all, grads_all)

    @pl.when(step == pairs)
    def _():
        load.wait()

    @pl.when(step >= pairs)
    def _():
        project_back(
            step - pairs,
            x_ref,
            gain_ref,
            w_ref,
            ar_ref,
            b_ref,
            zg_ref,
            grads_ref,
            dmid_ref,
            out_ref,
            dar_ref,
            db_ref,
        )


def back_part(
    length_valid, offsets, qt, k, kt, v, ot, gt, lse, x, gain, w_qkv, ar_qkv, b_qkv, zg, dmid
):
    length = k.shape[0]
    pairs = HEADS // 2

    def pair_of(i):
        return jnp.minimum(i, pairs - 1)

    def tile_of(i):
        return jnp.maximum(i - pairs, 0)

    turned = pl.BlockSpec((LANES, length), lambda i: (pair_of(i), 0))
    natural = pl.BlockSpec((length, LANES), lambda i: (0, pair_of(i)))
    tile = pl.BlockSpec((ROWS, D), lambda i: (tile_of(i), 0))
    out_shape = [
        jax.ShapeDtypeStruct((length, D), F32),
        jax.ShapeDtypeStruct((2 * LANES, D), F32),
        jax.ShapeDtypeStruct((LANES, 3 * D), F32),
    ]
    return pl.pallas_call(
        back_kernel,
        grid=(pairs + length // ROWS,),
        in_specs=[
            pl.BlockSpec(memory_space=pltpu.SMEM),
            whole(offsets.shape),
            turned,
            natural,
            turned,
            natural,
            turned,
            turned,
            pl.BlockSpec((1, 2, length), lambda i: (pair_of(i), 0, 0)),
            tile,
            whole((D,)),
            pl.BlockSpec(memory_space=pl.ANY),
            whole(ar_qkv.shape),
            whole(b_qkv.shape),
            pl.BlockSpec((6 * COLS, ROWS), lambda i: (0, tile_of(i))),
            tile,
        ],
        out_specs=[tile] + [whole(member.shape) for member in out_shape[1:]],
        out_shape=out_shape,
        scratch_shapes=[
            pltpu.VMEM((2, LANES, 2 * length), F32),
            pltpu.VMEM((2, length, LANES), BF16),
            pltpu.VMEM((length, length), BF16),
            pltpu.VMEM((length, length), BF16),
            pltpu.VMEM((3, length, D), BF16),
            pltpu.VMEM(w_qkv.shape, BF16),
            pltpu.SemaphoreType.DMA,
        ],
        compiler_params=params(),
        name="back_part",
    )(length_valid, offsets, qt, k, kt, v, ot, gt, lse, x, gain, w_qkv, ar_qkv, b_qkv, zg, dmid)


PARAM_ROWS = sum((COLS + EXPERTS) * fan_in + COLS * fan_out for fan_in, fan_out in FANS) // LANES


def piece_rows():
    result = []
    row = 0
    for fan_in, fan_out in FANS:
        starts = []
        for count in (fan_in * COLS, COLS * fan_out, fan_in * EXPERTS):
            starts.append(row)
            row += count // LANES
        result.append(tuple(starts))
    return result


def shard_rows(count):
    return -(-count // (LANES * 16)) * 16


def align_in(flat_ref, shard, start):
    first, shift = divmod(start, LANES)
    rows = shard.shape[0]
    if shift == 0:
        flat_ref[first : first + rows] = shard
        return
    turned = pltpu.roll(shard, shift, 1)
    lane = lane_iota((1, LANES))
    zeros = jnp.zeros((8, LANES), F32)
    upper = jnp.concatenate([turned, zeros], axis=0)
    lower = pltpu.roll(upper, 1, 0)
    kept = flat_ref[first : first + 8]
    merged = jnp.where(lane >= shift, upper, lower)
    inside = (row_iota((8, LANES)) == 0) & (lane_iota((8, LANES)) < shift)
    flat_ref[first : first + 8] = jnp.where(inside, kept, merged[:8])
    flat_ref[first + 8 : first + 8 + rows] = merged[8:]


def align_out(flat_ref, rows, start):
    first, shift = divmod(start, LANES)
    if shift == 0:
        return flat_ref[first : first + rows]
    block = flat_ref[first : first + rows + 8]
    turned = pltpu.roll(block, LANES - shift, 1)
    below = pltpu.roll(turned, rows + 7, 0)
    lane = lane_iota((1, LANES))
    return jnp.where(lane < LANES - shift, turned, below)[:rows]


GROUP = 64


def narrow_to_rows(flat_ref, fan_in, items, out_ref, begin=0):
    groups = fan_in // GROUP
    lane = lane_iota((1, LANES))
    lines = [
        [
            flat_ref[pl.ds(base + k, groups, stride=width * GROUP // LANES), :]
            for k in range(width * GROUP // LANES)
        ]
        for base, width, _ in items
    ]
    for b in range(GROUP):
        result = jnp.zeros((groups, LANES), F32)
        for line, (_, width, place) in zip(lines, items):
            first, shift = divmod(width * b, LANES)
            amount = (place - shift) % LANES
            value = line[first] if amount == 0 else pltpu.roll(line[first], amount, 1)
            if shift + width > LANES:
                value = jnp.where(
                    lane < place + LANES - shift, value, pltpu.roll(line[first + 1], amount, 1)
                )
            inside = (lane >= place) & (lane < place + width)
            result = jnp.where(inside, value, result)
        out_ref[pl.ds(begin + b, groups, stride=GROUP), :] = result


def rows_to_narrow(in_ref, fan_in, items, flat_ref, begin=0):
    groups = fan_in // GROUP
    lane = lane_iota((1, LANES))
    lines = [
        [jnp.zeros((groups, LANES), F32) for _ in range(width * GROUP // LANES)]
        for _, width, _ in items
    ]
    for b in range(GROUP):
        source = in_ref[pl.ds(begin + b, groups, stride=GROUP), :]
        for line, (_, width, place) in zip(lines, items):
            first, shift = divmod(width * b, LANES)
            amount = (shift - place) % LANES
            value = source if amount == 0 else pltpu.roll(source, amount, 1)
            inside = (lane >= shift) & (lane < shift + width)
            line[first] = jnp.where(inside, value, line[first])
            if shift + width > LANES:
                line[first + 1] = jnp.where(lane < shift + width - LANES, value, line[first + 1])
    for line, (base, width, _) in zip(lines, items):
        for k, value in enumerate(line):
            flat_ref[pl.ds(base + k, groups, stride=width * GROUP // LANES), :] = value


def single_items(block):
    starts = piece_rows()
    after_out, after_in = (block + 4) // 5, (block + 2) // 4
    down = (block - 2) * after_in
    bases = []
    for piece, width in ((0, COLS), (2, EXPERTS)):
        out, inner, outer = (starts[index][piece] for index in range(3, 6))
        base = out + (inner - out) * after_out + (outer - inner) * after_in
        bases.append(base + down * (D * width // LANES))
    return [(bases[0], COLS, 0), (bases[1], EXPERTS, COLS)]


SINGLE_BLOCKS = 2 + FF // D


def spread_matrix(experts, source, place):
    row = row_iota((LANES, LANES)) - source
    lane = lane_iota((LANES, LANES)) - place
    hit = (lane >= RANK * row) & (lane < RANK * row + RANK) & (row >= 0) & (row < experts)
    return jnp.where(hit, 1.0, 0.0)


def keep_matrix():
    row = row_iota((LANES, LANES))
    return jnp.where((row == lane_iota((LANES, LANES))) & (row < COLS), 1.0, 0.0)


FIRST_COUNT = sum((COLS + EXPERTS) * fan_in + COLS * fan_out for fan_in, fan_out in FANS[:3])


def unpack_ups(flat, base, fan_out, first, out_ref, column):
    width = fan_out // LANES
    above = jnp.zeros((first, LANES), F32)
    below = jnp.zeros((LANES - COLS - first, LANES), F32)
    for k in range(width):
        part = flat[pl.ds(base + k, COLS, stride=width), :]
        parts = [part, below] if first == 0 else [above, part, below]
        lanes = slice(column + k * LANES, column + (k + 1) * LANES)
        out_ref[:, lanes] = jnp.concatenate(parts, axis=0).astype(BF16)


def unpack_first(flat, ar_ref, b_ref, down, router):
    starts = piece_rows()
    narrow_to_rows(flat, D, [(starts[k][0], COLS, k * COLS) for k in range(3)], down)
    narrow_to_rows(flat, D, [(starts[k][2], EXPERTS, k * EXPERTS) for k in range(3)], router)
    routers = router[...].astype(BF16)
    for half in range(2):
        matrix = spread_matrix(3 * EXPERTS, 0, 3 * COLS - half * LANES).astype(BF16)
        packed = dot(routers, matrix)
        packed = packed if half else packed + down[...]
        ar_ref[:, half * LANES : (half + 1) * LANES] = packed.astype(BF16)
    for index in range(3):
        unpack_ups(flat, starts[index][1], D, index * COLS, b_ref, index * D)


def flat_rows(count):
    return PARAM_ROWS + shard_rows(count) + 20


def unpack_rest(flat, outs, work):
    starts = piece_rows()
    matrix = (keep_matrix() + spread_matrix(EXPERTS, COLS, COLS)).astype(BF16)

    def block(index, _):
        narrow_to_rows(flat, D, single_items(index), work, index * D)
        return 0

    lax.fori_loop(0, SINGLE_BLOCKS, block, 0)
    begin = 0
    for index in range(3, 6):
        fan_in, fan_out = FANS[index]
        ar_ref, b_ref = outs[2 * index - 6], outs[2 * index - 5]
        ar_ref[...] = dot(work[begin : begin + fan_in].astype(BF16), matrix).astype(BF16)
        unpack_ups(flat, starts[index][1], fan_out, 0, b_ref, 0)
        begin += fan_in


def split_dot(value, matrix):
    high = value.astype(BF16)
    return dot(high, matrix) + dot((value - high.astype(F32)).astype(BF16), matrix)


def first_of_four(experts, source, place):
    row = row_iota((LANES, LANES)) - source
    lane = lane_iota((LANES, LANES)) - place
    hit = (row == RANK * lane) & (lane >= 0) & (lane < experts)
    return jnp.where(hit, 1.0, 0.0)


def assemble_ups(flat, base, fan_out, first, grad_ref, column):
    width = fan_out // LANES
    for k in range(width):
        lanes = slice(column + k * LANES, column + (k + 1) * LANES)
        flat[pl.ds(base + k, COLS, stride=width), :] = grad_ref[first : first + COLS, lanes]


def assemble_rest(flat, grads, work):
    starts = piece_rows()
    matrix = (keep_matrix() + first_of_four(EXPERTS, COLS, COLS)).astype(BF16)
    begin = 0
    for index in range(3, 6):
        fan_in, fan_out = FANS[index]
        dar_ref, db_ref = grads[2 * index - 6], grads[2 * index - 5]
        work[begin : begin + fan_in] = split_dot(pad_rows(dar_ref[...], LANES).T, matrix)
        assemble_ups(flat, starts[index][1], fan_out, 0, db_ref, 0)
        begin += fan_in

    def block(index, _):
        rows_to_narrow(work, D, single_items(index), flat, index * D)
        return 0

    lax.fori_loop(0, SINGLE_BLOCKS, block, 0)


def assemble_first(flat, dar_ref, db_ref, down, router):
    starts = piece_rows()
    down[...] = dar_ref[:LANES].T
    rows_to_narrow(down, D, [(starts[k][0], COLS, k * COLS) for k in range(3)], flat)
    first_router = 3 * COLS
    turned = dar_ref[first_router : first_router + LANES].T
    router[...] = split_dot(turned, first_of_four(3 * EXPERTS, 0, 0).astype(BF16))
    rows_to_narrow(router, D, [(starts[k][2], EXPERTS, k * EXPERTS) for k in range(3)], flat)
    for index in range(3):
        assemble_ups(flat, starts[index][1], D, index * COLS, db_ref, index * D)


MESH = pl.DeviceIdType.MESH


def place_of(axes, sizes):
    me = lax.axis_index(axes[0]) * sizes[1] + lax.axis_index(axes[1])

    def coordinates(number):
        return (number // sizes[1], number % sizes[1])

    return me, coordinates


def partners_of(me):
    low = me % 8
    core = low % 2
    y = (low // 2) % 2
    x = low // 4
    over_x = low + 4 * (1 - 2 * x)
    over_y = low + 2 * (1 - 2 * y)
    first = over_x * (1 - core) + over_y * core
    second = over_y * (1 - core) + over_x * core
    both = first + second - low
    other = 1 - 2 * core
    return low, first, second, both, other, over_x, over_y


def greet(peers):
    for peer in peers:
        pl.semaphore_signal(
            pltpu.get_barrier_semaphore(), inc=1, device_id=peer, device_id_type=MESH
        )


def await_greetings(count):
    pl.semaphore_wait(pltpu.get_barrier_semaphore(), count)


class Ring:
    def __init__(self, axes, sizes, send, receive):
        self.me, self.coordinates = place_of(axes, sizes)
        self.groups = sizes[0] * sizes[1] // 8
        self.group = self.me // 8
        places = partners_of(self.me)
        self.low, self.first, self.second, self.both, self.other, self.over_x, self.over_y = places
        self.mate = self.low + self.other
        self.send, self.receive = send, receive
        self.copies = {}

    def device(self, group, low):
        return self.coordinates(group * 8 + low)

    def greet(self):
        peers = [
            self.device((self.group + step) % self.groups, self.low)
            for step in range(1, self.groups)
        ]
        peers += [self.device(self.group, low) for low in (self.first, self.second, self.mate)]
        greet(peers)

    def await_greetings(self):
        await_greetings(self.groups + 2)

    def copy(self, slot, source, target, peer, arrival=None):
        return pltpu.make_async_remote_copy(
            src_ref=source,
            dst_ref=target,
            send_sem=self.send.at[slot],
            recv_sem=self.receive.at[slot if arrival is None else arrival],
            device_id=peer,
            device_id_type=MESH,
        )


def gather_phases(ring, span, shard_ref, out_ref, local, greets):
    begin, end = span
    base = ring.groups
    inside = (ring.group >= begin) & (ring.group < end)

    def around(step):
        target = (ring.group + step) % ring.groups
        return ring.copy(
            step,
            shard_ref,
            out_ref.at[ring.group - begin, ring.low],
            ring.device(target, ring.low),
            base + 7 + ring.group,
        )

    def arrived(group):
        return ring.copy(
            0,
            shard_ref,
            out_ref.at[group - begin, ring.low],
            ring.device(group, ring.low),
            base + 7 + group,
        )

    def push(slot, part, partner):
        return ring.copy(
            base + slot, out_ref.at[:, part], out_ref.at[:, part], ring.device(ring.group, partner)
        )

    one = push(0, ring.low, ring.first)
    two = push(1, ring.low, ring.second)
    three = push(2, ring.first, ring.second)
    cores = [
        push(3 + index, part, ring.mate)
        for index, part in enumerate((ring.low, ring.first, ring.second, ring.both))
    ]

    def own():
        return pltpu.make_async_copy(
            shard_ref, out_ref.at[ring.group - begin, ring.low], local
        )

    def phase0():
        if greets:
            ring.greet()
            ring.await_greetings()

        @pl.when(inside)
        def _():
            own().start()
            for step in range(1, ring.groups):
                around(step).start()

    def phase1():
        @pl.when(inside)
        def _():
            own().wait()
            for step in range(1, ring.groups):
                around(step).wait_send()

        for group in range(begin, end):

            @pl.when(ring.group != group)
            def _():
                arrived(group).wait_recv()

        for copy in (one, two, cores[0]):
            copy.start()

    def phase2():
        one.wait()
        three.start()
        cores[1].start()

    def phase3():
        two.wait()
        cores[2].start()
        three.wait()
        cores[3].start()

    def phase4():
        for copy in cores:
            copy.wait()

    return phase0, phase1, phase2, phase3, phase4


def gather_semaphores(groups):
    return [
        pltpu.SemaphoreType.DMA((groups + 7,)),
        pltpu.SemaphoreType.DMA((2 * groups + 7,)),
        pltpu.SemaphoreType.DMA,
    ]


def start_kernel(
    link,
    count,
    values_ref,
    buckets_ref,
    table_ref,
    gain_ref,
    x_hbm,
    w_hbm,
    *refs,
):
    hbm_outs, off_ref, ar_ref, b_ref = refs[:6], refs[6], refs[7], refs[8]
    rest_refs = refs[9:15]
    x_ref, w_ref, normed, dense = refs[15:19]
    outs = refs[19:25]
    qt_ref, k_ref, kt_ref, v_ref, vt_ref, zg_ref = outs
    flat, down, router, work, offsets_ref, shard_ref, loaded, stored, *more = refs[25:]
    loads = [
        pltpu.make_async_copy(x_hbm, x_ref, loaded.at[0]),
        pltpu.make_async_copy(w_hbm, w_ref, loaded.at[1]),
    ]
    stores = [
        pltpu.make_async_copy(source, target, stored.at[index])
        for index, (source, target) in enumerate(zip(outs, hbm_outs))
    ]
    for load in loads:
        load.start()
    values = values_ref[...].astype(F32)
    values = jnp.pad(values, (0, shard_ref.shape[0] * LANES - count))
    shard_ref[...] = values.reshape(shard_ref.shape).astype(BF16)
    if link is None:
        first = [lambda: None] * 5
        rest = first

        def shard_of(index):
            return shard_ref[...]
    else:
        axes, sizes, spans = link
        land_a, land_b, *sems = more
        first = gather_phases(
            Ring(axes, sizes, *sems[:2]), spans[0], shard_ref, land_a, sems[2], True
        )
        rest = gather_phases(
            Ring(axes, sizes, *sems[3:5]), spans[1], shard_ref, land_b, sems[5], False
        )

        def shard_of(index):
            group, low = divmod(index, 8)
            begin = spans[1][0]
            return land_a[group, low] if group < begin else land_b[group - begin, low]

    length = x_ref.shape[0]

    def dense_tile(index):
        rows = slice(index * length // 2, (index + 1) * length // 2)
        values = x_ref[rows].astype(F32)
        low = (values * rms_inverse(values) * gain_ref[...].reshape(1, D)).astype(BF16)
        normed[rows] = low

        def columns(part, _):
            lanes = pl.ds(pl.multiple_of(part * D, D), D)
            dense[rows, lanes] = dot(normed[rows], w_ref[:, lanes])
            return 0

        lax.fori_loop(0, 3, columns, 0)

    def project():
        packed = dot(normed[...], ar_ref[...]).T
        lowrank = packed[: 3 * COLS]
        gates = jnp.concatenate(
            [gates_of(packed[place : place + COLS]) for place in range(3 * COLS, 6 * COLS, COLS)],
            axis=0,
        )
        zg_ref[: 3 * COLS] = lowrank
        zg_ref[3 * COLS :] = gates
        stores[5].start()
        mixed = pad_rows(lowrank * gates, LANES).astype(BF16).T
        for part in range(3):
            columns = slice(part * D, (part + 1) * D)
            value = dense[:, columns] + dot(mixed, b_ref[:, columns])
            if part == 0:
                qt_ref[...] = (value * QUERY_SCALE).astype(BF16).T
                stores[0].start()
            else:
                low = value.astype(BF16)
                natural, turned = ((k_ref, kt_ref), (v_ref, vt_ref))[part - 1]
                natural[...] = low
                turned[...] = low.T
                stores[2 * part - 1].start()
                stores[2 * part].start()

    first[0]()
    rest[0]()
    for load in loads:
        load.wait()
    dense_tile(0)
    first[1]()
    rest[1]()
    dense_tile(1)
    first[2]()
    buckets = buckets_ref[...].reshape(1, buckets_ref.shape[0])
    hits = jnp.where(row_iota((table_ref.shape[1], buckets.shape[1])) == buckets, LOG2E, 0.0)
    offsets_ref[...] = jnp.zeros_like(offsets_ref)
    offsets_ref[:, : buckets.shape[1]] = exact_dot(table_ref[...], hits)
    flip = (row_iota((LANES, LANES)) + lane_iota((LANES, LANES)) == LANES - 1).astype(F32)
    blocks = offsets_ref.shape[1] // LANES
    for block in range(blocks):
        lanes = slice(block * LANES, (block + 1) * LANES)
        turned = slice((blocks - 1 - block) * LANES, (blocks - block) * LANES)
        off_ref[:, turned] = exact_dot(offsets_ref[:, lanes], flip)
    off_ref[...] = pltpu.roll(off_ref[...], offsets_ref.shape[1] - 1, 1)
    first[3]()
    rest[2]()
    first[4]()
    for index in range(-(-FIRST_COUNT // count)):
        align_in(flat, shard_of(index).astype(F32), index * count)
    unpack_first(flat, ar_ref, b_ref, down, router)
    rest[3]()
    project()
    rest[4]()
    for index in range(FIRST_COUNT // count, PARAM_ROWS * LANES // count):
        align_in(flat, shard_of(index).astype(F32), index * count)
    unpack_rest(flat, rest_refs, work)
    for store in stores:
        store.wait()


def start(x, gain, w_qkv, shard, buckets, rel_table, count, axes, sizes, spans):
    length = x.shape[0]
    groups = sizes[0] * sizes[1] // 8
    link = (axes, sizes, spans) if groups else None
    rest_shapes = [
        shape for fan_in, fan_out in FANS[3:] for shape in ((fan_in, LANES), (LANES, fan_out))
    ]
    wide = [
        ((D, length), BF16),
        ((length, D), BF16),
        ((D, length), BF16),
        ((length, D), BF16),
        ((D, length), BF16),
        ((6 * COLS, length), F32),
    ]
    small = [
        ((HEADS, 2 * length), F32),
        ((D, 2 * LANES), BF16),
        ((LANES, 3 * D), BF16),
    ] + [(shape, BF16) for shape in rest_shapes]
    scratch = [
        pltpu.VMEM(x.shape, BF16),
        pltpu.VMEM(w_qkv.shape, BF16),
        pltpu.VMEM(x.shape, BF16),
        pltpu.VMEM((length, 3 * D), F32),
    ]
    scratch += [pltpu.VMEM(*member) for member in wide]
    scratch += [
        pltpu.VMEM((flat_rows(count), LANES), F32),
        pltpu.VMEM((D, LANES), F32),
        pltpu.VMEM((D, LANES), F32),
        pltpu.VMEM((SINGLE_BLOCKS * D, LANES), F32),
        pltpu.VMEM((HEADS, 2 * length), F32),
        pltpu.VMEM((shard_rows(count), LANES), BF16),
        pltpu.SemaphoreType.DMA((2,)),
        pltpu.SemaphoreType.DMA((len(wide),)),
    ]
    if link:
        rows = shard_rows(count)
        scratch += [pltpu.VMEM((end - begin, 8, rows, LANES), BF16) for begin, end in spans]
        scratch += gather_semaphores(groups) * 2
    vmem = pl.BlockSpec(memory_space=pltpu.VMEM)
    anywhere = pl.BlockSpec(memory_space=pl.ANY)
    return pl.pallas_call(
        functools.partial(start_kernel, link, count),
        in_specs=[vmem] * 4 + [anywhere] * 2,
        out_specs=[anywhere] * len(wide) + [vmem] * len(small),
        out_shape=[jax.ShapeDtypeStruct(*member) for member in wide + small],
        scratch_shapes=scratch,
        compiler_params=params(collective_id=0, has_side_effects=True) if link else params(),
        name="start",
    )(shard, buckets, rel_table, gain, x, w_qkv)


def reduce_phases(ring, span, parts_ref, boxes, greets, sums_ref=None, sum_boxes=None):
    begin, end = span
    outbox, inbox, half, own, far_out, far_in, out_ref = boxes
    groups = ring.groups
    inside = (ring.group >= begin) & (ring.group < end)
    core_parts = (ring.first, ring.both, ring.second, ring.low)
    near = [ring.mate] * 4 + [ring.second, ring.second, ring.first]

    def push(slot):
        return ring.copy(slot, outbox.at[slot], inbox.at[slot], ring.device(ring.group, near[slot]))

    def fill(slot, value):
        outbox[slot] = value.astype(BF16)
        push(slot).start()

    def around(group):
        return ring.copy(
            7 + group - begin,
            far_out.at[group - begin],
            far_in.at[ring.group],
            ring.device(group, ring.low),
            7 + ring.group,
        )

    def arrived(group):
        return ring.copy(
            7,
            far_out.at[0],
            far_in.at[group],
            ring.device(group, ring.low),
            7 + group,
        )

    base = 7 + groups
    sum_peers = (ring.mate, ring.over_x, ring.over_y)

    def push_sums(slot):
        near_out, near_in = sum_boxes
        return ring.copy(
            base + slot,
            near_out.at[slot],
            near_in.at[slot],
            ring.device(ring.group, sum_peers[slot]),
        )

    def around_sums(step):
        near_out, near_in = sum_boxes
        target = (ring.group + step) % groups
        return ring.copy(
            base + 2 + step,
            near_out.at[3],
            near_in.at[3 + ring.group],
            ring.device(target, ring.low),
        )

    def start_sums(slot, value):
        if sum_boxes is not None:
            sum_boxes[0][slot] = value
            push_sums(slot).start()

    def phase0():
        if greets:
            ring.await_greetings()
        if sum_boxes is not None:
            start_sums(0, sums_ref[...])
        for slot, part in enumerate(core_parts):
            fill(slot, parts_ref[:, part + ring.other])

    def phase1():
        push(0).wait()
        fill(4, parts_ref[:, ring.second] + inbox[0].astype(F32))
        push(1).wait()
        fill(5, parts_ref[:, ring.both] + inbox[1].astype(F32))
        if sum_boxes is not None:
            push_sums(0).wait()
            start_sums(1, sum_boxes[0][0] + sum_boxes[1][0])

    def add1():
        push(2).wait()
        half[...] = parts_ref[:, ring.first] + inbox[2].astype(F32)
        push(3).wait()
        own[...] = parts_ref[:, ring.low] + inbox[3].astype(F32)

    def phase2():
        push(5).wait()
        fill(6, half[...] + inbox[5].astype(F32))
        if sum_boxes is not None:
            push_sums(1).wait()
            start_sums(2, sum_boxes[0][1] + sum_boxes[1][1])

    def add2():
        push(4).wait()
        own[...] = own[...] + inbox[4].astype(F32)

    def phase3():
        push(6).wait()
        own[...] = own[...] + inbox[6].astype(F32)
        far_out[...] = own[...].astype(BF16)
        for group in range(begin, end):

            @pl.when(ring.group != group)
            def _():
                around(group).start()

        if sum_boxes is not None:
            near_out, near_in = sum_boxes
            push_sums(2).wait()
            near_out[3] = near_out[2] + near_in[2]
            for step in range(1, groups):
                around_sums(step).start()
            near_in[3 + ring.group] = near_out[3]

    def phase4(finish_sums=None):
        for group in range(begin, end):

            @pl.when(ring.group != group)
            def _():
                around(group).wait_send()

        @pl.when(inside)
        def _():
            for group in range(groups):

                @pl.when(ring.group != group)
                def _():
                    arrived(group).wait_recv()

            total = own[ring.group - begin]
            for step in range(1, groups):
                total = total + far_in[(ring.group + step) % groups].astype(F32)
            out_ref[...] = total

        if sum_boxes is not None:
            near_out, near_in = sum_boxes
            for step in range(1, groups):
                around_sums(step).wait()
            whole_sum = near_in[3]
            for index in range(1, groups):
                whole_sum = whole_sum + near_in[3 + index]
            finish_sums(whole_sum)

    return phase0, phase1, add1, phase2, add2, phase3, phase4


def reduce_scratch(groups, count, rows):
    return [
        pltpu.VMEM((7, count, rows, LANES), BF16),
        pltpu.VMEM((7, count, rows, LANES), BF16),
        pltpu.VMEM((count, rows, LANES), F32),
        pltpu.VMEM((count, rows, LANES), F32),
        pltpu.VMEM((count, rows, LANES), BF16),
        pltpu.VMEM((groups, rows, LANES), BF16),
    ]


def finish_kernel(link, count, dar_ref, db_ref, *refs):
    grads, sums_ref = refs[:6], refs[6]
    out_ref, roots_ref, flat, down, router, work, *more = refs[7:]

    def finish_sums(total):
        roots_ref[...] = jnp.sqrt(total / (total[:, 4:5] * D))[0, :4]

    if link is not None:
        axes, sizes, spans = link
        parts_a, parts_b, near_out, near_in, *more = more
        boxes_a, boxes_b, sems = more[:7], more[7:14], more[14:]
        ring = Ring(axes, sizes, sems[0], sems[1])
        ring.greet()
    assemble_rest(flat, grads, work)
    if link is None:
        assemble_first(flat, dar_ref, db_ref, down, router)
        out_ref[...] = align_out(flat, shard_rows(count), 0).reshape(-1)[:count]
        finish_sums(sums_ref[...])
        return
    rows = shard_rows(count)
    split = spans[1][0]

    def align(parts, span):
        for group in range(*span):
            for low in range(8):
                parts[group - span[0], low] = align_out(flat, rows, (8 * group + low) * count)

    rest = reduce_phases(ring, spans[1], parts_b, boxes_b, True, sums_ref, (near_out, near_in))
    first = reduce_phases(
        Ring(axes, sizes, sems[2], sems[3]), spans[0], parts_a, boxes_a, False
    )
    align(parts_b, spans[1])
    rest[0]()
    assemble_first(flat, dar_ref, db_ref, down, router)
    rest[1]()
    align(parts_a, spans[0])
    first[0]()
    rest[2]()
    for step in (1, 2):
        first[step]()
    for step in (3, 4, 5):
        rest[step]()
        first[step]()
    rest[6](finish_sums)
    first[6]()

    @pl.when(ring.group < split)
    def _():
        out_ref[...] = boxes_a[6][...].reshape(-1)[:count]

    @pl.when(ring.group >= split)
    def _():
        out_ref[...] = boxes_b[6][...].reshape(-1)[:count]


def finish(dar, db, grads, sums, count, axes, sizes, spans):
    rows = shard_rows(count)
    groups = sizes[0] * sizes[1] // 8
    link = (axes, sizes, spans) if groups else None
    scratch = [
        pltpu.VMEM((flat_rows(count), LANES), F32),
        pltpu.VMEM((D, LANES), F32),
        pltpu.VMEM((D, LANES), F32),
        pltpu.VMEM((SINGLE_BLOCKS * D, LANES), F32),
    ]
    if link:
        widths = [end - begin for begin, end in spans]
        scratch += [pltpu.VMEM((width, 8, rows, LANES), F32) for width in widths]
        scratch += [
            pltpu.VMEM((4, *sums.shape), F32),
            pltpu.VMEM((3 + groups, *sums.shape), F32),
        ]
        for width in widths:
            scratch += reduce_scratch(groups, width, rows) + [pltpu.VMEM((rows, LANES), F32)]
        scratch += [pltpu.SemaphoreType.DMA((10 + 2 * groups,))] * 4
    vmem = pl.BlockSpec(memory_space=pltpu.VMEM)
    return pl.pallas_call(
        functools.partial(finish_kernel, link, count),
        in_specs=[vmem] * (3 + len(grads)),
        out_specs=[vmem] * 2,
        out_shape=[
            jax.ShapeDtypeStruct((count,), F32),
            jax.ShapeDtypeStruct((4,), F32),
        ],
        scratch_shapes=scratch,
        compiler_params=params(collective_id=1, has_side_effects=True) if link else params(),
        name="finish",
    )(dar, db, *grads, sums)


def per_device(
    tokens,
    lengths,
    buckets,
    rel_table,
    gain_attn,
    gain_ff,
    w_qkv,
    w_out,
    w_in,
    w_down,
    adapters,
    cotangent,
    axes,
    sizes,
):
    seq_count, length, width = tokens.shape
    x = tokens.reshape(length, width)
    cot = cotangent.reshape(length, width)
    devices = sizes[0] * sizes[1]
    count = adapters.shape[0]
    groups = devices // 8
    split_groups = min(-(-FIRST_COUNT // (8 * count)), max(groups - 1, 1))
    spans = ((0, split_groups), (split_groups, groups))
    qt, k, kt, v, vt, zg, offsets, ar_qkv, b_qkv, *packed = start(
        x, gain_attn, w_qkv, adapters, buckets, rel_table.T, count, axes, sizes, spans
    )
    ot, lse = attend(lengths, offsets, qt, k, kt, vt)
    block_out, dmid, gt, sums, *grads = middle_part(
        lengths, ot, x, cot, gain_ff, w_out, w_in, w_down, packed
    )
    tokens_grad, dar_qkv, db_qkv = back_part(
        lengths,
        offsets,
        qt,
        k,
        kt,
        v,
        ot,
        gt,
        lse,
        x,
        gain_attn,
        w_qkv,
        ar_qkv,
        b_qkv,
        zg,
        dmid,
    )
    mine, roots = finish(dar_qkv, db_qkv, grads, sums, count, axes, sizes, spans)
    grad_shard = mine
    root_squares = roots
    return (
        block_out.reshape(tokens.shape),
        tokens_grad.reshape(tokens.shape),
        grad_shard,
        root_squares,
    )


def solution(mesh):
    axes = tuple(mesh.axis_names)
    sizes = tuple(mesh.shape[axis] for axis in axes)
    sequence = P(axes, None, None)
    placed = (
        sequence,
        P(axes),
        P(),
        P(),
        P(),
        P(),
        P(),
        P(),
        P(),
        P(),
        P(axes),
        sequence,
    )
    return jax.shard_map(
        functools.partial(per_device, axes=axes, sizes=sizes),
        mesh=mesh,
        in_specs=placed,
        out_specs=(sequence, sequence, P(axes), P()),
        check_vma=False,
    )
```

```python
import functools

import jax
import jax.numpy as jnp
from jax import lax
from jax.experimental import pallas as pl
from jax.experimental.pallas import tpu as pltpu
from jax.sharding import PartitionSpec as P

D = 768
FF = 3072
HEADS = 12
HDIM = 64
EXPERTS = 10
RANK = 4
FANS = ((D, D), (D, D), (D, D), (D, D), (D, FF), (FF, D))
COLS = EXPERTS * RANK
LANES = 128

EPSILON = 1e-06
MASKED = -1000000000.0
GELU_SCALE = 0.7978845608028654
GELU_CUBIC = 0.044715
LOG2E = 1.4426950408889634
LN2 = 0.6931471805599453
QUERY_SCALE = 0.125 * LOG2E

ROWS = 256
MIDDLE_ROWS = 512
CHUNK = 512
QBLOCK = 256
UP_ROWS = 48
DOWN_ROWS = 2 * COLS
VMEM_BYTES = 60 * 1024 * 1024

F32 = jnp.float32
BF16 = jnp.bfloat16


def dot(a, b):
    return lax.dot_general(a, b, (((1,), (0,)), ((), ())), preferred_element_type=F32)


def dot_nt(a, b):
    return lax.dot_general(a, b, (((1,), (1,)), ((), ())), preferred_element_type=F32)


def dot_tn(a, b):
    return lax.dot_general(a, b, (((0,), (0,)), ((), ())), preferred_element_type=F32)


def exact_dot(a, b):
    return lax.dot_general(
        a,
        b,
        (((1,), (0,)), ((), ())),
        preferred_element_type=F32,
        precision=lax.Precision.HIGHEST,
    )


def lane_iota(shape):
    return lax.broadcasted_iota(jnp.int32, shape, 1)


def row_iota(shape):
    return lax.broadcasted_iota(jnp.int32, shape, 0)


def gates_of(logits):
    weights = jnp.exp(logits - jnp.max(logits, axis=0, keepdims=True))
    return weights * (4.0 / jnp.sum(weights, axis=0, keepdims=True))


def gate_grads(grad_mixed, lowrank, gates):
    product = grad_mixed * lowrank
    summed = product
    for step in range(1, RANK):
        summed = summed + pltpu.roll(product, COLS - step, 0)
    centre = jnp.sum(gates * product, axis=0, keepdims=True)
    first = row_iota(gates.shape) % RANK == 0
    return grad_mixed * gates, jnp.where(first, gates * (summed - centre), 0.0)


def pad_rows(value, rows):
    return jnp.concatenate([value, jnp.zeros((rows - value.shape[0], value.shape[1]), F32)], axis=0)


def single_gates(packed):
    turned = packed.T
    lowrank = turned[:COLS]
    gates = gates_of(turned[COLS : 2 * COLS])
    mixed = pad_rows(lowrank * gates, LANES).astype(BF16)
    return lowrank, gates, mixed, mixed.T


def single_deltas(grad_mixed, lowrank, gates):
    parts = gate_grads(grad_mixed.T[:COLS], lowrank, gates)
    delta = pad_rows(jnp.concatenate(parts, axis=0), LANES).astype(BF16)
    return delta, delta.T


def rms_inverse(values):
    return lax.rsqrt(jnp.mean(values * values, axis=-1, keepdims=True) + EPSILON)


def rms_backward(values, gain, inverse, grad_normed):
    weighted = grad_normed * gain
    return inverse * weighted - values * (
        inverse * inverse * inverse * jnp.mean(values * weighted, axis=-1, keepdims=True)
    )


def params(**more):
    return pltpu.CompilerParams(vmem_limit_bytes=VMEM_BYTES, **more)


def whole(shape):
    zeros = (0,) * len(shape)
    return pl.BlockSpec(shape, lambda *_: zeros, pipeline_mode=pl.Buffered(1))


def bias_table(offset_row, length):
    spread = jnp.broadcast_to(offset_row, (LANES, 2 * length))
    return pltpu.roll(spread, 2 * length - (LANES - 1), 1, stride=1, stride_axis=0)


def add_bias(scores, table_ref, start, length):
    width = scores.shape[1]
    parts = []
    for block in range(length // LANES):
        offset = start - LANES * block + (length - LANES)
        parts.append(
            scores[block * LANES : (block + 1) * LANES] + table_ref[:, offset : offset + width]
        )
    return jnp.concatenate(parts, axis=0)


def key_extras(length_ref, shape, odd):
    lane = lane_iota(shape) - (0 if odd else HDIM)
    invalid = row_iota(shape) >= length_ref[0]
    extras = jnp.where((lane == 0) & invalid, MASKED, 0.0)
    return jnp.where((lane >= 1) & (lane <= 3), 1.0, extras).astype(BF16)


def head_lanes(odd):
    lane = lane_iota((1, LANES))
    return ((lane >= HDIM) if odd else (lane < HDIM)).astype(F32).astype(BF16)


def extra_rows(rows):
    width = rows[0].shape[1]
    index = row_iota((8, width))
    block = jnp.zeros((8, width), F32)
    for place, row in enumerate(rows):
        block = jnp.where(index == place, row, block)
    return jnp.concatenate([block, jnp.zeros((HDIM - 8, width), F32)], axis=0).astype(BF16)


def split_three(row):
    high = row.astype(BF16).astype(F32)
    middle = (row - high).astype(BF16).astype(F32)
    return high, middle, row - high - middle


def join_rows(rows, extras, odd):
    return jnp.concatenate([extras, rows] if odd else [rows, extras], axis=0)


def attend_kernel(
    length_ref, off_ref, qt_ref, k_ref, kt_ref, vt_ref, o_ref, lse_ref, table, key_more, plain
):
    length = k_ref.shape[0]
    step = pl.program_id(0)

    @pl.when(step == 0)
    def _():
        for odd in range(2):
            key_more[odd] = key_extras(length_ref, k_ref.shape, odd)

    starts = range(0, length, QBLOCK)
    ones = jnp.ones((1, length), F32)

    def half_of(odd):
        return slice(odd * HDIM, (odd + 1) * HDIM)

    def keys_of(odd):
        return k_ref[...] * head_lanes(odd) + key_more[odd]

    def values_of(odd):
        return jnp.concatenate([vt_ref[half_of(odd), :], jnp.ones((16, length), BF16)], axis=0)

    def finish(odd, start, shift, weights):
        columns = slice(start, start + QBLOCK)
        summed = dot(values_of(odd), weights)
        total = summed[HDIM : HDIM + 1]
        o_ref[half_of(odd), columns] = (summed[:HDIM] / total).astype(BF16)
        lse_ref[0, odd : odd + 1, columns] = shift + jnp.log2(total)
        return total

    def bounded(odd):
        offsets = off_ref[pl.ds(2 * step + odd, 1), :]
        table[odd] = bias_table(offsets, length)
        squares = jnp.square(kt_ref[half_of(odd), :].astype(F32))
        sizes = jnp.sum(squares, axis=0, keepdims=True)
        sizes = jnp.where(lane_iota(sizes.shape) < length_ref[0], sizes, 0.0)
        largest = jnp.max(sizes, axis=1, keepdims=True)
        rows = qt_ref[half_of(odd), :].astype(F32)
        norms = jnp.sqrt(jnp.sum(rows * rows, axis=0, keepdims=True) * largest)
        bound = 1.001 * norms + jnp.max(offsets, axis=1, keepdims=True)
        queries = join_rows(
            qt_ref[half_of(odd), :],
            extra_rows([ones] + [-part for part in split_three(bound)]),
            odd,
        )
        keys = keys_of(odd)
        scores = [dot(keys, queries[:, start : start + QBLOCK]) for start in starts]
        weights = [
            jnp.exp2(add_bias(part, table.at[odd], start, length)).astype(BF16)
            for part, start in zip(scores, starts)
        ]
        least = None
        for start, part in zip(starts, weights):
            total = finish(odd, start, bound[:, start : start + QBLOCK], part)
            least = total if least is None else jnp.minimum(least, total)
        return least

    def exact(odd):
        plain[...] = join_rows(qt_ref[half_of(odd), :], extra_rows([ones]), odd)
        keys = keys_of(odd)

        def block(index, _):
            columns = pl.ds(pl.multiple_of(index * LANES, LANES), LANES)
            raw = dot(keys, plain[:, columns])
            parts = []
            for row in range(0, length, LANES):
                place = pl.multiple_of(index * LANES - row + (length - LANES), LANES)
                parts.append(raw[row : row + LANES] + table[odd, :, pl.ds(place, LANES)])
            scores = jnp.concatenate(parts, axis=0)
            peak = jnp.max(scores, axis=0, keepdims=True)
            summed = dot(values_of(odd), jnp.exp2(scores - peak).astype(BF16))
            total = summed[HDIM : HDIM + 1]
            o_ref[half_of(odd), columns] = (summed[:HDIM] / total).astype(BF16)
            lse_ref[0, odd : odd + 1, columns] = peak + jnp.log2(total)
            return 0

        lax.fori_loop(0, length // LANES, block, 0)

    least = jnp.minimum(bounded(0), bounded(1))

    @pl.when(jnp.logical_not(jnp.min(least) > 2.0**-100))
    def _():
        for odd in range(2):
            exact(odd)


def attend(length_valid, offsets, qt, k, kt, vt):
    length = k.shape[0]
    turned = pl.BlockSpec((LANES, length), lambda p: (p, 0))
    natural = pl.BlockSpec((length, LANES), lambda p: (0, p))
    return pl.pallas_call(
        attend_kernel,
        grid=(HEADS // 2,),
        in_specs=[
            pl.BlockSpec(memory_space=pltpu.SMEM),
            whole(offsets.shape),
            turned,
            natural,
            turned,
            turned,
        ],
        out_specs=[turned, pl.BlockSpec((1, 2, length), lambda p: (p, 0, 0))],
        out_shape=[
            jax.ShapeDtypeStruct((D, length), BF16),
            jax.ShapeDtypeStruct((HEADS // 2, 2, length), F32),
        ],
        scratch_shapes=[
            pltpu.VMEM((2, LANES, 2 * length), F32),
            pltpu.VMEM((2, length, LANES), BF16),
            pltpu.VMEM((LANES, length), BF16),
        ],
        compiler_params=params(),
        name="attend",
    )(length_valid, offsets, qt, k, kt, vt)


def middle_kernel(
    length_ref,
    ot_ref,
    x_ref,
    cot_ref,
    gain_ref,
    w_out_ref,
    w_in_hbm,
    w_down_hbm,
    ar_out_ref,
    b_out_ref,
    ar_in_ref,
    b_in_ref,
    ar_down_ref,
    b_down_ref,
    out_ref,
    dmid_ref,
    gt_ref,
    sums_ref,
    dar_out_ref,
    db_out_ref,
    dar_in_ref,
    db_in_ref,
    dar_down_ref,
    db_down_ref,
    active,
    slope,
    sloped,
    grad_hidden,
    feeds,
    w_in_ref,
    w_down_ref,
    loaded,
):
    step = pl.program_id(0)
    loads = [
        pltpu.make_async_copy(w_in_hbm, w_in_ref, loaded.at[0]),
        pltpu.make_async_copy(w_down_hbm, w_down_ref, loaded.at[1]),
    ]

    @pl.when(step == 0)
    def _():
        for load in loads:
            load.start()
        for ref in (
            sums_ref,
            dar_out_ref,
            db_out_ref,
            dar_in_ref,
            db_in_ref,
            dar_down_ref,
            db_down_ref,
        ):
            ref[...] = jnp.zeros_like(ref)

    attended = ot_ref[...].T
    inputs = x_ref[...].astype(F32)
    gain = gain_ref[...].reshape(1, D)
    cot = cot_ref[...]

    packed_out = dot(attended, ar_out_ref[...])
    branch = dot(attended, w_out_ref[...])
    low_out, gates_out, mixed_out, natural = single_gates(packed_out)
    grad_mixed_down = dot_nt(cot, b_down_ref[...])
    branch = branch + dot(natural, b_out_ref[...])
    middle = inputs + branch
    inverse = rms_inverse(middle)
    normed = (middle * inverse * gain).astype(BF16)

    packed_in = dot(normed, ar_in_ref[...])
    low_in, gates_in, mixed_in, natural = single_gates(packed_in)

    def columns_of(index):
        return pl.ds(pl.multiple_of(index * CHUNK, CHUNK), CHUNK)

    def hidden_of(chunk):
        return dot(normed, w_in_ref[:, chunk]) + dot(natural, b_in_ref[:, chunk])

    def activate(chunk, values):
        grad_dense = dot_nt(cot, w_down_ref[chunk])
        square = values * values
        tangent = jnp.tanh(values * (GELU_SCALE + (GELU_SCALE * GELU_CUBIC) * square))
        half = 0.5 + 0.5 * tangent
        smooth = values * half
        active[:, chunk] = smooth.astype(BF16)
        steep = half + smooth * (1.0 - tangent) * (
            GELU_SCALE + (3.0 * GELU_SCALE * GELU_CUBIC) * square
        )
        slope[:, chunk] = steep.astype(BF16)
        sloped[:, chunk] = grad_dense * steep

    def forward_pair(pair, _):
        chunk_a = columns_of(2 * pair)
        chunk_b = columns_of(2 * pair + 1)
        hidden_a = hidden_of(chunk_a)
        hidden_b = hidden_of(chunk_b)
        activate(chunk_a, hidden_a)
        activate(chunk_b, hidden_b)
        return 0

    @pl.when(step == 0)
    def _():
        for load in loads:
            load.wait()

    lax.fori_loop(0, FF // (2 * CHUNK), forward_pair, 0)

    packed_down = dot(active[...], ar_down_ref[...])
    for first in range(0, D, 256):
        part = slice(first, first + 256)
        feeds[:, part] = dot(active[...], w_down_ref[:, part])
    feed = feeds[...]
    low_down, gates_down, mixed_down, natural = single_gates(packed_down)
    delta_down, natural_delta = single_deltas(grad_mixed_down, low_down, gates_down)
    db_down_ref[...] += dot(mixed_down[:UP_ROWS], cot)
    feed = feed + dot(natural, b_down_ref[...])
    output = middle + feed
    out_ref[...] = output.astype(BF16)

    for first in range(0, FF, CHUNK):
        chunk = slice(first, first + CHUNK)
        grad_low = dot_nt(natural_delta, ar_down_ref[chunk])
        grad_hidden[:, chunk] = (
            sloped[:, chunk] + grad_low * slope[:, chunk].astype(F32)
        ).astype(BF16)

    rows = row_iota((MIDDLE_ROWS, 1)) + step * MIDDLE_ROWS
    valid = (rows < length_ref[0]).astype(F32)
    lane = lane_iota((8, LANES))
    totals = jnp.where((lane == 4) & (step == 0), length_ref[0].astype(F32), 0.0)
    for place, member in enumerate((inputs, branch, feed, output)):
        kept = member * valid
        totals = jnp.where(lane == place, jnp.sum(kept * kept), totals)
    sums_ref[...] += totals

    grad_mixed = dot_nt(grad_hidden[...], b_in_ref[...])
    for first in range(0, D, 256):
        part = slice(first, first + 256)
        feeds[:, part] = dot_nt(grad_hidden[...], w_in_ref[part])
    grad_normed = feeds[...]
    delta_in, natural_delta = single_deltas(grad_mixed, low_in, gates_in)
    grad_normed = grad_normed + dot_nt(natural_delta, ar_in_ref[...])
    dar_in_ref[...] += dot(delta_in[:DOWN_ROWS], normed)

    grad_middle = cot.astype(F32) + rms_backward(middle, gain, inverse, grad_normed)
    dmid_ref[...] = grad_middle
    grad_branch = grad_middle.astype(BF16)
    grad_mixed = dot_nt(grad_branch, b_out_ref[...])
    grad_attended = dot_nt(grad_branch, w_out_ref[...])
    dar_down_ref[...] += dot(delta_down[:DOWN_ROWS], active[...])
    db_in_ref[...] += dot(mixed_in[:UP_ROWS], grad_hidden[...])
    delta_out, natural_delta = single_deltas(grad_mixed, low_out, gates_out)
    grad_attended = grad_attended + dot_nt(natural_delta, ar_out_ref[...])
    gt_ref[...] = grad_attended.astype(BF16).T
    dar_out_ref[...] += dot(delta_out[:DOWN_ROWS], attended)
    db_out_ref[...] += dot(mixed_out[:UP_ROWS], grad_branch)


def middle_part(length_valid, ot, x, cot, gain, w_out, w_in, w_down, adapters):
    length = x.shape[0]
    tile = pl.BlockSpec((MIDDLE_ROWS, D), lambda i: (i, 0))
    turned = pl.BlockSpec((D, MIDDLE_ROWS), lambda i: (0, i))
    grad_shapes = [
        jax.ShapeDtypeStruct(shape, F32)
        for fan_in, fan_out in FANS[3:]
        for shape in ((DOWN_ROWS, fan_in), (UP_ROWS, fan_out))
    ]
    out_shape = [
        jax.ShapeDtypeStruct((length, D), BF16),
        jax.ShapeDtypeStruct((length, D), F32),
        jax.ShapeDtypeStruct((D, length), BF16),
        jax.ShapeDtypeStruct((8, LANES), F32),
    ] + grad_shapes
    return pl.pallas_call(
        middle_kernel,
        grid=(length // MIDDLE_ROWS,),
        in_specs=[pl.BlockSpec(memory_space=pltpu.SMEM), turned, tile, tile]
        + [whole(gain.shape), whole(w_out.shape)]
        + [pl.BlockSpec(memory_space=pl.ANY)] * 2
        + [whole(member.shape) for member in adapters],
        out_specs=[tile, tile, turned] + [whole(member.shape) for member in out_shape[3:]],
        out_shape=out_shape,
        scratch_shapes=[
            pltpu.VMEM((MIDDLE_ROWS, FF), BF16),
            pltpu.VMEM((MIDDLE_ROWS, FF), BF16),
            pltpu.VMEM((MIDDLE_ROWS, FF), F32),
            pltpu.VMEM((MIDDLE_ROWS, FF), BF16),
            pltpu.VMEM((MIDDLE_ROWS, D), F32),
            pltpu.VMEM(w_in.shape, BF16),
            pltpu.VMEM(w_down.shape, BF16),
            pltpu.SemaphoreType.DMA((2,)),
        ],
        compiler_params=params(),
        name="middle_part",
    )(length_valid, ot, x, cot, gain, w_out, w_in, w_down, *adapters)


def attend_back(
    pair,
    length_ref,
    off_ref,
    qt_ref,
    k_ref,
    kt_ref,
    v_ref,
    ot_ref,
    gt_ref,
    lse_ref,
    grads_ref,
    table,
    key_more,
    weights_all,
    grads_all,
):
    length = k_ref.shape[0]
    lane = lane_iota((1, LANES))
    first_lanes = lane < HDIM
    grad_query_parts = []
    for odd in range(2):
        half = slice(odd * HDIM, (odd + 1) * HDIM)
        table[odd] = bias_table(off_ref[pl.ds(2 * pair + odd, 1), :], length)
        keys = k_ref[...] * head_lanes(odd) + key_more[odd]
        place = lane - (0 if odd else HDIM)
        value_more = ((place >= 0) & (place < 3)).astype(F32).astype(BF16)
        values = v_ref[...] * head_lanes(odd) + value_more
        ones = jnp.ones((1, length), F32)
        lse = lse_ref[0, odd : odd + 1, :]
        queries = join_rows(
            qt_ref[half, :], extra_rows([ones] + [-part for part in split_three(lse)]), odd
        )
        delta = jnp.sum(
            ot_ref[half, :].astype(F32) * gt_ref[half, :].astype(F32), axis=0, keepdims=True
        )
        grads = join_rows(
            gt_ref[half, :], extra_rows([-part for part in split_three(delta)]), odd
        )
        query_blocks = []
        previous = None
        for start in range(0, length, QBLOCK):
            columns = slice(start, start + QBLOCK)
            raw = dot(keys, queries[:, columns])
            grad_raw = dot(values, grads[:, columns])
            if previous is not None:
                query_blocks.append(dot(kt_ref[half, :], previous))
            weights = jnp.exp2(add_bias(raw, table.at[odd], start, length))
            weights_all[:, columns] = weights.astype(BF16)
            previous = (weights * grad_raw).astype(BF16)
            grads_all[:, columns] = previous
        query_blocks.append(dot(kt_ref[half, :], previous))
        grad_query_parts.append(jnp.concatenate(query_blocks, axis=1) * 0.125)
        grad_values = dot_nt(weights_all[...], gt_ref[...])
        grad_keys = dot_nt(grads_all[...], qt_ref[...]) * LN2
        if odd:
            grad_values = jnp.where(first_lanes, even_values, grad_values)
            grad_keys = jnp.where(first_lanes, even_keys, grad_keys)
        else:
            even_values, even_keys = grad_values, grad_keys
    columns = pl.ds(pl.multiple_of(pair * LANES, LANES), LANES)
    grads_ref[0, :, columns] = jnp.concatenate(grad_query_parts, axis=0).T.astype(BF16)
    grads_ref[1, :, columns] = grad_keys.astype(BF16)
    grads_ref[2, :, columns] = grad_values.astype(BF16)


def project_back(
    tile, x_ref, gain_ref, w_ref, ar_ref, b_ref, zg_ref, grads_ref, dmid_ref, out_ref, dar_ref, db_ref
):
    values = x_ref[...].astype(F32)
    gain = gain_ref[...].reshape(1, D)
    inverse = rms_inverse(values)
    normed = (values * inverse * gain).astype(BF16)
    lowrank = zg_ref[: 3 * COLS]
    gates = zg_ref[3 * COLS :]
    mixed = pad_rows(lowrank * gates, LANES).astype(BF16)
    rows = pl.ds(pl.multiple_of(tile * ROWS, ROWS), ROWS)
    grads = [grads_ref[index, rows] for index in range(3)]
    columns = [slice(index * D, (index + 1) * D) for index in range(3)]
    grad_mixed = jnp.zeros((ROWS, LANES), F32)
    for grad, lanes in zip(grads, columns):
        grad_mixed = grad_mixed + dot_nt(grad, b_ref[:, lanes])
    grad_normed = jnp.zeros((ROWS, D), F32)
    for grad, lanes in zip(grads, columns):
        grad_normed = grad_normed + dot_nt(grad, w_ref[:, lanes])
        db_ref[:, lanes] += dot(mixed, grad)
    turned = grad_mixed.T
    parts = []
    for first in range(0, 3 * COLS, COLS):
        place = slice(first, first + COLS)
        parts.append(gate_grads(turned[place], lowrank[place], gates[place]))
    delta = jnp.concatenate([part[0] for part in parts] + [part[1] for part in parts], axis=0)
    delta = pad_rows(delta, 2 * LANES).astype(BF16)
    grad_normed = grad_normed + dot_nt(delta.T, ar_ref[...])
    dar_ref[...] += dot(delta, normed)
    out_ref[...] = dmid_ref[...] + rms_backward(values, gain, inverse, grad_normed)


def back_kernel(*refs):
    length_ref = refs[0]
    heads_refs = refs[:9]
    x_ref, gain_ref, w_hbm, ar_ref, b_ref, zg_ref, dmid_ref = refs[9:16]
    out_ref, dar_ref, db_ref = refs[16:19]
    table, key_more, weights_all, grads_all, grads_ref, w_ref, loaded = refs[19:]
    step = pl.program_id(0)
    pairs = HEADS // 2
    load = pltpu.make_async_copy(w_hbm, w_ref, loaded)

    @pl.when(step == 0)
    def _():
        load.start()
        dar_ref[...] = jnp.zeros_like(dar_ref)
        db_ref[...] = jnp.zeros_like(db_ref)
        for odd in range(2):
            key_more[odd] = key_extras(length_ref, key_more.shape[1:], odd)

    @pl.when(step < pairs)
    def _():
        attend_back(step, *heads_refs, grads_ref, table, key_more, weights_all, grads_all)

    @pl.when(step == pairs)
    def _():
        load.wait()

    @pl.when(step >= pairs)
    def _():
        project_back(
            step - pairs,
            x_ref,
            gain_ref,
            w_ref,
            ar_ref,
            b_ref,
            zg_ref,
            grads_ref,
            dmid_ref,
            out_ref,
            dar_ref,
            db_ref,
        )


def back_part(
    length_valid, offsets, qt, k, kt, v, ot, gt, lse, x, gain, w_qkv, ar_qkv, b_qkv, zg, dmid
):
    length = k.shape[0]
    pairs = HEADS // 2

    def pair_of(i):
        return jnp.minimum(i, pairs - 1)

    def tile_of(i):
        return jnp.maximum(i - pairs, 0)

    turned = pl.BlockSpec((LANES, length), lambda i: (pair_of(i), 0))
    natural = pl.BlockSpec((length, LANES), lambda i: (0, pair_of(i)))
    tile = pl.BlockSpec((ROWS, D), lambda i: (tile_of(i), 0))
    out_shape = [
        jax.ShapeDtypeStruct((length, D), F32),
        jax.ShapeDtypeStruct((2 * LANES, D), F32),
        jax.ShapeDtypeStruct((LANES, 3 * D), F32),
    ]
    return pl.pallas_call(
        back_kernel,
        grid=(pairs + length // ROWS,),
        in_specs=[
            pl.BlockSpec(memory_space=pltpu.SMEM),
            whole(offsets.shape),
            turned,
            natural,
            turned,
            natural,
            turned,
            turned,
            pl.BlockSpec((1, 2, length), lambda i: (pair_of(i), 0, 0)),
            tile,
            whole((D,)),
            pl.BlockSpec(memory_space=pl.ANY),
            whole(ar_qkv.shape),
            whole(b_qkv.shape),
            pl.BlockSpec((6 * COLS, ROWS), lambda i: (0, tile_of(i))),
            tile,
        ],
        out_specs=[tile] + [whole(member.shape) for member in out_shape[1:]],
        out_shape=out_shape,
        scratch_shapes=[
            pltpu.VMEM((2, LANES, 2 * length), F32),
            pltpu.VMEM((2, length, LANES), BF16),
            pltpu.VMEM((length, length), BF16),
            pltpu.VMEM((length, length), BF16),
            pltpu.VMEM((3, length, D), BF16),
            pltpu.VMEM(w_qkv.shape, BF16),
            pltpu.SemaphoreType.DMA,
        ],
        compiler_params=params(),
        name="back_part",
    )(length_valid, offsets, qt, k, kt, v, ot, gt, lse, x, gain, w_qkv, ar_qkv, b_qkv, zg, dmid)


PARAM_ROWS = sum((COLS + EXPERTS) * fan_in + COLS * fan_out for fan_in, fan_out in FANS) // LANES


def piece_rows():
    result = []
    row = 0
    for fan_in, fan_out in FANS:
        starts = []
        for count in (fan_in * COLS, COLS * fan_out, fan_in * EXPERTS):
            starts.append(row)
            row += count // LANES
        result.append(tuple(starts))
    return result


def shard_rows(count):
    return -(-count // (LANES * 16)) * 16


def align_in(flat_ref, shard, start):
    first, shift = divmod(start, LANES)
    rows = shard.shape[0]
    if shift == 0:
        flat_ref[first : first + rows] = shard
        return
    turned = pltpu.roll(shard, shift, 1)
    lane = lane_iota((1, LANES))
    zeros = jnp.zeros((8, LANES), F32)
    upper = jnp.concatenate([turned, zeros], axis=0)
    lower = pltpu.roll(upper, 1, 0)
    kept = flat_ref[first : first + 8]
    merged = jnp.where(lane >= shift, upper, lower)
    inside = (row_iota((8, LANES)) == 0) & (lane_iota((8, LANES)) < shift)
    flat_ref[first : first + 8] = jnp.where(inside, kept, merged[:8])
    flat_ref[first + 8 : first + 8 + rows] = merged[8:]


def align_out(flat_ref, rows, start):
    first, shift = divmod(start, LANES)
    if shift == 0:
        return flat_ref[first : first + rows]
    block = flat_ref[first : first + rows + 8]
    turned = pltpu.roll(block, LANES - shift, 1)
    below = pltpu.roll(turned, rows + 7, 0)
    lane = lane_iota((1, LANES))
    return jnp.where(lane < LANES - shift, turned, below)[:rows]


GROUP = 64


def narrow_to_rows(flat_ref, fan_in, items, out_ref, begin=0):
    groups = fan_in // GROUP
    lane = lane_iota((1, LANES))
    lines = [
        [
            flat_ref[pl.ds(base + k, groups, stride=width * GROUP // LANES), :]
            for k in range(width * GROUP // LANES)
        ]
        for base, width, _ in items
    ]
    for b in range(GROUP):
        result = jnp.zeros((groups, LANES), F32)
        for line, (_, width, place) in zip(lines, items):
            first, shift = divmod(width * b, LANES)
            amount = (place - shift) % LANES
            value = line[first] if amount == 0 else pltpu.roll(line[first], amount, 1)
            if shift + width > LANES:
                value = jnp.where(
                    lane < place + LANES - shift, value, pltpu.roll(line[first + 1], amount, 1)
                )
            inside = (lane >= place) & (lane < place + width)
            result = jnp.where(inside, value, result)
        out_ref[pl.ds(begin + b, groups, stride=GROUP), :] = result


def rows_to_narrow(in_ref, fan_in, items, flat_ref, begin=0):
    groups = fan_in // GROUP
    lane = lane_iota((1, LANES))
    lines = [
        [jnp.zeros((groups, LANES), F32) for _ in range(width * GROUP // LANES)]
        for _, width, _ in items
    ]
    for b in range(GROUP):
        source = in_ref[pl.ds(begin + b, groups, stride=GROUP), :]
        for line, (_, width, place) in zip(lines, items):
            first, shift = divmod(width * b, LANES)
            amount = (shift - place) % LANES
            value = source if amount == 0 else pltpu.roll(source, amount, 1)
            inside = (lane >= shift) & (lane < shift + width)
            line[first] = jnp.where(inside, value, line[first])
            if shift + width > LANES:
                line[first + 1] = jnp.where(lane < shift + width - LANES, value, line[first + 1])
    for line, (base, width, _) in zip(lines, items):
        for k, value in enumerate(line):
            flat_ref[pl.ds(base + k, groups, stride=width * GROUP // LANES), :] = value


def single_items(block):
    starts = piece_rows()
    after_out, after_in = (block + 4) // 5, (block + 2) // 4
    down = (block - 2) * after_in
    bases = []
    for piece, width in ((0, COLS), (2, EXPERTS)):
        out, inner, outer = (starts[index][piece] for index in range(3, 6))
        base = out + (inner - out) * after_out + (outer - inner) * after_in
        bases.append(base + down * (D * width // LANES))
    return [(bases[0], COLS, 0), (bases[1], EXPERTS, COLS)]


SINGLE_BLOCKS = 2 + FF // D


def spread_matrix(experts, source, place):
    row = row_iota((LANES, LANES)) - source
    lane = lane_iota((LANES, LANES)) - place
    hit = (lane >= RANK * row) & (lane < RANK * row + RANK) & (row >= 0) & (row < experts)
    return jnp.where(hit, 1.0, 0.0)


def keep_matrix():
    row = row_iota((LANES, LANES))
    return jnp.where((row == lane_iota((LANES, LANES))) & (row < COLS), 1.0, 0.0)


FIRST_COUNT = sum((COLS + EXPERTS) * fan_in + COLS * fan_out for fan_in, fan_out in FANS[:3])


def unpack_ups(flat, base, fan_out, first, out_ref, column):
    width = fan_out // LANES
    above = jnp.zeros((first, LANES), F32)
    below = jnp.zeros((LANES - COLS - first, LANES), F32)
    for k in range(width):
        part = flat[pl.ds(base + k, COLS, stride=width), :]
        parts = [part, below] if first == 0 else [above, part, below]
        lanes = slice(column + k * LANES, column + (k + 1) * LANES)
        out_ref[:, lanes] = jnp.concatenate(parts, axis=0).astype(BF16)


def unpack_first(flat, ar_ref, b_ref, down, router):
    starts = piece_rows()
    narrow_to_rows(flat, D, [(starts[k][0], COLS, k * COLS) for k in range(3)], down)
    narrow_to_rows(flat, D, [(starts[k][2], EXPERTS, k * EXPERTS) for k in range(3)], router)
    routers = router[...].astype(BF16)
    for half in range(2):
        matrix = spread_matrix(3 * EXPERTS, 0, 3 * COLS - half * LANES).astype(BF16)
        packed = dot(routers, matrix)
        packed = packed if half else packed + down[...]
        ar_ref[:, half * LANES : (half + 1) * LANES] = packed.astype(BF16)
    for index in range(3):
        unpack_ups(flat, starts[index][1], D, index * COLS, b_ref, index * D)


def flat_rows(count):
    return PARAM_ROWS + shard_rows(count) + 20


def unpack_rest(flat, outs, work):
    starts = piece_rows()
    matrix = (keep_matrix() + spread_matrix(EXPERTS, COLS, COLS)).astype(BF16)

    def block(index, _):
        narrow_to_rows(flat, D, single_items(index), work, index * D)
        return 0

    lax.fori_loop(0, SINGLE_BLOCKS, block, 0)
    begin = 0
    for index in range(3, 6):
        fan_in, fan_out = FANS[index]
        ar_ref, b_ref = outs[2 * index - 6], outs[2 * index - 5]
        ar_ref[...] = dot(work[begin : begin + fan_in].astype(BF16), matrix).astype(BF16)
        unpack_ups(flat, starts[index][1], fan_out, 0, b_ref, 0)
        begin += fan_in


def split_dot(value, matrix):
    high = value.astype(BF16)
    return dot(high, matrix) + dot((value - high.astype(F32)).astype(BF16), matrix)


def first_of_four(experts, source, place):
    row = row_iota((LANES, LANES)) - source
    lane = lane_iota((LANES, LANES)) - place
    hit = (row == RANK * lane) & (lane >= 0) & (lane < experts)
    return jnp.where(hit, 1.0, 0.0)


def assemble_ups(flat, base, fan_out, first, grad_ref, column):
    width = fan_out // LANES
    for k in range(width):
        lanes = slice(column + k * LANES, column + (k + 1) * LANES)
        flat[pl.ds(base + k, COLS, stride=width), :] = grad_ref[first : first + COLS, lanes]


def assemble_rest(flat, grads, work):
    starts = piece_rows()
    matrix = (keep_matrix() + first_of_four(EXPERTS, COLS, COLS)).astype(BF16)
    begin = 0
    for index in range(3, 6):
        fan_in, fan_out = FANS[index]
        dar_ref, db_ref = grads[2 * index - 6], grads[2 * index - 5]
        work[begin : begin + fan_in] = split_dot(pad_rows(dar_ref[...], LANES).T, matrix)
        assemble_ups(flat, starts[index][1], fan_out, 0, db_ref, 0)
        begin += fan_in

    def block(index, _):
        rows_to_narrow(work, D, single_items(index), flat, index * D)
        return 0

    lax.fori_loop(0, SINGLE_BLOCKS, block, 0)


def assemble_first(flat, dar_ref, db_ref, down, router):
    starts = piece_rows()
    down[...] = dar_ref[:LANES].T
    rows_to_narrow(down, D, [(starts[k][0], COLS, k * COLS) for k in range(3)], flat)
    first_router = 3 * COLS
    turned = dar_ref[first_router : first_router + LANES].T
    router[...] = split_dot(turned, first_of_four(3 * EXPERTS, 0, 0).astype(BF16))
    rows_to_narrow(router, D, [(starts[k][2], EXPERTS, k * EXPERTS) for k in range(3)], flat)
    for index in range(3):
        assemble_ups(flat, starts[index][1], D, index * COLS, db_ref, index * D)


MESH = pl.DeviceIdType.MESH


def place_of(axes, sizes):
    me = lax.axis_index(axes[0]) * sizes[1] + lax.axis_index(axes[1])

    def coordinates(number):
        return (number // sizes[1], number % sizes[1])

    return me, coordinates


def partners_of(me):
    low = me % 8
    core = low % 2
    y = (low // 2) % 2
    x = low // 4
    over_x = low + 4 * (1 - 2 * x)
    over_y = low + 2 * (1 - 2 * y)
    first = over_x * (1 - core) + over_y * core
    second = over_y * (1 - core) + over_x * core
    both = first + second - low
    other = 1 - 2 * core
    return low, first, second, both, other, over_x, over_y


def greet(peers):
    for peer in peers:
        pl.semaphore_signal(
            pltpu.get_barrier_semaphore(), inc=1, device_id=peer, device_id_type=MESH
        )


def await_greetings(count):
    pl.semaphore_wait(pltpu.get_barrier_semaphore(), count)


class Ring:
    def __init__(self, axes, sizes, send, receive):
        self.me, self.coordinates = place_of(axes, sizes)
        self.groups = sizes[0] * sizes[1] // 8
        self.group = self.me // 8
        places = partners_of(self.me)
        self.low, self.first, self.second, self.both, self.other, self.over_x, self.over_y = places
        self.mate = self.low + self.other
        self.send, self.receive = send, receive
        self.copies = {}

    def device(self, group, low):
        return self.coordinates(group * 8 + low)

    def greet(self):
        peers = [
            self.device((self.group + step) % self.groups, self.low)
            for step in range(1, self.groups)
        ]
        peers += [self.device(self.group, low) for low in (self.first, self.second, self.mate)]
        greet(peers)

    def await_greetings(self):
        await_greetings(self.groups + 2)

    def copy(self, slot, source, target, peer, arrival=None):
        return pltpu.make_async_remote_copy(
            src_ref=source,
            dst_ref=target,
            send_sem=self.send.at[slot],
            recv_sem=self.receive.at[slot if arrival is None else arrival],
            device_id=peer,
            device_id_type=MESH,
        )


def gather_phases(ring, span, shard_ref, out_ref, local, greets):
    begin, end = span
    base = ring.groups
    inside = (ring.group >= begin) & (ring.group < end)

    def around(step):
        target = (ring.group + step) % ring.groups
        return ring.copy(
            step,
            shard_ref,
            out_ref.at[ring.group - begin, ring.low],
            ring.device(target, ring.low),
            base + 7 + ring.group,
        )

    def arrived(group):
        return ring.copy(
            0,
            shard_ref,
            out_ref.at[group - begin, ring.low],
            ring.device(group, ring.low),
            base + 7 + group,
        )

    def push(slot, part, partner):
        return ring.copy(
            base + slot, out_ref.at[:, part], out_ref.at[:, part], ring.device(ring.group, partner)
        )

    one = push(0, ring.low, ring.first)
    two = push(1, ring.low, ring.second)
    three = push(2, ring.first, ring.second)
    cores = [
        push(3 + index, part, ring.mate)
        for index, part in enumerate((ring.low, ring.first, ring.second, ring.both))
    ]

    def own():
        return pltpu.make_async_copy(
            shard_ref, out_ref.at[ring.group - begin, ring.low], local
        )

    def phase0():
        if greets:
            ring.greet()
            ring.await_greetings()

        @pl.when(inside)
        def _():
            own().start()
            for step in range(1, ring.groups):
                around(step).start()

    def phase1():
        @pl.when(inside)
        def _():
            own().wait()
            for step in range(1, ring.groups):
                around(step).wait_send()

        for group in range(begin, end):

            @pl.when(ring.group != group)
            def _():
                arrived(group).wait_recv()

        for copy in (one, two, cores[0]):
            copy.start()

    def phase2():
        one.wait()
        three.start()
        cores[1].start()

    def phase3():
        two.wait()
        cores[2].start()
        three.wait()
        cores[3].start()

    def phase4():
        for copy in cores:
            copy.wait()

    return phase0, phase1, phase2, phase3, phase4


def gather_semaphores(groups):
    return [
        pltpu.SemaphoreType.DMA((groups + 7,)),
        pltpu.SemaphoreType.DMA((2 * groups + 7,)),
        pltpu.SemaphoreType.DMA,
    ]


def start_kernel(
    link,
    count,
    values_ref,
    buckets_ref,
    table_ref,
    gain_ref,
    x_hbm,
    w_hbm,
    *refs,
):
    hbm_outs, off_ref, ar_ref, b_ref = refs[:6], refs[6], refs[7], refs[8]
    rest_refs = refs[9:15]
    x_ref, w_ref, normed, dense = refs[15:19]
    outs = refs[19:25]
    qt_ref, k_ref, kt_ref, v_ref, vt_ref, zg_ref = outs
    flat, down, router, work, offsets_ref, shard_ref, loaded, stored, *more = refs[25:]
    loads = [
        pltpu.make_async_copy(x_hbm, x_ref, loaded.at[0]),
        pltpu.make_async_copy(w_hbm, w_ref, loaded.at[1]),
    ]
    stores = [
        pltpu.make_async_copy(source, target, stored.at[index])
        for index, (source, target) in enumerate(zip(outs, hbm_outs))
    ]
    for load in loads:
        load.start()
    values = values_ref[...].astype(F32)
    values = jnp.pad(values, (0, shard_ref.shape[0] * LANES - count))
    shard_ref[...] = values.reshape(shard_ref.shape).astype(BF16)
    if link is None:
        first = [lambda: None] * 5
        rest = first

        def shard_of(index):
            return shard_ref[...]
    else:
        axes, sizes, spans = link
        land_a, land_b, *sems = more
        first = gather_phases(
            Ring(axes, sizes, *sems[:2]), spans[0], shard_ref, land_a, sems[2], True
        )
        rest = gather_phases(
            Ring(axes, sizes, *sems[3:5]), spans[1], shard_ref, land_b, sems[5], False
        )

        def shard_of(index):
            group, low = divmod(index, 8)
            begin = spans[1][0]
            return land_a[group, low] if group < begin else land_b[group - begin, low]

    length = x_ref.shape[0]

    def dense_tile(index):
        rows = slice(index * length // 2, (index + 1) * length // 2)
        values = x_ref[rows].astype(F32)
        low = (values * rms_inverse(values) * gain_ref[...].reshape(1, D)).astype(BF16)
        normed[rows] = low

        def columns(part, _):
            lanes = pl.ds(pl.multiple_of(part * D, D), D)
            dense[rows, lanes] = dot(normed[rows], w_ref[:, lanes])
            return 0

        lax.fori_loop(0, 3, columns, 0)

    def project():
        packed = dot(normed[...], ar_ref[...]).T
        lowrank = packed[: 3 * COLS]
        gates = jnp.concatenate(
            [gates_of(packed[place : place + COLS]) for place in range(3 * COLS, 6 * COLS, COLS)],
            axis=0,
        )
        zg_ref[: 3 * COLS] = lowrank
        zg_ref[3 * COLS :] = gates
        stores[5].start()
        mixed = pad_rows(lowrank * gates, LANES).astype(BF16).T
        for part in range(3):
            columns = slice(part * D, (part + 1) * D)
            value = dense[:, columns] + dot(mixed, b_ref[:, columns])
            if part == 0:
                qt_ref[...] = (value * QUERY_SCALE).astype(BF16).T
                stores[0].start()
            else:
                low = value.astype(BF16)
                natural, turned = ((k_ref, kt_ref), (v_ref, vt_ref))[part - 1]
                natural[...] = low
                turned[...] = low.T
                stores[2 * part - 1].start()
                stores[2 * part].start()

    first[0]()
    rest[0]()
    for load in loads:
        load.wait()
    dense_tile(0)
    first[1]()
    rest[1]()
    dense_tile(1)
    first[2]()
    buckets = buckets_ref[...].reshape(1, buckets_ref.shape[0])
    hits = jnp.where(row_iota((table_ref.shape[1], buckets.shape[1])) == buckets, LOG2E, 0.0)
    offsets_ref[...] = jnp.zeros_like(offsets_ref)
    offsets_ref[:, : buckets.shape[1]] = exact_dot(table_ref[...], hits)
    flip = (row_iota((LANES, LANES)) + lane_iota((LANES, LANES)) == LANES - 1).astype(F32)
    blocks = offsets_ref.shape[1] // LANES
    for block in range(blocks):
        lanes = slice(block * LANES, (block + 1) * LANES)
        turned = slice((blocks - 1 - block) * LANES, (blocks - block) * LANES)
        off_ref[:, turned] = exact_dot(offsets_ref[:, lanes], flip)
    off_ref[...] = pltpu.roll(off_ref[...], offsets_ref.shape[1] - 1, 1)
    first[3]()
    rest[2]()
    first[4]()
    for index in range(-(-FIRST_COUNT // count)):
        align_in(flat, shard_of(index).astype(F32), index * count)
    unpack_first(flat, ar_ref, b_ref, down, router)
    rest[3]()
    project()
    rest[4]()
    for index in range(FIRST_COUNT // count, PARAM_ROWS * LANES // count):
        align_in(flat, shard_of(index).astype(F32), index * count)
    unpack_rest(flat, rest_refs, work)
    for store in stores:
        store.wait()


def start(x, gain, w_qkv, shard, buckets, rel_table, count, axes, sizes, spans):
    length = x.shape[0]
    groups = sizes[0] * sizes[1] // 8
    link = (axes, sizes, spans) if groups else None
    rest_shapes = [
        shape for fan_in, fan_out in FANS[3:] for shape in ((fan_in, LANES), (LANES, fan_out))
    ]
    wide = [
        ((D, length), BF16),
        ((length, D), BF16),
        ((D, length), BF16),
        ((length, D), BF16),
        ((D, length), BF16),
        ((6 * COLS, length), F32),
    ]
    small = [
        ((HEADS, 2 * length), F32),
        ((D, 2 * LANES), BF16),
        ((LANES, 3 * D), BF16),
    ] + [(shape, BF16) for shape in rest_shapes]
    scratch = [
        pltpu.VMEM(x.shape, BF16),
        pltpu.VMEM(w_qkv.shape, BF16),
        pltpu.VMEM(x.shape, BF16),
        pltpu.VMEM((length, 3 * D), F32),
    ]
    scratch += [pltpu.VMEM(*member) for member in wide]
    scratch += [
        pltpu.VMEM((flat_rows(count), LANES), F32),
        pltpu.VMEM((D, LANES), F32),
        pltpu.VMEM((D, LANES), F32),
        pltpu.VMEM((SINGLE_BLOCKS * D, LANES), F32),
        pltpu.VMEM((HEADS, 2 * length), F32),
        pltpu.VMEM((shard_rows(count), LANES), BF16),
        pltpu.SemaphoreType.DMA((2,)),
        pltpu.SemaphoreType.DMA((len(wide),)),
    ]
    if link:
        rows = shard_rows(count)
        scratch += [pltpu.VMEM((end - begin, 8, rows, LANES), BF16) for begin, end in spans]
        scratch += gather_semaphores(groups) * 2
    vmem = pl.BlockSpec(memory_space=pltpu.VMEM)
    anywhere = pl.BlockSpec(memory_space=pl.ANY)
    return pl.pallas_call(
        functools.partial(start_kernel, link, count),
        in_specs=[vmem] * 4 + [anywhere] * 2,
        out_specs=[anywhere] * len(wide) + [vmem] * len(small),
        out_shape=[jax.ShapeDtypeStruct(*member) for member in wide + small],
        scratch_shapes=scratch,
        compiler_params=params(collective_id=0, has_side_effects=True) if link else params(),
        name="start",
    )(shard, buckets, rel_table, gain, x, w_qkv)


def reduce_phases(ring, span, parts_ref, boxes, greets, sums_ref=None, sum_boxes=None):
    begin, end = span
    outbox, inbox, half, own, far_out, far_in, out_ref = boxes
    groups = ring.groups
    inside = (ring.group >= begin) & (ring.group < end)
    core_parts = (ring.first, ring.both, ring.second, ring.low)
    near = [ring.mate] * 4 + [ring.second, ring.second, ring.first]

    def push(slot):
        return ring.copy(slot, outbox.at[slot], inbox.at[slot], ring.device(ring.group, near[slot]))

    def fill(slot, value):
        outbox[slot] = value.astype(BF16)
        push(slot).start()

    def around(group):
        return ring.copy(
            7 + group - begin,
            far_out.at[group - begin],
            far_in.at[ring.group],
            ring.device(group, ring.low),
            7 + ring.group,
        )

    def arrived(group):
        return ring.copy(
            7,
            far_out.at[0],
            far_in.at[group],
            ring.device(group, ring.low),
            7 + group,
        )

    base = 7 + groups
    sum_peers = (ring.mate, ring.over_x, ring.over_y)

    def push_sums(slot):
        near_out, near_in = sum_boxes
        return ring.copy(
            base + slot,
            near_out.at[slot],
            near_in.at[slot],
            ring.device(ring.group, sum_peers[slot]),
        )

    def around_sums(step):
        near_out, near_in = sum_boxes
        target = (ring.group + step) % groups
        return ring.copy(
            base + 2 + step,
            near_out.at[3],
            near_in.at[3 + ring.group],
            ring.device(target, ring.low),
        )

    def start_sums(slot, value):
        if sum_boxes is not None:
            sum_boxes[0][slot] = value
            push_sums(slot).start()

    def phase0():
        if greets:
            ring.await_greetings()
        if sum_boxes is not None:
            start_sums(0, sums_ref[...])
        for slot, part in enumerate(core_parts):
            fill(slot, parts_ref[:, part + ring.other])

    def phase1():
        push(0).wait()
        fill(4, parts_ref[:, ring.second] + inbox[0].astype(F32))
        push(1).wait()
        fill(5, parts_ref[:, ring.both] + inbox[1].astype(F32))
        if sum_boxes is not None:
            push_sums(0).wait()
            start_sums(1, sum_boxes[0][0] + sum_boxes[1][0])

    def add1():
        push(2).wait()
        half[...] = parts_ref[:, ring.first] + inbox[2].astype(F32)
        push(3).wait()
        own[...] = parts_ref[:, ring.low] + inbox[3].astype(F32)

    def phase2():
        push(5).wait()
        fill(6, half[...] + inbox[5].astype(F32))
        if sum_boxes is not None:
            push_sums(1).wait()
            start_sums(2, sum_boxes[0][1] + sum_boxes[1][1])

    def add2():
        push(4).wait()
        own[...] = own[...] + inbox[4].astype(F32)

    def phase3():
        push(6).wait()
        own[...] = own[...] + inbox[6].astype(F32)
        far_out[...] = own[...].astype(BF16)
        for group in range(begin, end):

            @pl.when(ring.group != group)
            def _():
                around(group).start()

        if sum_boxes is not None:
            near_out, near_in = sum_boxes
            push_sums(2).wait()
            near_out[3] = near_out[2] + near_in[2]
            for step in range(1, groups):
                around_sums(step).start()
            near_in[3 + ring.group] = near_out[3]

    def phase4(finish_sums=None):
        for group in range(begin, end):

            @pl.when(ring.group != group)
            def _():
                around(group).wait_send()

        @pl.when(inside)
        def _():
            for group in range(groups):

                @pl.when(ring.group != group)
                def _():
                    arrived(group).wait_recv()

            total = own[ring.group - begin]
            for step in range(1, groups):
                total = total + far_in[(ring.group + step) % groups].astype(F32)
            out_ref[...] = total

        if sum_boxes is not None:
            near_out, near_in = sum_boxes
            for step in range(1, groups):
                around_sums(step).wait()
            whole_sum = near_in[3]
            for index in range(1, groups):
                whole_sum = whole_sum + near_in[3 + index]
            finish_sums(whole_sum)

    return phase0, phase1, add1, phase2, add2, phase3, phase4


def reduce_scratch(groups, count, rows):
    return [
        pltpu.VMEM((7, count, rows, LANES), BF16),
        pltpu.VMEM((7, count, rows, LANES), BF16),
        pltpu.VMEM((count, rows, LANES), F32),
        pltpu.VMEM((count, rows, LANES), F32),
        pltpu.VMEM((count, rows, LANES), BF16),
        pltpu.VMEM((groups, rows, LANES), BF16),
    ]


def finish_kernel(link, count, dar_ref, db_ref, *refs):
    grads, sums_ref = refs[:6], refs[6]
    out_ref, roots_ref, flat, down, router, work, *more = refs[7:]

    def finish_sums(total):
        roots_ref[...] = jnp.sqrt(total / (total[:, 4:5] * D))[0, :4]

    if link is not None:
        axes, sizes, spans = link
        parts_a, parts_b, near_out, near_in, *more = more
        boxes_a, boxes_b, sems = more[:7], more[7:14], more[14:]
        ring = Ring(axes, sizes, sems[0], sems[1])
        ring.greet()
    assemble_rest(flat, grads, work)
    if link is None:
        assemble_first(flat, dar_ref, db_ref, down, router)
        out_ref[...] = align_out(flat, shard_rows(count), 0).reshape(-1)[:count]
        finish_sums(sums_ref[...])
        return
    rows = shard_rows(count)
    split = spans[1][0]

    def align(parts, span):
        for group in range(*span):
            for low in range(8):
                parts[group - span[0], low] = align_out(flat, rows, (8 * group + low) * count)

    rest = reduce_phases(ring, spans[1], parts_b, boxes_b, True, sums_ref, (near_out, near_in))
    first = reduce_phases(
        Ring(axes, sizes, sems[2], sems[3]), spans[0], parts_a, boxes_a, False
    )
    align(parts_b, spans[1])
    rest[0]()
    assemble_first(flat, dar_ref, db_ref, down, router)
    rest[1]()
    align(parts_a, spans[0])
    first[0]()
    rest[2]()
    for step in (1, 2):
        first[step]()
    for step in (3, 4, 5):
        rest[step]()
        first[step]()
    rest[6](finish_sums)
    first[6]()

    @pl.when(ring.group < split)
    def _():
        out_ref[...] = boxes_a[6][...].reshape(-1)[:count]

    @pl.when(ring.group >= split)
    def _():
        out_ref[...] = boxes_b[6][...].reshape(-1)[:count]


def finish(dar, db, grads, sums, count, axes, sizes, spans):
    rows = shard_rows(count)
    groups = sizes[0] * sizes[1] // 8
    link = (axes, sizes, spans) if groups else None
    scratch = [
        pltpu.VMEM((flat_rows(count), LANES), F32),
        pltpu.VMEM((D, LANES), F32),
        pltpu.VMEM((D, LANES), F32),
        pltpu.VMEM((SINGLE_BLOCKS * D, LANES), F32),
    ]
    if link:
        widths = [end - begin for begin, end in spans]
        scratch += [pltpu.VMEM((width, 8, rows, LANES), F32) for width in widths]
        scratch += [
            pltpu.VMEM((4, *sums.shape), F32),
            pltpu.VMEM((3 + groups, *sums.shape), F32),
        ]
        for width in widths:
            scratch += reduce_scratch(groups, width, rows) + [pltpu.VMEM((rows, LANES), F32)]
        scratch += [pltpu.SemaphoreType.DMA((10 + 2 * groups,))] * 4
    vmem = pl.BlockSpec(memory_space=pltpu.VMEM)
    return pl.pallas_call(
        functools.partial(finish_kernel, link, count),
        in_specs=[vmem] * (3 + len(grads)),
        out_specs=[vmem] * 2,
        out_shape=[
            jax.ShapeDtypeStruct((count,), F32),
            jax.ShapeDtypeStruct((4,), F32),
        ],
        scratch_shapes=scratch,
        compiler_params=params(collective_id=1, has_side_effects=True) if link else params(),
        name="finish",
    )(dar, db, *grads, sums)


def deliver_kernel(grads_ref, roots_ref, grads_out, roots_out):
    grads_out[...] = grads_ref[...]
    roots_out[...] = roots_ref[...]


def deliver(grads, roots):
    vmem = pl.BlockSpec(memory_space=pltpu.VMEM)
    return pl.pallas_call(
        deliver_kernel,
        in_specs=[vmem] * 2,
        out_specs=[vmem] * 2,
        out_shape=[jax.ShapeDtypeStruct(member.shape, F32) for member in (grads, roots)],
        compiler_params=params(),
        name="deliver",
    )(grads, roots)


def per_device(
    tokens,
    lengths,
    buckets,
    rel_table,
    gain_attn,
    gain_ff,
    w_qkv,
    w_out,
    w_in,
    w_down,
    adapters,
    cotangent,
    axes,
    sizes,
):
    seq_count, length, width = tokens.shape
    x = tokens.reshape(length, width)
    cot = cotangent.reshape(length, width)
    devices = sizes[0] * sizes[1]
    count = adapters.shape[0]
    groups = devices // 8
    split_groups = min(-(-FIRST_COUNT // (8 * count)), max(groups - 1, 1))
    spans = ((0, split_groups), (split_groups, groups))
    qt, k, kt, v, vt, zg, offsets, ar_qkv, b_qkv, *packed = start(
        x, gain_attn, w_qkv, adapters, buckets, rel_table.T, count, axes, sizes, spans
    )
    ot, lse = attend(lengths, offsets, qt, k, kt, vt)
    block_out, dmid, gt, sums, *grads = middle_part(
        lengths, ot, x, cot, gain_ff, w_out, w_in, w_down, packed
    )
    tokens_grad, dar_qkv, db_qkv = back_part(
        lengths,
        offsets,
        qt,
        k,
        kt,
        v,
        ot,
        gt,
        lse,
        x,
        gain_attn,
        w_qkv,
        ar_qkv,
        b_qkv,
        zg,
        dmid,
    )
    mine, roots = deliver(
        *finish(dar_qkv, db_qkv, grads, sums, count, axes, sizes, spans)
    )
    grad_shard = mine
    root_squares = roots
    return (
        block_out.reshape(tokens.shape),
        tokens_grad.reshape(tokens.shape),
        grad_shard,
        root_squares,
    )


def solution(mesh):
    axes = tuple(mesh.axis_names)
    sizes = tuple(mesh.shape[axis] for axis in axes)
    sequence = P(axes, None, None)
    placed = (
        sequence,
        P(axes),
        P(),
        P(),
        P(),
        P(),
        P(),
        P(),
        P(),
        P(),
        P(axes),
        sequence,
    )
    return jax.shard_map(
        functools.partial(per_device, axes=axes, sizes=sizes),
        mesh=mesh,
        in_specs=placed,
        out_specs=(sequence, sequence, P(axes), P()),
        check_vma=False,
    )
```

```python
import functools

import jax
import jax.numpy as jnp
from jax import lax
from jax.experimental import pallas as pl
from jax.experimental.pallas import tpu as pltpu
from jax.sharding import PartitionSpec as P

D = 768
FF = 3072
HEADS = 12
HDIM = 64
EXPERTS = 10
RANK = 4
FANS = ((D, D), (D, D), (D, D), (D, D), (D, FF), (FF, D))
COLS = EXPERTS * RANK
LANES = 128

EPSILON = 1e-06
MASKED = -1000000000.0
GELU_SCALE = 0.7978845608028654
GELU_CUBIC = 0.044715
LOG2E = 1.4426950408889634
LN2 = 0.6931471805599453
QUERY_SCALE = 0.125 * LOG2E

ROWS = 256
MIDDLE_ROWS = 512
CHUNK = 512
QBLOCK = 256
UP_ROWS = 48
DOWN_ROWS = 2 * COLS
VMEM_BYTES = 60 * 1024 * 1024

F32 = jnp.float32
BF16 = jnp.bfloat16


def dot(a, b):
    return lax.dot_general(a, b, (((1,), (0,)), ((), ())), preferred_element_type=F32)


def dot_nt(a, b):
    return lax.dot_general(a, b, (((1,), (1,)), ((), ())), preferred_element_type=F32)


def dot_tn(a, b):
    return lax.dot_general(a, b, (((0,), (0,)), ((), ())), preferred_element_type=F32)


def exact_dot(a, b):
    return lax.dot_general(
        a,
        b,
        (((1,), (0,)), ((), ())),
        preferred_element_type=F32,
        precision=lax.Precision.HIGHEST,
    )


def lane_iota(shape):
    return lax.broadcasted_iota(jnp.int32, shape, 1)


def row_iota(shape):
    return lax.broadcasted_iota(jnp.int32, shape, 0)


def gates_of(logits):
    weights = jnp.exp(logits - jnp.max(logits, axis=0, keepdims=True))
    return weights * (4.0 / jnp.sum(weights, axis=0, keepdims=True))


def gate_grads(grad_mixed, lowrank, gates):
    product = grad_mixed * lowrank
    summed = product
    for step in range(1, RANK):
        summed = summed + pltpu.roll(product, COLS - step, 0)
    centre = jnp.sum(gates * product, axis=0, keepdims=True)
    first = row_iota(gates.shape) % RANK == 0
    return grad_mixed * gates, jnp.where(first, gates * (summed - centre), 0.0)


def pad_rows(value, rows):
    return jnp.concatenate([value, jnp.zeros((rows - value.shape[0], value.shape[1]), F32)], axis=0)


def single_gates(packed):
    turned = packed.T
    lowrank = turned[:COLS]
    gates = gates_of(turned[COLS : 2 * COLS])
    mixed = pad_rows(lowrank * gates, LANES).astype(BF16)
    return lowrank, gates, mixed, mixed.T


def single_deltas(grad_mixed, lowrank, gates):
    parts = gate_grads(grad_mixed.T[:COLS], lowrank, gates)
    delta = pad_rows(jnp.concatenate(parts, axis=0), LANES).astype(BF16)
    return delta, delta.T


def rms_inverse(values):
    return lax.rsqrt(jnp.mean(values * values, axis=-1, keepdims=True) + EPSILON)


def rms_backward(values, gain, inverse, grad_normed):
    weighted = grad_normed * gain
    return inverse * weighted - values * (
        inverse * inverse * inverse * jnp.mean(values * weighted, axis=-1, keepdims=True)
    )


def params(**more):
    return pltpu.CompilerParams(vmem_limit_bytes=VMEM_BYTES, **more)


def whole(shape):
    zeros = (0,) * len(shape)
    return pl.BlockSpec(shape, lambda *_: zeros, pipeline_mode=pl.Buffered(1))


def bias_table(offset_row, length):
    spread = jnp.broadcast_to(offset_row, (LANES, 2 * length))
    return pltpu.roll(spread, 2 * length - (LANES - 1), 1, stride=1, stride_axis=0)


def add_bias(scores, table_ref, start, length):
    width = scores.shape[1]
    parts = []
    for block in range(length // LANES):
        offset = start - LANES * block + (length - LANES)
        parts.append(
            scores[block * LANES : (block + 1) * LANES] + table_ref[:, offset : offset + width]
        )
    return jnp.concatenate(parts, axis=0)


def key_extras(length_ref, shape, odd):
    lane = lane_iota(shape) - (0 if odd else HDIM)
    invalid = row_iota(shape) >= length_ref[0]
    extras = jnp.where((lane == 0) & invalid, MASKED, 0.0)
    return jnp.where((lane >= 1) & (lane <= 3), 1.0, extras).astype(BF16)


def head_lanes(odd):
    lane = lane_iota((1, LANES))
    return ((lane >= HDIM) if odd else (lane < HDIM)).astype(F32).astype(BF16)


def extra_rows(rows):
    width = rows[0].shape[1]
    index = row_iota((8, width))
    block = jnp.zeros((8, width), F32)
    for place, row in enumerate(rows):
        block = jnp.where(index == place, row, block)
    return jnp.concatenate([block, jnp.zeros((HDIM - 8, width), F32)], axis=0).astype(BF16)


def split_three(row):
    high = row.astype(BF16).astype(F32)
    middle = (row - high).astype(BF16).astype(F32)
    return high, middle, row - high - middle


def join_rows(rows, extras, odd):
    return jnp.concatenate([extras, rows] if odd else [rows, extras], axis=0)


def attend_kernel(
    length_ref, off_ref, qt_ref, k_ref, kt_ref, vt_ref, o_ref, lse_ref, table, key_more, plain
):
    length = k_ref.shape[0]
    step = pl.program_id(0)

    @pl.when(step == 0)
    def _():
        for odd in range(2):
            key_more[odd] = key_extras(length_ref, k_ref.shape, odd)

    starts = range(0, length, QBLOCK)
    ones = jnp.ones((1, length), F32)

    def half_of(odd):
        return slice(odd * HDIM, (odd + 1) * HDIM)

    def keys_of(odd):
        return k_ref[...] * head_lanes(odd) + key_more[odd]

    def values_of(odd):
        return jnp.concatenate([vt_ref[half_of(odd), :], jnp.ones((16, length), BF16)], axis=0)

    def finish(odd, start, shift, weights):
        columns = slice(start, start + QBLOCK)
        summed = dot(values_of(odd), weights)
        total = summed[HDIM : HDIM + 1]
        o_ref[half_of(odd), columns] = (summed[:HDIM] / total).astype(BF16)
        lse_ref[0, odd : odd + 1, columns] = shift + jnp.log2(total)
        return total

    def bounded(odd):
        offsets = off_ref[pl.ds(2 * step + odd, 1), :]
        table[odd] = bias_table(offsets, length)
        squares = jnp.square(kt_ref[half_of(odd), :].astype(F32))
        sizes = jnp.sum(squares, axis=0, keepdims=True)
        sizes = jnp.where(lane_iota(sizes.shape) < length_ref[0], sizes, 0.0)
        largest = jnp.max(sizes, axis=1, keepdims=True)
        rows = qt_ref[half_of(odd), :].astype(F32)
        norms = jnp.sqrt(jnp.sum(rows * rows, axis=0, keepdims=True) * largest)
        bound = 1.001 * norms + jnp.max(offsets, axis=1, keepdims=True)
        queries = join_rows(
            qt_ref[half_of(odd), :],
            extra_rows([ones] + [-part for part in split_three(bound)]),
            odd,
        )
        keys = keys_of(odd)
        scores = [dot(keys, queries[:, start : start + QBLOCK]) for start in starts]
        weights = [
            jnp.exp2(add_bias(part, table.at[odd], start, length)).astype(BF16)
            for part, start in zip(scores, starts)
        ]
        least = None
        for start, part in zip(starts, weights):
            total = finish(odd, start, bound[:, start : start + QBLOCK], part)
            least = total if least is None else jnp.minimum(least, total)
        return least

    def exact(odd):
        plain[...] = join_rows(qt_ref[half_of(odd), :], extra_rows([ones]), odd)
        keys = keys_of(odd)

        def block(index, _):
            columns = pl.ds(pl.multiple_of(index * LANES, LANES), LANES)
            raw = dot(keys, plain[:, columns])
            parts = []
            for row in range(0, length, LANES):
                place = pl.multiple_of(index * LANES - row + (length - LANES), LANES)
                parts.append(raw[row : row + LANES] + table[odd, :, pl.ds(place, LANES)])
            scores = jnp.concatenate(parts, axis=0)
            peak = jnp.max(scores, axis=0, keepdims=True)
            summed = dot(values_of(odd), jnp.exp2(scores - peak).astype(BF16))
            total = summed[HDIM : HDIM + 1]
            o_ref[half_of(odd), columns] = (summed[:HDIM] / total).astype(BF16)
            lse_ref[0, odd : odd + 1, columns] = peak + jnp.log2(total)
            return 0

        lax.fori_loop(0, length // LANES, block, 0)

    least = jnp.minimum(bounded(0), bounded(1))

    @pl.when(jnp.logical_not(jnp.min(least) > 2.0**-100))
    def _():
        for odd in range(2):
            exact(odd)


def attend(length_valid, offsets, qt, k, kt, vt):
    length = k.shape[0]
    turned = pl.BlockSpec((LANES, length), lambda p: (p, 0))
    natural = pl.BlockSpec((length, LANES), lambda p: (0, p))
    return pl.pallas_call(
        attend_kernel,
        grid=(HEADS // 2,),
        in_specs=[
            pl.BlockSpec(memory_space=pltpu.SMEM),
            whole(offsets.shape),
            turned,
            natural,
            turned,
            turned,
        ],
        out_specs=[turned, pl.BlockSpec((1, 2, length), lambda p: (p, 0, 0))],
        out_shape=[
            jax.ShapeDtypeStruct((D, length), BF16),
            jax.ShapeDtypeStruct((HEADS // 2, 2, length), F32),
        ],
        scratch_shapes=[
            pltpu.VMEM((2, LANES, 2 * length), F32),
            pltpu.VMEM((2, length, LANES), BF16),
            pltpu.VMEM((LANES, length), BF16),
        ],
        compiler_params=params(),
        name="attend",
    )(length_valid, offsets, qt, k, kt, vt)


def middle_kernel(
    length_ref,
    ot_ref,
    x_ref,
    cot_ref,
    gain_ref,
    w_out_ref,
    w_in_hbm,
    w_down_hbm,
    ar_out_ref,
    b_out_ref,
    ar_in_ref,
    b_in_ref,
    ar_down_ref,
    b_down_ref,
    out_ref,
    dmid_ref,
    gt_ref,
    sums_ref,
    dar_out_ref,
    db_out_ref,
    dar_in_ref,
    db_in_ref,
    dar_down_ref,
    db_down_ref,
    active,
    slope,
    sloped,
    grad_hidden,
    feeds,
    w_in_ref,
    w_down_ref,
    loaded,
):
    step = pl.program_id(0)
    loads = [
        pltpu.make_async_copy(w_in_hbm, w_in_ref, loaded.at[0]),
        pltpu.make_async_copy(w_down_hbm, w_down_ref, loaded.at[1]),
    ]

    @pl.when(step == 0)
    def _():
        for load in loads:
            load.start()
        for ref in (
            sums_ref,
            dar_out_ref,
            db_out_ref,
            dar_in_ref,
            db_in_ref,
            dar_down_ref,
            db_down_ref,
        ):
            ref[...] = jnp.zeros_like(ref)

    attended = ot_ref[...].T
    inputs = x_ref[...].astype(F32)
    gain = gain_ref[...].reshape(1, D)
    cot = cot_ref[...]

    packed_out = dot(attended, ar_out_ref[...])
    branch = dot(attended, w_out_ref[...])
    low_out, gates_out, mixed_out, natural = single_gates(packed_out)
    grad_mixed_down = dot_nt(cot, b_down_ref[...])
    branch = branch + dot(natural, b_out_ref[...])
    middle = inputs + branch
    inverse = rms_inverse(middle)
    normed = (middle * inverse * gain).astype(BF16)

    packed_in = dot(normed, ar_in_ref[...])
    low_in, gates_in, mixed_in, natural = single_gates(packed_in)

    def columns_of(index):
        return pl.ds(pl.multiple_of(index * CHUNK, CHUNK), CHUNK)

    def hidden_of(chunk):
        return dot(normed, w_in_ref[:, chunk]) + dot(natural, b_in_ref[:, chunk])

    def activate(chunk, values):
        grad_dense = dot_nt(cot, w_down_ref[chunk])
        square = values * values
        tangent = jnp.tanh(values * (GELU_SCALE + (GELU_SCALE * GELU_CUBIC) * square))
        half = 0.5 + 0.5 * tangent
        smooth = values * half
        active[:, chunk] = smooth.astype(BF16)
        steep = half + smooth * (1.0 - tangent) * (
            GELU_SCALE + (3.0 * GELU_SCALE * GELU_CUBIC) * square
        )
        slope[:, chunk] = steep.astype(BF16)
        sloped[:, chunk] = grad_dense * steep

    def forward_pair(pair, _):
        chunk_a = columns_of(2 * pair)
        chunk_b = columns_of(2 * pair + 1)
        hidden_a = hidden_of(chunk_a)
        hidden_b = hidden_of(chunk_b)
        activate(chunk_a, hidden_a)
        activate(chunk_b, hidden_b)
        return 0

    @pl.when(step == 0)
    def _():
        for load in loads:
            load.wait()

    lax.fori_loop(0, FF // (2 * CHUNK), forward_pair, 0)

    packed_down = dot(active[...], ar_down_ref[...])
    for first in range(0, D, 256):
        part = slice(first, first + 256)
        feeds[:, part] = dot(active[...], w_down_ref[:, part])
    feed = feeds[...]
    low_down, gates_down, mixed_down, natural = single_gates(packed_down)
    delta_down, natural_delta = single_deltas(grad_mixed_down, low_down, gates_down)
    db_down_ref[...] += dot(mixed_down[:UP_ROWS], cot)
    feed = feed + dot(natural, b_down_ref[...])
    output = middle + feed
    out_ref[...] = output.astype(BF16)

    for first in range(0, FF, CHUNK):
        chunk = slice(first, first + CHUNK)
        grad_low = dot_nt(natural_delta, ar_down_ref[chunk])
        grad_hidden[:, chunk] = (
            sloped[:, chunk] + grad_low * slope[:, chunk].astype(F32)
        ).astype(BF16)

    rows = row_iota((MIDDLE_ROWS, 1)) + step * MIDDLE_ROWS
    valid = (rows < length_ref[0]).astype(F32)
    lane = lane_iota((8, LANES))
    totals = jnp.where((lane == 4) & (step == 0), length_ref[0].astype(F32), 0.0)
    for place, member in enumerate((inputs, branch, feed, output)):
        kept = member * valid
        totals = jnp.where(lane == place, jnp.sum(kept * kept), totals)
    sums_ref[...] += totals

    grad_mixed = dot_nt(grad_hidden[...], b_in_ref[...])
    for first in range(0, D, 256):
        part = slice(first, first + 256)
        feeds[:, part] = dot_nt(grad_hidden[...], w_in_ref[part])
    grad_normed = feeds[...]
    delta_in, natural_delta = single_deltas(grad_mixed, low_in, gates_in)
    grad_normed = grad_normed + dot_nt(natural_delta, ar_in_ref[...])
    dar_in_ref[...] += dot(delta_in[:DOWN_ROWS], normed)

    grad_middle = cot.astype(F32) + rms_backward(middle, gain, inverse, grad_normed)
    dmid_ref[...] = grad_middle
    grad_branch = grad_middle.astype(BF16)
    grad_mixed = dot_nt(grad_branch, b_out_ref[...])
    grad_attended = dot_nt(grad_branch, w_out_ref[...])
    dar_down_ref[...] += dot(delta_down[:DOWN_ROWS], active[...])
    db_in_ref[...] += dot(mixed_in[:UP_ROWS], grad_hidden[...])
    delta_out, natural_delta = single_deltas(grad_mixed, low_out, gates_out)
    grad_attended = grad_attended + dot_nt(natural_delta, ar_out_ref[...])
    gt_ref[...] = grad_attended.astype(BF16).T
    dar_out_ref[...] += dot(delta_out[:DOWN_ROWS], attended)
    db_out_ref[...] += dot(mixed_out[:UP_ROWS], grad_branch)


def middle_part(length_valid, ot, x, cot, gain, w_out, w_in, w_down, adapters):
    length = x.shape[0]
    tile = pl.BlockSpec((MIDDLE_ROWS, D), lambda i: (i, 0))
    turned = pl.BlockSpec((D, MIDDLE_ROWS), lambda i: (0, i))
    grad_shapes = [
        jax.ShapeDtypeStruct(shape, F32)
        for fan_in, fan_out in FANS[3:]
        for shape in ((DOWN_ROWS, fan_in), (UP_ROWS, fan_out))
    ]
    out_shape = [
        jax.ShapeDtypeStruct((length, D), BF16),
        jax.ShapeDtypeStruct((length, D), F32),
        jax.ShapeDtypeStruct((D, length), BF16),
        jax.ShapeDtypeStruct((8, LANES), F32),
    ] + grad_shapes
    return pl.pallas_call(
        middle_kernel,
        grid=(length // MIDDLE_ROWS,),
        in_specs=[pl.BlockSpec(memory_space=pltpu.SMEM), turned, tile, tile]
        + [whole(gain.shape), whole(w_out.shape)]
        + [pl.BlockSpec(memory_space=pl.ANY)] * 2
        + [whole(member.shape) for member in adapters],
        out_specs=[tile, tile, turned] + [whole(member.shape) for member in out_shape[3:]],
        out_shape=out_shape,
        scratch_shapes=[
            pltpu.VMEM((MIDDLE_ROWS, FF), BF16),
            pltpu.VMEM((MIDDLE_ROWS, FF), BF16),
            pltpu.VMEM((MIDDLE_ROWS, FF), F32),
            pltpu.VMEM((MIDDLE_ROWS, FF), BF16),
            pltpu.VMEM((MIDDLE_ROWS, D), F32),
            pltpu.VMEM(w_in.shape, BF16),
            pltpu.VMEM(w_down.shape, BF16),
            pltpu.SemaphoreType.DMA((2,)),
        ],
        compiler_params=params(),
        name="middle_part",
    )(length_valid, ot, x, cot, gain, w_out, w_in, w_down, *adapters)


def attend_back(
    pair,
    length_ref,
    off_ref,
    qt_ref,
    k_ref,
    kt_ref,
    v_ref,
    ot_ref,
    gt_ref,
    lse_ref,
    grads_ref,
    table,
    key_more,
    weights_all,
    grads_all,
):
    length = k_ref.shape[0]
    lane = lane_iota((1, LANES))
    first_lanes = lane < HDIM
    grad_query_parts = []
    for odd in range(2):
        half = slice(odd * HDIM, (odd + 1) * HDIM)
        table[odd] = bias_table(off_ref[pl.ds(2 * pair + odd, 1), :], length)
        keys = k_ref[...] * head_lanes(odd) + key_more[odd]
        place = lane - (0 if odd else HDIM)
        value_more = ((place >= 0) & (place < 3)).astype(F32).astype(BF16)
        values = v_ref[...] * head_lanes(odd) + value_more
        ones = jnp.ones((1, length), F32)
        lse = lse_ref[0, odd : odd + 1, :]
        queries = join_rows(
            qt_ref[half, :], extra_rows([ones] + [-part for part in split_three(lse)]), odd
        )
        delta = jnp.sum(
            ot_ref[half, :].astype(F32) * gt_ref[half, :].astype(F32), axis=0, keepdims=True
        )
        grads = join_rows(
            gt_ref[half, :], extra_rows([-part for part in split_three(delta)]), odd
        )
        query_blocks = []
        previous = None
        for start in range(0, length, QBLOCK):
            columns = slice(start, start + QBLOCK)
            raw = dot(keys, queries[:, columns])
            grad_raw = dot(values, grads[:, columns])
            if previous is not None:
                query_blocks.append(dot(kt_ref[half, :], previous))
            weights = jnp.exp2(add_bias(raw, table.at[odd], start, length))
            weights_all[:, columns] = weights.astype(BF16)
            previous = (weights * grad_raw).astype(BF16)
            grads_all[:, columns] = previous
        query_blocks.append(dot(kt_ref[half, :], previous))
        grad_query_parts.append(jnp.concatenate(query_blocks, axis=1) * 0.125)
        grad_values = dot_nt(weights_all[...], gt_ref[...])
        grad_keys = dot_nt(grads_all[...], qt_ref[...]) * LN2
        if odd:
            grad_values = jnp.where(first_lanes, even_values, grad_values)
            grad_keys = jnp.where(first_lanes, even_keys, grad_keys)
        else:
            even_values, even_keys = grad_values, grad_keys
    columns = pl.ds(pl.multiple_of(pair * LANES, LANES), LANES)
    grads_ref[0, :, columns] = jnp.concatenate(grad_query_parts, axis=0).T.astype(BF16)
    grads_ref[1, :, columns] = grad_keys.astype(BF16)
    grads_ref[2, :, columns] = grad_values.astype(BF16)


def project_back(
    tile, x_ref, gain_ref, w_ref, ar_ref, b_ref, zg_ref, grads_ref, dmid_ref, out_ref, dar_ref, db_ref
):
    values = x_ref[...].astype(F32)
    gain = gain_ref[...].reshape(1, D)
    inverse = rms_inverse(values)
    normed = (values * inverse * gain).astype(BF16)
    lowrank = zg_ref[: 3 * COLS]
    gates = zg_ref[3 * COLS :]
    mixed = pad_rows(lowrank * gates, LANES).astype(BF16)
    rows = pl.ds(pl.multiple_of(tile * ROWS, ROWS), ROWS)
    grads = [grads_ref[index, rows] for index in range(3)]
    columns = [slice(index * D, (index + 1) * D) for index in range(3)]
    grad_mixed = jnp.zeros((ROWS, LANES), F32)
    for grad, lanes in zip(grads, columns):
        grad_mixed = grad_mixed + dot_nt(grad, b_ref[:, lanes])
    grad_normed = jnp.zeros((ROWS, D), F32)
    for grad, lanes in zip(grads, columns):
        grad_normed = grad_normed + dot_nt(grad, w_ref[:, lanes])
    turned = grad_mixed.T
    for grad, lanes in zip(grads, columns):
        db_ref[:, lanes] += dot(mixed, grad)
    parts = []
    for first in range(0, 3 * COLS, COLS):
        place = slice(first, first + COLS)
        parts.append(gate_grads(turned[place], lowrank[place], gates[place]))
    delta = jnp.concatenate([part[0] for part in parts] + [part[1] for part in parts], axis=0)
    delta = pad_rows(delta, 2 * LANES).astype(BF16)
    grad_normed = grad_normed + dot_nt(delta.T, ar_ref[...])
    dar_ref[...] += dot(delta, normed)
    out_ref[...] = dmid_ref[...] + rms_backward(values, gain, inverse, grad_normed)


def back_kernel(*refs):
    length_ref = refs[0]
    heads_refs = refs[:9]
    x_ref, gain_ref, w_hbm, ar_ref, b_ref, zg_ref, dmid_ref = refs[9:16]
    out_ref, dar_ref, db_ref = refs[16:19]
    table, key_more, weights_all, grads_all, grads_ref, w_ref, loaded = refs[19:]
    step = pl.program_id(0)
    pairs = HEADS // 2
    load = pltpu.make_async_copy(w_hbm, w_ref, loaded)

    @pl.when(step == 0)
    def _():
        load.start()
        dar_ref[...] = jnp.zeros_like(dar_ref)
        db_ref[...] = jnp.zeros_like(db_ref)
        for odd in range(2):
            key_more[odd] = key_extras(length_ref, key_more.shape[1:], odd)

    @pl.when(step < pairs)
    def _():
        attend_back(step, *heads_refs, grads_ref, table, key_more, weights_all, grads_all)

    @pl.when(step == pairs)
    def _():
        load.wait()

    @pl.when(step >= pairs)
    def _():
        project_back(
            step - pairs,
            x_ref,
            gain_ref,
            w_ref,
            ar_ref,
            b_ref,
            zg_ref,
            grads_ref,
            dmid_ref,
            out_ref,
            dar_ref,
            db_ref,
        )


def back_part(
    length_valid, offsets, qt, k, kt, v, ot, gt, lse, x, gain, w_qkv, ar_qkv, b_qkv, zg, dmid
):
    length = k.shape[0]
    pairs = HEADS // 2

    def pair_of(i):
        return jnp.minimum(i, pairs - 1)

    def tile_of(i):
        return jnp.maximum(i - pairs, 0)

    turned = pl.BlockSpec((LANES, length), lambda i: (pair_of(i), 0))
    natural = pl.BlockSpec((length, LANES), lambda i: (0, pair_of(i)))
    tile = pl.BlockSpec((ROWS, D), lambda i: (tile_of(i), 0))
    out_shape = [
        jax.ShapeDtypeStruct((length, D), F32),
        jax.ShapeDtypeStruct((2 * LANES, D), F32),
        jax.ShapeDtypeStruct((LANES, 3 * D), F32),
    ]
    return pl.pallas_call(
        back_kernel,
        grid=(pairs + length // ROWS,),
        in_specs=[
            pl.BlockSpec(memory_space=pltpu.SMEM),
            whole(offsets.shape),
            turned,
            natural,
            turned,
            natural,
            turned,
            turned,
            pl.BlockSpec((1, 2, length), lambda i: (pair_of(i), 0, 0)),
            tile,
            whole((D,)),
            pl.BlockSpec(memory_space=pl.ANY),
            whole(ar_qkv.shape),
            whole(b_qkv.shape),
            pl.BlockSpec((6 * COLS, ROWS), lambda i: (0, tile_of(i))),
            tile,
        ],
        out_specs=[tile] + [whole(member.shape) for member in out_shape[1:]],
        out_shape=out_shape,
        scratch_shapes=[
            pltpu.VMEM((2, LANES, 2 * length), F32),
            pltpu.VMEM((2, length, LANES), BF16),
            pltpu.VMEM((length, length), BF16),
            pltpu.VMEM((length, length), BF16),
            pltpu.VMEM((3, length, D), BF16),
            pltpu.VMEM(w_qkv.shape, BF16),
            pltpu.SemaphoreType.DMA,
        ],
        compiler_params=params(),
        name="back_part",
    )(length_valid, offsets, qt, k, kt, v, ot, gt, lse, x, gain, w_qkv, ar_qkv, b_qkv, zg, dmid)


PARAM_ROWS = sum((COLS + EXPERTS) * fan_in + COLS * fan_out for fan_in, fan_out in FANS) // LANES


def piece_rows():
    result = []
    row = 0
    for fan_in, fan_out in FANS:
        starts = []
        for count in (fan_in * COLS, COLS * fan_out, fan_in * EXPERTS):
            starts.append(row)
            row += count // LANES
        result.append(tuple(starts))
    return result


def shard_rows(count):
    return -(-count // (LANES * 16)) * 16


def align_in(flat_ref, shard, start):
    first, shift = divmod(start, LANES)
    rows = shard.shape[0]
    if shift == 0:
        flat_ref[first : first + rows] = shard
        return
    turned = pltpu.roll(shard, shift, 1)
    lane = lane_iota((1, LANES))
    zeros = jnp.zeros((8, LANES), F32)
    upper = jnp.concatenate([turned, zeros], axis=0)
    lower = pltpu.roll(upper, 1, 0)
    kept = flat_ref[first : first + 8]
    merged = jnp.where(lane >= shift, upper, lower)
    inside = (row_iota((8, LANES)) == 0) & (lane_iota((8, LANES)) < shift)
    flat_ref[first : first + 8] = jnp.where(inside, kept, merged[:8])
    flat_ref[first + 8 : first + 8 + rows] = merged[8:]


def align_out(flat_ref, rows, start):
    first, shift = divmod(start, LANES)
    if shift == 0:
        return flat_ref[first : first + rows]
    block = flat_ref[first : first + rows + 8]
    turned = pltpu.roll(block, LANES - shift, 1)
    below = pltpu.roll(turned, rows + 7, 0)
    lane = lane_iota((1, LANES))
    return jnp.where(lane < LANES - shift, turned, below)[:rows]


GROUP = 64


def narrow_to_rows(flat_ref, fan_in, items, out_ref, begin=0):
    groups = fan_in // GROUP
    lane = lane_iota((1, LANES))
    lines = [
        [
            flat_ref[pl.ds(base + k, groups, stride=width * GROUP // LANES), :]
            for k in range(width * GROUP // LANES)
        ]
        for base, width, _ in items
    ]
    for b in range(GROUP):
        result = jnp.zeros((groups, LANES), F32)
        for line, (_, width, place) in zip(lines, items):
            first, shift = divmod(width * b, LANES)
            amount = (place - shift) % LANES
            value = line[first] if amount == 0 else pltpu.roll(line[first], amount, 1)
            if shift + width > LANES:
                value = jnp.where(
                    lane < place + LANES - shift, value, pltpu.roll(line[first + 1], amount, 1)
                )
            inside = (lane >= place) & (lane < place + width)
            result = jnp.where(inside, value, result)
        out_ref[pl.ds(begin + b, groups, stride=GROUP), :] = result


def rows_to_narrow(in_ref, fan_in, items, flat_ref, begin=0):
    groups = fan_in // GROUP
    lane = lane_iota((1, LANES))
    lines = [
        [jnp.zeros((groups, LANES), F32) for _ in range(width * GROUP // LANES)]
        for _, width, _ in items
    ]
    for b in range(GROUP):
        source = in_ref[pl.ds(begin + b, groups, stride=GROUP), :]
        for line, (_, width, place) in zip(lines, items):
            first, shift = divmod(width * b, LANES)
            amount = (shift - place) % LANES
            value = source if amount == 0 else pltpu.roll(source, amount, 1)
            inside = (lane >= shift) & (lane < shift + width)
            line[first] = jnp.where(inside, value, line[first])
            if shift + width > LANES:
                line[first + 1] = jnp.where(lane < shift + width - LANES, value, line[first + 1])
    for line, (base, width, _) in zip(lines, items):
        for k, value in enumerate(line):
            flat_ref[pl.ds(base + k, groups, stride=width * GROUP // LANES), :] = value


def single_items(block):
    starts = piece_rows()
    after_out, after_in = (block + 4) // 5, (block + 2) // 4
    down = (block - 2) * after_in
    bases = []
    for piece, width in ((0, COLS), (2, EXPERTS)):
        out, inner, outer = (starts[index][piece] for index in range(3, 6))
        base = out + (inner - out) * after_out + (outer - inner) * after_in
        bases.append(base + down * (D * width // LANES))
    return [(bases[0], COLS, 0), (bases[1], EXPERTS, COLS)]


SINGLE_BLOCKS = 2 + FF // D


def spread_matrix(experts, source, place):
    row = row_iota((LANES, LANES)) - source
    lane = lane_iota((LANES, LANES)) - place
    hit = (lane >= RANK * row) & (lane < RANK * row + RANK) & (row >= 0) & (row < experts)
    return jnp.where(hit, 1.0, 0.0)


def keep_matrix():
    row = row_iota((LANES, LANES))
    return jnp.where((row == lane_iota((LANES, LANES))) & (row < COLS), 1.0, 0.0)


FIRST_COUNT = sum((COLS + EXPERTS) * fan_in + COLS * fan_out for fan_in, fan_out in FANS[:3])


def unpack_ups(flat, base, fan_out, first, out_ref, column):
    width = fan_out // LANES
    above = jnp.zeros((first, LANES), F32)
    below = jnp.zeros((LANES - COLS - first, LANES), F32)
    for k in range(width):
        part = flat[pl.ds(base + k, COLS, stride=width), :]
        parts = [part, below] if first == 0 else [above, part, below]
        lanes = slice(column + k * LANES, column + (k + 1) * LANES)
        out_ref[:, lanes] = jnp.concatenate(parts, axis=0).astype(BF16)


def unpack_first(flat, ar_ref, b_ref, down, router):
    starts = piece_rows()
    narrow_to_rows(flat, D, [(starts[k][0], COLS, k * COLS) for k in range(3)], down)
    narrow_to_rows(flat, D, [(starts[k][2], EXPERTS, k * EXPERTS) for k in range(3)], router)
    routers = router[...].astype(BF16)
    for half in range(2):
        matrix = spread_matrix(3 * EXPERTS, 0, 3 * COLS - half * LANES).astype(BF16)
        packed = dot(routers, matrix)
        packed = packed if half else packed + down[...]
        ar_ref[:, half * LANES : (half + 1) * LANES] = packed.astype(BF16)
    for index in range(3):
        unpack_ups(flat, starts[index][1], D, index * COLS, b_ref, index * D)


def flat_rows(count):
    return PARAM_ROWS + shard_rows(count) + 20


def unpack_rest(flat, outs, work):
    starts = piece_rows()
    matrix = (keep_matrix() + spread_matrix(EXPERTS, COLS, COLS)).astype(BF16)

    def block(index, _):
        narrow_to_rows(flat, D, single_items(index), work, index * D)
        return 0

    lax.fori_loop(0, SINGLE_BLOCKS, block, 0)
    begin = 0
    for index in range(3, 6):
        fan_in, fan_out = FANS[index]
        ar_ref, b_ref = outs[2 * index - 6], outs[2 * index - 5]
        ar_ref[...] = dot(work[begin : begin + fan_in].astype(BF16), matrix).astype(BF16)
        unpack_ups(flat, starts[index][1], fan_out, 0, b_ref, 0)
        begin += fan_in


def split_dot(value, matrix):
    high = value.astype(BF16)
    return dot(high, matrix) + dot((value - high.astype(F32)).astype(BF16), matrix)


def first_of_four(experts, source, place):
    row = row_iota((LANES, LANES)) - source
    lane = lane_iota((LANES, LANES)) - place
    hit = (row == RANK * lane) & (lane >= 0) & (lane < experts)
    return jnp.where(hit, 1.0, 0.0)


def assemble_ups(flat, base, fan_out, first, grad_ref, column):
    width = fan_out // LANES
    for k in range(width):
        lanes = slice(column + k * LANES, column + (k + 1) * LANES)
        flat[pl.ds(base + k, COLS, stride=width), :] = grad_ref[first : first + COLS, lanes]


def assemble_rest(flat, grads, work):
    starts = piece_rows()
    matrix = (keep_matrix() + first_of_four(EXPERTS, COLS, COLS)).astype(BF16)
    begin = 0
    for index in range(3, 6):
        fan_in, fan_out = FANS[index]
        dar_ref, db_ref = grads[2 * index - 6], grads[2 * index - 5]
        work[begin : begin + fan_in] = split_dot(pad_rows(dar_ref[...], LANES).T, matrix)
        assemble_ups(flat, starts[index][1], fan_out, 0, db_ref, 0)
        begin += fan_in

    def block(index, _):
        rows_to_narrow(work, D, single_items(index), flat, index * D)
        return 0

    lax.fori_loop(0, SINGLE_BLOCKS, block, 0)


def assemble_first(flat, dar_ref, db_ref, down, router):
    starts = piece_rows()
    down[...] = dar_ref[:LANES].T
    rows_to_narrow(down, D, [(starts[k][0], COLS, k * COLS) for k in range(3)], flat)
    first_router = 3 * COLS
    turned = dar_ref[first_router : first_router + LANES].T
    router[...] = split_dot(turned, first_of_four(3 * EXPERTS, 0, 0).astype(BF16))
    rows_to_narrow(router, D, [(starts[k][2], EXPERTS, k * EXPERTS) for k in range(3)], flat)
    for index in range(3):
        assemble_ups(flat, starts[index][1], D, index * COLS, db_ref, index * D)


MESH = pl.DeviceIdType.MESH


def place_of(axes, sizes):
    me = lax.axis_index(axes[0]) * sizes[1] + lax.axis_index(axes[1])

    def coordinates(number):
        return (number // sizes[1], number % sizes[1])

    return me, coordinates


def partners_of(me):
    low = me % 8
    core = low % 2
    y = (low // 2) % 2
    x = low // 4
    over_x = low + 4 * (1 - 2 * x)
    over_y = low + 2 * (1 - 2 * y)
    first = over_x * (1 - core) + over_y * core
    second = over_y * (1 - core) + over_x * core
    both = first + second - low
    other = 1 - 2 * core
    return low, first, second, both, other, over_x, over_y


def greet(peers):
    for peer in peers:
        pl.semaphore_signal(
            pltpu.get_barrier_semaphore(), inc=1, device_id=peer, device_id_type=MESH
        )


def await_greetings(count):
    pl.semaphore_wait(pltpu.get_barrier_semaphore(), count)


class Ring:
    def __init__(self, axes, sizes, send, receive):
        self.me, self.coordinates = place_of(axes, sizes)
        self.groups = sizes[0] * sizes[1] // 8
        self.group = self.me // 8
        places = partners_of(self.me)
        self.low, self.first, self.second, self.both, self.other, self.over_x, self.over_y = places
        self.mate = self.low + self.other
        self.send, self.receive = send, receive
        self.copies = {}

    def device(self, group, low):
        return self.coordinates(group * 8 + low)

    def greet(self):
        peers = [
            self.device((self.group + step) % self.groups, self.low)
            for step in range(1, self.groups)
        ]
        peers += [self.device(self.group, low) for low in (self.first, self.second, self.mate)]
        greet(peers)

    def await_greetings(self):
        await_greetings(self.groups + 2)

    def copy(self, slot, source, target, peer, arrival=None):
        return pltpu.make_async_remote_copy(
            src_ref=source,
            dst_ref=target,
            send_sem=self.send.at[slot],
            recv_sem=self.receive.at[slot if arrival is None else arrival],
            device_id=peer,
            device_id_type=MESH,
        )


def gather_phases(ring, span, shard_ref, out_ref, local, greets):
    begin, end = span
    base = ring.groups
    inside = (ring.group >= begin) & (ring.group < end)

    def around(step):
        target = (ring.group + step) % ring.groups
        return ring.copy(
            step,
            shard_ref,
            out_ref.at[ring.group - begin, ring.low],
            ring.device(target, ring.low),
            base + 7 + ring.group,
        )

    def arrived(group):
        return ring.copy(
            0,
            shard_ref,
            out_ref.at[group - begin, ring.low],
            ring.device(group, ring.low),
            base + 7 + group,
        )

    def push(slot, part, partner):
        return ring.copy(
            base + slot, out_ref.at[:, part], out_ref.at[:, part], ring.device(ring.group, partner)
        )

    one = push(0, ring.low, ring.first)
    two = push(1, ring.low, ring.second)
    three = push(2, ring.first, ring.second)
    cores = [
        push(3 + index, part, ring.mate)
        for index, part in enumerate((ring.low, ring.first, ring.second, ring.both))
    ]

    def own():
        return pltpu.make_async_copy(
            shard_ref, out_ref.at[ring.group - begin, ring.low], local
        )

    def phase0():
        if greets:
            ring.greet()
            ring.await_greetings()

        @pl.when(inside)
        def _():
            own().start()
            for step in range(1, ring.groups):
                around(step).start()

    def phase1():
        @pl.when(inside)
        def _():
            own().wait()
            for step in range(1, ring.groups):
                around(step).wait_send()

        for group in range(begin, end):

            @pl.when(ring.group != group)
            def _():
                arrived(group).wait_recv()

        for copy in (one, two, cores[0]):
            copy.start()

    def phase2():
        one.wait()
        three.start()
        cores[1].start()

    def phase3():
        two.wait()
        cores[2].start()
        three.wait()
        cores[3].start()

    def phase4():
        for copy in cores:
            copy.wait()

    return phase0, phase1, phase2, phase3, phase4


def gather_semaphores(groups):
    return [
        pltpu.SemaphoreType.DMA((groups + 7,)),
        pltpu.SemaphoreType.DMA((2 * groups + 7,)),
        pltpu.SemaphoreType.DMA,
    ]


def start_kernel(
    link,
    count,
    values_ref,
    buckets_ref,
    table_ref,
    gain_ref,
    x_hbm,
    w_hbm,
    *refs,
):
    hbm_outs, off_ref, ar_ref, b_ref = refs[:6], refs[6], refs[7], refs[8]
    rest_refs = refs[9:15]
    x_ref, w_ref, normed, dense = refs[15:19]
    outs = refs[19:25]
    qt_ref, k_ref, kt_ref, v_ref, vt_ref, zg_ref = outs
    flat, down, router, work, offsets_ref, shard_ref, loaded, stored, *more = refs[25:]
    loads = [
        pltpu.make_async_copy(x_hbm, x_ref, loaded.at[0]),
        pltpu.make_async_copy(w_hbm, w_ref, loaded.at[1]),
    ]
    stores = [
        pltpu.make_async_copy(source, target, stored.at[index])
        for index, (source, target) in enumerate(zip(outs, hbm_outs))
    ]
    for load in loads:
        load.start()
    values = values_ref[...].astype(F32)
    values = jnp.pad(values, (0, shard_ref.shape[0] * LANES - count))
    shard_ref[...] = values.reshape(shard_ref.shape).astype(BF16)
    if link is None:
        first = [lambda: None] * 5
        rest = first

        def shard_of(index):
            return shard_ref[...]
    else:
        axes, sizes, spans = link
        land_a, land_b, *sems = more
        first = gather_phases(
            Ring(axes, sizes, *sems[:2]), spans[0], shard_ref, land_a, sems[2], True
        )
        rest = gather_phases(
            Ring(axes, sizes, *sems[3:5]), spans[1], shard_ref, land_b, sems[5], False
        )

        def shard_of(index):
            group, low = divmod(index, 8)
            begin = spans[1][0]
            return land_a[group, low] if group < begin else land_b[group - begin, low]

    length = x_ref.shape[0]

    def dense_tile(index):
        rows = slice(index * length // 2, (index + 1) * length // 2)
        values = x_ref[rows].astype(F32)
        low = (values * rms_inverse(values) * gain_ref[...].reshape(1, D)).astype(BF16)
        normed[rows] = low

        def columns(part, _):
            lanes = pl.ds(pl.multiple_of(part * D, D), D)
            dense[rows, lanes] = dot(normed[rows], w_ref[:, lanes])
            return 0

        lax.fori_loop(0, 3, columns, 0)

    def project():
        packed = dot(normed[...], ar_ref[...]).T
        lowrank = packed[: 3 * COLS]
        gates = jnp.concatenate(
            [gates_of(packed[place : place + COLS]) for place in range(3 * COLS, 6 * COLS, COLS)],
            axis=0,
        )
        zg_ref[: 3 * COLS] = lowrank
        zg_ref[3 * COLS :] = gates
        stores[5].start()
        mixed = pad_rows(lowrank * gates, LANES).astype(BF16).T
        for part in range(3):
            columns = slice(part * D, (part + 1) * D)
            value = dense[:, columns] + dot(mixed, b_ref[:, columns])
            if part == 0:
                qt_ref[...] = (value * QUERY_SCALE).astype(BF16).T
                stores[0].start()
            else:
                low = value.astype(BF16)
                natural, turned = ((k_ref, kt_ref), (v_ref, vt_ref))[part - 1]
                natural[...] = low
                turned[...] = low.T
                stores[2 * part - 1].start()
                stores[2 * part].start()

    first[0]()
    rest[0]()
    for load in loads:
        load.wait()
    dense_tile(0)
    first[1]()
    rest[1]()
    dense_tile(1)
    first[2]()
    buckets = buckets_ref[...].reshape(1, buckets_ref.shape[0])
    hits = jnp.where(row_iota((table_ref.shape[1], buckets.shape[1])) == buckets, LOG2E, 0.0)
    offsets_ref[...] = jnp.zeros_like(offsets_ref)
    offsets_ref[:, : buckets.shape[1]] = exact_dot(table_ref[...], hits)
    flip = (row_iota((LANES, LANES)) + lane_iota((LANES, LANES)) == LANES - 1).astype(F32)
    blocks = offsets_ref.shape[1] // LANES
    for block in range(blocks):
        lanes = slice(block * LANES, (block + 1) * LANES)
        turned = slice((blocks - 1 - block) * LANES, (blocks - block) * LANES)
        off_ref[:, turned] = exact_dot(offsets_ref[:, lanes], flip)
    off_ref[...] = pltpu.roll(off_ref[...], offsets_ref.shape[1] - 1, 1)
    first[3]()
    rest[2]()
    first[4]()
    for index in range(-(-FIRST_COUNT // count)):
        align_in(flat, shard_of(index).astype(F32), index * count)
    unpack_first(flat, ar_ref, b_ref, down, router)
    rest[3]()
    project()
    rest[4]()
    for index in range(FIRST_COUNT // count, PARAM_ROWS * LANES // count):
        align_in(flat, shard_of(index).astype(F32), index * count)
    unpack_rest(flat, rest_refs, work)
    for store in stores:
        store.wait()


def start(x, gain, w_qkv, shard, buckets, rel_table, count, axes, sizes, spans):
    length = x.shape[0]
    groups = sizes[0] * sizes[1] // 8
    link = (axes, sizes, spans) if groups else None
    rest_shapes = [
        shape for fan_in, fan_out in FANS[3:] for shape in ((fan_in, LANES), (LANES, fan_out))
    ]
    wide = [
        ((D, length), BF16),
        ((length, D), BF16),
        ((D, length), BF16),
        ((length, D), BF16),
        ((D, length), BF16),
        ((6 * COLS, length), F32),
    ]
    small = [
        ((HEADS, 2 * length), F32),
        ((D, 2 * LANES), BF16),
        ((LANES, 3 * D), BF16),
    ] + [(shape, BF16) for shape in rest_shapes]
    scratch = [
        pltpu.VMEM(x.shape, BF16),
        pltpu.VMEM(w_qkv.shape, BF16),
        pltpu.VMEM(x.shape, BF16),
        pltpu.VMEM((length, 3 * D), F32),
    ]
    scratch += [pltpu.VMEM(*member) for member in wide]
    scratch += [
        pltpu.VMEM((flat_rows(count), LANES), F32),
        pltpu.VMEM((D, LANES), F32),
        pltpu.VMEM((D, LANES), F32),
        pltpu.VMEM((SINGLE_BLOCKS * D, LANES), F32),
        pltpu.VMEM((HEADS, 2 * length), F32),
        pltpu.VMEM((shard_rows(count), LANES), BF16),
        pltpu.SemaphoreType.DMA((2,)),
        pltpu.SemaphoreType.DMA((len(wide),)),
    ]
    if link:
        rows = shard_rows(count)
        scratch += [pltpu.VMEM((end - begin, 8, rows, LANES), BF16) for begin, end in spans]
        scratch += gather_semaphores(groups) * 2
    vmem = pl.BlockSpec(memory_space=pltpu.VMEM)
    anywhere = pl.BlockSpec(memory_space=pl.ANY)
    return pl.pallas_call(
        functools.partial(start_kernel, link, count),
        in_specs=[vmem] * 4 + [anywhere] * 2,
        out_specs=[anywhere] * len(wide) + [vmem] * len(small),
        out_shape=[jax.ShapeDtypeStruct(*member) for member in wide + small],
        scratch_shapes=scratch,
        compiler_params=params(collective_id=0, has_side_effects=True) if link else params(),
        name="start",
    )(shard, buckets, rel_table, gain, x, w_qkv)


def reduce_phases(ring, span, parts_ref, boxes, greets, sums_ref=None, sum_boxes=None):
    begin, end = span
    outbox, inbox, half, own, far_out, far_in, out_ref = boxes
    groups = ring.groups
    inside = (ring.group >= begin) & (ring.group < end)
    core_parts = (ring.first, ring.both, ring.second, ring.low)
    near = [ring.mate] * 4 + [ring.second, ring.second, ring.first]

    def push(slot):
        return ring.copy(slot, outbox.at[slot], inbox.at[slot], ring.device(ring.group, near[slot]))

    def fill(slot, value):
        outbox[slot] = value.astype(BF16)
        push(slot).start()

    def around(group):
        return ring.copy(
            7 + group - begin,
            far_out.at[group - begin],
            far_in.at[ring.group],
            ring.device(group, ring.low),
            7 + ring.group,
        )

    def arrived(group):
        return ring.copy(
            7,
            far_out.at[0],
            far_in.at[group],
            ring.device(group, ring.low),
            7 + group,
        )

    base = 7 + groups
    sum_peers = (ring.mate, ring.over_x, ring.over_y)

    def push_sums(slot):
        near_out, near_in = sum_boxes
        return ring.copy(
            base + slot,
            near_out.at[slot],
            near_in.at[slot],
            ring.device(ring.group, sum_peers[slot]),
        )

    def around_sums(step):
        near_out, near_in = sum_boxes
        target = (ring.group + step) % groups
        return ring.copy(
            base + 2 + step,
            near_out.at[3],
            near_in.at[3 + ring.group],
            ring.device(target, ring.low),
        )

    def start_sums(slot, value):
        if sum_boxes is not None:
            sum_boxes[0][slot] = value
            push_sums(slot).start()

    def phase0():
        if greets:
            ring.await_greetings()
        if sum_boxes is not None:
            start_sums(0, sums_ref[...])
        for slot, part in enumerate(core_parts):
            fill(slot, parts_ref[:, part + ring.other])

    def phase1():
        push(0).wait()
        fill(4, parts_ref[:, ring.second] + inbox[0].astype(F32))
        push(1).wait()
        fill(5, parts_ref[:, ring.both] + inbox[1].astype(F32))
        if sum_boxes is not None:
            push_sums(0).wait()
            start_sums(1, sum_boxes[0][0] + sum_boxes[1][0])

    def add1():
        push(2).wait()
        half[...] = parts_ref[:, ring.first] + inbox[2].astype(F32)
        push(3).wait()
        own[...] = parts_ref[:, ring.low] + inbox[3].astype(F32)

    def phase2():
        push(5).wait()
        fill(6, half[...] + inbox[5].astype(F32))
        if sum_boxes is not None:
            push_sums(1).wait()
            start_sums(2, sum_boxes[0][1] + sum_boxes[1][1])

    def add2():
        push(4).wait()
        own[...] = own[...] + inbox[4].astype(F32)

    def phase3():
        push(6).wait()
        own[...] = own[...] + inbox[6].astype(F32)
        far_out[...] = own[...].astype(BF16)
        for group in range(begin, end):

            @pl.when(ring.group != group)
            def _():
                around(group).start()

        if sum_boxes is not None:
            near_out, near_in = sum_boxes
            push_sums(2).wait()
            near_out[3] = near_out[2] + near_in[2]
            for step in range(1, groups):
                around_sums(step).start()
            near_in[3 + ring.group] = near_out[3]

    def phase4(finish_sums=None):
        for group in range(begin, end):

            @pl.when(ring.group != group)
            def _():
                around(group).wait_send()

        @pl.when(inside)
        def _():
            for group in range(groups):

                @pl.when(ring.group != group)
                def _():
                    arrived(group).wait_recv()

            total = own[ring.group - begin]
            for step in range(1, groups):
                total = total + far_in[(ring.group + step) % groups].astype(F32)
            out_ref[...] = total

        if sum_boxes is not None:
            near_out, near_in = sum_boxes
            for step in range(1, groups):
                around_sums(step).wait()
            whole_sum = near_in[3]
            for index in range(1, groups):
                whole_sum = whole_sum + near_in[3 + index]
            finish_sums(whole_sum)

    return phase0, phase1, add1, phase2, add2, phase3, phase4


def reduce_scratch(groups, count, rows):
    return [
        pltpu.VMEM((7, count, rows, LANES), BF16),
        pltpu.VMEM((7, count, rows, LANES), BF16),
        pltpu.VMEM((count, rows, LANES), F32),
        pltpu.VMEM((count, rows, LANES), F32),
        pltpu.VMEM((count, rows, LANES), BF16),
        pltpu.VMEM((groups, rows, LANES), BF16),
    ]


def finish_kernel(link, count, dar_ref, db_ref, *refs):
    grads, sums_ref = refs[:6], refs[6]
    out_ref, roots_ref, flat, down, router, work, *more = refs[7:]

    def finish_sums(total):
        roots_ref[...] = jnp.sqrt(total / (total[:, 4:5] * D))[0, :4]

    if link is not None:
        axes, sizes, spans = link
        parts_a, parts_b, near_out, near_in, *more = more
        boxes_a, boxes_b, sems = more[:7], more[7:14], more[14:]
        ring = Ring(axes, sizes, sems[0], sems[1])
        ring.greet()
    assemble_rest(flat, grads, work)
    if link is None:
        assemble_first(flat, dar_ref, db_ref, down, router)
        out_ref[...] = align_out(flat, shard_rows(count), 0).reshape(-1)[:count]
        finish_sums(sums_ref[...])
        return
    rows = shard_rows(count)
    split = spans[1][0]

    def align(parts, span):
        for group in range(*span):
            for low in range(8):
                parts[group - span[0], low] = align_out(flat, rows, (8 * group + low) * count)

    rest = reduce_phases(ring, spans[1], parts_b, boxes_b, True, sums_ref, (near_out, near_in))
    first = reduce_phases(
        Ring(axes, sizes, sems[2], sems[3]), spans[0], parts_a, boxes_a, False
    )
    align(parts_b, spans[1])
    rest[0]()
    assemble_first(flat, dar_ref, db_ref, down, router)
    rest[1]()
    align(parts_a, spans[0])
    first[0]()
    rest[2]()
    for step in (1, 2):
        first[step]()
    for step in (3, 4, 5):
        rest[step]()
        first[step]()
    rest[6](finish_sums)
    first[6]()

    @pl.when(ring.group < split)
    def _():
        out_ref[...] = boxes_a[6][...].reshape(-1)[:count]

    @pl.when(ring.group >= split)
    def _():
        out_ref[...] = boxes_b[6][...].reshape(-1)[:count]


def finish(dar, db, grads, sums, count, axes, sizes, spans):
    rows = shard_rows(count)
    groups = sizes[0] * sizes[1] // 8
    link = (axes, sizes, spans) if groups else None
    scratch = [
        pltpu.VMEM((flat_rows(count), LANES), F32),
        pltpu.VMEM((D, LANES), F32),
        pltpu.VMEM((D, LANES), F32),
        pltpu.VMEM((SINGLE_BLOCKS * D, LANES), F32),
    ]
    if link:
        widths = [end - begin for begin, end in spans]
        scratch += [pltpu.VMEM((width, 8, rows, LANES), F32) for width in widths]
        scratch += [
            pltpu.VMEM((4, *sums.shape), F32),
            pltpu.VMEM((3 + groups, *sums.shape), F32),
        ]
        for width in widths:
            scratch += reduce_scratch(groups, width, rows) + [pltpu.VMEM((rows, LANES), F32)]
        scratch += [pltpu.SemaphoreType.DMA((10 + 2 * groups,))] * 4
    vmem = pl.BlockSpec(memory_space=pltpu.VMEM)
    return pl.pallas_call(
        functools.partial(finish_kernel, link, count),
        in_specs=[vmem] * (3 + len(grads)),
        out_specs=[vmem] * 2,
        out_shape=[
            jax.ShapeDtypeStruct((count,), F32),
            jax.ShapeDtypeStruct((4,), F32),
        ],
        scratch_shapes=scratch,
        compiler_params=params(collective_id=1, has_side_effects=True) if link else params(),
        name="finish",
    )(dar, db, *grads, sums)


def deliver_kernel(grads_ref, roots_ref, grads_out, roots_out):
    grads_out[...] = grads_ref[...]
    roots_out[...] = roots_ref[...]


def deliver(grads, roots):
    vmem = pl.BlockSpec(memory_space=pltpu.VMEM)
    return pl.pallas_call(
        deliver_kernel,
        in_specs=[vmem] * 2,
        out_specs=[vmem] * 2,
        out_shape=[jax.ShapeDtypeStruct(member.shape, F32) for member in (grads, roots)],
        compiler_params=params(),
        name="deliver",
    )(grads, roots)


def per_device(
    tokens,
    lengths,
    buckets,
    rel_table,
    gain_attn,
    gain_ff,
    w_qkv,
    w_out,
    w_in,
    w_down,
    adapters,
    cotangent,
    axes,
    sizes,
):
    seq_count, length, width = tokens.shape
    x = tokens.reshape(length, width)
    cot = cotangent.reshape(length, width)
    devices = sizes[0] * sizes[1]
    count = adapters.shape[0]
    groups = devices // 8
    split_groups = min(-(-FIRST_COUNT // (8 * count)), max(groups - 1, 1))
    spans = ((0, split_groups), (split_groups, groups))
    qt, k, kt, v, vt, zg, offsets, ar_qkv, b_qkv, *packed = start(
        x, gain_attn, w_qkv, adapters, buckets, rel_table.T, count, axes, sizes, spans
    )
    ot, lse = attend(lengths, offsets, qt, k, kt, vt)
    block_out, dmid, gt, sums, *grads = middle_part(
        lengths, ot, x, cot, gain_ff, w_out, w_in, w_down, packed
    )
    tokens_grad, dar_qkv, db_qkv = back_part(
        lengths,
        offsets,
        qt,
        k,
        kt,
        v,
        ot,
        gt,
        lse,
        x,
        gain_attn,
        w_qkv,
        ar_qkv,
        b_qkv,
        zg,
        dmid,
    )
    mine, roots = deliver(
        *finish(dar_qkv, db_qkv, grads, sums, count, axes, sizes, spans)
    )
    grad_shard = mine
    root_squares = roots
    return (
        block_out.reshape(tokens.shape),
        tokens_grad.reshape(tokens.shape),
        grad_shard,
        root_squares,
    )


def solution(mesh):
    axes = tuple(mesh.axis_names)
    sizes = tuple(mesh.shape[axis] for axis in axes)
    sequence = P(axes, None, None)
    placed = (
        sequence,
        P(axes),
        P(),
        P(),
        P(),
        P(),
        P(),
        P(),
        P(),
        P(),
        P(axes),
        sequence,
    )
    return jax.shard_map(
        functools.partial(per_device, axes=axes, sizes=sizes),
        mesh=mesh,
        in_specs=placed,
        out_specs=(sequence, sequence, P(axes), P()),
        check_vma=False,
    )
```
